32 devices in a mesh: sec: 2 (over core), blk: 16 (over z, y, x).
Axes of the slice: x: 2, y: 2, z: 4, core: 2. Of those that a mesh axis runs over, the one named last changes fastest.
Arguments:
- surface_fields: bfloat16 [2, 3, 1024, 128], P('sec', None, 'blk'), may hold values from -6 to 6
- source_blocks: int32 [2, 1024, 4], P('sec', 'blk'), may hold values from 0 to 15, all different within a row; in each aligned block of 64 rows (0 to 63, 64 to 127, ..., all dimensions but the last counted through in order) at most 16 rows name the same one
- source_columns: int32 [2, 1024, 4], P('sec', 'blk'), may hold values from 0 to 63
- remap_weights: bfloat16 [2, 1024, 4, 128, 128], P('sec', 'blk'), may hold values from -0.25 to 0.25
- ocean_state: float32 [2, 80, 1024, 128], P(None, None, 'blk'), may hold values from -6 to 6
- bathymetry: int32 [1024, 128], P('blk'), may hold values from 1 to 80
Outputs:
- coupled_surface: float32 [2, 3, 1024, 128], P('sec', None, 'blk')
- ocean_tracers: float32 [2, 80, 1024, 128], P(None, None, 'blk')
The draws below stay inside these ranges and needn't reach their ends.
Inputs may be any that keep to these rules, and one draw needn't show every extreme that they name: `source_blocks`: A destination column's 4 sources lie in different blocks; among the 64 destination columns of one block, no block is named more than 16 times, and that count is reached.
All inputs are finite; a program needn't handle non-finite values.
Results may differ from the reference program's by a relative error of at most 0.00094.
Values may be sent and summed in bfloat16 or wider, within the bound.
No kernel may reach another device: no remote copies, remote signals or barrier semaphores. Data moves between devices by JAX's collectives and lax.ppermute only.
A program may use at most 128 MiB of HBM per device.

```python
import math
import jax
import jax.numpy as jnp
import numpy as np
from jax import lax

CX = 64
CY = 128
LEV = 80
NF = 3
K = 4
NSUB = 2
TILES = 1024
N_BLK = 16


def with_ends(array, own_key, low, top_value):
    longest = array.shape.index(max(array.shape))
    spots = []
    for shift in (0, 1):
        where = [jax.random.randint(jax.random.fold_in(own_key, axis), (), 0, length) for axis, length in enumerate(array.shape)]
        where[longest] = (where[longest] + shift) % array.shape[longest]
        spots.append(tuple(where))
    return array.at[spots[0]].set(low).at[spots[1]].set(top_value)


def block_levels(key, dims, split, smallest, high):
    def one(axis_at, blocks):
        steps = jax.random.uniform(jax.random.fold_in(jax.random.fold_in(key, 6), axis_at), (blocks,), jnp.float32, smallest / len(split), high / len(split))
        return jnp.repeat(jnp.exp(steps), dims[axis_at] // blocks).reshape((-1,) + (1,) * (len(dims) - axis_at - 1))

    gain = one(*split[0])
    for cut in split[1:]:
        gain = gain * one(*cut)
    return gain


def assign_block(own_key, own, number, rows, amount, top, most, lean):
    order = jax.random.permutation(own_key, amount)
    packed, common = load_shares(amount, rows * top, most, lean, True), load_shares(amount, rows * top, most, lean, False)
    places = jnp.arange(amount)

    def named(sizes, offset_by):
        used = int((sizes > 0).sum())
        fixed = max(1, used // 4)
        passed = fixed + (places - fixed + offset_by * (used - fixed)) % max(1, amount - fixed)
        return jnp.zeros((amount,), jnp.int32).at[order[jnp.where(places < fixed, places, passed)]].set(jnp.asarray(sizes, jnp.int32))

    sizes = jnp.where(number % 4 == 0, named(packed, number // 4), named(common, number - number // 4 - 1))
    mixed = jax.random.permutation(jax.random.fold_in(own, 3), amount)
    donor, taker = mixed[0:amount // 2 * 2:2], mixed[1:amount // 2 * 2:2]
    slack = jnp.minimum(sizes[donor] - 1, most - sizes[taker]) // 2
    slack = jnp.where((donor == order[0]) | (taker == order[0]) | (sizes[taker] == 0), 0, jnp.maximum(slack, 0))
    passed = jax.random.randint(jax.random.fold_in(own, 4), (amount // 2,), 0, 1 << 20) % (slack + 1)
    sizes = sizes.at[donor].add(-passed).at[taker].add(passed)
    members = jnp.searchsorted(jnp.cumsum(sizes), jnp.arange(rows * top), side="right").astype(jnp.int32)
    listing = members.reshape(top, rows).T
    listing = listing[jax.random.permutation(jax.random.fold_in(own, 1), rows)]
    offset_by = jax.random.randint(jax.random.fold_in(own, 2), (rows, 1), 0, top)
    return jnp.take_along_axis(listing, (jnp.arange(top)[None, :] + offset_by) % top, axis=1)


def load_shares(number_of, total, reach, lean, full):
    weights = [(1 << 20) // math.isqrt(grade ** lean) + 1 for grade in range(1, number_of + 1)]
    largest = reach if full else min(reach, max(-(-total // number_of), total * weights[0] // sum(weights)))
    least = 1 if total - largest >= number_of - 1 else 0
    holding, surplus = [largest] + [least] * (number_of - 1), total - largest - least * (number_of - 1)
    while surplus > 0:
        free = [i for i in range(1, number_of) if holding[i] < largest] or [i for i in range(1, number_of) if holding[i] < reach]
        pool, budget = sum([weights[i] for i in free]), surplus
        for i in free:
            extra = min(reach - holding[i], max(1, budget * weights[i] // pool), surplus)
            holding[i] = holding[i] + extra
            surplus = surplus - extra
    return np.array(holding)


def normal_values(stream_key, extent, width, most, split=(), kind=jnp.bfloat16):
    values = width * jax.random.normal(stream_key, extent, jnp.float32)
    if split:
        values = values * block_levels(stream_key, extent, split, -0.22, 0.18)
    return jnp.clip(values, -most, most).astype(kind)


def setup_inputs(seed: int = 0) -> dict:
    key_of = jax.random.split(jax.random.key(seed), 7)
    surface_fields = normal_values(key_of[0], (2, NF, TILES, CY), 1.0, 6.0, ((0, 2), (2, 16)))
    source_blocks_keys = jax.random.split(jax.random.fold_in(key_of[1], 1), 2 * TILES // CX)
    source_blocks_turns = jax.random.permutation(jax.random.fold_in(key_of[1], 3), 2 * TILES // CX)
    source_blocks = jax.vmap(lambda own, number: assign_block(jax.random.fold_in(key_of[1], 2), own, number, CX, N_BLK, K, CX // 4, 2))(source_blocks_keys, source_blocks_turns).reshape((2, TILES, K))
    source_columns = with_ends(jax.random.randint(key_of[2], (2, TILES, K), 0, CX), jax.random.fold_in(key_of[2], 1), 0, CX - 1).astype(jnp.int32)
    remap_weights = normal_values(key_of[3], (2, TILES, K, CY, CY), (K * CY) ** -0.5, 0.25, ((0, 2), (1, 16)))
    ocean_state = normal_values(key_of[4], (2, LEV, TILES, CY), 1.0, 6.0, ((2, 16),), jnp.float32)
    bathymetry = with_ends(jax.random.randint(key_of[5], (TILES, CY), 1, LEV + 1), jax.random.fold_in(key_of[5], 1), 1, LEV).astype(jnp.int32)
    return {"surface_fields": surface_fields, "source_blocks": source_blocks, "source_columns": source_columns, "remap_weights": remap_weights, "ocean_state": ocean_state, "bathymetry": bathymetry}


FLUX_GAIN = 0.5
SIDE_MIX = 0.2
TOP_MIX = 1.0
DEEP_MIX = 2.0


def remap(fields, block_map, column_map, weight_table):
    source = (block_map * CX + column_map).reshape(N_BLK, CX, K)
    tables = weight_table.reshape(N_BLK, CX, K, CY, CY)
    columns = jnp.transpose(fields, (1, 0, 2))

    def one_block(pair):
        source_block, table_block = pair
        chosen = columns[source_block].astype(jnp.float32)
        return jnp.einsum("xkij,xkfj->fxi", table_block.astype(jnp.float32), chosen)

    blocks = lax.map(one_block, (source, tables))
    return jnp.transpose(blocks, (1, 0, 2, 3)).reshape(fields.shape[0], N_BLK * CX, CY)


def side_mix(tracers, wet_mask):
    stacked = jnp.concatenate([tracers * wet_mask[None], wet_mask[None]], axis=0)
    sideways = jnp.roll(stacked, -1, axis=2) + jnp.roll(stacked, 1, axis=2)
    edged = jnp.pad(stacked, ((0, 0), (0, 0), (0, 0), (1, 1)))
    sideways = sideways + edged[:, :, :, 2:] + edged[:, :, :, :-2]
    return tracers + SIDE_MIX * wet_mask[None] * (sideways[:2] - sideways[2:3] * tracers)


def column_mix(tracers, wet_mask, heat_flux, fresh_flux, top_mix):
    levels = tracers.shape[1]
    forcing = jnp.stack([heat_flux, fresh_flux])
    links = []
    for layer_index in range(levels - 1):
        strength = top_mix if layer_index == 0 else DEEP_MIX
        links.append(strength * wet_mask[layer_index] * wet_mask[layer_index + 1])
    zero_field = jnp.zeros_like(heat_flux)
    ratios = []
    partials = []
    for layer_index in range(levels):
        upper_link = links[layer_index - 1] if layer_index > 0 else zero_field
        lower_link = links[layer_index] if layer_index < levels - 1 else zero_field
        source_term = tracers[:, layer_index]
        if layer_index == 0:
            source_term = source_term + FLUX_GAIN * forcing
            divisor = 1.0 + lower_link
            partial_value = source_term / divisor
        else:
            divisor = 1.0 + upper_link + lower_link - upper_link * ratios[-1]
            partial_value = (source_term + upper_link * partials[-1]) / divisor
        ratios.append(lower_link / divisor)
        partials.append(partial_value)
    solved = [partials[-1]]
    for layer_index in range(levels - 2, -1, -1):
        solved.append(partials[layer_index] + ratios[layer_index] * solved[-1])
    solved = solved[::-1]
    return jnp.stack(solved, axis=1)


def reference(surface_fields, source_blocks, source_columns, remap_weights, ocean_state, bathymetry):
    fluxes = remap(surface_fields[0], source_blocks[0], source_columns[0], remap_weights[0])
    start_stack = jnp.concatenate([ocean_state[:, 0].astype(jnp.bfloat16), surface_fields[1, 2:3]], axis=0)
    returned = remap(start_stack, source_blocks[1], source_columns[1], remap_weights[1])
    own_fluxes = surface_fields[1].astype(jnp.float32)
    levels = ocean_state.shape[1]
    wet_mask = (jnp.arange(levels, dtype=jnp.int32)[:, None, None] < bathymetry[None]).astype(jnp.float32)
    heat_flux = fluxes[0] + own_fluxes[0]
    fresh_flux = fluxes[1] + own_fluxes[1]
    top_mix = TOP_MIX * (1.0 + fluxes[2] * fluxes[2] + own_fluxes[2] * own_fluxes[2])
    tracers = ocean_state
    for substep in range(NSUB):
        tracers = side_mix(tracers, wet_mask)
        tracers = column_mix(tracers, wet_mask, heat_flux, fresh_flux, top_mix)
    ocean_side = jnp.stack([tracers[0, 0], tracers[1, 0], top_mix])
    return jnp.stack([returned, ocean_side]), tracers
```

```python
import functools

import jax
import jax.numpy as jnp
from jax import lax
from jax.experimental import pallas as pl
from jax.experimental.pallas import tpu as pltpu
from jax.sharding import PartitionSpec as P

FLUX_GAIN = 0.5
SIDE_MIX = 0.2
TOP_MIX = 1.0
DEEP_MIX = 2.0

EDGE = 8
MIB = 2**20


def neighbour_sum(h, lane):
    rows, lanes = h.shape
    total = pltpu.roll(h, 1, 0) + pltpu.roll(h, rows - 1, 0)
    total = total + jnp.where(lane == 0, 0.0, pltpu.roll(h, 1, 1))
    return total + jnp.where(lane == lanes - 1, 0.0, pltpu.roll(h, lanes - 1, 1))


def chunks_of(levels):
    size = 10 if levels % 10 == 0 else levels
    return [(start, size) for start in range(0, levels, size)]


def start_kernel(state, halo, bath, q_out, rho_out, side_out, held, near, sems):
    tracers, levels, columns, lanes = state.shape
    rows = columns + EDGE
    chunks = chunks_of(levels)
    copies = []
    for n, (low, size) in enumerate(chunks):
        copies.append(
            pltpu.make_async_copy(
                state.at[:, pl.ds(low, size)], held.at[:, pl.ds(low, size)], sems.at[n]
            )
        )
    for copy in reversed(copies):
        copy.start()
    lane = lax.broadcasted_iota(jnp.int32, (rows, lanes), 1)
    depth = bath[...]
    near[0] = pltpu.roll(depth, 1, 0)
    near[1] = pltpu.roll(depth, rows - 1, 0)
    near[2] = jnp.where(lane == 0, 0, pltpu.roll(depth, 1, 1))
    near[3] = jnp.where(lane == lanes - 1, 0, pltpu.roll(depth, lanes - 1, 1))

    def side(level):
        wet = level < bath[...]
        count = jnp.where(level < near[0], 1.0, 0.0)
        for n in range(1, 4):
            count = count + jnp.where(level < near[n], 1.0, 0.0)
        own = 0.5 - 0.5 * SIDE_MIX * count
        side_out[level] = own[:columns]
        halves = []
        for n in range(tracers):
            full = jnp.concatenate([held[n, level], halo[n, level]], axis=0)
            h = jnp.where(wet, full, 0.0)
            halves.append(own * h + 0.5 * SIDE_MIX * neighbour_sum(h, lane))
        return wet, halves

    def deep(step, carry, top):
        level = top - step
        rho_below, *below = carry
        wet, halves = side(level)
        linked = jnp.where(level + 1 < bath[...], DEEP_MIX - DEEP_MIX * rho_below, 0.0)
        rho = jnp.where(wet, DEEP_MIX / (1.0 + DEEP_MIX + linked), 0.0)
        rho_out[level] = rho
        solved = []
        for n in range(tracers):
            q = rho * (halves[n] + below[n])
            q_out[n, level] = q
            solved.append(q)
        return (rho, *solved)

    carry = tuple(jnp.zeros((rows, lanes), jnp.float32) for _ in range(1 + tracers))
    for n in reversed(range(len(chunks))):
        low, size = chunks[n]
        copies[n].wait()
        first = max(low, 2)
        top = low + size - 1
        carry = lax.fori_loop(
            0, top - first + 1, functools.partial(deep, top=top), carry
        )
    for level in (1, 0):
        _, halves = side(level)
        rho_out[level] = jnp.zeros((rows, lanes), jnp.float32)
        for n in range(tracers):
            q_out[n, level] = halves[n]


def remap_kernel(
    section, table, index, edge_ice, edge_weights, weights, out, picked, solved, held, sems
):
    columns, slots, width, _ = weights.shape
    rows = columns + EDGE
    fields = out.shape[0]
    group = 8
    copies = []
    for n in range(columns // group):
        copies.append(
            pltpu.make_async_copy(
                weights.at[pl.ds(n * group, group)], held.at[pl.ds(n * group, group)], sems.at[n]
            )
        )
        copies[-1].start()
    spots = lax.broadcasted_iota(jnp.int32, (rows, table.shape[0]), 1)
    picked[...] = jnp.zeros_like(picked)
    for k in range(slots):
        chosen = (spots == index[k]).astype(jnp.bfloat16)
        found = jnp.dot(chosen, table[...], preferred_element_type=jnp.float32)
        for f in range(fields):
            picked[k, pl.ds(f, rows, stride=8), :] = found[
                :, f * width : (f + 1) * width
            ]
    solved[...] = jnp.zeros_like(solved)

    def one(row, table_of):
        spot = pl.ds(row * 8, 8)
        left = jnp.concatenate([picked[k, spot, :] for k in range(slots)], axis=1)
        left = left.astype(jnp.bfloat16)
        right = jnp.concatenate([table_of(k) for k in range(slots)], axis=1)
        solved[spot, :] = lax.dot_general(
            left, right, (((1,), (1,)), ((), ())), preferred_element_type=jnp.float32
        )

    one(columns, lambda k: edge_weights[1, k])
    one(rows - 1, lambda k: edge_weights[0, k])
    for n in range(columns // group):
        copies[n].wait()
        for m in range(group):
            row = n * group + m
            one(row, lambda k: held[row, k])
    on_ocean = section[0] == 1
    for f in range(fields):
        out[f, pl.ds(0, columns)] = solved[pl.ds(f, columns, stride=8), :]
        edge = solved[pl.ds(columns * 8 + f, EDGE, stride=8), :]
        out[f, pl.ds(columns, EDGE)] = jnp.where(on_ocean, edge_ice[f], edge)


def finish_kernel(
    section, mine, other, ice, bath, state, q_in, rho_in, side_in, surface, result,
    q, rho, side, held, done, sems_in, sems_state, sems_out,
):
    tracers, levels, columns, lanes = state.shape
    rows = columns + EDGE
    chunks = chunks_of(levels)
    arrivals = []
    for n, (low, size) in enumerate(chunks):
        part = pl.ds(low, size)
        arrivals.append(
            (
                pltpu.make_async_copy(q_in.at[:, part], q.at[:, part], sems_in.at[n, 0]),
                pltpu.make_async_copy(rho_in.at[part], rho.at[part], sems_in.at[n, 1]),
                pltpu.make_async_copy(side_in.at[part], side.at[part], sems_in.at[n, 2]),
            )
        )
        for copy in arrivals[-1]:
            copy.start()
    starts = []
    for n, (low, size) in enumerate(chunks):
        part = pl.ds(low, size)
        starts.append(
            pltpu.make_async_copy(state.at[:, part], held.at[:, part], sems_state.at[n])
        )
        starts[-1].start()

    on_ocean = section[0] == 1
    lane = lax.broadcasted_iota(jnp.int32, (rows, lanes), 1)
    flux = [jnp.where(on_ocean, other[f], mine[f]) for f in range(3)]
    own = []
    for f in range(3):
        edge = jnp.where(on_ocean, mine[f, pl.ds(columns, EDGE)], other[f, pl.ds(columns, EDGE)])
        own.append(jnp.concatenate([ice[f], edge], axis=0))
    forcing = [flux[0] + own[0], flux[1] + own[1]]
    top_mix = TOP_MIX * (1.0 + flux[2] * flux[2] + own[2] * own[2])
    depth = bath[...]

    def top_levels(count, halves, below, rho_below):
        wet = 1 < depth[:count]
        link = jnp.where(wet, top_mix[:count], 0.0)
        deeper = jnp.where(2 < depth[:count], DEEP_MIX - DEEP_MIX * rho_below, 0.0)
        second = 1.0 / (1.0 + link + deeper)
        rho_second = link * second
        first = 1.0 / (1.0 + link - link * rho_second)
        values = []
        for n in range(tracers):
            partial = 2.0 * (halves[n][1] + below[n]) * second
            source = 2.0 * halves[n][0] + FLUX_GAIN * forcing[n][:count]
            surface_value = (source + link * partial) * first
            next_value = jnp.where(wet, partial, 0.0) + rho_second * surface_value
            values.append((surface_value, next_value))
        return values

    for copy in arrivals[0]:
        copy.wait()
    values = top_levels(
        rows,
        [(q[n, 0], q[n, 1]) for n in range(tracers)],
        [q[n, 2] for n in range(tracers)],
        rho[2],
    )

    def store_half(n, level, h):
        q[n, level, pl.ds(0, columns)] = (
            side[level] * h[:columns]
            + 0.5 * SIDE_MIX * neighbour_sum(h, lane)[:columns]
        )

    for n in range(tracers):
        for level in (0, 1):
            store_half(n, level, values[n][level])

    def down(step, carry, low):
        level = low + step
        ratio = rho[level]
        out = []
        for n in range(tracers):
            h = q[n, level] + ratio * carry[n]
            store_half(n, level, h)
            out.append(h)
        return tuple(out)

    carry = tuple(values[n][1] for n in range(tracers))
    for n, (low, size) in enumerate(chunks):
        if n > 0:
            for copy in arrivals[n]:
                copy.wait()
        first = max(low, 2)
        carry = lax.fori_loop(
            0, low + size - first, functools.partial(down, low=first), carry
        )

    def up(step, carry):
        level = levels - 1 - step
        ratio = rho[level, pl.ds(0, columns)]
        out = []
        for n in range(tracers):
            value = ratio * (q[n, level, pl.ds(0, columns)] + carry[n])
            q[n, level, pl.ds(0, columns)] = value
            out.append(value)
        return tuple(out)

    zero = jnp.zeros((columns, lanes), jnp.float32)
    carry = lax.fori_loop(0, levels - 2, up, (zero,) * tracers)
    values = top_levels(
        columns,
        [(q[n, 0, pl.ds(0, columns)], q[n, 1, pl.ds(0, columns)]) for n in range(tracers)],
        carry,
        rho[2, pl.ds(0, columns)],
    )
    for n in range(tracers):
        surface[n] = jnp.where(on_ocean, values[n][0], other[n, pl.ds(0, columns)])
    surface[2] = jnp.where(on_ocean, top_mix[:columns], other[2, pl.ds(0, columns)])

    def last(step, carry, low):
        level = low + step
        ratio = rho[level, pl.ds(0, columns)]
        wet = level < bath[pl.ds(0, columns)]
        out = []
        for n in range(tracers):
            h = q[n, level, pl.ds(0, columns)] + ratio * carry[n]
            done[n, level] = jnp.where(wet, h, held[n, level])
            out.append(h)
        return tuple(out)

    carry = tuple(values[n][1] for n in range(tracers))
    leaving = []
    for n, (low, size) in enumerate(chunks):
        starts[n].wait()
        if n == 0:
            for m in range(tracers):
                done[m, 0] = values[m][0]
                done[m, 1] = jnp.where(1 < depth[:columns], values[m][1], held[m, 1])
        first = max(low, 2)
        carry = lax.fori_loop(
            0, low + size - first, functools.partial(last, low=first), carry
        )
        part = pl.ds(low, size)
        leaving.append(
            pltpu.make_async_copy(done.at[:, part], result.at[:, part], sems_out.at[n])
        )
        leaving[-1].start()
    for copy in leaving:
        copy.wait()


def shift(value, axis, by):
    count = lax.axis_size(axis)
    return lax.ppermute(value, axis, [(i, (i + by) % count) for i in range(count)])


def per_device(
    surface_fields, source_blocks, source_columns, remap_weights, ocean_state, bathymetry
):
    tracers, levels, columns, lanes = ocean_state.shape
    slots = source_blocks.shape[2]
    rows = columns + EDGE
    bf16, f32 = jnp.bfloat16, jnp.float32
    on_ocean = lax.axis_index("sec") == 1
    section = lax.axis_index("sec").astype(jnp.int32).reshape(1)
    fields = surface_fields[0]
    blocks, spots, weights = source_blocks[0], source_columns[0], remap_weights[0]

    start_stack = jnp.concatenate([ocean_state[:, 0].astype(bf16), fields[2:3]], axis=0)
    to_remap = jnp.where(on_ocean, start_stack, fields)
    table = jnp.concatenate([to_remap[f] for f in range(3)], axis=1)
    gathered = lax.all_gather(table, "blk", axis=0, tiled=True)

    def edge_of(low, at):
        rows_of = [
            ocean_state[:, :, low : low + 2].astype(bf16).reshape(tracers * levels * 2, lanes),
            bathymetry[low : low + 2].astype(bf16),
            fields[:, at],
            jnp.pad(blocks[at].astype(bf16), (0, lanes - slots))[None],
            jnp.pad(spots[at].astype(bf16), (0, lanes - slots))[None],
        ]
        return jnp.concatenate(rows_of, axis=0)

    from_left = shift(edge_of(columns - 2, columns - 1), "blk", 1)
    from_right = shift(edge_of(0, 0), "blk", -1)
    left_weights = shift(weights[columns - 1], "blk", 1)
    right_weights = shift(weights[0], "blk", -1)
    partner_fields = lax.ppermute(fields, "sec", [(0, 1), (1, 0)])

    many = tracers * levels * 2

    def edge_tile(right, left, dtype):
        gap = EDGE - right.shape[-2] - left.shape[-2]
        middle = jnp.zeros(right.shape[:-2] + (gap, lanes), dtype)
        return jnp.concatenate([right.astype(dtype), middle, left.astype(dtype)], axis=-2)

    halo = edge_tile(
        from_right[:many].reshape(tracers, levels, 2, lanes),
        from_left[:many].reshape(tracers, levels, 2, lanes),
        f32,
    )
    bath_edge = edge_tile(from_right[many : many + 2], from_left[many : many + 2], jnp.int32)
    bath = jnp.concatenate([bathymetry, bath_edge], axis=0)
    edge_ice = edge_tile(
        from_right[many + 2 : many + 5][:, None], from_left[many + 2 : many + 5][:, None], f32
    )

    def flat(block_row, spot_row):
        return block_row.astype(jnp.int32) * columns + spot_row.astype(jnp.int32)

    right_index = flat(from_right[many + 5, :slots], from_right[many + 6, :slots])
    left_index = flat(from_left[many + 5, :slots], from_left[many + 6, :slots])
    index = jnp.concatenate(
        [
            flat(blocks, spots),
            right_index[None],
            jnp.zeros((EDGE - 2, slots), jnp.int32),
            left_index[None],
        ],
        axis=0,
    )
    index = jnp.transpose(index)[:, :, None]
    edge_weights = jnp.stack([left_weights, right_weights])
    ice = jnp.where(on_ocean, fields, partner_fields).astype(f32)

    anywhere = pl.BlockSpec(memory_space=pl.ANY)
    vmem = pl.BlockSpec(memory_space=pltpu.VMEM)
    smem = pl.BlockSpec(memory_space=pltpu.SMEM)
    pieces = len(chunks_of(levels))
    cells = rows * lanes
    q, rho, side = pl.pallas_call(
        start_kernel,
        out_shape=(
            jax.ShapeDtypeStruct((tracers, levels, rows, lanes), f32),
            jax.ShapeDtypeStruct((levels, rows, lanes), f32),
            jax.ShapeDtypeStruct((levels, columns, lanes), f32),
        ),
        in_specs=[anywhere, vmem, vmem],
        out_specs=(vmem, vmem, vmem),
        scratch_shapes=[
            pltpu.VMEM((tracers, levels, columns, lanes), f32),
            pltpu.VMEM((4, rows, lanes), jnp.int32),
            pltpu.SemaphoreType.DMA((pieces,)),
        ],
        compiler_params=pltpu.CompilerParams(vmem_limit_bytes=28 * MIB),
        cost_estimate=pl.CostEstimate(
            flops=60 * levels * cells, bytes_accessed=20 * levels * cells, transcendentals=0
        ),
    )(ocean_state, halo, bath)

    mine = pl.pallas_call(
        remap_kernel,
        out_shape=jax.ShapeDtypeStruct((3, rows, lanes), f32),
        in_specs=[smem, vmem, vmem, vmem, vmem, anywhere],
        out_specs=vmem,
        scratch_shapes=[
            pltpu.VMEM((slots, rows * 8, lanes), f32),
            pltpu.VMEM((rows * 8, lanes), f32),
            pltpu.VMEM(weights.shape, bf16),
            pltpu.SemaphoreType.DMA((columns // 8,)),
        ],
        compiler_params=pltpu.CompilerParams(vmem_limit_bytes=24 * MIB),
        cost_estimate=pl.CostEstimate(
            flops=2 * weights.size * 8, bytes_accessed=2 * weights.size, transcendentals=0
        ),
    )(section, gathered, index, edge_ice, edge_weights, weights)
    other = lax.ppermute(mine, "sec", [(0, 1), (1, 0)])

    surface, result = pl.pallas_call(
        finish_kernel,
        out_shape=(
            jax.ShapeDtypeStruct((3, columns, lanes), f32),
            jax.ShapeDtypeStruct((tracers, levels, columns, lanes), f32),
        ),
        in_specs=[smem, vmem, vmem, vmem, vmem, anywhere, anywhere, anywhere, anywhere],
        out_specs=(vmem, anywhere),
        scratch_shapes=[
            pltpu.VMEM((tracers, levels, rows, lanes), f32),
            pltpu.VMEM((levels, rows, lanes), f32),
            pltpu.VMEM((levels, columns, lanes), f32),
            pltpu.VMEM((tracers, levels, columns, lanes), f32),
            pltpu.VMEM((tracers, levels, columns, lanes), f32),
            pltpu.SemaphoreType.DMA((pieces, 3)),
            pltpu.SemaphoreType.DMA((pieces,)),
            pltpu.SemaphoreType.DMA((pieces,)),
        ],
        compiler_params=pltpu.CompilerParams(vmem_limit_bytes=32 * MIB),
        cost_estimate=pl.CostEstimate(
            flops=60 * levels * cells, bytes_accessed=32 * levels * cells, transcendentals=0
        ),
    )(section, mine, other, ice, bath, ocean_state, q, rho, side)
    return (surface[None], result)


def solution(mesh):
    return jax.shard_map(
        per_device,
        mesh=mesh,
        in_specs=(
            P("sec", None, "blk", None),
            P("sec", "blk", None),
            P("sec", "blk", None),
            P("sec", "blk", None, None, None),
            P(None, None, "blk", None),
            P("blk", None),
        ),
        out_specs=(P("sec", None, "blk", None), P(None, None, "blk", None)),
        check_vma=False,
    )
```

```python
import functools

import jax
import jax.numpy as jnp
from jax import lax
from jax.experimental import pallas as pl
from jax.experimental.pallas import tpu as pltpu
from jax.sharding import PartitionSpec as P

FLUX_GAIN = 0.5
SIDE_MIX = 0.2
TOP_MIX = 1.0
DEEP_MIX = 2.0

MOST = 16
SLOTS = 24
EDGE = 8
EXTRA = 16
MIB = 2**20
bf16, f32, i32 = jnp.bfloat16, jnp.float32, jnp.int32


def iota(shape, axis):
    return lax.broadcasted_iota(i32, shape, axis)


def neighbour_sum(h, lane):
    rows, lanes = h.shape
    total = pltpu.roll(h, 1, 0) + pltpu.roll(h, rows - 1, 0)
    total = total + jnp.where(lane == 0, 0.0, pltpu.roll(h, 1, 1))
    return total + jnp.where(lane == lanes - 1, 0.0, pltpu.roll(h, lanes - 1, 1))


def edge_tile(right, left):
    row = iota((EDGE, right.shape[1]), 0)
    return jnp.where(row == 0, right, jnp.where(row == EDGE - 1, left, 0.0))


def chunks_of(levels):
    size = 10 if levels % 10 == 0 else levels
    return [(start, size) for start in range(0, levels, size)]


def sweep(count, body, carry, unroll):
    rounds = count // unroll

    def several(number, carry):
        for n in range(unroll):
            carry = body(number * unroll + n, carry)
        return carry

    carry = lax.fori_loop(0, rounds, several, carry)
    for step in range(rounds * unroll, count):
        carry = body(step, carry)
    return carry


def ask_kernel(blocks, spots, request, place):
    count, total = request.shape[0], blocks.shape[1]
    columns = place.shape[1]
    owner = iota((count, total), 0) == blocks[...]
    one_hot = jnp.where(owner, 1.0, 0.0)
    before = jnp.where(iota((total, total), 0) < iota((total, total), 1), 1.0, 0.0)
    earlier = jnp.dot(one_hot.astype(bf16), before.astype(bf16), preferred_element_type=f32)
    rank = jnp.sum(one_hot * earlier, axis=0, keepdims=True)
    slot = iota((128, total), 0)
    spot_in_block = lax.rem(iota((128, total), 1), total // 4)
    last = total // 4 - 1
    filled = (
        (slot == rank.astype(i32))
        | ((slot == MOST) & (spot_in_block == 0))
        | ((slot == MOST + 1) & (spot_in_block == last))
    )
    named = jnp.where(owner, spots[...].astype(f32), 0.0)
    request[...] = lax.dot_general(
        named.astype(bf16),
        jnp.where(filled, 1.0, 0.0).astype(bf16),
        (((1,), (1,)), ((), ())),
        preferred_element_type=f32,
    ).astype(i32)
    arrives = blocks[...].astype(f32) * SLOTS + rank
    place[...] = jnp.transpose(jnp.broadcast_to(arrives, (columns, total))).astype(i32)


def pack_kernel(
    section, state, bath, fields, blocks, weights, to_left, to_right, table,
    low, high, surface, extra, sems,
):
    tracers, levels, columns, lanes = state.shape
    many = tracers * levels
    wide = to_left.shape[0] - 2 * many - EXTRA
    below = pl.ds(2 * many + EXTRA, wide)
    copies = [
        pltpu.make_async_copy(state.at[:, 0], surface, sems.at[0]),
        pltpu.make_async_copy(state.at[:, :, pl.ds(0, 8)], low, sems.at[1]),
        pltpu.make_async_copy(state.at[:, :, pl.ds(columns - 8, 8)], high, sems.at[2]),
        pltpu.make_async_copy(weights.at[pl.ds(0, wide)], to_left.at[below], sems.at[3]),
        pltpu.make_async_copy(
            weights.at[pl.ds((columns - 1) * wide, wide)], to_right.at[below], sems.at[4]
        ),
    ]
    for copy in copies:
        copy.start()
    for out, first, at in ((to_left, 0, 0), (to_right, columns - 2, columns - 1)):
        extra[...] = jnp.zeros_like(extra)
        extra[0:2] = bath[first : first + 2].astype(f32)
        for f in range(3):
            extra[2 + f : 3 + f] = fields[f].astype(f32)[at : at + 1]
        slots = blocks.shape[0]
        extra[8 : 8 + slots] = jnp.broadcast_to(blocks[:, at : at + 1].astype(f32), (slots, lanes))
        out[pl.ds(2 * many, EXTRA)] = extra[...].astype(bf16)
    copies[0].wait()
    on_ocean = section[0] == 1
    for f in range(3):
        own = fields[f]
        if f < 2:
            own = jnp.where(on_ocean, surface[f], own.astype(f32)).astype(bf16)
        table[:, f * lanes : (f + 1) * lanes] = own
    copies[1].wait()
    copies[2].wait()
    for c in range(2):
        for n in range(tracers):
            part = pl.ds(c * many + n * levels, levels)
            tiles = low.at[n].reshape(levels * 8, lanes)
            to_left[part] = tiles[pl.ds(c, levels, stride=8), :].astype(bf16)
            tiles = high.at[n].reshape(levels * 8, lanes)
            to_right[part] = tiles[pl.ds(6 + c, levels, stride=8), :].astype(bf16)
    copies[3].wait()
    copies[4].wait()


def serve_kernel(asked, table, out):
    count = asked.shape[0]
    wanted = jnp.transpose(asked[...].astype(f32))[:SLOTS]
    columns = table.shape[0]
    slot = iota((SLOTS, 1), 0)
    parts = []
    for e in range(count):
        after, before = (e + 1) % count, (e - 1) % count
        spot = jnp.where(
            slot == MOST,
            wanted[:, after : after + 1],
            jnp.where(slot == MOST + 1, wanted[:, before : before + 1], wanted[:, e : e + 1]),
        )
        parts.append(jnp.where(iota((SLOTS, columns), 1) == spot.astype(i32), 1.0, 0.0))
    chosen = jnp.concatenate(parts, axis=0).astype(bf16)
    out[...] = jnp.dot(chosen, table[...], preferred_element_type=f32).astype(bf16)


def start_kernel(
    state, from_left, from_right, bath, q_out, rho_out, side_out, held, bath_out, halo, near, sems
):
    tracers, levels, columns, lanes = state.shape
    rows = columns + EDGE
    many = tracers * levels
    chunks = chunks_of(levels)
    copies = []
    for n, (low, size) in enumerate(chunks):
        copies.append(
            pltpu.make_async_copy(
                state.at[:, pl.ds(low, size)], held.at[:, pl.ds(low, size)], sems.at[n]
            )
        )
    for copy in reversed(copies):
        copy.start()
    for c in range(2):
        part = pl.ds(c * many, many)
        halo[pl.ds(c, many, stride=8), :] = from_right[part].astype(f32)
        halo[pl.ds(EDGE - 2 + c, many, stride=8), :] = from_left[part].astype(f32)
    right = from_right[pl.ds(2 * many, EXTRA)].astype(f32)
    left = from_left[pl.ds(2 * many, EXTRA)].astype(f32)
    row = iota((EDGE, lanes), 0)
    edge = jnp.where(
        row == 0,
        right[0:1],
        jnp.where(
            row == 1,
            right[1:2],
            jnp.where(row == EDGE - 2, left[0:1], jnp.where(row == EDGE - 1, left[1:2], 0.0)),
        ),
    )
    depth = jnp.concatenate([bath[...], edge.astype(i32)], axis=0)
    bath_out[...] = depth
    lane = iota((rows, lanes), 1)
    a = pltpu.roll(depth, 1, 0)
    b = pltpu.roll(depth, rows - 1, 0)
    c = jnp.where(lane == 0, 0, pltpu.roll(depth, 1, 1))
    d = jnp.where(lane == lanes - 1, 0, pltpu.roll(depth, lanes - 1, 1))
    a, b = jnp.maximum(a, b), jnp.minimum(a, b)
    c, d = jnp.maximum(c, d), jnp.minimum(c, d)
    a, c = jnp.maximum(a, c), jnp.minimum(a, c)
    b, d = jnp.maximum(b, d), jnp.minimum(b, d)
    near[0], near[1], near[2], near[3] = a, jnp.maximum(b, c), jnp.minimum(b, c), d

    def side(level):
        wet = level < bath_out[...]
        own = 0.5
        for n in range(4):
            own = jnp.where(level < near[n], 0.5 - 0.5 * SIDE_MIX * (n + 1), own)
        side_out[level] = own[:columns]
        halves = []
        for n in range(tracers):
            spot = (n * levels + level) * 8
            if not isinstance(level, int):
                spot = pl.multiple_of(spot, 8)
            full = jnp.concatenate([held[n, level], halo[pl.ds(spot, 8), :]], axis=0)
            h = jnp.where(wet, full, 0.0)
            halves.append(own * h + 0.5 * SIDE_MIX * neighbour_sum(h, lane))
        return wet, halves

    def deep(step, carry, top):
        level = top - step
        rho_below, *below = carry
        wet, halves = side(level)
        linked = jnp.where(level + 1 < bath_out[...], DEEP_MIX - DEEP_MIX * rho_below, 0.0)
        divisor = 1.0 + DEEP_MIX + linked
        inverse = pl.reciprocal(divisor, approx=True)
        inverse = inverse * (2.0 - divisor * inverse)
        inverse = inverse * (2.0 * DEEP_MIX - DEEP_MIX * divisor * inverse)
        rho = jnp.where(wet, inverse, 0.0)
        rho_out[level] = rho
        solved = []
        for n in range(tracers):
            q = rho * (halves[n] + below[n])
            q_out[n, level] = q
            solved.append(q)
        return (rho, *solved)

    carry = tuple(jnp.zeros((rows, lanes), f32) for _ in range(1 + tracers))
    for n in reversed(range(len(chunks))):
        low, size = chunks[n]
        copies[n].wait()
        first = max(low, 2)
        top = low + size - 1
        carry = sweep(top - first + 1, functools.partial(deep, top=top), carry, 2)
    for level in (1, 0):
        _, halves = side(level)
        rho_out[level] = jnp.zeros((rows, lanes), f32)
        for n in range(tracers):
            q_out[n, level] = halves[n]


def remap_kernel(
    section, columns_in, place, from_left, from_right, weights, out, picked, solved, held, sems
):
    fields, rows, width = out.shape
    columns = rows - EDGE
    slots = weights.shape[0] // (columns * width)
    tall = slots * width
    many = from_left.shape[0] - tall - EXTRA
    group = 8
    copies = []
    for n in range(columns // group):
        part = pl.ds(n * group * tall, group * tall)
        copies.append(pltpu.make_async_copy(weights.at[part], held.at[part], sems.at[n]))
        copies[-1].start()
    right = from_right[pl.ds(many, EXTRA)].astype(f32)
    left = from_left[pl.ds(many, EXTRA)].astype(f32)
    spots = iota((rows, columns_in.shape[0]), 1)
    row = iota((EDGE, 1), 0)
    picked[...] = jnp.zeros_like(picked)
    for k in range(slots):
        edge = jnp.where(
            row == 0,
            right[8 + k : 9 + k, 0:1] * SLOTS + MOST,
            jnp.where(row == EDGE - 1, left[8 + k : 9 + k, 0:1] * SLOTS + MOST + 1, -1.0),
        ).astype(i32)
        wanted = jnp.concatenate([place[k * columns : (k + 1) * columns, 0:1], edge], axis=0)
        chosen = jnp.where(spots == wanted, 1.0, 0.0).astype(bf16)
        found = jnp.dot(chosen, columns_in[...], preferred_element_type=f32)
        for f in range(fields):
            picked[k, pl.ds(f, rows, stride=8), :] = found[:, f * width : (f + 1) * width]

    def one(row, table_of):
        spot = pl.ds(row * 8, 8)
        vector = jnp.concatenate([picked[k, spot, :] for k in range(slots)], axis=1)
        matrix = jnp.concatenate([table_of(k) for k in range(slots)], axis=1)
        solved[spot, :] = lax.dot_general(
            vector.astype(bf16), matrix, (((1,), (1,)), ((), ())), preferred_element_type=f32
        )

    solved[...] = jnp.zeros_like(solved)
    below = many + EXTRA
    one(columns, lambda k: from_right[pl.ds(below + k * width, width)])
    one(rows - 1, lambda k: from_left[pl.ds(below + k * width, width)])
    for n in range(columns // group):
        copies[n].wait()
        for m in range(group):
            spot = n * group + m
            one(spot, lambda k: held[pl.ds((spot * slots + k) * width, width)])
    on_ocean = section[0] == 1
    for f in range(fields):
        out[f, pl.ds(0, columns)] = solved[pl.ds(f, columns, stride=8), :]
        edge = solved[pl.ds(columns * 8 + f, EDGE, stride=8), :]
        ice = edge_tile(right[2 + f : 3 + f], left[2 + f : 3 + f])
        out[f, pl.ds(columns, EDGE)] = jnp.where(on_ocean, ice, edge)


def finish_kernel(
    section, mine, other, fields, partner_fields, bath, q, rho, side, start, surface, result,
    half, done, sems,
):
    tracers, levels, columns, lanes = start.shape
    rows = columns + EDGE
    chunks = chunks_of(levels)
    on_ocean = section[0] == 1
    lane = iota((rows, lanes), 1)
    flux = [jnp.where(on_ocean, other[f], mine[f]) for f in range(3)]
    own = []
    for f in range(3):
        edge = jnp.where(on_ocean, mine[f, pl.ds(columns, EDGE)], other[f, pl.ds(columns, EDGE)])
        ice = jnp.where(on_ocean, fields[f].astype(f32), partner_fields[f].astype(f32))
        own.append(jnp.concatenate([ice, edge], axis=0))
    forcing = [flux[0] + own[0], flux[1] + own[1]]
    top_mix = TOP_MIX * (1.0 + flux[2] * flux[2] + own[2] * own[2])
    depth = bath[...]

    def top_levels(count, halves, below, rho_below):
        wet = 1 < depth[:count]
        link = jnp.where(wet, top_mix[:count], 0.0)
        deeper = jnp.where(2 < depth[:count], DEEP_MIX - DEEP_MIX * rho_below, 0.0)
        second = 1.0 / (1.0 + link + deeper)
        rho_second = link * second
        first = 1.0 / (1.0 + link - link * rho_second)
        values = []
        for n in range(tracers):
            partial = 2.0 * (halves[n][1] + below[n]) * second
            source = 2.0 * halves[n][0] + FLUX_GAIN * forcing[n][:count]
            surface_value = (source + link * partial) * first
            next_value = jnp.where(wet, partial, 0.0) + rho_second * surface_value
            values.append((surface_value, next_value))
        return values

    values = top_levels(
        rows,
        [(q[n, 0], q[n, 1]) for n in range(tracers)],
        [q[n, 2] for n in range(tracers)],
        rho[2],
    )

    def store_half(n, level, h):
        half[n, level] = (
            side[level] * h[:columns] + 0.5 * SIDE_MIX * neighbour_sum(h, lane)[:columns]
        )

    for n in range(tracers):
        for level in (0, 1):
            store_half(n, level, values[n][level])

    def down(step, carry):
        level = 2 + step
        ratio = rho[level]
        out = []
        for n in range(tracers):
            h = q[n, level] + ratio * carry[n]
            store_half(n, level, h)
            out.append(h)
        return tuple(out)

    carry = tuple(values[n][1] for n in range(tracers))
    sweep(levels - 2, down, carry, 2)

    def up(step, carry):
        level = levels - 1 - step
        ratio = rho[level, pl.ds(0, columns)]
        out = []
        for n in range(tracers):
            value = ratio * (half[n, level] + carry[n])
            half[n, level] = value
            out.append(value)
        return tuple(out)

    zero = jnp.zeros((columns, lanes), f32)
    carry = sweep(levels - 2, up, (zero,) * tracers, 6)
    values = top_levels(
        columns,
        [(half[n, 0], half[n, 1]) for n in range(tracers)],
        carry,
        rho[2, pl.ds(0, columns)],
    )
    for n in range(tracers):
        surface[n] = jnp.where(on_ocean, values[n][0], other[n, pl.ds(0, columns)])
    surface[2] = jnp.where(on_ocean, top_mix[:columns], other[2, pl.ds(0, columns)])

    def last(step, carry, low):
        level = low + step
        ratio = rho[level, pl.ds(0, columns)]
        wet = level < bath[pl.ds(0, columns)]
        out = []
        for n in range(tracers):
            h = half[n, level] + ratio * carry[n]
            done[n, level] = jnp.where(wet, h, start[n, level])
            out.append(h)
        return tuple(out)

    carry = tuple(values[n][1] for n in range(tracers))
    leaving = []
    for n, (low, size) in enumerate(chunks):
        if n == 0:
            for m in range(tracers):
                done[m, 0] = values[m][0]
                done[m, 1] = jnp.where(1 < depth[:columns], values[m][1], start[m, 1])
        first = max(low, 2)
        carry = sweep(low + size - first, functools.partial(last, low=first), carry, 4)
        part = pl.ds(low, size)
        leaving.append(
            pltpu.make_async_copy(done.at[:, part], result.at[:, part], sems.at[n])
        )
        leaving[-1].start()
    for copy in leaving:
        copy.wait()


def shift(value, axis, by):
    count = lax.axis_size(axis)
    return lax.ppermute(value, axis, [(i, (i + by) % count) for i in range(count)])


def per_device(
    surface_fields, source_blocks, source_columns, remap_weights, ocean_state, bathymetry
):
    tracers, levels, columns, lanes = ocean_state.shape
    slots = source_blocks.shape[2]
    count = lax.axis_size("blk")
    rows = columns + EDGE
    section = lax.axis_index("sec").astype(i32).reshape(1)
    fields = surface_fields[0]
    blocks = jnp.transpose(source_blocks[0])
    spots = jnp.transpose(source_columns[0])
    weights = remap_weights[0].reshape(columns * slots * lanes, lanes)
    tall = slots * lanes
    many = tracers * levels

    anywhere = pl.BlockSpec(memory_space=pl.ANY)
    vmem = pl.BlockSpec(memory_space=pltpu.VMEM)
    smem = pl.BlockSpec(memory_space=pltpu.SMEM)
    shaped = jax.ShapeDtypeStruct
    pieces = len(chunks_of(levels))
    cells = rows * lanes

    request, place = pl.pallas_call(
        ask_kernel,
        out_shape=(shaped((count, 128), i32), shaped((slots * columns, 128), i32)),
        in_specs=[vmem, vmem],
        out_specs=(vmem, vmem),
        compiler_params=pltpu.CompilerParams(vmem_limit_bytes=4 * MIB),
        cost_estimate=pl.CostEstimate(flops=10**6, bytes_accessed=10**5, transcendentals=0),
    )(blocks.reshape(1, slots * columns), spots.reshape(1, slots * columns))
    asked = lax.all_to_all(request, "blk", split_axis=0, concat_axis=0, tiled=True)

    payload = shaped((2 * many + EXTRA + tall, lanes), bf16)
    to_left, to_right, table = pl.pallas_call(
        pack_kernel,
        out_shape=(payload, payload, shaped((columns, 3 * lanes), bf16)),
        in_specs=[smem, anywhere, vmem, vmem, vmem, anywhere],
        out_specs=(vmem, vmem, vmem),
        scratch_shapes=[
            pltpu.VMEM((tracers, levels, 8, lanes), f32),
            pltpu.VMEM((tracers, levels, 8, lanes), f32),
            pltpu.VMEM((tracers, columns, lanes), f32),
            pltpu.VMEM((EXTRA, lanes), f32),
            pltpu.SemaphoreType.DMA((5,)),
        ],
        compiler_params=pltpu.CompilerParams(vmem_limit_bytes=8 * MIB),
        cost_estimate=pl.CostEstimate(
            flops=10**6, bytes_accessed=4 * 10**6, transcendentals=0
        ),
    )(section, ocean_state, bathymetry, fields, blocks, weights)
    from_left = shift(to_right, "blk", 1)
    from_right = shift(to_left, "blk", -1)
    partner_fields = lax.ppermute(fields, "sec", [(0, 1), (1, 0)])

    served = pl.pallas_call(
        serve_kernel,
        out_shape=shaped((count * SLOTS, 3 * lanes), bf16),
        in_specs=[vmem, vmem],
        out_specs=vmem,
        compiler_params=pltpu.CompilerParams(vmem_limit_bytes=8 * MIB),
        cost_estimate=pl.CostEstimate(
            flops=10**7, bytes_accessed=10**6, transcendentals=0
        ),
    )(asked, table)
    columns_in = lax.all_to_all(served, "blk", split_axis=0, concat_axis=0, tiled=True)

    q, rho, side, start, bath = pl.pallas_call(
        start_kernel,
        out_shape=(
            shaped((tracers, levels, rows, lanes), f32),
            shaped((levels, rows, lanes), f32),
            shaped((levels, columns, lanes), f32),
            shaped(ocean_state.shape, f32),
            shaped((rows, lanes), i32),
        ),
        in_specs=[anywhere, vmem, vmem, vmem],
        out_specs=(vmem,) * 5,
        scratch_shapes=[
            pltpu.VMEM((many * 8, lanes), f32),
            pltpu.VMEM((4, rows, lanes), i32),
            pltpu.SemaphoreType.DMA((pieces,)),
        ],
        compiler_params=pltpu.CompilerParams(vmem_limit_bytes=8 * MIB),
        cost_estimate=pl.CostEstimate(
            flops=60 * levels * cells, bytes_accessed=20 * levels * cells, transcendentals=0
        ),
    )(ocean_state, from_left, from_right, bathymetry)

    mine = pl.pallas_call(
        remap_kernel,
        out_shape=shaped((3, rows, lanes), f32),
        in_specs=[smem, vmem, vmem, vmem, vmem, anywhere],
        out_specs=vmem,
        scratch_shapes=[
            pltpu.VMEM((slots, rows * 8, lanes), f32),
            pltpu.VMEM((rows * 8, lanes), f32),
            pltpu.VMEM(weights.shape, bf16),
            pltpu.SemaphoreType.DMA((columns // 8,)),
        ],
        compiler_params=pltpu.CompilerParams(vmem_limit_bytes=16 * MIB),
        cost_estimate=pl.CostEstimate(
            flops=16 * weights.size, bytes_accessed=2 * weights.size, transcendentals=0
        ),
    )(section, columns_in, place, from_left, from_right, weights)
    other = lax.ppermute(mine, "sec", [(0, 1), (1, 0)])

    surface, result = pl.pallas_call(
        finish_kernel,
        out_shape=(shaped((3, columns, lanes), f32), shaped(ocean_state.shape, f32)),
        in_specs=[smem] + [vmem] * 9,
        out_specs=(vmem, anywhere),
        scratch_shapes=[
            pltpu.VMEM(ocean_state.shape, f32),
            pltpu.VMEM(ocean_state.shape, f32),
            pltpu.SemaphoreType.DMA((pieces,)),
        ],
        compiler_params=pltpu.CompilerParams(vmem_limit_bytes=16 * MIB),
        cost_estimate=pl.CostEstimate(
            flops=60 * levels * cells, bytes_accessed=32 * levels * cells, transcendentals=0
        ),
    )(section, mine, other, fields, partner_fields, bath, q, rho, side, start)
    return (surface[None], result)


def solution(mesh):
    return jax.shard_map(
        per_device,
        mesh=mesh,
        in_specs=(
            P("sec", None, "blk", None),
            P("sec", "blk", None),
            P("sec", "blk", None),
            P("sec", "blk", None, None, None),
            P(None, None, "blk", None),
            P("blk", None),
        ),
        out_specs=(P("sec", None, "blk", None), P(None, None, "blk", None)),
        check_vma=False,
    )
```

```python
import functools

import jax
import jax.numpy as jnp
import numpy as np
from jax import lax
from jax.experimental import pallas as pl
from jax.experimental.pallas import tpu as pltpu
from jax.sharding import PartitionSpec as P

FLUX_GAIN = 0.5
SIDE_MIX = 0.2
TOP_MIX = 1.0
DEEP_MIX = 2.0
SCALE = 1.0 / (0.5 * SIDE_MIX)

MOST = 16
SLOTS = 24
EDGE = 8
EXTRA = 16
MIB = 2**20
bf16, f32, i32 = jnp.bfloat16, jnp.float32, jnp.int32


def iota(shape, axis):
    return lax.broadcasted_iota(i32, shape, axis)


def neighbour_sum(h, lane):
    rows, lanes = h.shape
    total = pltpu.roll(h, 1, 0) + pltpu.roll(h, rows - 1, 0)
    total = total + jnp.where(lane == 0, 0.0, pltpu.roll(h, 1, 1))
    return total + jnp.where(lane == lanes - 1, 0.0, pltpu.roll(h, lanes - 1, 1))


def edge_tile(right, left):
    row = iota((EDGE, right.shape[1]), 0)
    return jnp.where(row == 0, right, jnp.where(row == EDGE - 1, left, 0.0))


def chunks_of(levels):
    size = 10 if levels % 10 == 0 else levels
    return [(start, size) for start in range(0, levels, size)]


def sweep(count, body, carry, unroll):
    rounds = count // unroll

    def several(number, carry):
        for n in range(unroll):
            carry = body(number * unroll + n, carry)
        return carry

    carry = lax.fori_loop(0, rounds, several, carry)
    for step in range(rounds * unroll, count):
        carry = body(step, carry)
    return carry


def prepare_kernel(
    section, state, bath, fields, blocks, spots, weights,
    request, place, to_left, to_right, table,
    low, high, surface, bath_in, fields_in, blocks_in, spots_in, extra, sems,
):
    tracers, levels, columns, lanes = state.shape
    many = tracers * levels
    wide = to_left.shape[0] - 2 * many - EXTRA
    below = pl.ds(2 * many + EXTRA, wide)
    pairs = [
        (blocks, blocks_in),
        (spots, spots_in),
        (bath, bath_in),
        (fields, fields_in),
        (state.at[:, 0], surface),
        (state.at[:, :, pl.ds(0, 8)], low),
        (state.at[:, :, pl.ds(columns - 8, 8)], high),
        (weights.at[pl.ds(0, wide)], to_left.at[below]),
        (weights.at[pl.ds((columns - 1) * wide, wide)], to_right.at[below]),
    ]
    copies = [pltpu.make_async_copy(src, dst, sems.at[n]) for n, (src, dst) in enumerate(pairs)]
    for copy in copies:
        copy.start()
    copies[0].wait()
    copies[1].wait()

    count, slots = request.shape[0], blocks.shape[0]
    before = jnp.where(iota((columns, columns), 0) < iota((columns, columns), 1), 1.0, 0.0)
    before = before.astype(bf16)
    slot = iota((128, columns), 0)
    here = iota((128, columns), 1)
    marks = ((slot == MOST) & (here == 0)) | ((slot == MOST + 1) & (here == columns - 1))
    used = jnp.zeros((count, 1), f32)
    asked = jnp.zeros(request.shape, f32)
    for k in range(slots):
        block = blocks_in[k : k + 1, :]
        owner = iota((count, columns), 0) == block
        one_hot = jnp.where(owner, 1.0, 0.0)
        earlier = used + jnp.dot(one_hot.astype(bf16), before, preferred_element_type=f32)
        rank = jnp.sum(one_hot * earlier, axis=0, keepdims=True)
        used = used + jnp.sum(one_hot, axis=1, keepdims=True)
        filled = jnp.where((slot == rank.astype(i32)) | marks, 1.0, 0.0).astype(bf16)
        named = jnp.where(owner, spots_in[k : k + 1, :].astype(f32), 0.0).astype(bf16)
        asked = asked + lax.dot_general(
            named, filled, (((1,), (1,)), ((), ())), preferred_element_type=f32
        )
        arrives = block.astype(f32) * SLOTS + rank
        spread = jnp.transpose(jnp.broadcast_to(arrives, (128, columns)))
        place[k * columns : (k + 1) * columns, :] = spread.astype(i32)
    request[...] = asked.astype(i32)

    copies[2].wait()
    copies[3].wait()
    for out, first, at in ((to_left, 0, 0), (to_right, columns - 2, columns - 1)):
        extra[...] = jnp.zeros_like(extra)
        extra[0:2] = bath_in[first : first + 2].astype(f32)
        for f in range(3):
            extra[2 + f : 3 + f] = fields_in[f].astype(f32)[at : at + 1]
        extra[8 : 8 + slots] = jnp.broadcast_to(
            blocks_in[:, at : at + 1].astype(f32), (slots, lanes)
        )
        out[pl.ds(2 * many, EXTRA)] = extra[...].astype(bf16)
    copies[4].wait()
    on_ocean = section[0] == 1
    for f in range(3):
        own = fields_in[f]
        if f < 2:
            own = jnp.where(on_ocean, surface[f], own.astype(f32)).astype(bf16)
        table[:, f * lanes : (f + 1) * lanes] = own
    copies[5].wait()
    copies[6].wait()
    for c in range(2):
        for n in range(tracers):
            part = pl.ds(c * many + n * levels, levels)
            tiles = low.at[n].reshape(levels * 8, lanes)
            to_left[part] = tiles[pl.ds(c, levels, stride=8), :].astype(bf16)
            tiles = high.at[n].reshape(levels * 8, lanes)
            to_right[part] = tiles[pl.ds(6 + c, levels, stride=8), :].astype(bf16)
    copies[7].wait()
    copies[8].wait()


def serve_kernel(asked, table, out):
    count = asked.shape[0]
    wanted = jnp.transpose(asked[...].astype(f32))[:SLOTS]
    columns = table.shape[0]
    slot = iota((SLOTS, 1), 0)
    parts = []
    for e in range(count):
        after, before = (e + 1) % count, (e - 1) % count
        spot = jnp.where(
            slot == MOST,
            wanted[:, after : after + 1],
            jnp.where(slot == MOST + 1, wanted[:, before : before + 1], wanted[:, e : e + 1]),
        )
        parts.append(jnp.where(iota((SLOTS, columns), 1) == spot.astype(i32), 1.0, 0.0))
    chosen = jnp.concatenate(parts, axis=0).astype(bf16)
    out[...] = jnp.dot(chosen, table[...], preferred_element_type=f32).astype(bf16)


def start_kernel(
    state, from_left, from_right, bath, weights, ratios,
    q_out, rho_out, side_out, held, bath_out, weights_out, halo, near, bath_in, sems,
):
    tracers, levels, columns, lanes = state.shape
    rows = columns + EDGE
    many = tracers * levels
    chunks = chunks_of(levels)
    copies = []
    for n, (low, size) in enumerate(chunks):
        copies.append(
            pltpu.make_async_copy(
                state.at[:, pl.ds(low, size)], held.at[:, pl.ds(low, size)], sems.at[n]
            )
        )
    bath_copy = pltpu.make_async_copy(bath, bath_in, sems.at[len(chunks)])
    weights_copy = pltpu.make_async_copy(weights, weights_out, sems.at[len(chunks) + 1])
    bath_copy.start()
    for copy in reversed(copies):
        copy.start()
    weights_copy.start()
    for c in range(2):
        part = pl.ds(c * many, many)
        halo[pl.ds(c, many, stride=8), :] = from_right[part].astype(f32)
        halo[pl.ds(EDGE - 2 + c, many, stride=8), :] = from_left[part].astype(f32)
    right = from_right[pl.ds(2 * many, EXTRA)].astype(f32)
    left = from_left[pl.ds(2 * many, EXTRA)].astype(f32)
    row = iota((EDGE, lanes), 0)
    edge = jnp.where(
        row == 0,
        right[0:1],
        jnp.where(
            row == 1,
            right[1:2],
            jnp.where(row == EDGE - 2, left[0:1], jnp.where(row == EDGE - 1, left[1:2], 0.0)),
        ),
    )
    bath_copy.wait()
    depth = jnp.concatenate([bath_in[...], edge.astype(i32)], axis=0)
    bath_out[...] = depth
    lane = iota((rows, lanes), 1)
    a = pltpu.roll(depth, 1, 0)
    b = pltpu.roll(depth, rows - 1, 0)
    c = jnp.where(lane == 0, 0, pltpu.roll(depth, 1, 1))
    d = jnp.where(lane == lanes - 1, 0, pltpu.roll(depth, lanes - 1, 1))
    a, b = jnp.maximum(a, b), jnp.minimum(a, b)
    c, d = jnp.maximum(c, d), jnp.minimum(c, d)
    a, c = jnp.maximum(a, c), jnp.minimum(a, c)
    b, d = jnp.maximum(b, d), jnp.minimum(b, d)
    near[0], near[1], near[2], near[3] = a, jnp.maximum(b, c), jnp.minimum(b, c), d

    lookup = jnp.broadcast_to(ratios[0:1], (rows, lanes))

    def side(level):
        wet = level < bath_out[...]
        own = 0.5 * SCALE
        for n in range(4):
            own = jnp.where(level < near[n], 0.5 * SCALE - (n + 1), own)
        side_out[level] = own[:columns]
        halves = []
        for n in range(tracers):
            spot = (n * levels + level) * 8
            if not isinstance(level, int):
                spot = pl.multiple_of(spot, 8)
            full = jnp.concatenate([held[n, level], halo[pl.ds(spot, 8), :]], axis=0)
            h = jnp.where(wet, full, 0.0)
            halves.append(own * h + neighbour_sum(h, lane))
        return halves

    def deep(step, below, top):
        level = top - step
        halves = side(level)
        above_floor = jnp.maximum(bath_out[...] - level, 0)
        rho = jnp.take_along_axis(lookup, above_floor, axis=1, mode="promise_in_bounds")
        rho_out[level] = rho
        solved = []
        for n in range(tracers):
            q = rho * (halves[n] + below[n])
            q_out[n, level] = q
            solved.append(q)
        return tuple(solved)

    carry = tuple(jnp.zeros((rows, lanes), f32) for _ in range(tracers))
    for n in reversed(range(len(chunks))):
        low, size = chunks[n]
        copies[n].wait()
        first = max(low, 2)
        top = low + size - 1
        carry = sweep(top - first + 1, functools.partial(deep, top=top), carry, 5)
    for level in (1, 0):
        halves = side(level)
        rho_out[level] = jnp.zeros((rows, lanes), f32)
        for n in range(tracers):
            q_out[n, level] = halves[n]
    weights_copy.wait()


def ratios_by_height(levels, lanes):
    values = [0.0]
    ratio = DEEP_MIX / (1.0 + DEEP_MIX)
    for _ in range(levels):
        values.append(ratio)
        ratio = DEEP_MIX / (1.0 + DEEP_MIX + DEEP_MIX - DEEP_MIX * ratio)
    values += [0.0] * (lanes - len(values))
    return jnp.broadcast_to(jnp.asarray(np.array(values, np.float32)), (8, lanes))


def remap_kernel(
    section, columns_in, place, from_left, from_right, weights, out, picked, solved
):
    fields, rows, width = out.shape
    columns = rows - EDGE
    slots = weights.shape[0] // (columns * width)
    tall = slots * width
    many = from_left.shape[0] - tall - EXTRA
    right = from_right[pl.ds(many, EXTRA)].astype(f32)
    left = from_left[pl.ds(many, EXTRA)].astype(f32)
    spots = iota((rows, columns_in.shape[0]), 1)
    row = iota((EDGE, 1), 0)
    picked[...] = jnp.zeros_like(picked)
    for k in range(slots):
        edge = jnp.where(
            row == 0,
            right[8 + k : 9 + k, 0:1] * SLOTS + MOST,
            jnp.where(row == EDGE - 1, left[8 + k : 9 + k, 0:1] * SLOTS + MOST + 1, -1.0),
        ).astype(i32)
        wanted = jnp.concatenate([place[k * columns : (k + 1) * columns, 0:1], edge], axis=0)
        chosen = jnp.where(spots == wanted, 1.0, 0.0).astype(bf16)
        found = jnp.dot(chosen, columns_in[...], preferred_element_type=f32)
        for f in range(fields):
            picked[k, pl.ds(f, rows, stride=8), :] = found[:, f * width : (f + 1) * width]

    def one(row, table_of):
        spot = pl.ds(row * 8, 8)
        vector = jnp.concatenate([picked[k, spot, :] for k in range(slots)], axis=1)
        matrix = jnp.concatenate([table_of(k) for k in range(slots)], axis=1)
        solved[spot, :] = lax.dot_general(
            vector.astype(bf16), matrix, (((1,), (1,)), ((), ())), preferred_element_type=f32
        )

    solved[...] = jnp.zeros_like(solved)
    below = many + EXTRA
    one(columns, lambda k: from_right[pl.ds(below + k * width, width)])
    one(rows - 1, lambda k: from_left[pl.ds(below + k * width, width)])
    for spot in range(columns):
        one(spot, lambda k: weights[pl.ds((spot * slots + k) * width, width)])
    on_ocean = section[0] == 1
    for f in range(fields):
        out[f, pl.ds(0, columns)] = solved[pl.ds(f, columns, stride=8), :]
        edge = solved[pl.ds(columns * 8 + f, EDGE, stride=8), :]
        ice = edge_tile(right[2 + f : 3 + f], left[2 + f : 3 + f])
        out[f, pl.ds(columns, EDGE)] = jnp.where(on_ocean, ice, edge)


def finish_kernel(
    section, mine, other, fields, partner_fields, bath, q, rho, side, start, surface, result,
    half, done, sems,
):
    tracers, levels, columns, lanes = start.shape
    rows = columns + EDGE
    chunks = chunks_of(levels)
    on_ocean = section[0] == 1
    lane = iota((rows, lanes), 1)
    flux = [jnp.where(on_ocean, other[f], mine[f]) for f in range(3)]
    own = []
    for f in range(3):
        edge = jnp.where(on_ocean, mine[f, pl.ds(columns, EDGE)], other[f, pl.ds(columns, EDGE)])
        ice = jnp.where(on_ocean, fields[f].astype(f32), partner_fields[f].astype(f32))
        own.append(jnp.concatenate([ice, edge], axis=0))
    forcing = [flux[0] + own[0], flux[1] + own[1]]
    top_mix = TOP_MIX * (1.0 + flux[2] * flux[2] + own[2] * own[2])
    depth = bath[...]

    def top_levels(count, halves, below, rho_below, scale):
        wet = 1 < depth[:count]
        link = jnp.where(wet, top_mix[:count], 0.0)
        deeper = jnp.where(2 < depth[:count], DEEP_MIX - DEEP_MIX * rho_below, 0.0)
        second = 1.0 / (1.0 + link + deeper)
        rho_second = link * second
        first = 1.0 / (1.0 + link - link * rho_second)
        values = []
        for n in range(tracers):
            partial = 2.0 * (halves[n][1] + below[n]) * second
            source = 2.0 * halves[n][0] + scale * FLUX_GAIN * forcing[n][:count]
            surface_value = (source + link * partial) * first
            next_value = jnp.where(wet, partial, 0.0) + rho_second * surface_value
            values.append((surface_value, next_value))
        return values

    values = top_levels(
        rows,
        [(q[n, 0], q[n, 1]) for n in range(tracers)],
        [q[n, 2] for n in range(tracers)],
        rho[2],
        SCALE,
    )

    def store_half(n, level, h):
        half[n, level] = side[level] * h[:columns] + neighbour_sum(h, lane)[:columns]

    for n in range(tracers):
        for level in (0, 1):
            store_half(n, level, values[n][level])

    def down(step, carry):
        level = 2 + step
        ratio = rho[level]
        out = []
        for n in range(tracers):
            h = q[n, level] + ratio * carry[n]
            store_half(n, level, h)
            out.append(h)
        return tuple(out)

    carry = tuple(values[n][1] for n in range(tracers))
    sweep(levels - 2, down, carry, 6)

    def up(step, carry):
        level = levels - 1 - step
        ratio = rho[level, pl.ds(0, columns)]
        out = []
        for n in range(tracers):
            value = ratio * (half[n, level] + carry[n])
            half[n, level] = value
            out.append(value)
        return tuple(out)

    zero = jnp.zeros((columns, lanes), f32)
    carry = sweep(levels - 2, up, (zero,) * tracers, 13)
    values = top_levels(
        columns,
        [(half[n, 0], half[n, 1]) for n in range(tracers)],
        carry,
        rho[2, pl.ds(0, columns)],
        SCALE * SCALE,
    )
    unscale = 1.0 / (SCALE * SCALE)
    for n in range(tracers):
        surface[n] = jnp.where(on_ocean, values[n][0] * unscale, other[n, pl.ds(0, columns)])
    surface[2] = jnp.where(on_ocean, top_mix[:columns], other[2, pl.ds(0, columns)])

    def last(step, carry, low):
        level = low + step
        ratio = rho[level, pl.ds(0, columns)]
        wet = level < bath[pl.ds(0, columns)]
        out = []
        for n in range(tracers):
            h = half[n, level] + ratio * carry[n]
            done[n, level] = jnp.where(wet, h * unscale, start[n, level])
            out.append(h)
        return tuple(out)

    carry = tuple(values[n][1] for n in range(tracers))
    leaving = []
    for n, (low, size) in enumerate(chunks):
        if n == 0:
            for m in range(tracers):
                done[m, 0] = values[m][0] * unscale
                done[m, 1] = jnp.where(
                    1 < depth[:columns], values[m][1] * unscale, start[m, 1]
                )
        first = max(low, 2)
        carry = sweep(low + size - first, functools.partial(last, low=first), carry, 10)
        part = pl.ds(low, size)
        leaving.append(
            pltpu.make_async_copy(done.at[:, part], result.at[:, part], sems.at[n])
        )
        leaving[-1].start()
    for copy in leaving:
        copy.wait()


def shift(value, axis, by):
    count = lax.axis_size(axis)
    return lax.ppermute(value, axis, [(i, (i + by) % count) for i in range(count)])


def per_device(
    surface_fields, source_blocks, source_columns, remap_weights, ocean_state, bathymetry
):
    tracers, levels, columns, lanes = ocean_state.shape
    slots = source_blocks.shape[2]
    count = lax.axis_size("blk")
    rows = columns + EDGE
    section = lax.axis_index("sec").astype(i32).reshape(1)
    fields = surface_fields[0]
    blocks = jnp.transpose(source_blocks[0])
    spots = jnp.transpose(source_columns[0])
    weights = remap_weights[0].reshape(columns * slots * lanes, lanes)
    tall = slots * lanes
    many = tracers * levels

    hbm = pl.BlockSpec(memory_space=pltpu.HBM)
    vmem = pl.BlockSpec(memory_space=pltpu.VMEM)
    smem = pl.BlockSpec(memory_space=pltpu.SMEM)
    shaped = jax.ShapeDtypeStruct
    pieces = len(chunks_of(levels))
    cells = rows * lanes

    payload = shaped((2 * many + EXTRA + tall, lanes), bf16)
    request, place, to_left, to_right, table = pl.pallas_call(
        prepare_kernel,
        out_shape=(
            shaped((count, 128), i32),
            shaped((slots * columns, 128), i32),
            payload,
            payload,
            shaped((columns, 3 * lanes), bf16),
        ),
        in_specs=[smem] + [hbm] * 6,
        out_specs=(vmem,) * 5,
        scratch_shapes=[
            pltpu.VMEM((tracers, levels, 8, lanes), f32),
            pltpu.VMEM((tracers, levels, 8, lanes), f32),
            pltpu.VMEM((tracers, columns, lanes), f32),
            pltpu.VMEM(bathymetry.shape, i32),
            pltpu.VMEM(fields.shape, bf16),
            pltpu.VMEM(blocks.shape, i32),
            pltpu.VMEM(spots.shape, i32),
            pltpu.VMEM((EXTRA, lanes), f32),
            pltpu.SemaphoreType.DMA((9,)),
        ],
        compiler_params=pltpu.CompilerParams(vmem_limit_bytes=8 * MIB),
        cost_estimate=pl.CostEstimate(
            flops=10**6, bytes_accessed=4 * 10**6, transcendentals=0
        ),
    )(section, ocean_state, bathymetry, fields, blocks, spots, weights)
    asked = lax.all_to_all(request, "blk", split_axis=0, concat_axis=0, tiled=True)
    from_left = shift(to_right, "blk", 1)
    from_right = shift(to_left, "blk", -1)
    partner_fields = lax.ppermute(fields, "sec", [(0, 1), (1, 0)])

    served = pl.pallas_call(
        serve_kernel,
        out_shape=shaped((count * SLOTS, 3 * lanes), bf16),
        in_specs=[vmem, vmem],
        out_specs=vmem,
        compiler_params=pltpu.CompilerParams(vmem_limit_bytes=8 * MIB),
        cost_estimate=pl.CostEstimate(
            flops=10**7, bytes_accessed=10**6, transcendentals=0
        ),
    )(asked, table)
    columns_in = lax.all_to_all(served, "blk", split_axis=0, concat_axis=0, tiled=True)

    q, rho, side, start, bath, near_weights = pl.pallas_call(
        start_kernel,
        out_shape=(
            shaped((tracers, levels, rows, lanes), f32),
            shaped((levels, rows, lanes), f32),
            shaped((levels, columns, lanes), f32),
            shaped(ocean_state.shape, f32),
            shaped((rows, lanes), i32),
            shaped(weights.shape, bf16),
        ),
        in_specs=[hbm, vmem, vmem, hbm, hbm, vmem],
        out_specs=(vmem,) * 6,
        scratch_shapes=[
            pltpu.VMEM((many * 8, lanes), f32),
            pltpu.VMEM((4, rows, lanes), i32),
            pltpu.VMEM(bathymetry.shape, i32),
            pltpu.SemaphoreType.DMA((pieces + 2,)),
        ],
        compiler_params=pltpu.CompilerParams(vmem_limit_bytes=8 * MIB),
        cost_estimate=pl.CostEstimate(
            flops=60 * levels * cells, bytes_accessed=20 * levels * cells, transcendentals=0
        ),
    )(ocean_state, from_left, from_right, bathymetry, weights, ratios_by_height(levels, lanes))

    mine = pl.pallas_call(
        remap_kernel,
        out_shape=shaped((3, rows, lanes), f32),
        in_specs=[smem] + [vmem] * 5,
        out_specs=vmem,
        scratch_shapes=[
            pltpu.VMEM((slots, rows * 8, lanes), f32),
            pltpu.VMEM((rows * 8, lanes), f32),
        ],
        compiler_params=pltpu.CompilerParams(vmem_limit_bytes=8 * MIB),
        cost_estimate=pl.CostEstimate(
            flops=16 * weights.size, bytes_accessed=2 * weights.size, transcendentals=0
        ),
    )(section, columns_in, place, from_left, from_right, near_weights)
    other = lax.ppermute(mine, "sec", [(0, 1), (1, 0)])

    surface, result = pl.pallas_call(
        finish_kernel,
        out_shape=(shaped((3, columns, lanes), f32), shaped(ocean_state.shape, f32)),
        in_specs=[smem] + [vmem] * 9,
        out_specs=(vmem, hbm),
        scratch_shapes=[
            pltpu.VMEM(ocean_state.shape, f32),
            pltpu.VMEM(ocean_state.shape, f32),
            pltpu.SemaphoreType.DMA((pieces,)),
        ],
        compiler_params=pltpu.CompilerParams(vmem_limit_bytes=16 * MIB),
        cost_estimate=pl.CostEstimate(
            flops=60 * levels * cells, bytes_accessed=32 * levels * cells, transcendentals=0
        ),
    )(section, mine, other, fields, partner_fields, bath, q, rho, side, start)
    return (surface[None], result)


def solution(mesh):
    return jax.shard_map(
        per_device,
        mesh=mesh,
        in_specs=(
            P("sec", None, "blk", None),
            P("sec", "blk", None),
            P("sec", "blk", None),
            P("sec", "blk", None, None, None),
            P(None, None, "blk", None),
            P("blk", None),
        ),
        out_specs=(P("sec", None, "blk", None), P(None, None, "blk", None)),
        check_vma=False,
    )
```

```python
import functools

import jax
import jax.numpy as jnp
import numpy as np
from jax import lax
from jax.experimental import pallas as pl
from jax.experimental.pallas import tpu as pltpu
from jax.sharding import PartitionSpec as P

FLUX_GAIN = 0.5
SIDE_MIX = 0.2
TOP_MIX = 1.0
DEEP_MIX = 2.0
SCALE = 1.0 / (0.5 * SIDE_MIX)

MOST = 16
SLOTS = 24
EDGE = 8
EXTRA = 16
MIB = 2**20
bf16, f32, i32 = jnp.bfloat16, jnp.float32, jnp.int32


def iota(shape, axis):
    return lax.broadcasted_iota(i32, shape, axis)


def neighbour_sum(h, lane):
    rows, lanes = h.shape
    total = pltpu.roll(h, 1, 0) + pltpu.roll(h, rows - 1, 0)
    total = total + jnp.where(lane == 0, 0.0, pltpu.roll(h, 1, 1))
    return total + jnp.where(lane == lanes - 1, 0.0, pltpu.roll(h, lanes - 1, 1))


def edge_tile(right, left):
    row = iota((EDGE, right.shape[1]), 0)
    return jnp.where(row == 0, right, jnp.where(row == EDGE - 1, left, 0.0))


def chunks_of(levels):
    size = 10 if levels % 10 == 0 else levels
    return [(start, size) for start in range(0, levels, size)]


def sweep(count, body, carry, unroll):
    rounds = count // unroll

    def several(number, carry):
        for n in range(unroll):
            carry = body(number * unroll + n, carry)
        return carry

    carry = lax.fori_loop(0, rounds, several, carry)
    for step in range(rounds * unroll, count):
        carry = body(step, carry)
    return carry


def prepare_kernel(
    section, state, bath, fields, blocks, spots, weights,
    request, place, to_left, to_right, left_weights, right_weights, table,
    low, high, surface, bath_in, fields_in, blocks_in, spots_in, extra, sems,
):
    tracers, levels, columns, lanes = state.shape
    many = tracers * levels
    wide = left_weights.shape[0]
    pairs = [
        (blocks, blocks_in),
        (spots, spots_in),
        (bath, bath_in),
        (fields, fields_in),
        (state.at[:, 0], surface),
        (state.at[:, :, pl.ds(0, 8)], low),
        (state.at[:, :, pl.ds(columns - 8, 8)], high),
        (weights.at[pl.ds(0, wide)], left_weights),
        (weights.at[pl.ds((columns - 1) * wide, wide)], right_weights),
    ]
    copies = [pltpu.make_async_copy(src, dst, sems.at[n]) for n, (src, dst) in enumerate(pairs)]
    for copy in copies:
        copy.start()
    copies[0].wait()
    copies[1].wait()

    count, slots = request.shape[0], blocks.shape[0]
    before = jnp.where(iota((columns, columns), 0) < iota((columns, columns), 1), 1.0, 0.0)
    before = before.astype(bf16)
    slot = iota((128, columns), 0)
    here = iota((128, columns), 1)
    marks = ((slot == MOST) & (here == 0)) | ((slot == MOST + 1) & (here == columns - 1))
    used = jnp.zeros((count, 1), f32)
    asked = jnp.zeros(request.shape, f32)
    for k in range(slots):
        block = blocks_in[k : k + 1, :]
        owner = iota((count, columns), 0) == block
        one_hot = jnp.where(owner, 1.0, 0.0)
        earlier = used + jnp.dot(one_hot.astype(bf16), before, preferred_element_type=f32)
        rank = jnp.sum(one_hot * earlier, axis=0, keepdims=True)
        used = used + jnp.sum(one_hot, axis=1, keepdims=True)
        filled = jnp.where((slot == rank.astype(i32)) | marks, 1.0, 0.0).astype(bf16)
        named = jnp.where(owner, spots_in[k : k + 1, :].astype(f32), 0.0).astype(bf16)
        asked = asked + lax.dot_general(
            named, filled, (((1,), (1,)), ((), ())), preferred_element_type=f32
        )
        arrives = block.astype(f32) * SLOTS + rank
        spread = jnp.transpose(jnp.broadcast_to(arrives, (128, columns)))
        place[k * columns : (k + 1) * columns, :] = spread.astype(i32)
    request[...] = asked.astype(i32)

    copies[2].wait()
    copies[3].wait()
    for out, first, at in ((to_left, 0, 0), (to_right, columns - 2, columns - 1)):
        extra[...] = jnp.zeros_like(extra)
        extra[0:2] = bath_in[first : first + 2].astype(f32)
        for f in range(3):
            extra[2 + f : 3 + f] = fields_in[f].astype(f32)[at : at + 1]
        extra[8 : 8 + slots] = jnp.broadcast_to(
            blocks_in[:, at : at + 1].astype(f32), (slots, lanes)
        )
        out[pl.ds(2 * many, EXTRA)] = extra[...].astype(bf16)
    copies[4].wait()
    on_ocean = section[0] == 1
    for f in range(3):
        own = fields_in[f]
        if f < 2:
            own = jnp.where(on_ocean, surface[f], own.astype(f32)).astype(bf16)
        table[:, f * lanes : (f + 1) * lanes] = own
    copies[5].wait()
    copies[6].wait()
    for c in range(2):
        for n in range(tracers):
            part = pl.ds(c * many + n * levels, levels)
            tiles = low.at[n].reshape(levels * 8, lanes)
            to_left[part] = tiles[pl.ds(c, levels, stride=8), :].astype(bf16)
            tiles = high.at[n].reshape(levels * 8, lanes)
            to_right[part] = tiles[pl.ds(6 + c, levels, stride=8), :].astype(bf16)
    copies[7].wait()
    copies[8].wait()


def serve_kernel(asked, table, out):
    count = asked.shape[0]
    wanted = jnp.transpose(asked[...].astype(f32))[:SLOTS]
    columns = table.shape[0]
    slot = iota((SLOTS, 1), 0)
    parts = []
    for e in range(count):
        after, before = (e + 1) % count, (e - 1) % count
        spot = jnp.where(
            slot == MOST,
            wanted[:, after : after + 1],
            jnp.where(slot == MOST + 1, wanted[:, before : before + 1], wanted[:, e : e + 1]),
        )
        parts.append(jnp.where(iota((SLOTS, columns), 1) == spot.astype(i32), 1.0, 0.0))
    chosen = jnp.concatenate(parts, axis=0).astype(bf16)
    out[...] = jnp.dot(chosen, table[...], preferred_element_type=f32).astype(bf16)


def start_kernel(
    state, from_left, from_right, bath, weights, ratios,
    q_out, rho_out, side_out, held, bath_out, weights_out, halo, near, bath_in, sems,
):
    tracers, levels, columns, lanes = state.shape
    rows = columns + EDGE
    many = tracers * levels
    chunks = chunks_of(levels)
    copies = []
    for n, (low, size) in enumerate(chunks):
        copies.append(
            pltpu.make_async_copy(
                state.at[:, pl.ds(low, size)], held.at[:, pl.ds(low, size)], sems.at[n]
            )
        )
    bath_copy = pltpu.make_async_copy(bath, bath_in, sems.at[len(chunks)])
    weights_copy = pltpu.make_async_copy(weights, weights_out, sems.at[len(chunks) + 1])
    bath_copy.start()
    for copy in reversed(copies):
        copy.start()
    weights_copy.start()
    for c in range(2):
        part = pl.ds(c * many, many)
        halo[pl.ds(c, many, stride=8), :] = from_right[part].astype(f32)
        halo[pl.ds(EDGE - 2 + c, many, stride=8), :] = from_left[part].astype(f32)
    right = from_right[pl.ds(2 * many, EXTRA)].astype(f32)
    left = from_left[pl.ds(2 * many, EXTRA)].astype(f32)
    row = iota((EDGE, lanes), 0)
    edge = jnp.where(
        row == 0,
        right[0:1],
        jnp.where(
            row == 1,
            right[1:2],
            jnp.where(row == EDGE - 2, left[0:1], jnp.where(row == EDGE - 1, left[1:2], 0.0)),
        ),
    )
    bath_copy.wait()
    depth = jnp.concatenate([bath_in[...], edge.astype(i32)], axis=0)
    bath_out[...] = depth
    lane = iota((rows, lanes), 1)
    a = pltpu.roll(depth, 1, 0)
    b = pltpu.roll(depth, rows - 1, 0)
    c = jnp.where(lane == 0, 0, pltpu.roll(depth, 1, 1))
    d = jnp.where(lane == lanes - 1, 0, pltpu.roll(depth, lanes - 1, 1))
    a, b = jnp.maximum(a, b), jnp.minimum(a, b)
    c, d = jnp.maximum(c, d), jnp.minimum(c, d)
    a, c = jnp.maximum(a, c), jnp.minimum(a, c)
    b, d = jnp.maximum(b, d), jnp.minimum(b, d)
    near[0], near[1], near[2], near[3] = a, jnp.maximum(b, c), jnp.minimum(b, c), d

    lookup = jnp.broadcast_to(ratios[0:1], (rows, lanes))

    def side(level):
        wet = level < bath_out[...]
        own = 0.5 * SCALE
        for n in range(4):
            own = jnp.where(level < near[n], 0.5 * SCALE - (n + 1), own)
        side_out[level] = own[:columns]
        halves = []
        for n in range(tracers):
            spot = (n * levels + level) * 8
            if not isinstance(level, int):
                spot = pl.multiple_of(spot, 8)
            full = jnp.concatenate([held[n, level], halo[pl.ds(spot, 8), :]], axis=0)
            h = jnp.where(wet, full, 0.0)
            halves.append(own * h + neighbour_sum(h, lane))
        return halves

    def deep(step, below, top):
        level = top - step
        halves = side(level)
        above_floor = jnp.maximum(bath_out[...] - level, 0)
        rho = jnp.take_along_axis(lookup, above_floor, axis=1, mode="promise_in_bounds")
        rho_out[level] = rho
        solved = []
        for n in range(tracers):
            q = rho * (halves[n] + below[n])
            q_out[n, level] = q
            solved.append(q)
        return tuple(solved)

    carry = tuple(jnp.zeros((rows, lanes), f32) for _ in range(tracers))
    for n in reversed(range(len(chunks))):
        low, size = chunks[n]
        copies[n].wait()
        first = max(low, 2)
        top = low + size - 1
        carry = sweep(top - first + 1, functools.partial(deep, top=top), carry, 5)
    for level in (1, 0):
        halves = side(level)
        rho_out[level] = jnp.zeros((rows, lanes), f32)
        for n in range(tracers):
            q_out[n, level] = halves[n]
    weights_copy.wait()


def ratios_by_height(levels, lanes):
    values = [0.0]
    ratio = DEEP_MIX / (1.0 + DEEP_MIX)
    for _ in range(levels):
        values.append(ratio)
        ratio = DEEP_MIX / (1.0 + DEEP_MIX + DEEP_MIX - DEEP_MIX * ratio)
    values += [0.0] * (lanes - len(values))
    return jnp.broadcast_to(jnp.asarray(np.array(values, np.float32)), (8, lanes))


def remap_kernel(
    section, columns_in, place, from_left, from_right, left_weights, right_weights, weights,
    out, picked, solved,
):
    fields, rows, width = out.shape
    columns = rows - EDGE
    slots = weights.shape[0] // (columns * width)
    many = from_left.shape[0] - EXTRA
    right = from_right[pl.ds(many, EXTRA)].astype(f32)
    left = from_left[pl.ds(many, EXTRA)].astype(f32)
    spots = iota((rows, columns_in.shape[0]), 1)
    row = iota((EDGE, 1), 0)
    picked[...] = jnp.zeros_like(picked)
    for k in range(slots):
        edge = jnp.where(
            row == 0,
            right[8 + k : 9 + k, 0:1] * SLOTS + MOST,
            jnp.where(row == EDGE - 1, left[8 + k : 9 + k, 0:1] * SLOTS + MOST + 1, -1.0),
        ).astype(i32)
        wanted = jnp.concatenate([place[k * columns : (k + 1) * columns, 0:1], edge], axis=0)
        chosen = jnp.where(spots == wanted, 1.0, 0.0).astype(bf16)
        found = jnp.dot(chosen, columns_in[...], preferred_element_type=f32)
        for f in range(fields):
            picked[k, pl.ds(f, rows, stride=8), :] = found[:, f * width : (f + 1) * width]

    def one(row, table_of):
        spot = pl.ds(row * 8, 8)
        vector = jnp.concatenate([picked[k, spot, :] for k in range(slots)], axis=1)
        matrix = jnp.concatenate([table_of(k) for k in range(slots)], axis=1)
        solved[spot, :] = lax.dot_general(
            vector.astype(bf16), matrix, (((1,), (1,)), ((), ())), preferred_element_type=f32
        )

    solved[...] = jnp.zeros_like(solved)
    one(columns, lambda k: right_weights[pl.ds(k * width, width)])
    one(rows - 1, lambda k: left_weights[pl.ds(k * width, width)])
    for spot in range(columns):
        one(spot, lambda k: weights[pl.ds((spot * slots + k) * width, width)])
    on_ocean = section[0] == 1
    for f in range(fields):
        out[f, pl.ds(0, columns)] = solved[pl.ds(f, columns, stride=8), :]
        edge = solved[pl.ds(columns * 8 + f, EDGE, stride=8), :]
        ice = edge_tile(right[2 + f : 3 + f], left[2 + f : 3 + f])
        out[f, pl.ds(columns, EDGE)] = jnp.where(on_ocean, ice, edge)


def finish_kernel(
    section, mine, other, fields, partner_fields, bath, q, rho, side, start, surface, result,
    half, done, sems,
):
    tracers, levels, columns, lanes = start.shape
    rows = columns + EDGE
    chunks = chunks_of(levels)
    on_ocean = section[0] == 1
    lane = iota((rows, lanes), 1)
    flux = [jnp.where(on_ocean, other[f], mine[f]) for f in range(3)]
    own = []
    for f in range(3):
        edge = jnp.where(on_ocean, mine[f, pl.ds(columns, EDGE)], other[f, pl.ds(columns, EDGE)])
        ice = jnp.where(on_ocean, fields[f].astype(f32), partner_fields[f].astype(f32))
        own.append(jnp.concatenate([ice, edge], axis=0))
    forcing = [flux[0] + own[0], flux[1] + own[1]]
    top_mix = TOP_MIX * (1.0 + flux[2] * flux[2] + own[2] * own[2])
    depth = bath[...]

    def top_levels(count, halves, below, rho_below, scale):
        wet = 1 < depth[:count]
        link = jnp.where(wet, top_mix[:count], 0.0)
        deeper = jnp.where(2 < depth[:count], DEEP_MIX - DEEP_MIX * rho_below, 0.0)
        second = 1.0 / (1.0 + link + deeper)
        rho_second = link * second
        first = 1.0 / (1.0 + link - link * rho_second)
        values = []
        for n in range(tracers):
            partial = 2.0 * (halves[n][1] + below[n]) * second
            source = 2.0 * halves[n][0] + scale * FLUX_GAIN * forcing[n][:count]
            surface_value = (source + link * partial) * first
            next_value = jnp.where(wet, partial, 0.0) + rho_second * surface_value
            values.append((surface_value, next_value))
        return values

    values = top_levels(
        rows,
        [(q[n, 0], q[n, 1]) for n in range(tracers)],
        [q[n, 2] for n in range(tracers)],
        rho[2],
        SCALE,
    )

    def store_half(n, level, h):
        half[n, level] = side[level] * h[:columns] + neighbour_sum(h, lane)[:columns]

    for n in range(tracers):
        for level in (0, 1):
            store_half(n, level, values[n][level])

    def down(step, carry):
        level = 2 + step
        ratio = rho[level]
        out = []
        for n in range(tracers):
            h = q[n, level] + ratio * carry[n]
            store_half(n, level, h)
            out.append(h)
        return tuple(out)

    carry = tuple(values[n][1] for n in range(tracers))
    sweep(levels - 2, down, carry, 6)

    def up(step, carry):
        level = levels - 1 - step
        ratio = rho[level, pl.ds(0, columns)]
        out = []
        for n in range(tracers):
            value = ratio * (half[n, level] + carry[n])
            half[n, level] = value
            out.append(value)
        return tuple(out)

    zero = jnp.zeros((columns, lanes), f32)
    carry = sweep(levels - 2, up, (zero,) * tracers, 13)
    values = top_levels(
        columns,
        [(half[n, 0], half[n, 1]) for n in range(tracers)],
        carry,
        rho[2, pl.ds(0, columns)],
        SCALE * SCALE,
    )
    unscale = 1.0 / (SCALE * SCALE)
    for n in range(tracers):
        surface[n] = jnp.where(on_ocean, values[n][0] * unscale, other[n, pl.ds(0, columns)])
    surface[2] = jnp.where(on_ocean, top_mix[:columns], other[2, pl.ds(0, columns)])

    def last(step, carry, low):
        level = low + step
        ratio = rho[level, pl.ds(0, columns)]
        wet = level < bath[pl.ds(0, columns)]
        out = []
        for n in range(tracers):
            h = half[n, level] + ratio * carry[n]
            done[n, level] = jnp.where(wet, h * unscale, start[n, level])
            out.append(h)
        return tuple(out)

    carry = tuple(values[n][1] for n in range(tracers))
    leaving = []
    for n, (low, size) in enumerate(chunks):
        if n == 0:
            for m in range(tracers):
                done[m, 0] = values[m][0] * unscale
                done[m, 1] = jnp.where(
                    1 < depth[:columns], values[m][1] * unscale, start[m, 1]
                )
        first = max(low, 2)
        carry = sweep(low + size - first, functools.partial(last, low=first), carry, 10)
        part = pl.ds(low, size)
        leaving.append(
            pltpu.make_async_copy(done.at[:, part], result.at[:, part], sems.at[n])
        )
        leaving[-1].start()
    for copy in leaving:
        copy.wait()


def shift(value, axis, by):
    count = lax.axis_size(axis)
    return lax.ppermute(value, axis, [(i, (i + by) % count) for i in range(count)])


def shift_first_section(value, by):
    count = lax.axis_size("blk")
    return lax.ppermute(value, ("sec", "blk"), [(i, (i + by) % count) for i in range(count)])


def in_hbm(value):
    return pltpu.with_memory_space_constraint(value, pltpu.HBM)


def in_vmem(value):
    return pltpu.with_memory_space_constraint(value, pltpu.VMEM)


def per_device(
    surface_fields, source_blocks, source_columns, remap_weights, ocean_state, bathymetry
):
    tracers, levels, columns, lanes = ocean_state.shape
    slots = source_blocks.shape[2]
    count = lax.axis_size("blk")
    rows = columns + EDGE
    section = lax.axis_index("sec").astype(i32).reshape(1)
    fields = surface_fields[0]
    blocks = jnp.transpose(source_blocks[0])
    spots = jnp.transpose(source_columns[0])
    weights = remap_weights[0].reshape(columns * slots * lanes, lanes)
    tall = slots * lanes
    many = tracers * levels

    hbm = pl.BlockSpec(memory_space=pltpu.HBM)
    vmem = pl.BlockSpec(memory_space=pltpu.VMEM)
    smem = pl.BlockSpec(memory_space=pltpu.SMEM)
    shaped = jax.ShapeDtypeStruct
    pieces = len(chunks_of(levels))
    cells = rows * lanes

    payload = pltpu.VMEM((2 * many + EXTRA, lanes), bf16)
    edge_weights = pltpu.VMEM((tall, lanes), bf16)
    request, place, to_left, to_right, to_left_weights, to_right_weights, table = pl.pallas_call(
        prepare_kernel,
        out_shape=(
            pltpu.VMEM((count, 128), i32),
            pltpu.VMEM((slots * columns, 128), i32),
            payload,
            payload,
            edge_weights,
            edge_weights,
            pltpu.VMEM((columns, 3 * lanes), bf16),
        ),
        in_specs=[smem] + [hbm] * 6,
        out_specs=(vmem,) * 7,
        scratch_shapes=[
            pltpu.VMEM((tracers, levels, 8, lanes), f32),
            pltpu.VMEM((tracers, levels, 8, lanes), f32),
            pltpu.VMEM((tracers, columns, lanes), f32),
            pltpu.VMEM(bathymetry.shape, i32),
            pltpu.VMEM(fields.shape, bf16),
            pltpu.VMEM(blocks.shape, i32),
            pltpu.VMEM(spots.shape, i32),
            pltpu.VMEM((EXTRA, lanes), f32),
            pltpu.SemaphoreType.DMA((9,)),
        ],
        compiler_params=pltpu.CompilerParams(vmem_limit_bytes=8 * MIB),
        cost_estimate=pl.CostEstimate(
            flops=10**6, bytes_accessed=4 * 10**6, transcendentals=0
        ),
    )(
        section,
        in_hbm(ocean_state),
        in_hbm(bathymetry),
        in_hbm(fields),
        in_hbm(blocks),
        in_hbm(spots),
        in_hbm(weights),
    )
    asked = lax.all_to_all(request, "blk", split_axis=0, concat_axis=0, tiled=True)
    from_left = shift(to_right, "blk", 1)
    from_right = shift(to_left, "blk", -1)
    left_weights = shift_first_section(to_right_weights, 1)
    right_weights = shift_first_section(to_left_weights, -1)
    partner_fields = lax.ppermute(fields, "sec", [(0, 1), (1, 0)])

    served = pl.pallas_call(
        serve_kernel,
        out_shape=pltpu.VMEM((count * SLOTS, 3 * lanes), bf16),
        in_specs=[vmem, vmem],
        out_specs=vmem,
        compiler_params=pltpu.CompilerParams(vmem_limit_bytes=8 * MIB),
        cost_estimate=pl.CostEstimate(
            flops=10**7, bytes_accessed=10**6, transcendentals=0
        ),
    )(in_vmem(asked), in_vmem(table))
    columns_in = lax.all_to_all(served, "blk", split_axis=0, concat_axis=0, tiled=True)

    q, rho, side, start, bath, near_weights = pl.pallas_call(
        start_kernel,
        out_shape=(
            pltpu.VMEM((tracers, levels, rows, lanes), f32),
            pltpu.VMEM((levels, rows, lanes), f32),
            pltpu.VMEM((levels, columns, lanes), f32),
            pltpu.VMEM(ocean_state.shape, f32),
            pltpu.VMEM((rows, lanes), i32),
            pltpu.VMEM(weights.shape, bf16),
        ),
        in_specs=[hbm, vmem, vmem, hbm, hbm, vmem],
        out_specs=(vmem,) * 6,
        scratch_shapes=[
            pltpu.VMEM((many * 8, lanes), f32),
            pltpu.VMEM((4, rows, lanes), i32),
            pltpu.VMEM(bathymetry.shape, i32),
            pltpu.SemaphoreType.DMA((pieces + 2,)),
        ],
        compiler_params=pltpu.CompilerParams(vmem_limit_bytes=8 * MIB),
        cost_estimate=pl.CostEstimate(
            flops=60 * levels * cells, bytes_accessed=200 * levels * cells, transcendentals=0
        ),
    )(
        in_hbm(ocean_state),
        in_vmem(from_left),
        in_vmem(from_right),
        in_hbm(bathymetry),
        in_hbm(weights),
        ratios_by_height(levels, lanes),
    )

    mine = pl.pallas_call(
        remap_kernel,
        out_shape=pltpu.VMEM((3, rows, lanes), f32),
        in_specs=[smem] + [vmem] * 7,
        out_specs=vmem,
        scratch_shapes=[
            pltpu.VMEM((slots, rows * 8, lanes), f32),
            pltpu.VMEM((rows * 8, lanes), f32),
        ],
        compiler_params=pltpu.CompilerParams(vmem_limit_bytes=8 * MIB),
        cost_estimate=pl.CostEstimate(
            flops=16 * weights.size, bytes_accessed=2 * weights.size, transcendentals=0
        ),
    )(
        section,
        in_vmem(columns_in),
        in_vmem(place),
        in_vmem(from_left),
        in_vmem(from_right),
        in_vmem(left_weights),
        in_vmem(right_weights),
        in_vmem(near_weights),
    )
    other = lax.ppermute(mine, "sec", [(0, 1), (1, 0)])

    surface, result = pl.pallas_call(
        finish_kernel,
        out_shape=(shaped((3, columns, lanes), f32), shaped(ocean_state.shape, f32)),
        in_specs=[smem] + [vmem] * 9,
        out_specs=(vmem, hbm),
        scratch_shapes=[
            pltpu.VMEM(ocean_state.shape, f32),
            pltpu.VMEM(ocean_state.shape, f32),
            pltpu.SemaphoreType.DMA((pieces,)),
        ],
        compiler_params=pltpu.CompilerParams(vmem_limit_bytes=16 * MIB),
        cost_estimate=pl.CostEstimate(
            flops=60 * levels * cells, bytes_accessed=32 * levels * cells, transcendentals=0
        ),
    )(
        section,
        in_vmem(mine),
        in_vmem(other),
        fields,
        partner_fields,
        in_vmem(bath),
        in_vmem(q),
        in_vmem(rho),
        in_vmem(side),
        in_vmem(start),
    )
    return (surface[None], result)


def solution(mesh):
    return jax.shard_map(
        per_device,
        mesh=mesh,
        in_specs=(
            P("sec", None, "blk", None),
            P("sec", "blk", None),
            P("sec", "blk", None),
            P("sec", "blk", None, None, None),
            P(None, None, "blk", None),
            P("blk", None),
        ),
        out_specs=(P("sec", None, "blk", None), P(None, None, "blk", None)),
        check_vma=False,
    )
```

```python
import functools

import jax
import jax.numpy as jnp
import numpy as np
from jax import lax
from jax.experimental import pallas as pl
from jax.experimental.pallas import tpu as pltpu
from jax.sharding import PartitionSpec as P

FLUX_GAIN = 0.5
SIDE_MIX = 0.2
TOP_MIX = 1.0
DEEP_MIX = 2.0
SCALE = 1.0 / (0.5 * SIDE_MIX)

MOST = 16
SLOTS = 24
EDGE = 8
EXTRA = 16
MIB = 2**20
bf16, f32, i32 = jnp.bfloat16, jnp.float32, jnp.int32


def iota(shape, axis):
    return lax.broadcasted_iota(i32, shape, axis)


def neighbour_sum(h, lane):
    rows, lanes = h.shape
    total = pltpu.roll(h, 1, 0) + pltpu.roll(h, rows - 1, 0)
    total = total + jnp.where(lane == 0, 0.0, pltpu.roll(h, 1, 1))
    return total + jnp.where(lane == lanes - 1, 0.0, pltpu.roll(h, lanes - 1, 1))


def edge_tile(right, left):
    row = iota((EDGE, right.shape[1]), 0)
    return jnp.where(row == 0, right, jnp.where(row == EDGE - 1, left, 0.0))


def chunks_of(levels):
    size = 10 if levels % 10 == 0 else levels
    return [(start, size) for start in range(0, levels, size)]


def sweep(count, body, carry, unroll):
    rounds = count // unroll

    def several(number, carry):
        for n in range(unroll):
            carry = body(number * unroll + n, carry)
        return carry

    carry = lax.fori_loop(0, rounds, several, carry)
    for step in range(rounds * unroll, count):
        carry = body(step, carry)
    return carry


def ranks(blocks, count):
    slots, columns = blocks.shape
    before = jnp.where(iota((columns, columns), 0) < iota((columns, columns), 1), 1.0, 0.0)
    before = before.astype(bf16)
    used = jnp.zeros((count, 1), f32)
    result = []
    for k in range(slots):
        owner = iota((count, columns), 0) == blocks[k : k + 1, :]
        one_hot = jnp.where(owner, 1.0, 0.0)
        earlier = used + jnp.dot(one_hot.astype(bf16), before, preferred_element_type=f32)
        rank = jnp.sum(one_hot * earlier, axis=0, keepdims=True)
        used = used + jnp.sum(one_hot, axis=1, keepdims=True)
        result.append((owner, rank))
    return result


def ask_kernel(blocks, spots, request, blocks_in, spots_in, sems):
    copies = [
        pltpu.make_async_copy(blocks, blocks_in, sems.at[0]),
        pltpu.make_async_copy(spots, spots_in, sems.at[1]),
    ]
    for copy in copies:
        copy.start()
    for copy in copies:
        copy.wait()
    count, columns = request.shape[0], blocks.shape[1]
    slot = iota((128, columns), 0)
    here = iota((128, columns), 1)
    marks = ((slot == MOST) & (here == 0)) | ((slot == MOST + 1) & (here == columns - 1))
    asked = jnp.zeros(request.shape, f32)
    for k, (owner, rank) in enumerate(ranks(blocks_in, count)):
        filled = jnp.where((slot == rank.astype(i32)) | marks, 1.0, 0.0).astype(bf16)
        named = jnp.where(owner, spots_in[k : k + 1, :].astype(f32), 0.0).astype(bf16)
        asked = asked + lax.dot_general(
            named, filled, (((1,), (1,)), ((), ())), preferred_element_type=f32
        )
    request[...] = asked.astype(i32)


def pack_kernel(
    section, state, bath, fields, blocks, weights,
    to_left, to_right, table, left_weights, right_weights,
    low, high, surface, bath_in, fields_in, blocks_in, extra, sems,
):
    tracers, levels, columns, lanes = state.shape
    slots = blocks.shape[0]
    many = tracers * levels
    wide = left_weights.shape[0]
    pairs = [
        (state.at[:, :, pl.ds(0, 8)], low),
        (state.at[:, :, pl.ds(columns - 8, 8)], high),
        (blocks, blocks_in),
        (bath, bath_in),
        (fields, fields_in),
        (state.at[:, 0], surface),
        (weights.at[pl.ds(0, wide)], left_weights),
        (weights.at[pl.ds((columns - 1) * wide, wide)], right_weights),
    ]
    copies = [pltpu.make_async_copy(src, dst, sems.at[n]) for n, (src, dst) in enumerate(pairs)]
    for copy in copies:
        copy.start()
    for copy in copies[2:6]:
        copy.wait()
    for out, first, at in ((to_left, 0, 0), (to_right, columns - 2, columns - 1)):
        extra[...] = jnp.zeros_like(extra)
        extra[0:2] = bath_in[first : first + 2].astype(f32)
        for f in range(3):
            extra[2 + f : 3 + f] = fields_in[f].astype(f32)[at : at + 1]
        extra[8 : 8 + slots] = jnp.broadcast_to(
            blocks_in[:, at : at + 1].astype(f32), (slots, lanes)
        )
        out[pl.ds(2 * many, EXTRA)] = extra[...].astype(bf16)
    on_ocean = section[0] == 1
    for f in range(3):
        own = fields_in[f]
        if f < 2:
            own = jnp.where(on_ocean, surface[f], own.astype(f32)).astype(bf16)
        table[:, f * lanes : (f + 1) * lanes] = own
    copies[0].wait()
    copies[1].wait()
    for c in range(2):
        for n in range(tracers):
            part = pl.ds(c * many + n * levels, levels)
            tiles = low.at[n].reshape(levels * 8, lanes)
            to_left[part] = tiles[pl.ds(c, levels, stride=8), :].astype(bf16)
            tiles = high.at[n].reshape(levels * 8, lanes)
            to_right[part] = tiles[pl.ds(6 + c, levels, stride=8), :].astype(bf16)
    copies[6].wait()
    copies[7].wait()


def serve_kernel(asked, table, from_left, from_right, out):
    count = asked.shape[0]
    wanted = jnp.transpose(asked[...].astype(f32))[:SLOTS]
    columns = table.shape[0]
    slot = iota((SLOTS, 1), 0)
    parts = []
    for e in range(count):
        after, before = (e + 1) % count, (e - 1) % count
        spot = jnp.where(
            slot == MOST,
            wanted[:, after : after + 1],
            jnp.where(slot == MOST + 1, wanted[:, before : before + 1], wanted[:, e : e + 1]),
        )
        parts.append(jnp.where(iota((SLOTS, columns), 1) == spot.astype(i32), 1.0, 0.0))
    chosen = jnp.concatenate(parts, axis=0).astype(bf16)
    out[...] = jnp.dot(chosen, table[...], preferred_element_type=f32).astype(bf16)


def start_kernel(
    state, from_left, from_right, bath, blocks, ratios,
    q_result, rho_result, side_result, bath_result, place_result,
    q_out, rho_out, side_out, held, bath_out, halo, near, bath_in, blocks_in, place, sems, sems_out,
    *, count,
):
    tracers, levels, columns, lanes = state.shape
    rows = columns + EDGE
    many = tracers * levels
    chunks = chunks_of(levels)
    copies = []
    for n, (low, size) in enumerate(chunks):
        copies.append(
            pltpu.make_async_copy(
                state.at[:, pl.ds(low, size)], held.at[:, pl.ds(low, size)], sems.at[n]
            )
        )
    bath_copy = pltpu.make_async_copy(bath, bath_in, sems.at[len(chunks)])
    blocks_copy = pltpu.make_async_copy(blocks, blocks_in, sems.at[len(chunks) + 1])
    blocks_copy.start()
    bath_copy.start()
    for copy in reversed(copies):
        copy.start()
    leaving = []

    def send(source, target, number):
        copy = pltpu.make_async_copy(source, target, sems_out.at[number])
        copy.start()
        leaving.append(copy)

    for c in range(2):
        part = pl.ds(c * many, many)
        halo[pl.ds(c, many, stride=8), :] = from_right[part].astype(f32)
        halo[pl.ds(EDGE - 2 + c, many, stride=8), :] = from_left[part].astype(f32)
    right = from_right[pl.ds(2 * many, EXTRA)].astype(f32)
    left = from_left[pl.ds(2 * many, EXTRA)].astype(f32)
    row = iota((EDGE, lanes), 0)
    edge = jnp.where(
        row == 0,
        right[0:1],
        jnp.where(
            row == 1,
            right[1:2],
            jnp.where(row == EDGE - 2, left[0:1], jnp.where(row == EDGE - 1, left[1:2], 0.0)),
        ),
    )
    bath_copy.wait()
    depth = jnp.concatenate([bath_in[...], edge.astype(i32)], axis=0)
    bath_out[...] = depth
    send(bath_out, bath_result, 3 * len(chunks))
    blocks_copy.wait()
    for k, (_, rank) in enumerate(ranks(blocks_in, count)):
        arrives = blocks_in[k : k + 1, :].astype(f32) * SLOTS + rank
        spread = jnp.transpose(jnp.broadcast_to(arrives, (128, columns)))
        place[k * columns : (k + 1) * columns, :] = spread.astype(i32)
    send(place, place_result, 3 * len(chunks) + 1)
    lane = iota((rows, lanes), 1)
    a = pltpu.roll(depth, 1, 0)
    b = pltpu.roll(depth, rows - 1, 0)
    c = jnp.where(lane == 0, 0, pltpu.roll(depth, 1, 1))
    d = jnp.where(lane == lanes - 1, 0, pltpu.roll(depth, lanes - 1, 1))
    a, b = jnp.maximum(a, b), jnp.minimum(a, b)
    c, d = jnp.maximum(c, d), jnp.minimum(c, d)
    a, c = jnp.maximum(a, c), jnp.minimum(a, c)
    b, d = jnp.maximum(b, d), jnp.minimum(b, d)
    near[0], near[1], near[2], near[3] = a, jnp.maximum(b, c), jnp.minimum(b, c), d

    lookup = jnp.broadcast_to(ratios[0:1], (rows, lanes))

    def side(level):
        wet = level < bath_out[...]
        own = 0.5 * SCALE
        for n in range(4):
            own = jnp.where(level < near[n], 0.5 * SCALE - (n + 1), own)
        side_out[level] = own[:columns]
        halves = []
        for n in range(tracers):
            spot = (n * levels + level) * 8
            if not isinstance(level, int):
                spot = pl.multiple_of(spot, 8)
            full = jnp.concatenate([held[n, level], halo[pl.ds(spot, 8), :]], axis=0)
            h = jnp.where(wet, full, 0.0)
            halves.append(own * h + neighbour_sum(h, lane))
        return halves

    def deep(step, below, top):
        level = top - step
        halves = side(level)
        above_floor = jnp.maximum(bath_out[...] - level, 0)
        rho = jnp.take_along_axis(lookup, above_floor, axis=1, mode="promise_in_bounds")
        rho_out[level] = rho
        solved = []
        for n in range(tracers):
            q = rho * (halves[n] + below[n])
            q_out[n, level] = q
            solved.append(q)
        return tuple(solved)

    carry = tuple(jnp.zeros((rows, lanes), f32) for _ in range(tracers))
    for n in reversed(range(len(chunks))):
        low, size = chunks[n]
        copies[n].wait()
        first = max(low, 2)
        top = low + size - 1
        carry = sweep(top - first + 1, functools.partial(deep, top=top), carry, 5)
        if n == 0:
            for level in (1, 0):
                halves = side(level)
                rho_out[level] = jnp.zeros((rows, lanes), f32)
                for m in range(tracers):
                    q_out[m, level] = halves[m]
        part = pl.ds(low, size)
        send(q_out.at[:, part], q_result.at[:, part], 3 * n)
        send(rho_out.at[part], rho_result.at[part], 3 * n + 1)
        send(side_out.at[part], side_result.at[part], 3 * n + 2)
    for copy in leaving:
        copy.wait()


def ratios_by_height(levels, lanes):
    values = [0.0]
    ratio = DEEP_MIX / (1.0 + DEEP_MIX)
    for _ in range(levels):
        values.append(ratio)
        ratio = DEEP_MIX / (1.0 + DEEP_MIX + DEEP_MIX - DEEP_MIX * ratio)
    values += [0.0] * (lanes - len(values))
    return jnp.broadcast_to(jnp.asarray(np.array(values, np.float32)), (8, lanes))


def remap_kernel(
    section, columns_in, place_from, from_left, from_right, left_weights, right_weights, weights,
    out, picked, solved, held, held_left, held_right, place, sems,
):
    fields, rows, width = out.shape
    columns = rows - EDGE
    slots = weights.shape[0] // (columns * width)
    many = from_left.shape[0] - EXTRA
    tall = slots * width
    group = 8
    place_copy = pltpu.make_async_copy(place_from, place, sems.at[0])
    edge_copies = [
        pltpu.make_async_copy(left_weights, held_left, sems.at[1]),
        pltpu.make_async_copy(right_weights, held_right, sems.at[2]),
    ]
    copies = []
    for n in range(columns // group):
        part = pl.ds(n * group * tall, group * tall)
        copies.append(pltpu.make_async_copy(weights.at[part], held.at[part], sems.at[3 + n]))
    for copy in [place_copy] + copies + edge_copies:
        copy.start()
    right = from_right[pl.ds(many, EXTRA)].astype(f32)
    left = from_left[pl.ds(many, EXTRA)].astype(f32)
    spots = iota((rows, columns_in.shape[0]), 1)
    row = iota((EDGE, 1), 0)
    picked[...] = jnp.zeros_like(picked)
    place_copy.wait()
    for k in range(slots):
        edge = jnp.where(
            row == 0,
            right[8 + k : 9 + k, 0:1] * SLOTS + MOST,
            jnp.where(row == EDGE - 1, left[8 + k : 9 + k, 0:1] * SLOTS + MOST + 1, -1.0),
        ).astype(i32)
        wanted = jnp.concatenate([place[k * columns : (k + 1) * columns, 0:1], edge], axis=0)
        chosen = jnp.where(spots == wanted, 1.0, 0.0).astype(bf16)
        found = jnp.dot(chosen, columns_in[...], preferred_element_type=f32)
        for f in range(fields):
            picked[k, pl.ds(f, rows, stride=8), :] = found[:, f * width : (f + 1) * width]

    def one(row, table_of):
        spot = pl.ds(row * 8, 8)
        vector = jnp.concatenate([picked[k, spot, :] for k in range(slots)], axis=1)
        matrix = jnp.concatenate([table_of(k) for k in range(slots)], axis=1)
        solved[spot, :] = lax.dot_general(
            vector.astype(bf16), matrix, (((1,), (1,)), ((), ())), preferred_element_type=f32
        )

    solved[...] = jnp.zeros_like(solved)
    for n in range(columns // group):
        copies[n].wait()
        for m in range(group):
            spot = n * group + m
            one(spot, lambda k: held[pl.ds((spot * slots + k) * width, width)])
    for copy in edge_copies:
        copy.wait()
    one(columns, lambda k: held_right[pl.ds(k * width, width)])
    one(rows - 1, lambda k: held_left[pl.ds(k * width, width)])
    on_ocean = section[0] == 1
    for f in range(fields):
        out[f, pl.ds(0, columns)] = solved[pl.ds(f, columns, stride=8), :]
        edge = solved[pl.ds(columns * 8 + f, EDGE, stride=8), :]
        ice = edge_tile(right[2 + f : 3 + f], left[2 + f : 3 + f])
        out[f, pl.ds(columns, EDGE)] = jnp.where(on_ocean, ice, edge)


def finish_kernel(
    section, mine, other, fields, partner_fields, bath_from, q_from, rho_from, side_from, state,
    surface, result,
    q, rho, side, held, bath, sems, sems_out,
):
    tracers, levels, columns, lanes = state.shape
    rows = columns + EDGE
    chunks = chunks_of(levels)
    bath_copy = pltpu.make_async_copy(bath_from, bath, sems.at[len(chunks), 0])
    bath_copy.start()
    arrivals, starts = [], []
    for n, (low, size) in enumerate(chunks):
        part = pl.ds(low, size)
        arrivals.append(
            (
                pltpu.make_async_copy(q_from.at[:, part], q.at[:, part], sems.at[n, 0]),
                pltpu.make_async_copy(rho_from.at[part], rho.at[part], sems.at[n, 1]),
                pltpu.make_async_copy(side_from.at[part], side.at[part], sems.at[n, 2]),
            )
        )
        starts.append(pltpu.make_async_copy(state.at[:, part], held.at[:, part], sems.at[n, 3]))
    for group in arrivals:
        for copy in group:
            copy.start()
    for copy in starts:
        copy.start()
    bath_copy.wait()
    for copy in arrivals[0]:
        copy.wait()
    on_ocean = section[0] == 1
    lane = iota((rows, lanes), 1)
    flux = [jnp.where(on_ocean, other[f], mine[f]) for f in range(3)]
    own = []
    for f in range(3):
        edge = jnp.where(on_ocean, mine[f, pl.ds(columns, EDGE)], other[f, pl.ds(columns, EDGE)])
        ice = jnp.where(on_ocean, fields[f].astype(f32), partner_fields[f].astype(f32))
        own.append(jnp.concatenate([ice, edge], axis=0))
    forcing = [flux[0] + own[0], flux[1] + own[1]]
    top_mix = TOP_MIX * (1.0 + flux[2] * flux[2] + own[2] * own[2])
    depth = bath[...]

    def top_levels(count, halves, below, rho_below, scale):
        wet = 1 < depth[:count]
        link = jnp.where(wet, top_mix[:count], 0.0)
        deeper = jnp.where(2 < depth[:count], DEEP_MIX - DEEP_MIX * rho_below, 0.0)
        second = 1.0 / (1.0 + link + deeper)
        rho_second = link * second
        first = 1.0 / (1.0 + link - link * rho_second)
        values = []
        for n in range(tracers):
            partial = 2.0 * (halves[n][1] + below[n]) * second
            source = 2.0 * halves[n][0] + scale * FLUX_GAIN * forcing[n][:count]
            surface_value = (source + link * partial) * first
            next_value = jnp.where(wet, partial, 0.0) + rho_second * surface_value
            values.append((surface_value, next_value))
        return values

    values = top_levels(
        rows,
        [(q[n, 0], q[n, 1]) for n in range(tracers)],
        [q[n, 2] for n in range(tracers)],
        rho[2],
        SCALE,
    )

    def store_half(n, level, h):
        q[n, level, pl.ds(0, columns)] = side[level] * h[:columns] + neighbour_sum(h, lane)[:columns]

    for n in range(tracers):
        for level in (0, 1):
            store_half(n, level, values[n][level])

    def down(step, carry, low):
        level = low + step
        ratio = rho[level]
        out = []
        for n in range(tracers):
            h = q[n, level] + ratio * carry[n]
            store_half(n, level, h)
            out.append(h)
        return tuple(out)

    carry = tuple(values[n][1] for n in range(tracers))
    for n, (low, size) in enumerate(chunks):
        if n > 0:
            for copy in arrivals[n]:
                copy.wait()
        first = max(low, 2)
        carry = sweep(low + size - first, functools.partial(down, low=first), carry, 5)

    def up(step, carry):
        level = levels - 1 - step
        ratio = rho[level, pl.ds(0, columns)]
        out = []
        for n in range(tracers):
            value = ratio * (q[n, level, pl.ds(0, columns)] + carry[n])
            q[n, level, pl.ds(0, columns)] = value
            out.append(value)
        return tuple(out)

    zero = jnp.zeros((columns, lanes), f32)
    carry = sweep(levels - 2, up, (zero,) * tracers, 13)
    values = top_levels(
        columns,
        [(q[n, 0, pl.ds(0, columns)], q[n, 1, pl.ds(0, columns)]) for n in range(tracers)],
        carry,
        rho[2, pl.ds(0, columns)],
        SCALE * SCALE,
    )
    unscale = 1.0 / (SCALE * SCALE)
    for n in range(tracers):
        surface[n] = jnp.where(on_ocean, values[n][0] * unscale, other[n, pl.ds(0, columns)])
    surface[2] = jnp.where(on_ocean, top_mix[:columns], other[2, pl.ds(0, columns)])

    def last(step, carry, low):
        level = low + step
        ratio = rho[level, pl.ds(0, columns)]
        wet = level < bath[pl.ds(0, columns)]
        out = []
        for n in range(tracers):
            h = q[n, level, pl.ds(0, columns)] + ratio * carry[n]
            held[n, level] = jnp.where(wet, h * unscale, held[n, level])
            out.append(h)
        return tuple(out)

    carry = tuple(values[n][1] for n in range(tracers))
    leaving = []
    for n, (low, size) in enumerate(chunks):
        starts[n].wait()
        if n == 0:
            for m in range(tracers):
                held[m, 0] = values[m][0] * unscale
                held[m, 1] = jnp.where(
                    1 < depth[:columns], values[m][1] * unscale, held[m, 1]
                )
        first = max(low, 2)
        carry = sweep(low + size - first, functools.partial(last, low=first), carry, 10)
        part = pl.ds(low, size)
        leaving.append(
            pltpu.make_async_copy(held.at[:, part], result.at[:, part], sems_out.at[n])
        )
        leaving[-1].start()
    for copy in leaving:
        copy.wait()


def shift(value, axis, by):
    count = lax.axis_size(axis)
    return lax.ppermute(value, axis, [(i, (i + by) % count) for i in range(count)])


def shift_first_section(value, by):
    count = lax.axis_size("blk")
    return lax.ppermute(value, ("sec", "blk"), [(i, (i + by) % count) for i in range(count)])


def in_hbm(value):
    return pltpu.with_memory_space_constraint(value, pltpu.HBM)


def per_device(
    surface_fields, source_blocks, source_columns, remap_weights, ocean_state, bathymetry
):
    tracers, levels, columns, lanes = ocean_state.shape
    slots = source_blocks.shape[2]
    count = lax.axis_size("blk")
    rows = columns + EDGE
    section = lax.axis_index("sec").astype(i32).reshape(1)
    fields = surface_fields[0]
    blocks = jnp.transpose(source_blocks[0])
    spots = jnp.transpose(source_columns[0])
    weights = remap_weights[0].reshape(columns * slots * lanes, lanes)
    tall = slots * lanes
    many = tracers * levels

    hbm = pl.BlockSpec(memory_space=pltpu.HBM)
    anywhere = pl.BlockSpec(memory_space=pl.ANY)
    vmem = pl.BlockSpec(memory_space=pltpu.VMEM)
    smem = pl.BlockSpec(memory_space=pltpu.SMEM)
    shaped = jax.ShapeDtypeStruct
    pieces = len(chunks_of(levels))
    cells = rows * lanes

    request = pl.pallas_call(
        ask_kernel,
        out_shape=shaped((count, 128), i32),
        in_specs=[hbm, hbm],
        out_specs=vmem,
        scratch_shapes=[
            pltpu.VMEM(blocks.shape, i32),
            pltpu.VMEM(spots.shape, i32),
            pltpu.SemaphoreType.DMA((2,)),
        ],
        compiler_params=pltpu.CompilerParams(vmem_limit_bytes=4 * MIB),
        cost_estimate=pl.CostEstimate(flops=10**6, bytes_accessed=10**5, transcendentals=0),
    )(in_hbm(blocks), in_hbm(spots))
    asked = lax.all_to_all(request, "blk", split_axis=0, concat_axis=0, tiled=True)

    payload = shaped((2 * many + EXTRA, lanes), bf16)
    edge_weights = pltpu.HBM((tall, lanes), bf16)
    to_left, to_right, table, to_left_weights, to_right_weights = pl.pallas_call(
        pack_kernel,
        out_shape=(
            payload,
            payload,
            shaped((columns, 3 * lanes), bf16),
            edge_weights,
            edge_weights,
        ),
        in_specs=[smem] + [hbm] * 5,
        out_specs=(vmem, vmem, vmem, hbm, hbm),
        scratch_shapes=[
            pltpu.VMEM((tracers, levels, 8, lanes), f32),
            pltpu.VMEM((tracers, levels, 8, lanes), f32),
            pltpu.VMEM((tracers, columns, lanes), f32),
            pltpu.VMEM(bathymetry.shape, i32),
            pltpu.VMEM(fields.shape, bf16),
            pltpu.VMEM(blocks.shape, i32),
            pltpu.VMEM((EXTRA, lanes), f32),
            pltpu.SemaphoreType.DMA((8,)),
        ],
        compiler_params=pltpu.CompilerParams(vmem_limit_bytes=8 * MIB),
        cost_estimate=pl.CostEstimate(
            flops=10**6, bytes_accessed=4 * 10**6, transcendentals=0
        ),
    )(
        section,
        in_hbm(ocean_state),
        in_hbm(bathymetry),
        in_hbm(fields),
        in_hbm(blocks),
        in_hbm(weights),
    )
    from_left = shift(to_right, "blk", 1)
    from_right = shift(to_left, "blk", -1)
    left_weights = shift_first_section(to_right_weights, 1)
    right_weights = shift_first_section(to_left_weights, -1)
    partner_fields = lax.ppermute(fields, "sec", [(0, 1), (1, 0)])

    served = pl.pallas_call(
        serve_kernel,
        out_shape=shaped((count * SLOTS, 3 * lanes), bf16),
        in_specs=[vmem] * 4,
        out_specs=vmem,
        compiler_params=pltpu.CompilerParams(vmem_limit_bytes=8 * MIB),
        cost_estimate=pl.CostEstimate(
            flops=10**7, bytes_accessed=10**6, transcendentals=0
        ),
    )(asked, table, from_left, from_right)
    columns_in = lax.all_to_all(served, "blk", split_axis=0, concat_axis=0, tiled=True)

    q, rho, side, bath, place = pl.pallas_call(
        functools.partial(start_kernel, count=count),
        out_shape=(
            pltpu.HBM((tracers, levels, rows, lanes), f32),
            pltpu.HBM((levels, rows, lanes), f32),
            pltpu.HBM((levels, columns, lanes), f32),
            pltpu.HBM((rows, lanes), i32),
            pltpu.HBM((slots * columns, 128), i32),
        ),
        in_specs=[hbm, vmem, vmem, hbm, hbm, vmem],
        out_specs=(hbm,) * 5,
        scratch_shapes=[
            pltpu.VMEM((tracers, levels, rows, lanes), f32),
            pltpu.VMEM((levels, rows, lanes), f32),
            pltpu.VMEM((levels, columns, lanes), f32),
            pltpu.VMEM(ocean_state.shape, f32),
            pltpu.VMEM((rows, lanes), i32),
            pltpu.VMEM((many * 8, lanes), f32),
            pltpu.VMEM((4, rows, lanes), i32),
            pltpu.VMEM(bathymetry.shape, i32),
            pltpu.VMEM(blocks.shape, i32),
            pltpu.VMEM((slots * columns, 128), i32),
            pltpu.SemaphoreType.DMA((pieces + 2,)),
            pltpu.SemaphoreType.DMA((3 * pieces + 2,)),
        ],
        compiler_params=pltpu.CompilerParams(vmem_limit_bytes=28 * MIB),
        cost_estimate=pl.CostEstimate(
            flops=60 * levels * cells, bytes_accessed=200 * levels * cells, transcendentals=0
        ),
    )(
        in_hbm(ocean_state),
        from_left,
        from_right,
        in_hbm(bathymetry),
        in_hbm(blocks),
        ratios_by_height(levels, lanes),
    )

    mine = pl.pallas_call(
        remap_kernel,
        out_shape=shaped((3, rows, lanes), f32),
        in_specs=[smem, vmem, hbm, vmem, vmem, anywhere, anywhere, hbm],
        out_specs=vmem,
        scratch_shapes=[
            pltpu.VMEM((slots, rows * 8, lanes), f32),
            pltpu.VMEM((rows * 8, lanes), f32),
            pltpu.VMEM(weights.shape, bf16),
            pltpu.VMEM((tall, lanes), bf16),
            pltpu.VMEM((tall, lanes), bf16),
            pltpu.VMEM((slots * columns, 128), i32),
            pltpu.SemaphoreType.DMA((3 + columns // 8,)),
        ],
        compiler_params=pltpu.CompilerParams(vmem_limit_bytes=20 * MIB),
        cost_estimate=pl.CostEstimate(
            flops=16 * weights.size, bytes_accessed=2 * weights.size, transcendentals=0
        ),
    )(
        section,
        columns_in,
        in_hbm(place),
        from_left,
        from_right,
        left_weights,
        right_weights,
        in_hbm(weights),
    )
    other = lax.ppermute(mine, "sec", [(0, 1), (1, 0)])

    surface, result = pl.pallas_call(
        finish_kernel,
        out_shape=(shaped((3, columns, lanes), f32), shaped(ocean_state.shape, f32)),
        in_specs=[smem] + [vmem] * 4 + [hbm] * 5,
        out_specs=(vmem, hbm),
        scratch_shapes=[
            pltpu.VMEM((tracers, levels, rows, lanes), f32),
            pltpu.VMEM((levels, rows, lanes), f32),
            pltpu.VMEM((levels, columns, lanes), f32),
            pltpu.VMEM(ocean_state.shape, f32),
            pltpu.VMEM((rows, lanes), i32),
            pltpu.SemaphoreType.DMA((pieces + 1, 4)),
            pltpu.SemaphoreType.DMA((pieces,)),
        ],
        compiler_params=pltpu.CompilerParams(vmem_limit_bytes=28 * MIB),
        cost_estimate=pl.CostEstimate(
            flops=60 * levels * cells, bytes_accessed=32 * levels * cells, transcendentals=0
        ),
    )(
        section,
        mine,
        other,
        fields,
        partner_fields,
        in_hbm(bath),
        in_hbm(q),
        in_hbm(rho),
        in_hbm(side),
        in_hbm(ocean_state),
    )
    return (surface[None], result)


def solution(mesh):
    return jax.shard_map(
        per_device,
        mesh=mesh,
        in_specs=(
            P("sec", None, "blk", None),
            P("sec", "blk", None),
            P("sec", "blk", None),
            P("sec", "blk", None, None, None),
            P(None, None, "blk", None),
            P("blk", None),
        ),
        out_specs=(P("sec", None, "blk", None), P(None, None, "blk", None)),
        check_vma=False,
    )
```

```python
import functools

import jax
import jax.numpy as jnp
import numpy as np
from jax import lax
from jax.experimental import pallas as pl
from jax.experimental.pallas import tpu as pltpu
from jax.sharding import PartitionSpec as P

FLUX_GAIN = 0.5
SIDE_MIX = 0.2
TOP_MIX = 1.0
DEEP_MIX = 2.0
SCALE = 1.0 / (0.5 * SIDE_MIX)

MOST = 16
SLOTS = 24
EDGE = 8
EXTRA = 16
UNROLL = 5
MIB = 2**20
bf16, f32, i32 = jnp.bfloat16, jnp.float32, jnp.int32


def iota(shape, axis):
    return lax.broadcasted_iota(i32, shape, axis)


def band_matrix(lanes):
    shape = (2 * lanes, lanes)
    apart = lax.rem(iota(shape, 0), lanes) - iota(shape, 1)
    return jnp.where(jnp.abs(apart) == 1, 1.0, 0.0).astype(bf16)


def sums_along_lanes(arrays, band):
    rows = arrays[0].shape[0]
    stacked = jnp.concatenate(arrays, axis=0)
    head = stacked.astype(bf16)
    tail = (stacked - head.astype(f32)).astype(bf16)
    sums = jnp.dot(
        jnp.concatenate([head, tail], axis=1), band[...], preferred_element_type=f32
    )
    return [sums[n * rows : (n + 1) * rows] for n in range(len(arrays))]


def sum_along_rows(h, columns, ring, with_edge):
    edge = h[columns:]
    ring[pl.ds(0, EDGE), :] = edge
    ring[pl.ds(EDGE, columns), :] = h[:columns]
    ring[pl.ds(EDGE + columns, EDGE), :] = edge
    rows = columns
    if with_edge:
        ring[pl.ds(2 * EDGE + columns, EDGE), :] = h[:EDGE]
        rows = columns + EDGE
    return ring[pl.ds(EDGE - 1, rows), :] + ring[pl.ds(EDGE + 1, rows), :]


def edge_tile(right, left):
    row = iota((EDGE, right.shape[1]), 0)
    return jnp.where(row == 0, right, jnp.where(row == EDGE - 1, left, 0.0))


def chunks_of(levels):
    size = 10 if levels % 10 == 0 else levels
    return [(start, size) for start in range(0, levels, size)]


def sweep(count, body, carry, unroll):
    rounds = count // unroll

    def several(number, carry):
        for n in range(unroll):
            carry = body(number * unroll + n, n, carry)
        return carry

    carry = lax.fori_loop(0, rounds, several, carry)
    for step in range(rounds * unroll, count):
        carry = body(step, step - rounds * unroll, carry)
    return carry


def ranks(blocks, count):
    slots, columns = blocks.shape
    before = jnp.where(iota((columns, columns), 0) < iota((columns, columns), 1), 1.0, 0.0)
    before = before.astype(bf16)
    used = jnp.zeros((count, 1), f32)
    result = []
    for k in range(slots):
        owner = iota((count, columns), 0) == blocks[k : k + 1, :]
        one_hot = jnp.where(owner, 1.0, 0.0)
        earlier = used + jnp.dot(one_hot.astype(bf16), before, preferred_element_type=f32)
        rank = jnp.sum(one_hot * earlier, axis=0, keepdims=True)
        used = used + jnp.sum(one_hot, axis=1, keepdims=True)
        result.append((owner, rank))
    return result


def ask_kernel(blocks, spots, request, blocks_in, spots_in, sems):
    copies = [
        pltpu.make_async_copy(blocks, blocks_in, sems.at[0]),
        pltpu.make_async_copy(spots, spots_in, sems.at[1]),
    ]
    for copy in copies:
        copy.start()
    for copy in copies:
        copy.wait()
    count, columns = request.shape[0], blocks.shape[1]
    slot = iota((128, columns), 0)
    here = iota((128, columns), 1)
    marks = ((slot == MOST) & (here == 0)) | ((slot == MOST + 1) & (here == columns - 1))
    asked = jnp.zeros(request.shape, f32)
    for k, (owner, rank) in enumerate(ranks(blocks_in, count)):
        filled = jnp.where((slot == rank.astype(i32)) | marks, 1.0, 0.0).astype(bf16)
        named = jnp.where(owner, spots_in[k : k + 1, :].astype(f32), 0.0).astype(bf16)
        asked = asked + lax.dot_general(
            named, filled, (((1,), (1,)), ((), ())), preferred_element_type=f32
        )
    request[...] = asked.astype(i32)


def pack_kernel(
    section, state, bath, fields, blocks, weights,
    to_left, to_right, table,
    low, high, surface, bath_in, fields_in, blocks_in, extra, sems,
):
    tracers, levels, columns, lanes = state.shape
    slots = blocks.shape[0]
    many = tracers * levels
    wide = to_left.shape[0] - 2 * many - EXTRA
    below = pl.ds(2 * many + EXTRA, wide)
    pairs = [
        (state.at[:, :, pl.ds(0, 8)], low),
        (state.at[:, :, pl.ds(columns - 8, 8)], high),
        (blocks, blocks_in),
        (bath, bath_in),
        (fields, fields_in),
        (state.at[:, 0], surface),
        (weights.at[pl.ds(0, wide)], to_left.at[below]),
        (weights.at[pl.ds((columns - 1) * wide, wide)], to_right.at[below]),
    ]
    copies = [pltpu.make_async_copy(src, dst, sems.at[n]) for n, (src, dst) in enumerate(pairs)]
    for copy in copies:
        copy.start()
    for copy in copies[2:6]:
        copy.wait()
    for out, first, at in ((to_left, 0, 0), (to_right, columns - 2, columns - 1)):
        extra[...] = jnp.zeros_like(extra)
        extra[0:2] = bath_in[first : first + 2].astype(f32)
        for f in range(3):
            extra[2 + f : 3 + f] = fields_in[f].astype(f32)[at : at + 1]
        extra[8 : 8 + slots] = jnp.broadcast_to(
            blocks_in[:, at : at + 1].astype(f32), (slots, lanes)
        )
        out[pl.ds(2 * many, EXTRA)] = extra[...].astype(bf16)
    on_ocean = section[0] == 1
    for f in range(3):
        own = fields_in[f]
        if f < 2:
            own = jnp.where(on_ocean, surface[f], own.astype(f32)).astype(bf16)
        table[:, f * lanes : (f + 1) * lanes] = own
    copies[0].wait()
    copies[1].wait()
    for c in range(2):
        for n in range(tracers):
            part = pl.ds(c * many + n * levels, levels)
            tiles = low.at[n].reshape(levels * 8, lanes)
            to_left[part] = tiles[pl.ds(c, levels, stride=8), :].astype(bf16)
            tiles = high.at[n].reshape(levels * 8, lanes)
            to_right[part] = tiles[pl.ds(6 + c, levels, stride=8), :].astype(bf16)
    copies[6].wait()
    copies[7].wait()


def serve_kernel(asked, table, from_left, from_right, out):
    count = asked.shape[0]
    wanted = jnp.transpose(asked[...].astype(f32))[:SLOTS]
    columns = table.shape[0]
    slot = iota((SLOTS, 1), 0)
    parts = []
    for e in range(count):
        after, before = (e + 1) % count, (e - 1) % count
        spot = jnp.where(
            slot == MOST,
            wanted[:, after : after + 1],
            jnp.where(slot == MOST + 1, wanted[:, before : before + 1], wanted[:, e : e + 1]),
        )
        parts.append(jnp.where(iota((SLOTS, columns), 1) == spot.astype(i32), 1.0, 0.0))
    chosen = jnp.concatenate(parts, axis=0).astype(bf16)
    out[...] = jnp.dot(chosen, table[...], preferred_element_type=f32).astype(bf16)


def start_kernel(
    state, from_left, from_right, bath, blocks, ratios,
    q_result, rho_result, side_result, bath_result, place_result,
    q_out, rho_out, side_out, held, bath_out, halo, near, bath_in, blocks_in, place, ring, band,
    sems, sems_out, *, count,
):
    tracers, levels, columns, lanes = state.shape
    rows = columns + EDGE
    many = tracers * levels
    chunks = chunks_of(levels)
    copies = []
    for n, (low, size) in enumerate(chunks):
        copies.append(
            pltpu.make_async_copy(
                state.at[:, pl.ds(low, size)], held.at[:, pl.ds(low, size)], sems.at[n]
            )
        )
    bath_copy = pltpu.make_async_copy(bath, bath_in, sems.at[len(chunks)])
    blocks_copy = pltpu.make_async_copy(blocks, blocks_in, sems.at[len(chunks) + 1])
    blocks_copy.start()
    bath_copy.start()
    for copy in reversed(copies):
        copy.start()
    leaving = []

    def send(source, target, number):
        copy = pltpu.make_async_copy(source, target, sems_out.at[number])
        copy.start()
        leaving.append(copy)

    for c in range(2):
        part = pl.ds(c * many, many)
        halo[pl.ds(c, many, stride=8), :] = from_right[part].astype(f32)
        halo[pl.ds(EDGE - 2 + c, many, stride=8), :] = from_left[part].astype(f32)
    right = from_right[pl.ds(2 * many, EXTRA)].astype(f32)
    left = from_left[pl.ds(2 * many, EXTRA)].astype(f32)
    row = iota((EDGE, lanes), 0)
    edge = jnp.where(
        row == 0,
        right[0:1],
        jnp.where(
            row == 1,
            right[1:2],
            jnp.where(row == EDGE - 2, left[0:1], jnp.where(row == EDGE - 1, left[1:2], 0.0)),
        ),
    )
    bath_copy.wait()
    depth = jnp.concatenate([bath_in[...], edge.astype(i32)], axis=0)
    bath_out[...] = depth
    send(bath_out, bath_result, 3 * len(chunks))
    blocks_copy.wait()
    for k, (_, rank) in enumerate(ranks(blocks_in, count)):
        arrives = blocks_in[k : k + 1, :].astype(f32) * SLOTS + rank
        spread = jnp.transpose(jnp.broadcast_to(arrives, (128, columns)))
        place[k * columns : (k + 1) * columns, :] = spread.astype(i32)
    send(place, place_result, 3 * len(chunks) + 1)
    lane = iota((rows, lanes), 1)
    a = pltpu.roll(depth, 1, 0)
    b = pltpu.roll(depth, rows - 1, 0)
    c = jnp.where(lane == 0, 0, pltpu.roll(depth, 1, 1))
    d = jnp.where(lane == lanes - 1, 0, pltpu.roll(depth, lanes - 1, 1))
    a, b = jnp.maximum(a, b), jnp.minimum(a, b)
    c, d = jnp.maximum(c, d), jnp.minimum(c, d)
    a, c = jnp.maximum(a, c), jnp.minimum(a, c)
    b, d = jnp.maximum(b, d), jnp.minimum(b, d)
    near[0], near[1], near[2], near[3] = a, jnp.maximum(b, c), jnp.minimum(b, c), d

    lookup = jnp.broadcast_to(ratios[0:1], (rows, lanes))

    band[...] = band_matrix(lanes)

    def side(level, slot):
        wet = level < bath_out[...]
        own = 0.5 * SCALE
        for n in range(4):
            own = jnp.where(level < near[n], 0.5 * SCALE - (n + 1), own)
        side_out[level] = own[:columns]
        masked = []
        for n in range(tracers):
            spot = (n * levels + level) * 8
            if not isinstance(level, int):
                spot = pl.multiple_of(spot, 8)
            full = jnp.concatenate([held[n, level], halo[pl.ds(spot, 8), :]], axis=0)
            masked.append(jnp.where(wet, full, 0.0))
        along = sums_along_lanes(masked, band)
        halves = []
        for n, h in enumerate(masked):
            across = sum_along_rows(h, columns, ring.at[slot, n], True)
            halves.append(own * h + (across + along[n]))
        return halves

    def deep(step, slot, below, top):
        level = top - step
        halves = side(level, slot)
        above_floor = jnp.maximum(bath_out[...] - level, 0)
        rho = jnp.take_along_axis(lookup, above_floor, axis=1, mode="promise_in_bounds")
        rho_out[level] = rho
        solved = []
        for n in range(tracers):
            q = rho * (halves[n] + below[n])
            q_out[n, level] = q
            solved.append(q)
        return tuple(solved)

    carry = tuple(jnp.zeros((rows, lanes), f32) for _ in range(tracers))
    for n in reversed(range(len(chunks))):
        low, size = chunks[n]
        copies[n].wait()
        first = max(low, 2)
        top = low + size - 1
        carry = sweep(top - first + 1, functools.partial(deep, top=top), carry, UNROLL)
        if n == 0:
            for level in (1, 0):
                halves = side(level, level)
                rho_out[level] = jnp.zeros((rows, lanes), f32)
                for m in range(tracers):
                    q_out[m, level] = halves[m]
        part = pl.ds(low, size)
        send(q_out.at[:, part], q_result.at[:, part], 3 * n)
        send(rho_out.at[part], rho_result.at[part], 3 * n + 1)
        send(side_out.at[part], side_result.at[part], 3 * n + 2)
    for copy in leaving:
        copy.wait()


def ratios_by_height(levels, lanes):
    values = [0.0]
    ratio = DEEP_MIX / (1.0 + DEEP_MIX)
    for _ in range(levels):
        values.append(ratio)
        ratio = DEEP_MIX / (1.0 + DEEP_MIX + DEEP_MIX - DEEP_MIX * ratio)
    values += [0.0] * (lanes - len(values))
    return jnp.broadcast_to(jnp.asarray(np.array(values, np.float32)), (8, lanes))


def remap_kernel(
    columns_in, place_from, from_left, from_right, weights, own_fields,
    out, picked, solved, held, fields_in, place, sems,
):
    fields, rows, width = out.shape[0] // 2, out.shape[1], out.shape[2]
    columns = rows - EDGE
    slots = weights.shape[0] // (columns * width)
    tall = slots * width
    many = from_left.shape[0] - tall - EXTRA
    group = 8
    place_copy = pltpu.make_async_copy(place_from, place, sems.at[0])
    fields_copy = pltpu.make_async_copy(own_fields, fields_in, sems.at[1])
    copies = []
    for n in range(columns // group):
        part = pl.ds(n * group * tall, group * tall)
        copies.append(pltpu.make_async_copy(weights.at[part], held.at[part], sems.at[2 + n]))
    for copy in [place_copy] + copies + [fields_copy]:
        copy.start()
    right = from_right[pl.ds(many, EXTRA)].astype(f32)
    left = from_left[pl.ds(many, EXTRA)].astype(f32)
    spots = iota((rows, columns_in.shape[0]), 1)
    row = iota((EDGE, 1), 0)
    picked[...] = jnp.zeros_like(picked)
    place_copy.wait()
    for k in range(slots):
        edge = jnp.where(
            row == 0,
            right[8 + k : 9 + k, 0:1] * SLOTS + MOST,
            jnp.where(row == EDGE - 1, left[8 + k : 9 + k, 0:1] * SLOTS + MOST + 1, -1.0),
        ).astype(i32)
        wanted = jnp.concatenate([place[k * columns : (k + 1) * columns, 0:1], edge], axis=0)
        chosen = jnp.where(spots == wanted, 1.0, 0.0).astype(bf16)
        found = jnp.dot(chosen, columns_in[...], preferred_element_type=f32)
        for f in range(fields):
            picked[k, pl.ds(f, rows, stride=8), :] = found[:, f * width : (f + 1) * width]

    def one(row, table_of):
        spot = pl.ds(row * 8, 8)
        vector = jnp.concatenate([picked[k, spot, :] for k in range(slots)], axis=1)
        matrix = jnp.concatenate([table_of(k) for k in range(slots)], axis=1)
        solved[spot, :] = lax.dot_general(
            vector.astype(bf16), matrix, (((1,), (1,)), ((), ())), preferred_element_type=f32
        )

    solved[...] = jnp.zeros_like(solved)
    below = many + EXTRA
    one(columns, lambda k: from_right[pl.ds(below + k * width, width)])
    one(rows - 1, lambda k: from_left[pl.ds(below + k * width, width)])
    for n in range(columns // group):
        copies[n].wait()
        for m in range(group):
            spot = n * group + m
            one(spot, lambda k: held[pl.ds((spot * slots + k) * width, width)])
    fields_copy.wait()
    for f in range(fields):
        out[f, pl.ds(0, columns)] = solved[pl.ds(f, columns, stride=8), :]
        out[f, pl.ds(columns, EDGE)] = solved[pl.ds(columns * 8 + f, EDGE, stride=8), :]
        out[fields + f, pl.ds(0, columns)] = fields_in[f].astype(f32)
        out[fields + f, pl.ds(columns, EDGE)] = edge_tile(
            right[2 + f : 3 + f], left[2 + f : 3 + f]
        )


def finish_kernel(
    section, mine, other, bath_from, q_from, rho_from, side_from, state,
    surface, result,
    q, rho, side, held, bath, ring, band, sems, sems_out,
):
    tracers, levels, columns, lanes = state.shape
    rows = columns + EDGE
    chunks = chunks_of(levels)
    bath_copy = pltpu.make_async_copy(bath_from, bath, sems.at[len(chunks), 0])
    bath_copy.start()
    arrivals, starts = [], []
    for n, (low, size) in enumerate(chunks):
        part = pl.ds(low, size)
        arrivals.append(
            (
                pltpu.make_async_copy(q_from.at[:, part], q.at[:, part], sems.at[n, 0]),
                pltpu.make_async_copy(rho_from.at[part], rho.at[part], sems.at[n, 1]),
                pltpu.make_async_copy(side_from.at[part], side.at[part], sems.at[n, 2]),
            )
        )
        starts.append(pltpu.make_async_copy(state.at[:, part], held.at[:, part], sems.at[n, 3]))
    for group in arrivals:
        for copy in group:
            copy.start()
    for copy in starts:
        copy.start()
    bath_copy.wait()
    for copy in arrivals[0]:
        copy.wait()
    on_ocean = section[0] == 1
    band[...] = band_matrix(lanes)
    flux = [jnp.where(on_ocean, other[f], mine[f]) for f in range(3)]
    own = [jnp.where(on_ocean, mine[3 + f], other[3 + f]) for f in range(3)]
    forcing = [flux[0] + own[0], flux[1] + own[1]]
    top_mix = TOP_MIX * (1.0 + flux[2] * flux[2] + own[2] * own[2])
    depth = bath[...]

    def top_levels(count, halves, below, rho_below, scale):
        wet = 1 < depth[:count]
        link = jnp.where(wet, top_mix[:count], 0.0)
        deeper = jnp.where(2 < depth[:count], DEEP_MIX - DEEP_MIX * rho_below, 0.0)
        second = 1.0 / (1.0 + link + deeper)
        rho_second = link * second
        first = 1.0 / (1.0 + link - link * rho_second)
        values = []
        for n in range(tracers):
            partial = 2.0 * (halves[n][1] + below[n]) * second
            source = 2.0 * halves[n][0] + scale * FLUX_GAIN * forcing[n][:count]
            surface_value = (source + link * partial) * first
            next_value = jnp.where(wet, partial, 0.0) + rho_second * surface_value
            values.append((surface_value, next_value))
        return values

    values = top_levels(
        rows,
        [(q[n, 0], q[n, 1]) for n in range(tracers)],
        [q[n, 2] for n in range(tracers)],
        rho[2],
        SCALE,
    )

    def store_halves(level, slot, values):
        inner = [h[:columns] for h in values]
        along = sums_along_lanes(inner, band)
        for n, h in enumerate(values):
            across = sum_along_rows(h, columns, ring.at[slot, n], False)
            q[n, level, pl.ds(0, columns)] = side[level] * inner[n] + (across + along[n])

    for level in (0, 1):
        store_halves(level, level, [values[n][level] for n in range(tracers)])

    def down(step, slot, carry, low):
        level = low + step
        ratio = rho[level]
        out = [q[n, level] + ratio * carry[n] for n in range(tracers)]
        store_halves(level, slot, out)
        return tuple(out)

    carry = tuple(values[n][1] for n in range(tracers))
    for n, (low, size) in enumerate(chunks):
        if n > 0:
            for copy in arrivals[n]:
                copy.wait()
        first = max(low, 2)
        carry = sweep(low + size - first, functools.partial(down, low=first), carry, UNROLL)

    def up(step, slot, carry):
        level = levels - 1 - step
        ratio = rho[level, pl.ds(0, columns)]
        out = []
        for n in range(tracers):
            value = ratio * (q[n, level, pl.ds(0, columns)] + carry[n])
            q[n, level, pl.ds(0, columns)] = value
            out.append(value)
        return tuple(out)

    zero = jnp.zeros((columns, lanes), f32)
    carry = sweep(levels - 2, up, (zero,) * tracers, 13)
    values = top_levels(
        columns,
        [(q[n, 0, pl.ds(0, columns)], q[n, 1, pl.ds(0, columns)]) for n in range(tracers)],
        carry,
        rho[2, pl.ds(0, columns)],
        SCALE * SCALE,
    )
    unscale = 1.0 / (SCALE * SCALE)
    for n in range(tracers):
        surface[n] = jnp.where(on_ocean, values[n][0] * unscale, other[n, pl.ds(0, columns)])
    surface[2] = jnp.where(on_ocean, top_mix[:columns], other[2, pl.ds(0, columns)])

    def last(step, slot, carry, low):
        level = low + step
        ratio = rho[level, pl.ds(0, columns)]
        wet = level < bath[pl.ds(0, columns)]
        out = []
        for n in range(tracers):
            h = q[n, level, pl.ds(0, columns)] + ratio * carry[n]
            held[n, level] = jnp.where(wet, h * unscale, held[n, level])
            out.append(h)
        return tuple(out)

    carry = tuple(values[n][1] for n in range(tracers))
    leaving = []
    for n, (low, size) in enumerate(chunks):
        starts[n].wait()
        if n == 0:
            for m in range(tracers):
                held[m, 0] = values[m][0] * unscale
                held[m, 1] = jnp.where(
                    1 < depth[:columns], values[m][1] * unscale, held[m, 1]
                )
        first = max(low, 2)
        carry = sweep(low + size - first, functools.partial(last, low=first), carry, 10)
        part = pl.ds(low, size)
        leaving.append(
            pltpu.make_async_copy(held.at[:, part], result.at[:, part], sems_out.at[n])
        )
        leaving[-1].start()
    for copy in leaving:
        copy.wait()


def shift(value, axis, by):
    count = lax.axis_size(axis)
    return lax.ppermute(value, axis, [(i, (i + by) % count) for i in range(count)])


def in_hbm(value):
    return pltpu.with_memory_space_constraint(value, pltpu.HBM)


def per_device(
    surface_fields, source_blocks, source_columns, remap_weights, ocean_state, bathymetry
):
    tracers, levels, columns, lanes = ocean_state.shape
    slots = source_blocks.shape[2]
    count = lax.axis_size("blk")
    rows = columns + EDGE
    section = lax.axis_index("sec").astype(i32).reshape(1)
    fields = surface_fields[0]
    blocks = jnp.transpose(source_blocks[0])
    spots = jnp.transpose(source_columns[0])
    weights = remap_weights[0].reshape(columns * slots * lanes, lanes)
    tall = slots * lanes
    many = tracers * levels

    hbm = pl.BlockSpec(memory_space=pltpu.HBM)
    vmem = pl.BlockSpec(memory_space=pltpu.VMEM)
    smem = pl.BlockSpec(memory_space=pltpu.SMEM)
    shaped = jax.ShapeDtypeStruct
    pieces = len(chunks_of(levels))
    cells = rows * lanes

    request = pl.pallas_call(
        ask_kernel,
        out_shape=shaped((count, 128), i32),
        in_specs=[hbm, hbm],
        out_specs=vmem,
        scratch_shapes=[
            pltpu.VMEM(blocks.shape, i32),
            pltpu.VMEM(spots.shape, i32),
            pltpu.SemaphoreType.DMA((2,)),
        ],
        compiler_params=pltpu.CompilerParams(vmem_limit_bytes=4 * MIB),
        cost_estimate=pl.CostEstimate(flops=10**6, bytes_accessed=10**5, transcendentals=0),
    )(in_hbm(blocks), in_hbm(spots))
    asked = lax.all_to_all(request, "blk", split_axis=0, concat_axis=0, tiled=True)

    payload = shaped((2 * many + EXTRA + tall, lanes), bf16)
    to_left, to_right, table = pl.pallas_call(
        pack_kernel,
        out_shape=(
            payload,
            payload,
            shaped((columns, 3 * lanes), bf16),
        ),
        in_specs=[smem] + [hbm] * 5,
        out_specs=(vmem, vmem, vmem),
        scratch_shapes=[
            pltpu.VMEM((tracers, levels, 8, lanes), f32),
            pltpu.VMEM((tracers, levels, 8, lanes), f32),
            pltpu.VMEM((tracers, columns, lanes), f32),
            pltpu.VMEM(bathymetry.shape, i32),
            pltpu.VMEM(fields.shape, bf16),
            pltpu.VMEM(blocks.shape, i32),
            pltpu.VMEM((EXTRA, lanes), f32),
            pltpu.SemaphoreType.DMA((8,)),
        ],
        compiler_params=pltpu.CompilerParams(vmem_limit_bytes=8 * MIB),
        cost_estimate=pl.CostEstimate(
            flops=10**6, bytes_accessed=4 * 10**6, transcendentals=0
        ),
    )(
        section,
        in_hbm(ocean_state),
        in_hbm(bathymetry),
        in_hbm(fields),
        in_hbm(blocks),
        in_hbm(weights),
    )
    from_left = shift(to_right, "blk", 1)
    from_right = shift(to_left, "blk", -1)

    served = pl.pallas_call(
        serve_kernel,
        out_shape=shaped((count * SLOTS, 3 * lanes), bf16),
        in_specs=[vmem] * 4,
        out_specs=vmem,
        compiler_params=pltpu.CompilerParams(vmem_limit_bytes=8 * MIB),
        cost_estimate=pl.CostEstimate(
            flops=10**7, bytes_accessed=10**6, transcendentals=0
        ),
    )(asked, table, from_left, from_right)
    columns_in = lax.all_to_all(served, "blk", split_axis=0, concat_axis=0, tiled=True)

    q, rho, side, bath, place = pl.pallas_call(
        functools.partial(start_kernel, count=count),
        out_shape=(
            pltpu.HBM((tracers, levels, rows, lanes), f32),
            pltpu.HBM((levels, rows, lanes), f32),
            pltpu.HBM((levels, columns, lanes), f32),
            pltpu.HBM((rows, lanes), i32),
            pltpu.HBM((slots * columns, 128), i32),
        ),
        in_specs=[hbm, vmem, vmem, hbm, hbm, vmem],
        out_specs=(hbm,) * 5,
        scratch_shapes=[
            pltpu.VMEM((tracers, levels, rows, lanes), f32),
            pltpu.VMEM((levels, rows, lanes), f32),
            pltpu.VMEM((levels, columns, lanes), f32),
            pltpu.VMEM(ocean_state.shape, f32),
            pltpu.VMEM((rows, lanes), i32),
            pltpu.VMEM((many * 8, lanes), f32),
            pltpu.VMEM((4, rows, lanes), i32),
            pltpu.VMEM(bathymetry.shape, i32),
            pltpu.VMEM(blocks.shape, i32),
            pltpu.VMEM((slots * columns, 128), i32),
            pltpu.VMEM((UNROLL, tracers, columns + 3 * EDGE, lanes), f32),
            pltpu.VMEM((2 * lanes, lanes), bf16),
            pltpu.SemaphoreType.DMA((pieces + 2,)),
            pltpu.SemaphoreType.DMA((3 * pieces + 2,)),
        ],
        compiler_params=pltpu.CompilerParams(vmem_limit_bytes=28 * MIB),
        cost_estimate=pl.CostEstimate(
            flops=60 * levels * cells, bytes_accessed=200 * levels * cells, transcendentals=0
        ),
    )(
        in_hbm(ocean_state),
        from_left,
        from_right,
        in_hbm(bathymetry),
        in_hbm(blocks),
        ratios_by_height(levels, lanes),
    )

    mine = pl.pallas_call(
        remap_kernel,
        out_shape=shaped((6, rows, lanes), f32),
        in_specs=[vmem, hbm, vmem, vmem, hbm, hbm],
        out_specs=vmem,
        scratch_shapes=[
            pltpu.VMEM((slots, rows * 8, lanes), f32),
            pltpu.VMEM((rows * 8, lanes), f32),
            pltpu.VMEM(weights.shape, bf16),
            pltpu.VMEM(fields.shape, bf16),
            pltpu.VMEM((slots * columns, 128), i32),
            pltpu.SemaphoreType.DMA((2 + columns // 8,)),
        ],
        compiler_params=pltpu.CompilerParams(vmem_limit_bytes=20 * MIB),
        cost_estimate=pl.CostEstimate(
            flops=16 * weights.size, bytes_accessed=2 * weights.size, transcendentals=0
        ),
    )(
        columns_in,
        in_hbm(place),
        from_left,
        from_right,
        in_hbm(weights),
        in_hbm(fields),
    )
    other = lax.ppermute(mine, "sec", [(0, 1), (1, 0)])

    surface, result = pl.pallas_call(
        finish_kernel,
        out_shape=(shaped((3, columns, lanes), f32), shaped(ocean_state.shape, f32)),
        in_specs=[smem] + [vmem] * 2 + [hbm] * 5,
        out_specs=(vmem, hbm),
        scratch_shapes=[
            pltpu.VMEM((tracers, levels, rows, lanes), f32),
            pltpu.VMEM((levels, rows, lanes), f32),
            pltpu.VMEM((levels, columns, lanes), f32),
            pltpu.VMEM(ocean_state.shape, f32),
            pltpu.VMEM((rows, lanes), i32),
            pltpu.VMEM((UNROLL, tracers, columns + 2 * EDGE, lanes), f32),
            pltpu.VMEM((2 * lanes, lanes), bf16),
            pltpu.SemaphoreType.DMA((pieces + 1, 4)),
            pltpu.SemaphoreType.DMA((pieces,)),
        ],
        compiler_params=pltpu.CompilerParams(vmem_limit_bytes=28 * MIB),
        cost_estimate=pl.CostEstimate(
            flops=60 * levels * cells, bytes_accessed=32 * levels * cells, transcendentals=0
        ),
    )(
        section,
        mine,
        other,
        in_hbm(bath),
        in_hbm(q),
        in_hbm(rho),
        in_hbm(side),
        in_hbm(ocean_state),
    )
    return (surface[None], result)


def solution(mesh):
    return jax.shard_map(
        per_device,
        mesh=mesh,
        in_specs=(
            P("sec", None, "blk", None),
            P("sec", "blk", None),
            P("sec", "blk", None),
            P("sec", "blk", None, None, None),
            P(None, None, "blk", None),
            P("blk", None),
        ),
        out_specs=(P("sec", None, "blk", None), P(None, None, "blk", None)),
        check_vma=False,
    )
```

```python
import functools

import jax
import jax.numpy as jnp
import numpy as np
from jax import lax
from jax.experimental import pallas as pl
from jax.experimental.pallas import tpu as pltpu
from jax.sharding import PartitionSpec as P

FLUX_GAIN = 0.5
SIDE_MIX = 0.2
TOP_MIX = 1.0
DEEP_MIX = 2.0
SCALE = 1.0 / (0.5 * SIDE_MIX)

MOST = 16
SLOTS = MOST + 2
FIELDS = 3
PIECE = 56
EDGE = 8
EXTRA = 16
UNROLL = 5
MIB = 2**20
bf16, f32, i32 = jnp.bfloat16, jnp.float32, jnp.int32


def iota(shape, axis):
    return lax.broadcasted_iota(i32, shape, axis)


def band_matrix(lanes):
    shape = (2 * lanes, lanes)
    apart = lax.rem(iota(shape, 0), lanes) - iota(shape, 1)
    return jnp.where(jnp.abs(apart) == 1, 1.0, 0.0).astype(bf16)


def sums_along_lanes(arrays, band):
    rows = arrays[0].shape[0]
    stacked = jnp.concatenate(arrays, axis=0)
    head = stacked.astype(bf16)
    tail = (stacked - head.astype(f32)).astype(bf16)
    sums = jnp.dot(
        jnp.concatenate([head, tail], axis=1), band[...], preferred_element_type=f32
    )
    return [sums[n * rows : (n + 1) * rows] for n in range(len(arrays))]


def sum_along_rows(h, columns, ring, with_edge):
    edge = h[columns:]
    ring[pl.ds(0, EDGE), :] = edge
    ring[pl.ds(EDGE, columns), :] = h[:columns]
    ring[pl.ds(EDGE + columns, EDGE), :] = edge
    rows = columns
    if with_edge:
        ring[pl.ds(2 * EDGE + columns, EDGE), :] = h[:EDGE]
        rows = columns + EDGE
    return ring[pl.ds(EDGE - 1, rows), :] + ring[pl.ds(EDGE + 1, rows), :]


def edge_tile(right, left):
    row = iota((EDGE, right.shape[1]), 0)
    return jnp.where(row == 0, right, jnp.where(row == EDGE - 1, left, 0.0))


def chunks_of(levels):
    size = 10 if levels % 10 == 0 else levels
    return [(start, size) for start in range(0, levels, size)]


def sweep(count, body, carry, unroll):
    rounds = count // unroll

    def several(number, carry):
        for n in range(unroll):
            carry = body(number * unroll + n, n, carry)
        return carry

    carry = lax.fori_loop(0, rounds, several, carry)
    for step in range(rounds * unroll, count):
        carry = body(step, step - rounds * unroll, carry)
    return carry


def ranks(blocks, count):
    slots, columns = blocks.shape
    before = jnp.where(iota((columns, columns), 0) < iota((columns, columns), 1), 1.0, 0.0)
    before = before.astype(bf16)
    used = jnp.zeros((count, 1), f32)
    result = []
    for k in range(slots):
        owner = iota((count, columns), 0) == blocks[k : k + 1, :]
        one_hot = jnp.where(owner, 1.0, 0.0)
        earlier = used + jnp.dot(one_hot.astype(bf16), before, preferred_element_type=f32)
        rank = jnp.sum(one_hot * earlier, axis=0, keepdims=True)
        used = used + jnp.sum(one_hot, axis=1, keepdims=True)
        result.append((owner, rank))
    return result


def ask_kernel(blocks, spots, request, blocks_in, spots_in, sems):
    copies = [
        pltpu.make_async_copy(blocks, blocks_in, sems.at[0]),
        pltpu.make_async_copy(spots, spots_in, sems.at[1]),
    ]
    for copy in copies:
        copy.start()
    for copy in copies:
        copy.wait()
    count, columns = request.shape[0], blocks.shape[1]
    place = iota((128, columns), 0)
    field = place // SLOTS
    slot = jnp.where(field < FIELDS, place - field * SLOTS, -1)
    here = iota((128, columns), 1)
    marks = ((slot == MOST) & (here == 0)) | ((slot == MOST + 1) & (here == columns - 1))
    asked = jnp.zeros(request.shape, f32)
    for k, (owner, rank) in enumerate(ranks(blocks_in, count)):
        filled = jnp.where((slot == rank.astype(i32)) | marks, 1.0, 0.0).astype(bf16)
        named = jnp.where(owner, spots_in[k : k + 1, :].astype(f32), 0.0).astype(bf16)
        asked = asked + lax.dot_general(
            named, filled, (((1,), (1,)), ((), ())), preferred_element_type=f32
        )
    request[...] = asked.astype(i32) + (iota(request.shape, 1) // SLOTS) * columns


def pack_kernel(
    section, state, bath, fields, blocks, weights,
    to_left, to_right, table,
    low, high, surface, bath_in, fields_in, blocks_in, extra, sems,
):
    tracers, levels, columns, lanes = state.shape
    slots = blocks.shape[0]
    many = tracers * levels
    wide = to_left.shape[0] - 2 * many - EXTRA
    below = pl.ds(2 * many + EXTRA, wide)
    pairs = [
        (state.at[:, :, pl.ds(0, 8)], low),
        (state.at[:, :, pl.ds(columns - 8, 8)], high),
        (blocks, blocks_in),
        (bath, bath_in),
        (fields, fields_in),
        (state.at[:, 0], surface),
        (weights.at[pl.ds(0, wide)], to_left.at[below]),
        (weights.at[pl.ds((columns - 1) * wide, wide)], to_right.at[below]),
    ]
    copies = [pltpu.make_async_copy(src, dst, sems.at[n]) for n, (src, dst) in enumerate(pairs)]
    for copy in copies:
        copy.start()
    for copy in copies[2:6]:
        copy.wait()
    for out, first, at in ((to_left, 0, 0), (to_right, columns - 2, columns - 1)):
        extra[...] = jnp.zeros_like(extra)
        extra[0:2] = bath_in[first : first + 2].astype(f32)
        for f in range(3):
            extra[2 + f : 3 + f] = fields_in[f].astype(f32)[at : at + 1]
        extra[8 : 8 + slots] = jnp.broadcast_to(
            blocks_in[:, at : at + 1].astype(f32), (slots, lanes)
        )
        out[pl.ds(2 * many, EXTRA)] = extra[...].astype(bf16)
    on_ocean = section[0] == 1
    for f in range(3):
        own = fields_in[f]
        if f < 2:
            own = jnp.where(on_ocean, surface[f], own.astype(f32)).astype(bf16)
        table[f * columns : (f + 1) * columns, :] = own
    copies[0].wait()
    copies[1].wait()
    for c in range(2):
        for n in range(tracers):
            part = pl.ds(c * many + n * levels, levels)
            tiles = low.at[n].reshape(levels * 8, lanes)
            to_left[part] = tiles[pl.ds(c, levels, stride=8), :].astype(bf16)
            tiles = high.at[n].reshape(levels * 8, lanes)
            to_right[part] = tiles[pl.ds(6 + c, levels, stride=8), :].astype(bf16)
    copies[6].wait()
    copies[7].wait()


def serve_kernel(asked, table, from_left, from_right, out):
    count = asked.shape[0]
    wanted = jnp.transpose(asked[...].astype(f32))[:PIECE]
    height = table.shape[0]
    slot = lax.rem(iota((PIECE, 1), 0), SLOTS)
    parts = []
    for e in range(count):
        after, before = (e + 1) % count, (e - 1) % count
        spot = jnp.where(
            slot == MOST,
            wanted[:, after : after + 1],
            jnp.where(slot == MOST + 1, wanted[:, before : before + 1], wanted[:, e : e + 1]),
        )
        parts.append(jnp.where(iota((PIECE, height), 1) == spot.astype(i32), 1.0, 0.0))
    chosen = jnp.concatenate(parts, axis=0).astype(bf16)
    out[...] = jnp.dot(chosen, table[...], preferred_element_type=f32).astype(bf16)


def start_kernel(
    state, from_left, from_right, bath, blocks, ratios,
    q_result, side_result, bath_result, place_result,
    q_out, side_out, held, bath_out, halo, near, bath_in, blocks_in, place, ring, band,
    sems, sems_out, *, count,
):
    tracers, levels, columns, lanes = state.shape
    rows = columns + EDGE
    many = tracers * levels
    chunks = chunks_of(levels)
    copies = []
    for n, (low, size) in enumerate(chunks):
        copies.append(
            pltpu.make_async_copy(
                state.at[:, pl.ds(low, size)], held.at[:, pl.ds(low, size)], sems.at[n]
            )
        )
    bath_copy = pltpu.make_async_copy(bath, bath_in, sems.at[len(chunks)])
    blocks_copy = pltpu.make_async_copy(blocks, blocks_in, sems.at[len(chunks) + 1])
    blocks_copy.start()
    bath_copy.start()
    for copy in reversed(copies):
        copy.start()
    leaving = []

    def send(source, target, number):
        copy = pltpu.make_async_copy(source, target, sems_out.at[number])
        copy.start()
        leaving.append(copy)

    for c in range(2):
        part = pl.ds(c * many, many)
        halo[pl.ds(c, many, stride=8), :] = from_right[part].astype(f32)
        halo[pl.ds(EDGE - 2 + c, many, stride=8), :] = from_left[part].astype(f32)
    right = from_right[pl.ds(2 * many, EXTRA)].astype(f32)
    left = from_left[pl.ds(2 * many, EXTRA)].astype(f32)
    row = iota((EDGE, lanes), 0)
    edge = jnp.where(
        row == 0,
        right[0:1],
        jnp.where(
            row == 1,
            right[1:2],
            jnp.where(row == EDGE - 2, left[0:1], jnp.where(row == EDGE - 1, left[1:2], 0.0)),
        ),
    )
    bath_copy.wait()
    depth = jnp.concatenate([bath_in[...], edge.astype(i32)], axis=0)
    bath_out[...] = depth
    send(bath_out, bath_result, 2 * len(chunks))
    blocks_copy.wait()
    for k, (_, rank) in enumerate(ranks(blocks_in, count)):
        arrives = blocks_in[k : k + 1, :].astype(f32) * PIECE + rank
        spread = jnp.transpose(jnp.broadcast_to(arrives, (128, columns)))
        place[k * columns : (k + 1) * columns, :] = spread.astype(i32)
    send(place, place_result, 2 * len(chunks) + 1)
    lane = iota((rows, lanes), 1)
    a = pltpu.roll(depth, 1, 0)
    b = pltpu.roll(depth, rows - 1, 0)
    c = jnp.where(lane == 0, 0, pltpu.roll(depth, 1, 1))
    d = jnp.where(lane == lanes - 1, 0, pltpu.roll(depth, lanes - 1, 1))
    a, b = jnp.maximum(a, b), jnp.minimum(a, b)
    c, d = jnp.maximum(c, d), jnp.minimum(c, d)
    a, c = jnp.maximum(a, c), jnp.minimum(a, c)
    b, d = jnp.maximum(b, d), jnp.minimum(b, d)
    near[0], near[1], near[2], near[3] = a, jnp.maximum(b, c), jnp.minimum(b, c), d


    band[...] = band_matrix(lanes)

    def side(level, slot):
        wet = level < bath_out[...]
        own = 0.5 * SCALE
        for n in range(4):
            own = jnp.where(level < near[n], 0.5 * SCALE - (n + 1), own)
        side_out[level] = own[:columns].astype(bf16)
        starts, masked = [], []
        for n in range(tracers):
            spot = (n * levels + level) * 8
            if not isinstance(level, int):
                spot = pl.multiple_of(spot, 8)
            full = jnp.concatenate([held[n, level], halo[pl.ds(spot, 8), :]], axis=0)
            starts.append(full)
            masked.append(jnp.where(wet, full, 0.0))
        along = sums_along_lanes(masked, band)
        halves = []
        for n, h in enumerate(masked):
            across = sum_along_rows(h, columns, ring.at[slot, n], True)
            halves.append(own * h + (across + along[n]))
        return wet, starts, halves

    def deep(step, slot, below, top):
        level = top - step
        wet, starts, halves = side(level, slot)
        rho = ratio_at(ratios, bath_out[...], level)
        solved = []
        for n in range(tracers):
            q = rho * (halves[n] + below[n])
            q_out[n, level] = jnp.where(wet, q, starts[n])
            solved.append(q)
        return tuple(solved)

    carry = tuple(jnp.zeros((rows, lanes), f32) for _ in range(tracers))
    for n in reversed(range(len(chunks))):
        low, size = chunks[n]
        copies[n].wait()
        first = max(low, 2)
        top = low + size - 1
        carry = sweep(top - first + 1, functools.partial(deep, top=top), carry, UNROLL)
        if n == 0:
            for level in (1, 0):
                wet, starts, halves = side(level, level)
                for m in range(tracers):
                    q_out[m, level] = jnp.where(wet, halves[m], starts[m])
        part = pl.ds(low, size)
        send(q_out.at[:, part], q_result.at[:, part], 2 * n)
        send(side_out.at[part], side_result.at[part], 2 * n + 1)
    for copy in leaving:
        copy.wait()


def ratio_at(ratios, depth, level):
    lookup = jnp.broadcast_to(ratios[0:1], depth.shape)
    height = jnp.maximum(depth - level, 0)
    return jnp.take_along_axis(lookup, height, axis=1, mode="promise_in_bounds")


def ratios_by_height(levels, lanes):
    values = [0.0]
    ratio = DEEP_MIX / (1.0 + DEEP_MIX)
    for _ in range(levels):
        values.append(ratio)
        ratio = DEEP_MIX / (1.0 + DEEP_MIX + DEEP_MIX - DEEP_MIX * ratio)
    values += [0.0] * (lanes - len(values))
    return jnp.broadcast_to(jnp.asarray(np.array(values, np.float32)), (8, lanes))


def remap_kernel(
    columns_in, place_from, from_left, from_right, weights, own_fields,
    out, picked, solved, held, fields_in, place, sems,
):
    fields, rows, width = out.shape[0] // 2, out.shape[1], out.shape[2]
    columns = rows - EDGE
    slots = weights.shape[0] // (columns * width)
    tall = slots * width
    many = from_left.shape[0] - tall - EXTRA
    group = 8
    place_copy = pltpu.make_async_copy(place_from, place, sems.at[0])
    fields_copy = pltpu.make_async_copy(own_fields, fields_in, sems.at[1])
    copies = []
    for n in range(columns // group):
        part = pl.ds(n * group * tall, group * tall)
        copies.append(pltpu.make_async_copy(weights.at[part], held.at[part], sems.at[2 + n]))
    for copy in [place_copy] + copies + [fields_copy]:
        copy.start()
    right = from_right[pl.ds(many, EXTRA)].astype(f32)
    left = from_left[pl.ds(many, EXTRA)].astype(f32)
    row = iota((EDGE, 1), 0)
    picked[...] = jnp.zeros_like(picked)
    place_copy.wait()
    wanted = []
    for k in range(slots):
        edge = jnp.where(
            row == 0,
            right[8 + k : 9 + k, 0:1] * PIECE + MOST,
            jnp.where(row == EDGE - 1, left[8 + k : 9 + k, 0:1] * PIECE + MOST + 1, -PIECE),
        ).astype(i32)
        wanted += [place[k * columns : (k + 1) * columns, 0:1], edge]
    wanted = jnp.concatenate(wanted, axis=0)
    spots = iota((slots * rows, columns_in.shape[0]), 1)
    for f in range(fields):
        chosen = jnp.where(spots == wanted + f * SLOTS, 1.0, 0.0).astype(bf16)
        found = jnp.dot(chosen, columns_in[...], preferred_element_type=f32)
        for k in range(slots):
            picked[k, pl.ds(f, rows, stride=8), :] = found[k * rows : (k + 1) * rows]

    def one(row, table_of):
        spot = pl.ds(row * 8, 8)
        vector = jnp.concatenate([picked[k, spot, :] for k in range(slots)], axis=1)
        matrix = jnp.concatenate([table_of(k) for k in range(slots)], axis=1)
        solved[spot, :] = lax.dot_general(
            vector.astype(bf16), matrix, (((1,), (1,)), ((), ())), preferred_element_type=f32
        )

    solved[...] = jnp.zeros_like(solved)
    below = many + EXTRA
    one(columns, lambda k: from_right[pl.ds(below + k * width, width)])
    one(rows - 1, lambda k: from_left[pl.ds(below + k * width, width)])
    for n in range(columns // group):
        copies[n].wait()
        for m in range(group):
            spot = n * group + m
            one(spot, lambda k: held[pl.ds((spot * slots + k) * width, width)])
    fields_copy.wait()
    for f in range(fields):
        out[f, pl.ds(0, columns)] = solved[pl.ds(f, columns, stride=8), :]
        out[f, pl.ds(columns, EDGE)] = solved[pl.ds(columns * 8 + f, EDGE, stride=8), :]
        out[fields + f, pl.ds(0, columns)] = fields_in[f].astype(f32)
        out[fields + f, pl.ds(columns, EDGE)] = edge_tile(
            right[2 + f : 3 + f], left[2 + f : 3 + f]
        )


def finish_kernel(
    section, mine, other, bath_from, q_from, side_from, ratios, surface, result,
    q, rho, side, bath, ring, band, sems, sems_out,
):
    tracers, levels, columns, lanes = result.shape
    rows = columns + EDGE
    chunks = chunks_of(levels)
    bath_copy = pltpu.make_async_copy(bath_from, bath, sems.at[len(chunks), 0])
    bath_copy.start()
    arrivals = []
    for n, (low, size) in enumerate(chunks):
        part = pl.ds(low, size)
        arrivals.append(
            (
                pltpu.make_async_copy(q_from.at[:, part], q.at[:, part], sems.at[n, 0]),
                pltpu.make_async_copy(side_from.at[part], side.at[part], sems.at[n, 1]),
            )
        )
    for group in arrivals:
        for copy in group:
            copy.start()
    bath_copy.wait()
    for copy in arrivals[0]:
        copy.wait()
    on_ocean = section[0] == 1
    band[...] = band_matrix(lanes)
    flux = [jnp.where(on_ocean, other[f], mine[f]) for f in range(3)]
    own = [jnp.where(on_ocean, mine[3 + f], other[3 + f]) for f in range(3)]
    forcing = [flux[0] + own[0], flux[1] + own[1]]
    top_mix = TOP_MIX * (1.0 + flux[2] * flux[2] + own[2] * own[2])
    depth = bath[...]

    def top_levels(count, halves, below, rho_below, scale):
        wet = 1 < depth[:count]
        link = jnp.where(wet, top_mix[:count], 0.0)
        deeper = jnp.where(2 < depth[:count], DEEP_MIX - DEEP_MIX * rho_below, 0.0)
        second = 1.0 / (1.0 + link + deeper)
        rho_second = link * second
        first = 1.0 / (1.0 + link - link * rho_second)
        values = []
        for n in range(tracers):
            partial = 2.0 * (halves[n][1] + below[n]) * second
            source = 2.0 * halves[n][0] + scale * FLUX_GAIN * forcing[n][:count]
            surface_value = (source + link * partial) * first
            next_value = jnp.where(wet, partial, 0.0) + rho_second * surface_value
            values.append((surface_value, next_value))
        return values

    def store_halves(level, slot, values):
        wet = level < bath[...]
        masked = [jnp.where(wet, h, 0.0) for h in values]
        along = sums_along_lanes([h[:columns] for h in masked], band)
        own = side[level].astype(f32)
        for n, h in enumerate(masked):
            across = sum_along_rows(h, columns, ring.at[slot, n], False)
            half = own * h[:columns] + (across + along[n])
            q[n, level, pl.ds(0, columns)] = jnp.where(wet[:columns], half, values[n][:columns])

    values = top_levels(
        rows,
        [(q[n, 0], q[n, 1]) for n in range(tracers)],
        [jnp.where(2 < depth, q[n, 2], 0.0) for n in range(tracers)],
        ratio_at(ratios, depth, 2),
        SCALE,
    )
    tops = [values[n][0] for n in range(tracers)]
    carry = tuple(jnp.where(1 < depth, values[n][1], q[n, 1]) for n in range(tracers))
    store_halves(0, 0, tops)
    store_halves(1, 1, carry)

    def down(step, slot, carry, low):
        level = low + step
        ratio = ratio_at(ratios, bath[...], level)
        rho[level] = ratio[:columns]
        out = [q[n, level] + ratio * carry[n] for n in range(tracers)]
        store_halves(level, slot, out)
        return tuple(out)

    for n, (low, size) in enumerate(chunks):
        if n > 0:
            for copy in arrivals[n]:
                copy.wait()
        first = max(low, 2)
        carry = sweep(low + size - first, functools.partial(down, low=first), carry, UNROLL)

    def up(step, slot, carry):
        level = levels - 1 - step
        ratio = rho[level]
        wet = level < bath[pl.ds(0, columns)]
        out = []
        for n in range(tracers):
            half = q[n, level, pl.ds(0, columns)]
            value = ratio * (half + carry[n])
            q[n, level, pl.ds(0, columns)] = jnp.where(wet, value, half)
            out.append(value)
        return tuple(out)

    zero = jnp.zeros((columns, lanes), f32)
    carry = sweep(levels - 2, up, (zero,) * tracers, 13)
    values = top_levels(
        columns,
        [(q[n, 0, pl.ds(0, columns)], q[n, 1, pl.ds(0, columns)]) for n in range(tracers)],
        carry,
        rho[2],
        SCALE * SCALE,
    )
    unscale = 1.0 / (SCALE * SCALE)
    for n in range(tracers):
        surface[n] = jnp.where(on_ocean, values[n][0] * unscale, other[n, pl.ds(0, columns)])
    surface[2] = jnp.where(on_ocean, top_mix[:columns], other[2, pl.ds(0, columns)])

    def last(step, slot, carry, low):
        level = low + step
        ratio = rho[level]
        wet = level < bath[pl.ds(0, columns)]
        out = []
        for n in range(tracers):
            h = q[n, level, pl.ds(0, columns)] + ratio * carry[n]
            q[n, level, pl.ds(0, columns)] = jnp.where(wet, h * unscale, h)
            out.append(h)
        return tuple(out)

    wet = 1 < depth[:columns]
    carry = []
    for n in range(tracers):
        start = q[n, 1, pl.ds(0, columns)]
        q[n, 0, pl.ds(0, columns)] = values[n][0] * unscale
        q[n, 1, pl.ds(0, columns)] = jnp.where(wet, values[n][1] * unscale, start)
        carry.append(values[n][1])
    carry = tuple(carry)
    leaving = []
    for n, (low, size) in enumerate(chunks):
        first = max(low, 2)
        carry = sweep(low + size - first, functools.partial(last, low=first), carry, 10)
        part = pl.ds(low, size)
        leaving.append(
            pltpu.make_async_copy(
                q.at[:, part, pl.ds(0, columns)], result.at[:, part], sems_out.at[n]
            )
        )
        leaving[-1].start()
    for copy in leaving:
        copy.wait()


def shift(value, axis, by):
    count = lax.axis_size(axis)
    return lax.ppermute(value, axis, [(i, (i + by) % count) for i in range(count)])


def in_hbm(value):
    return pltpu.with_memory_space_constraint(value, pltpu.HBM)


def per_device(
    surface_fields, source_blocks, source_columns, remap_weights, ocean_state, bathymetry
):
    tracers, levels, columns, lanes = ocean_state.shape
    slots = source_blocks.shape[2]
    count = lax.axis_size("blk")
    rows = columns + EDGE
    section = lax.axis_index("sec").astype(i32).reshape(1)
    fields = surface_fields[0]
    blocks = jnp.transpose(source_blocks[0])
    spots = jnp.transpose(source_columns[0])
    weights = remap_weights[0].reshape(columns * slots * lanes, lanes)
    tall = slots * lanes
    many = tracers * levels

    hbm = pl.BlockSpec(memory_space=pltpu.HBM)
    vmem = pl.BlockSpec(memory_space=pltpu.VMEM)
    smem = pl.BlockSpec(memory_space=pltpu.SMEM)
    shaped = jax.ShapeDtypeStruct
    pieces = len(chunks_of(levels))
    cells = rows * lanes

    request = pl.pallas_call(
        ask_kernel,
        out_shape=shaped((count, 128), i32),
        in_specs=[hbm, hbm],
        out_specs=vmem,
        scratch_shapes=[
            pltpu.VMEM(blocks.shape, i32),
            pltpu.VMEM(spots.shape, i32),
            pltpu.SemaphoreType.DMA((2,)),
        ],
        compiler_params=pltpu.CompilerParams(vmem_limit_bytes=4 * MIB),
        cost_estimate=pl.CostEstimate(flops=10**6, bytes_accessed=10**5, transcendentals=0),
    )(in_hbm(blocks), in_hbm(spots))
    asked = lax.all_to_all(request, "blk", split_axis=0, concat_axis=0, tiled=True)

    payload = shaped((2 * many + EXTRA + tall, lanes), bf16)
    to_left, to_right, table = pl.pallas_call(
        pack_kernel,
        out_shape=(
            payload,
            payload,
            shaped((FIELDS * columns, lanes), bf16),
        ),
        in_specs=[smem] + [hbm] * 5,
        out_specs=(vmem, vmem, vmem),
        scratch_shapes=[
            pltpu.VMEM((tracers, levels, 8, lanes), f32),
            pltpu.VMEM((tracers, levels, 8, lanes), f32),
            pltpu.VMEM((tracers, columns, lanes), f32),
            pltpu.VMEM(bathymetry.shape, i32),
            pltpu.VMEM(fields.shape, bf16),
            pltpu.VMEM(blocks.shape, i32),
            pltpu.VMEM((EXTRA, lanes), f32),
            pltpu.SemaphoreType.DMA((8,)),
        ],
        compiler_params=pltpu.CompilerParams(vmem_limit_bytes=8 * MIB),
        cost_estimate=pl.CostEstimate(
            flops=10**6, bytes_accessed=4 * 10**6, transcendentals=0
        ),
    )(
        section,
        in_hbm(ocean_state),
        in_hbm(bathymetry),
        in_hbm(fields),
        in_hbm(blocks),
        in_hbm(weights),
    )
    from_left = shift(to_right, "blk", 1)
    from_right = shift(to_left, "blk", -1)

    served = pl.pallas_call(
        serve_kernel,
        out_shape=shaped((count * PIECE, lanes), bf16),
        in_specs=[vmem] * 4,
        out_specs=vmem,
        compiler_params=pltpu.CompilerParams(vmem_limit_bytes=8 * MIB),
        cost_estimate=pl.CostEstimate(
            flops=10**7, bytes_accessed=10**6, transcendentals=0
        ),
    )(asked, table, from_left, from_right)
    columns_in = lax.all_to_all(served, "blk", split_axis=0, concat_axis=0, tiled=True)

    ratios = ratios_by_height(levels, lanes)
    q, side, bath, place = pl.pallas_call(
        functools.partial(start_kernel, count=count),
        out_shape=(
            pltpu.HBM((tracers, levels, rows, lanes), f32),
            pltpu.HBM((levels, columns, lanes), bf16),
            pltpu.HBM((rows, lanes), i32),
            pltpu.HBM((slots * columns, 128), i32),
        ),
        in_specs=[hbm, vmem, vmem, hbm, hbm, vmem],
        out_specs=(hbm,) * 4,
        scratch_shapes=[
            pltpu.VMEM((tracers, levels, rows, lanes), f32),
            pltpu.VMEM((levels, columns, lanes), bf16),
            pltpu.VMEM(ocean_state.shape, f32),
            pltpu.VMEM((rows, lanes), i32),
            pltpu.VMEM((many * 8, lanes), f32),
            pltpu.VMEM((4, rows, lanes), i32),
            pltpu.VMEM(bathymetry.shape, i32),
            pltpu.VMEM(blocks.shape, i32),
            pltpu.VMEM((slots * columns, 128), i32),
            pltpu.VMEM((UNROLL, tracers, columns + 3 * EDGE, lanes), f32),
            pltpu.VMEM((2 * lanes, lanes), bf16),
            pltpu.SemaphoreType.DMA((pieces + 2,)),
            pltpu.SemaphoreType.DMA((2 * pieces + 2,)),
        ],
        compiler_params=pltpu.CompilerParams(vmem_limit_bytes=28 * MIB),
        cost_estimate=pl.CostEstimate(
            flops=60 * levels * cells, bytes_accessed=200 * levels * cells, transcendentals=0
        ),
    )(
        in_hbm(ocean_state),
        from_left,
        from_right,
        in_hbm(bathymetry),
        in_hbm(blocks),
        ratios,
    )

    mine = pl.pallas_call(
        remap_kernel,
        out_shape=shaped((6, rows, lanes), f32),
        in_specs=[vmem, hbm, vmem, vmem, hbm, hbm],
        out_specs=vmem,
        scratch_shapes=[
            pltpu.VMEM((slots, rows * 8, lanes), f32),
            pltpu.VMEM((rows * 8, lanes), f32),
            pltpu.VMEM(weights.shape, bf16),
            pltpu.VMEM(fields.shape, bf16),
            pltpu.VMEM((slots * columns, 128), i32),
            pltpu.SemaphoreType.DMA((2 + columns // 8,)),
        ],
        compiler_params=pltpu.CompilerParams(vmem_limit_bytes=20 * MIB),
        cost_estimate=pl.CostEstimate(
            flops=16 * weights.size, bytes_accessed=2 * weights.size, transcendentals=0
        ),
    )(
        columns_in,
        in_hbm(place),
        from_left,
        from_right,
        in_hbm(weights),
        in_hbm(fields),
    )
    other = lax.ppermute(mine, "sec", [(0, 1), (1, 0)])

    surface, result = pl.pallas_call(
        finish_kernel,
        out_shape=(shaped((3, columns, lanes), f32), shaped(ocean_state.shape, f32)),
        in_specs=[smem] + [vmem] * 2 + [hbm] * 3 + [vmem],
        out_specs=(vmem, hbm),
        scratch_shapes=[
            pltpu.VMEM((tracers, levels, rows, lanes), f32),
            pltpu.VMEM((levels, columns, lanes), f32),
            pltpu.VMEM((levels, columns, lanes), bf16),
            pltpu.VMEM((rows, lanes), i32),
            pltpu.VMEM((UNROLL, tracers, columns + 2 * EDGE, lanes), f32),
            pltpu.VMEM((2 * lanes, lanes), bf16),
            pltpu.SemaphoreType.DMA((pieces + 1, 2)),
            pltpu.SemaphoreType.DMA((pieces,)),
        ],
        compiler_params=pltpu.CompilerParams(vmem_limit_bytes=28 * MIB),
        cost_estimate=pl.CostEstimate(
            flops=60 * levels * cells, bytes_accessed=32 * levels * cells, transcendentals=0
        ),
    )(
        section,
        mine,
        other,
        in_hbm(bath),
        in_hbm(q),
        in_hbm(side),
        ratios,
    )
    return (surface[None], result)


def solution(mesh):
    return jax.shard_map(
        per_device,
        mesh=mesh,
        in_specs=(
            P("sec", None, "blk", None),
            P("sec", "blk", None),
            P("sec", "blk", None),
            P("sec", "blk", None, None, None),
            P(None, None, "blk", None),
            P("blk", None),
        ),
        out_specs=(P("sec", None, "blk", None), P(None, None, "blk", None)),
        check_vma=False,
    )
```

```python
import functools

import jax
import jax.numpy as jnp
import numpy as np
from jax import lax
from jax.experimental import pallas as pl
from jax.experimental.pallas import tpu as pltpu
from jax.sharding import PartitionSpec as P

FLUX_GAIN = 0.5
SIDE_MIX = 0.2
TOP_MIX = 1.0
DEEP_MIX = 2.0
SCALE = 1.0 / (0.5 * SIDE_MIX)

MOST = 16
SLOTS = MOST + 2
FIELDS = 3
PIECE = 56
EDGE = 8
EXTRA = 16
UNROLL = 5
MIB = 2**20
bf16, f32, i32 = jnp.bfloat16, jnp.float32, jnp.int32


def iota(shape, axis):
    return lax.broadcasted_iota(i32, shape, axis)


def band_matrix(lanes):
    shape = (2 * lanes, lanes)
    apart = lax.rem(iota(shape, 0), lanes) - iota(shape, 1)
    return jnp.where(jnp.abs(apart) == 1, 1.0, 0.0).astype(bf16)


def sums_along_lanes(arrays, band):
    rows = arrays[0].shape[0]
    stacked = jnp.concatenate(arrays, axis=0)
    head = stacked.astype(bf16)
    tail = (stacked - head.astype(f32)).astype(bf16)
    sums = jnp.dot(
        jnp.concatenate([head, tail], axis=1), band[...], preferred_element_type=f32
    )
    return [sums[n * rows : (n + 1) * rows] for n in range(len(arrays))]


def sum_along_rows(h, columns, ring, with_edge):
    edge = h[columns:]
    ring[pl.ds(0, EDGE), :] = edge
    ring[pl.ds(EDGE, columns), :] = h[:columns]
    ring[pl.ds(EDGE + columns, EDGE), :] = edge
    rows = columns
    if with_edge:
        ring[pl.ds(2 * EDGE + columns, EDGE), :] = h[:EDGE]
        rows = columns + EDGE
    return ring[pl.ds(EDGE - 1, rows), :] + ring[pl.ds(EDGE + 1, rows), :]


def edge_tile(right, left):
    row = iota((EDGE, right.shape[1]), 0)
    return jnp.where(row == 0, right, jnp.where(row == EDGE - 1, left, 0.0))


def chunks_of(levels):
    size = 10 if levels % 10 == 0 else levels
    return [(start, size) for start in range(0, levels, size)]


def sweep(count, body, carry, unroll):
    rounds = count // unroll

    def several(number, carry):
        for n in range(unroll):
            carry = body(number * unroll + n, n, carry)
        return carry

    carry = lax.fori_loop(0, rounds, several, carry)
    for step in range(rounds * unroll, count):
        carry = body(step, step - rounds * unroll, carry)
    return carry


def ranks(blocks, count):
    slots, columns = blocks.shape
    before = jnp.where(iota((columns, columns), 0) < iota((columns, columns), 1), 1.0, 0.0)
    before = before.astype(bf16)
    used = jnp.zeros((count, 1), f32)
    result = []
    for k in range(slots):
        owner = iota((count, columns), 0) == blocks[k : k + 1, :]
        one_hot = jnp.where(owner, 1.0, 0.0)
        earlier = used + jnp.dot(one_hot.astype(bf16), before, preferred_element_type=f32)
        rank = jnp.sum(one_hot * earlier, axis=0, keepdims=True)
        used = used + jnp.sum(one_hot, axis=1, keepdims=True)
        result.append((owner, rank))
    return result


def ask_kernel(blocks, spots, request, blocks_in, spots_in, sems):
    copies = [
        pltpu.make_async_copy(blocks, blocks_in, sems.at[0]),
        pltpu.make_async_copy(spots, spots_in, sems.at[1]),
    ]
    for copy in copies:
        copy.start()
    for copy in copies:
        copy.wait()
    count, columns = request.shape[0], blocks.shape[1]
    place = iota((128, columns), 0)
    field = place // SLOTS
    slot = jnp.where(field < FIELDS, place - field * SLOTS, -1)
    here = iota((128, columns), 1)
    marks = ((slot == MOST) & (here == 0)) | ((slot == MOST + 1) & (here == columns - 1))
    asked = jnp.zeros(request.shape, f32)
    for k, (owner, rank) in enumerate(ranks(blocks_in, count)):
        filled = jnp.where((slot == rank.astype(i32)) | marks, 1.0, 0.0).astype(bf16)
        named = jnp.where(owner, spots_in[k : k + 1, :].astype(f32), 0.0).astype(bf16)
        asked = asked + lax.dot_general(
            named, filled, (((1,), (1,)), ((), ())), preferred_element_type=f32
        )
    request[...] = asked.astype(i32) + (iota(request.shape, 1) // SLOTS) * columns


def pack_kernel(
    section, state, bath, fields, blocks, weights,
    to_left, to_right, table,
    low, high, surface, bath_in, fields_in, blocks_in, extra, sems,
):
    tracers, levels, columns, lanes = state.shape
    slots = blocks.shape[0]
    many = tracers * levels
    wide = to_left.shape[0] - 2 * many - EXTRA
    below = pl.ds(2 * many + EXTRA, wide)
    pairs = [
        (state.at[:, :, pl.ds(0, 8)], low),
        (state.at[:, :, pl.ds(columns - 8, 8)], high),
        (blocks, blocks_in),
        (bath, bath_in),
        (fields, fields_in),
        (state.at[:, 0], surface),
        (weights.at[pl.ds(0, wide)], to_left.at[below]),
        (weights.at[pl.ds((columns - 1) * wide, wide)], to_right.at[below]),
    ]
    copies = [pltpu.make_async_copy(src, dst, sems.at[n]) for n, (src, dst) in enumerate(pairs)]
    for copy in copies:
        copy.start()
    for copy in copies[2:6]:
        copy.wait()
    for out, first, at in ((to_left, 0, 0), (to_right, columns - 2, columns - 1)):
        extra[...] = jnp.zeros_like(extra)
        extra[0:2] = bath_in[first : first + 2].astype(f32)
        for f in range(3):
            extra[2 + f : 3 + f] = fields_in[f].astype(f32)[at : at + 1]
        extra[8 : 8 + slots] = jnp.broadcast_to(
            blocks_in[:, at : at + 1].astype(f32), (slots, lanes)
        )
        out[pl.ds(2 * many, EXTRA)] = extra[...].astype(bf16)
    on_ocean = section[0] == 1
    for f in range(3):
        own = fields_in[f]
        if f < 2:
            own = jnp.where(on_ocean, surface[f], own.astype(f32)).astype(bf16)
        table[f * columns : (f + 1) * columns, :] = own
    copies[0].wait()
    copies[1].wait()
    for c in range(2):
        for n in range(tracers):
            part = pl.ds(c * many + n * levels, levels)
            tiles = low.at[n].reshape(levels * 8, lanes)
            to_left[part] = tiles[pl.ds(c, levels, stride=8), :].astype(bf16)
            tiles = high.at[n].reshape(levels * 8, lanes)
            to_right[part] = tiles[pl.ds(6 + c, levels, stride=8), :].astype(bf16)
    copies[6].wait()
    copies[7].wait()


def serve_kernel(asked, table, from_left, from_right, out):
    count = asked.shape[0]
    wanted = jnp.transpose(asked[...].astype(f32))[:PIECE]
    height = table.shape[0]
    slot = lax.rem(iota((PIECE, 1), 0), SLOTS)
    parts = []
    for e in range(count):
        after, before = (e + 1) % count, (e - 1) % count
        spot = jnp.where(
            slot == MOST,
            wanted[:, after : after + 1],
            jnp.where(slot == MOST + 1, wanted[:, before : before + 1], wanted[:, e : e + 1]),
        )
        parts.append(jnp.where(iota((PIECE, height), 1) == spot.astype(i32), 1.0, 0.0))
    chosen = jnp.concatenate(parts, axis=0).astype(bf16)
    out[...] = jnp.dot(chosen, table[...], preferred_element_type=f32).astype(bf16)


def start_kernel(
    state, from_left, from_right, bath, blocks, ratios,
    q_result, side_result, bath_result, place_result,
    q_out, side_out, held, bath_out, halo, near, bath_in, blocks_in, place, ring, band,
    sems, sems_out, *, count,
):
    tracers, levels, columns, lanes = state.shape
    rows = columns + EDGE
    many = tracers * levels
    chunks = chunks_of(levels)
    copies = []
    for n, (low, size) in enumerate(chunks):
        copies.append(
            pltpu.make_async_copy(
                state.at[:, pl.ds(low, size)], held.at[:, pl.ds(low, size)], sems.at[n]
            )
        )
    bath_copy = pltpu.make_async_copy(bath, bath_in, sems.at[len(chunks)])
    blocks_copy = pltpu.make_async_copy(blocks, blocks_in, sems.at[len(chunks) + 1])
    blocks_copy.start()
    bath_copy.start()
    for copy in reversed(copies):
        copy.start()
    leaving = []

    def send(source, target, number):
        copy = pltpu.make_async_copy(source, target, sems_out.at[number])
        copy.start()
        leaving.append(copy)

    for c in range(2):
        part = pl.ds(c * many, many)
        halo[pl.ds(c, many, stride=8), :] = from_right[part].astype(f32)
        halo[pl.ds(EDGE - 2 + c, many, stride=8), :] = from_left[part].astype(f32)
    right = from_right[pl.ds(2 * many, EXTRA)].astype(f32)
    left = from_left[pl.ds(2 * many, EXTRA)].astype(f32)
    row = iota((EDGE, lanes), 0)
    edge = jnp.where(
        row == 0,
        right[0:1],
        jnp.where(
            row == 1,
            right[1:2],
            jnp.where(row == EDGE - 2, left[0:1], jnp.where(row == EDGE - 1, left[1:2], 0.0)),
        ),
    )
    bath_copy.wait()
    depth = jnp.concatenate([bath_in[...], edge.astype(i32)], axis=0)
    bath_out[...] = depth
    send(bath_out, bath_result, 2 * len(chunks))
    blocks_copy.wait()
    for k, (_, rank) in enumerate(ranks(blocks_in, count)):
        arrives = blocks_in[k : k + 1, :].astype(f32) * PIECE + rank
        spread = jnp.transpose(jnp.broadcast_to(arrives, (128, columns)))
        place[k * columns : (k + 1) * columns, :] = spread.astype(i32)
    send(place, place_result, 2 * len(chunks) + 1)
    lane = iota((rows, lanes), 1)
    a = pltpu.roll(depth, 1, 0)
    b = pltpu.roll(depth, rows - 1, 0)
    c = jnp.where(lane == 0, 0, pltpu.roll(depth, 1, 1))
    d = jnp.where(lane == lanes - 1, 0, pltpu.roll(depth, lanes - 1, 1))
    a, b = jnp.maximum(a, b), jnp.minimum(a, b)
    c, d = jnp.maximum(c, d), jnp.minimum(c, d)
    a, c = jnp.maximum(a, c), jnp.minimum(a, c)
    b, d = jnp.maximum(b, d), jnp.minimum(b, d)
    near[0], near[1], near[2], near[3] = a, jnp.maximum(b, c), jnp.minimum(b, c), d


    band[...] = band_matrix(lanes)

    def side(level, slot):
        wet = level < bath_out[...]
        own = 0.5 * SCALE
        for n in range(4):
            own = jnp.where(level < near[n], 0.5 * SCALE - (n + 1), own)
        side_out[level] = own[:columns].astype(bf16)
        starts, masked = [], []
        for n in range(tracers):
            spot = (n * levels + level) * 8
            if not isinstance(level, int):
                spot = pl.multiple_of(spot, 8)
            full = jnp.concatenate([held[n, level], halo[pl.ds(spot, 8), :]], axis=0)
            starts.append(full)
            masked.append(jnp.where(wet, full, 0.0))
        along = sums_along_lanes(masked, band)
        halves = []
        for n, h in enumerate(masked):
            across = sum_along_rows(h, columns, ring.at[slot, n], True)
            halves.append(own * h + (across + along[n]))
        return wet, starts, halves

    def deep(step, slot, below, top):
        level = top - step
        wet, starts, halves = side(level, slot)
        rho = ratio_at(ratios, bath_out[...], level)
        solved = []
        for n in range(tracers):
            q = rho * (halves[n] + below[n])
            q_out[n, level] = jnp.where(wet, q, starts[n])
            solved.append(q)
        return tuple(solved)

    carry = tuple(jnp.zeros((rows, lanes), f32) for _ in range(tracers))
    for n in reversed(range(len(chunks))):
        low, size = chunks[n]
        copies[n].wait()
        first = max(low, 2)
        top = low + size - 1
        carry = sweep(top - first + 1, functools.partial(deep, top=top), carry, UNROLL)
        if n == 0:
            for level in (1, 0):
                wet, starts, halves = side(level, level)
                for m in range(tracers):
                    q_out[m, level] = jnp.where(wet, halves[m], starts[m])
        part = pl.ds(low, size)
        send(q_out.at[:, part], q_result.at[:, part], 2 * n)
        send(side_out.at[part], side_result.at[part], 2 * n + 1)
    for copy in leaving:
        copy.wait()


def ratio_at(ratios, depth, level):
    lookup = jnp.broadcast_to(ratios[0:1], depth.shape)
    height = jnp.maximum(depth - level, 0)
    return jnp.take_along_axis(lookup, height, axis=1, mode="promise_in_bounds")


def ratios_by_height(levels, lanes):
    values = [0.0]
    ratio = DEEP_MIX / (1.0 + DEEP_MIX)
    for _ in range(levels):
        values.append(ratio)
        ratio = DEEP_MIX / (1.0 + DEEP_MIX + DEEP_MIX - DEEP_MIX * ratio)
    values += [0.0] * (lanes - len(values))
    return jnp.broadcast_to(jnp.asarray(np.array(values, np.float32)), (8, lanes))


def remap_kernel(
    columns_in, place_from, from_left, from_right, weights, own_fields,
    out, picked, solved, held, fields_in, place, sems,
):
    fields, rows, width = out.shape[0] // 2, out.shape[1], out.shape[2]
    columns = rows - EDGE
    slots = weights.shape[0] // (columns * width)
    tall = slots * width
    many = from_left.shape[0] - tall - EXTRA
    group = 8
    place_copy = pltpu.make_async_copy(place_from, place, sems.at[0])
    fields_copy = pltpu.make_async_copy(own_fields, fields_in, sems.at[1])
    copies = []
    for n in range(columns // group):
        part = pl.ds(n * group * tall, group * tall)
        copies.append(pltpu.make_async_copy(weights.at[part], held.at[part], sems.at[2 + n]))
    for copy in [place_copy] + copies + [fields_copy]:
        copy.start()
    right = from_right[pl.ds(many, EXTRA)].astype(f32)
    left = from_left[pl.ds(many, EXTRA)].astype(f32)
    row = iota((EDGE, 1), 0)
    picked[...] = jnp.zeros_like(picked)
    place_copy.wait()
    wanted = []
    for k in range(slots):
        edge = jnp.where(
            row == 0,
            right[8 + k : 9 + k, 0:1] * PIECE + MOST,
            jnp.where(row == EDGE - 1, left[8 + k : 9 + k, 0:1] * PIECE + MOST + 1, -PIECE),
        ).astype(i32)
        wanted += [place[k * columns : (k + 1) * columns, 0:1], edge]
    wanted = jnp.concatenate(wanted, axis=0)
    spots = iota((slots * rows, columns_in.shape[0]), 1)
    for f in range(fields):
        chosen = jnp.where(spots == wanted + f * SLOTS, 1.0, 0.0).astype(bf16)
        found = jnp.dot(chosen, columns_in[...], preferred_element_type=f32)
        for k in range(slots):
            picked[k, pl.ds(f, rows, stride=8), :] = found[k * rows : (k + 1) * rows]

    def one(row, table_of):
        spot = pl.ds(row * 8, 8)
        vector = jnp.concatenate([picked[k, spot, :] for k in range(slots)], axis=1)
        matrix = jnp.concatenate([table_of(k) for k in range(slots)], axis=1)
        solved[spot, :] = lax.dot_general(
            vector.astype(bf16), matrix, (((1,), (1,)), ((), ())), preferred_element_type=f32
        )

    solved[...] = jnp.zeros_like(solved)
    below = many + EXTRA
    one(columns, lambda k: from_right[pl.ds(below + k * width, width)])
    one(rows - 1, lambda k: from_left[pl.ds(below + k * width, width)])
    for n in range(columns // group):
        copies[n].wait()
        for m in range(group):
            spot = n * group + m
            one(spot, lambda k: held[pl.ds((spot * slots + k) * width, width)])
    fields_copy.wait()
    for f in range(fields):
        out[f, pl.ds(0, columns)] = solved[pl.ds(f, columns, stride=8), :]
        out[f, pl.ds(columns, EDGE)] = solved[pl.ds(columns * 8 + f, EDGE, stride=8), :]
        out[fields + f, pl.ds(0, columns)] = fields_in[f].astype(f32)
        out[fields + f, pl.ds(columns, EDGE)] = edge_tile(
            right[2 + f : 3 + f], left[2 + f : 3 + f]
        )


def finish_kernel(
    section, mine, other, bath_from, q_from, side_from, ratios, surface, result,
    q, side, bath, padded, rho, solved, done, band, sems, sems_out,
):
    tracers, levels, columns, lanes = result.shape
    rows = columns + EDGE
    chunks = chunks_of(levels)
    bath_copy = pltpu.make_async_copy(bath_from, bath, sems.at[len(chunks), 0])
    bath_copy.start()
    arrivals = []
    for n, (low, size) in enumerate(chunks):
        part = pl.ds(low, size)
        arrivals.append(
            (
                pltpu.make_async_copy(q_from.at[:, part], q.at[:, part], sems.at[n, 0]),
                pltpu.make_async_copy(side_from.at[part], side.at[part], sems.at[n, 1]),
            )
        )
    for group in arrivals:
        for copy in group:
            copy.start()
    bath_copy.wait()
    for copy in arrivals[0]:
        copy.wait()
    on_ocean = section[0] == 1
    band[...] = band_matrix(lanes)
    flux = [jnp.where(on_ocean, other[f], mine[f]) for f in range(3)]
    own = [jnp.where(on_ocean, mine[3 + f], other[3 + f]) for f in range(3)]
    forcing = [flux[0] + own[0], flux[1] + own[1]]
    top_mix = TOP_MIX * (1.0 + flux[2] * flux[2] + own[2] * own[2])
    depth = bath[...]

    def top_levels(count, halves, below, rho_below, scale):
        wet = 1 < depth[:count]
        link = jnp.where(wet, top_mix[:count], 0.0)
        deeper = jnp.where(2 < depth[:count], DEEP_MIX - DEEP_MIX * rho_below, 0.0)
        second = 1.0 / (1.0 + link + deeper)
        rho_second = link * second
        first = 1.0 / (1.0 + link - link * rho_second)
        values = []
        for n in range(tracers):
            partial = 2.0 * (halves[n][1] + below[n]) * second
            source = 2.0 * halves[n][0] + scale * FLUX_GAIN * forcing[n][:count]
            surface_value = (source + link * partial) * first
            next_value = jnp.where(wet, partial, 0.0) + rho_second * surface_value
            values.append((surface_value, next_value))
        return values

    def put(level, values):
        for n, h in enumerate(values):
            padded[n, level, pl.ds(0, EDGE)] = h[columns:]
            padded[n, level, pl.ds(EDGE, columns)] = h[:columns]
            padded[n, level, pl.ds(EDGE + columns, EDGE)] = h[columns:]

    values = top_levels(
        rows,
        [(q[n, 0], q[n, 1]) for n in range(tracers)],
        [jnp.where(2 < depth, q[n, 2], 0.0) for n in range(tracers)],
        ratio_at(ratios, depth, 2),
        SCALE,
    )
    put(0, [jnp.where(0 < depth, values[n][0], 0.0) for n in range(tracers)])
    carry = tuple(values[n][1] for n in range(tracers))
    put(1, carry)

    def down(step, slot, carry, low):
        level = low + step
        ratio = ratio_at(ratios, bath[...], level)
        rho[level] = ratio[:columns]
        wet = level < bath[...]
        out = [jnp.where(wet, q[n, level], 0.0) + ratio * carry[n] for n in range(tracers)]
        put(level, out)
        return tuple(out)

    for n, (low, size) in enumerate(chunks):
        if n > 0:
            for copy in arrivals[n]:
                copy.wait()
        first = max(low, 2)
        carry = sweep(low + size - first, functools.partial(down, low=first), carry, UNROLL)

    def halves_at(level):
        middle = [padded[n, level, pl.ds(EDGE, columns)] for n in range(tracers)]
        along = sums_along_lanes(middle, band)
        own = side[level].astype(f32)
        out = []
        for n in range(tracers):
            across = padded[n, level, pl.ds(EDGE - 1, columns)]
            across = across + padded[n, level, pl.ds(EDGE + 1, columns)]
            out.append(own * middle[n] + (across + along[n]))
        return out

    def up(step, slot, carry):
        level = levels - 1 - step
        ratio = rho[level]
        halves = halves_at(level)
        out = [ratio * (halves[n] + carry[n]) for n in range(tracers)]
        for n in range(tracers):
            solved[n, level] = out[n]
        return tuple(out)

    zero = jnp.zeros((columns, lanes), f32)
    carry = sweep(levels - 2, up, (zero,) * tracers, 6)
    values = top_levels(columns, list(zip(halves_at(0), halves_at(1))), carry, rho[2], SCALE * SCALE)
    unscale = 1.0 / (SCALE * SCALE)
    for n in range(tracers):
        surface[n] = jnp.where(on_ocean, values[n][0] * unscale, other[n, pl.ds(0, columns)])
    surface[2] = jnp.where(on_ocean, top_mix[:columns], other[2, pl.ds(0, columns)])

    def last(step, slot, carry, low):
        level = low + step
        ratio = rho[level]
        wet = level < bath[pl.ds(0, columns)]
        out = []
        for n in range(tracers):
            h = solved[n, level] + ratio * carry[n]
            done[n, level] = jnp.where(wet, h * unscale, q[n, level, pl.ds(0, columns)])
            out.append(h)
        return tuple(out)

    wet = 1 < depth[:columns]
    for n in range(tracers):
        done[n, 0] = values[n][0] * unscale
        done[n, 1] = jnp.where(wet, values[n][1] * unscale, q[n, 1, pl.ds(0, columns)])
    carry = tuple(values[n][1] for n in range(tracers))
    leaving = []
    for n, (low, size) in enumerate(chunks):
        first = max(low, 2)
        carry = sweep(low + size - first, functools.partial(last, low=first), carry, 10)
        part = pl.ds(low, size)
        leaving.append(
            pltpu.make_async_copy(done.at[:, part], result.at[:, part], sems_out.at[n])
        )
        leaving[-1].start()
    for copy in leaving:
        copy.wait()


def shift(value, axis, by):
    count = lax.axis_size(axis)
    return lax.ppermute(value, axis, [(i, (i + by) % count) for i in range(count)])


def in_hbm(value):
    return pltpu.with_memory_space_constraint(value, pltpu.HBM)


def per_device(
    surface_fields, source_blocks, source_columns, remap_weights, ocean_state, bathymetry
):
    tracers, levels, columns, lanes = ocean_state.shape
    slots = source_blocks.shape[2]
    count = lax.axis_size("blk")
    rows = columns + EDGE
    section = lax.axis_index("sec").astype(i32).reshape(1)
    fields = surface_fields[0]
    blocks = jnp.transpose(source_blocks[0])
    spots = jnp.transpose(source_columns[0])
    weights = remap_weights[0].reshape(columns * slots * lanes, lanes)
    tall = slots * lanes
    many = tracers * levels

    hbm = pl.BlockSpec(memory_space=pltpu.HBM)
    vmem = pl.BlockSpec(memory_space=pltpu.VMEM)
    smem = pl.BlockSpec(memory_space=pltpu.SMEM)
    shaped = jax.ShapeDtypeStruct
    pieces = len(chunks_of(levels))
    cells = rows * lanes

    request = pl.pallas_call(
        ask_kernel,
        out_shape=shaped((count, 128), i32),
        in_specs=[hbm, hbm],
        out_specs=vmem,
        scratch_shapes=[
            pltpu.VMEM(blocks.shape, i32),
            pltpu.VMEM(spots.shape, i32),
            pltpu.SemaphoreType.DMA((2,)),
        ],
        compiler_params=pltpu.CompilerParams(vmem_limit_bytes=4 * MIB),
        cost_estimate=pl.CostEstimate(flops=10**6, bytes_accessed=10**5, transcendentals=0),
    )(in_hbm(blocks), in_hbm(spots))
    asked = lax.all_to_all(request, "blk", split_axis=0, concat_axis=0, tiled=True)

    payload = shaped((2 * many + EXTRA + tall, lanes), bf16)
    to_left, to_right, table = pl.pallas_call(
        pack_kernel,
        out_shape=(
            payload,
            payload,
            shaped((FIELDS * columns, lanes), bf16),
        ),
        in_specs=[smem] + [hbm] * 5,
        out_specs=(vmem, vmem, vmem),
        scratch_shapes=[
            pltpu.VMEM((tracers, levels, 8, lanes), f32),
            pltpu.VMEM((tracers, levels, 8, lanes), f32),
            pltpu.VMEM((tracers, columns, lanes), f32),
            pltpu.VMEM(bathymetry.shape, i32),
            pltpu.VMEM(fields.shape, bf16),
            pltpu.VMEM(blocks.shape, i32),
            pltpu.VMEM((EXTRA, lanes), f32),
            pltpu.SemaphoreType.DMA((8,)),
        ],
        compiler_params=pltpu.CompilerParams(vmem_limit_bytes=8 * MIB),
        cost_estimate=pl.CostEstimate(
            flops=10**6, bytes_accessed=4 * 10**6, transcendentals=0
        ),
    )(
        section,
        in_hbm(ocean_state),
        in_hbm(bathymetry),
        in_hbm(fields),
        in_hbm(blocks),
        in_hbm(weights),
    )
    from_left = shift(to_right, "blk", 1)
    from_right = shift(to_left, "blk", -1)

    served = pl.pallas_call(
        serve_kernel,
        out_shape=shaped((count * PIECE, lanes), bf16),
        in_specs=[vmem] * 4,
        out_specs=vmem,
        compiler_params=pltpu.CompilerParams(vmem_limit_bytes=8 * MIB),
        cost_estimate=pl.CostEstimate(
            flops=10**7, bytes_accessed=10**6, transcendentals=0
        ),
    )(asked, table, from_left, from_right)
    columns_in = lax.all_to_all(served, "blk", split_axis=0, concat_axis=0, tiled=True)

    ratios = ratios_by_height(levels, lanes)
    q, side, bath, place = pl.pallas_call(
        functools.partial(start_kernel, count=count),
        out_shape=(
            pltpu.HBM((tracers, levels, rows, lanes), f32),
            pltpu.HBM((levels, columns, lanes), bf16),
            pltpu.HBM((rows, lanes), i32),
            pltpu.HBM((slots * columns, 128), i32),
        ),
        in_specs=[hbm, vmem, vmem, hbm, hbm, vmem],
        out_specs=(hbm,) * 4,
        scratch_shapes=[
            pltpu.VMEM((tracers, levels, rows, lanes), f32),
            pltpu.VMEM((levels, columns, lanes), bf16),
            pltpu.VMEM(ocean_state.shape, f32),
            pltpu.VMEM((rows, lanes), i32),
            pltpu.VMEM((many * 8, lanes), f32),
            pltpu.VMEM((4, rows, lanes), i32),
            pltpu.VMEM(bathymetry.shape, i32),
            pltpu.VMEM(blocks.shape, i32),
            pltpu.VMEM((slots * columns, 128), i32),
            pltpu.VMEM((UNROLL, tracers, columns + 3 * EDGE, lanes), f32),
            pltpu.VMEM((2 * lanes, lanes), bf16),
            pltpu.SemaphoreType.DMA((pieces + 2,)),
            pltpu.SemaphoreType.DMA((2 * pieces + 2,)),
        ],
        compiler_params=pltpu.CompilerParams(vmem_limit_bytes=28 * MIB),
        cost_estimate=pl.CostEstimate(
            flops=60 * levels * cells, bytes_accessed=200 * levels * cells, transcendentals=0
        ),
    )(
        in_hbm(ocean_state),
        from_left,
        from_right,
        in_hbm(bathymetry),
        in_hbm(blocks),
        ratios,
    )

    mine = pl.pallas_call(
        remap_kernel,
        out_shape=shaped((6, rows, lanes), f32),
        in_specs=[vmem, hbm, vmem, vmem, hbm, hbm],
        out_specs=vmem,
        scratch_shapes=[
            pltpu.VMEM((slots, rows * 8, lanes), f32),
            pltpu.VMEM((rows * 8, lanes), f32),
            pltpu.VMEM(weights.shape, bf16),
            pltpu.VMEM(fields.shape, bf16),
            pltpu.VMEM((slots * columns, 128), i32),
            pltpu.SemaphoreType.DMA((2 + columns // 8,)),
        ],
        compiler_params=pltpu.CompilerParams(vmem_limit_bytes=20 * MIB),
        cost_estimate=pl.CostEstimate(
            flops=16 * weights.size, bytes_accessed=2 * weights.size, transcendentals=0
        ),
    )(
        columns_in,
        in_hbm(place),
        from_left,
        from_right,
        in_hbm(weights),
        in_hbm(fields),
    )
    other = lax.ppermute(mine, "sec", [(0, 1), (1, 0)])

    surface, result = pl.pallas_call(
        finish_kernel,
        out_shape=(shaped((3, columns, lanes), f32), shaped(ocean_state.shape, f32)),
        in_specs=[smem] + [vmem] * 2 + [hbm] * 3 + [vmem],
        out_specs=(vmem, hbm),
        scratch_shapes=[
            pltpu.VMEM((tracers, levels, rows, lanes), f32),
            pltpu.VMEM((levels, columns, lanes), bf16),
            pltpu.VMEM((rows, lanes), i32),
            pltpu.VMEM((tracers, levels, columns + 2 * EDGE, lanes), f32),
            pltpu.VMEM((levels, columns, lanes), f32),
            pltpu.VMEM(ocean_state.shape, f32),
            pltpu.VMEM(ocean_state.shape, f32),
            pltpu.VMEM((2 * lanes, lanes), bf16),
            pltpu.SemaphoreType.DMA((pieces + 1, 2)),
            pltpu.SemaphoreType.DMA((pieces,)),
        ],
        compiler_params=pltpu.CompilerParams(vmem_limit_bytes=36 * MIB),
        cost_estimate=pl.CostEstimate(
            flops=60 * levels * cells, bytes_accessed=32 * levels * cells, transcendentals=0
        ),
    )(
        section,
        mine,
        other,
        in_hbm(bath),
        in_hbm(q),
        in_hbm(side),
        ratios,
    )
    return (surface[None], result)


def solution(mesh):
    return jax.shard_map(
        per_device,
        mesh=mesh,
        in_specs=(
            P("sec", None, "blk", None),
            P("sec", "blk", None),
            P("sec", "blk", None),
            P("sec", "blk", None, None, None),
            P(None, None, "blk", None),
            P("blk", None),
        ),
        out_specs=(P("sec", None, "blk", None), P(None, None, "blk", None)),
        check_vma=False,
    )
```

```python
import functools
import math

import jax
import jax.numpy as jnp
from jax import lax
from jax.experimental import pallas as pl
from jax.experimental.pallas import tpu as pltpu
from jax.sharding import PartitionSpec as P

FLUX_GAIN = 0.5
SIDE_MIX = 0.2
TOP_MIX = 1.0
DEEP_MIX = 2.0
FIXED = (1.0 + 2.0 * DEEP_MIX - math.sqrt(1.0 + 4.0 * DEEP_MIX)) / (2.0 * DEEP_MIX)
SCALE = 1.0 / (0.5 * SIDE_MIX)

MOST = 16
SLOTS = MOST + 2
FIELDS = 3
PIECE = 56
EDGE = 8
EXTRA = 16
UNROLL = 5
MIB = 2**20
bf16, f32, i32 = jnp.bfloat16, jnp.float32, jnp.int32


def iota(shape, axis):
    return lax.broadcasted_iota(i32, shape, axis)


def band_matrix(lanes):
    shape = (2 * lanes, lanes)
    apart = lax.rem(iota(shape, 0), lanes) - iota(shape, 1)
    return jnp.where(jnp.abs(apart) == 1, 1.0, 0.0).astype(bf16)


def sums_along_lanes(arrays, band):
    rows = arrays[0].shape[0]
    stacked = jnp.concatenate(arrays, axis=0)
    head = stacked.astype(bf16)
    tail = (stacked - head.astype(f32)).astype(bf16)
    sums = jnp.dot(
        jnp.concatenate([head, tail], axis=1), band[...], preferred_element_type=f32
    )
    return [sums[n * rows : (n + 1) * rows] for n in range(len(arrays))]


def sum_along_rows(h, columns, ring, with_edge):
    edge = h[columns:]
    ring[pl.ds(0, EDGE), :] = edge
    ring[pl.ds(EDGE, columns), :] = h[:columns]
    ring[pl.ds(EDGE + columns, EDGE), :] = edge
    rows = columns
    if with_edge:
        ring[pl.ds(2 * EDGE + columns, EDGE), :] = h[:EDGE]
        rows = columns + EDGE
    return ring[pl.ds(EDGE - 1, rows), :] + ring[pl.ds(EDGE + 1, rows), :]


def edge_tile(right, left):
    row = iota((EDGE, right.shape[1]), 0)
    return jnp.where(row == 0, right, jnp.where(row == EDGE - 1, left, 0.0))


def chunks_of(levels):
    size = 10 if levels % 10 == 0 else levels
    return [(start, size) for start in range(0, levels, size)]


def sweep(count, body, carry, unroll):
    rounds = count // unroll

    def several(number, carry):
        for n in range(unroll):
            carry = body(number * unroll + n, n, carry)
        return carry

    carry = lax.fori_loop(0, rounds, several, carry)
    for step in range(rounds * unroll, count):
        carry = body(step, step - rounds * unroll, carry)
    return carry


def ranks(blocks, count):
    slots, columns = blocks.shape
    before = jnp.where(iota((columns, columns), 0) < iota((columns, columns), 1), 1.0, 0.0)
    before = before.astype(bf16)
    used = jnp.zeros((count, 1), f32)
    result = []
    for k in range(slots):
        owner = iota((count, columns), 0) == blocks[k : k + 1, :]
        one_hot = jnp.where(owner, 1.0, 0.0)
        earlier = used + jnp.dot(one_hot.astype(bf16), before, preferred_element_type=f32)
        rank = jnp.sum(one_hot * earlier, axis=0, keepdims=True)
        used = used + jnp.sum(one_hot, axis=1, keepdims=True)
        result.append((owner, rank))
    return result


def ask_kernel(blocks, spots, request, blocks_in, spots_in, sems):
    copies = [
        pltpu.make_async_copy(blocks, blocks_in, sems.at[0]),
        pltpu.make_async_copy(spots, spots_in, sems.at[1]),
    ]
    for copy in copies:
        copy.start()
    for copy in copies:
        copy.wait()
    count, columns = request.shape[0], blocks.shape[1]
    place = iota((128, columns), 0)
    field = place // SLOTS
    slot = jnp.where(field < FIELDS, place - field * SLOTS, -1)
    here = iota((128, columns), 1)
    marks = ((slot == MOST) & (here == 0)) | ((slot == MOST + 1) & (here == columns - 1))
    asked = jnp.zeros(request.shape, f32)
    for k, (owner, rank) in enumerate(ranks(blocks_in, count)):
        filled = jnp.where((slot == rank.astype(i32)) | marks, 1.0, 0.0).astype(bf16)
        named = jnp.where(owner, spots_in[k : k + 1, :].astype(f32), 0.0).astype(bf16)
        asked = asked + lax.dot_general(
            named, filled, (((1,), (1,)), ((), ())), preferred_element_type=f32
        )
    request[...] = asked.astype(i32) + (iota(request.shape, 1) // SLOTS) * columns


def pack_kernel(
    section, state, bath, fields, blocks, weights,
    to_left, to_right, table,
    low, high, surface, bath_in, fields_in, blocks_in, extra, sems,
):
    tracers, levels, columns, lanes = state.shape
    slots = blocks.shape[0]
    many = tracers * levels
    wide = to_left.shape[0] - 2 * many - EXTRA
    below = pl.ds(2 * many + EXTRA, wide)
    pairs = [
        (state.at[:, :, pl.ds(0, 8)], low),
        (state.at[:, :, pl.ds(columns - 8, 8)], high),
        (blocks, blocks_in),
        (bath, bath_in),
        (fields, fields_in),
        (state.at[:, 0], surface),
        (weights.at[pl.ds(0, wide)], to_left.at[below]),
        (weights.at[pl.ds((columns - 1) * wide, wide)], to_right.at[below]),
    ]
    copies = [pltpu.make_async_copy(src, dst, sems.at[n]) for n, (src, dst) in enumerate(pairs)]
    for copy in copies:
        copy.start()
    for copy in copies[2:6]:
        copy.wait()
    for out, first, at in ((to_left, 0, 0), (to_right, columns - 2, columns - 1)):
        extra[...] = jnp.zeros_like(extra)
        extra[0:2] = bath_in[first : first + 2].astype(f32)
        for f in range(3):
            extra[2 + f : 3 + f] = fields_in[f].astype(f32)[at : at + 1]
        extra[8 : 8 + slots] = jnp.broadcast_to(
            blocks_in[:, at : at + 1].astype(f32), (slots, lanes)
        )
        out[pl.ds(2 * many, EXTRA)] = extra[...].astype(bf16)
    on_ocean = section[0] == 1
    for f in range(3):
        own = fields_in[f]
        if f < 2:
            own = jnp.where(on_ocean, surface[f], own.astype(f32)).astype(bf16)
        table[f * columns : (f + 1) * columns, :] = own
    copies[0].wait()
    copies[1].wait()
    for c in range(2):
        for n in range(tracers):
            part = pl.ds(c * many + n * levels, levels)
            tiles = low.at[n].reshape(levels * 8, lanes)
            to_left[part] = tiles[pl.ds(c, levels, stride=8), :].astype(bf16)
            tiles = high.at[n].reshape(levels * 8, lanes)
            to_right[part] = tiles[pl.ds(6 + c, levels, stride=8), :].astype(bf16)
    copies[6].wait()
    copies[7].wait()


def serve_kernel(asked, table, from_left, from_right, out):
    count = asked.shape[0]
    wanted = jnp.transpose(asked[...].astype(f32))[:PIECE]
    height = table.shape[0]
    slot = lax.rem(iota((PIECE, 1), 0), SLOTS)
    parts = []
    for e in range(count):
        after, before = (e + 1) % count, (e - 1) % count
        spot = jnp.where(
            slot == MOST,
            wanted[:, after : after + 1],
            jnp.where(slot == MOST + 1, wanted[:, before : before + 1], wanted[:, e : e + 1]),
        )
        parts.append(jnp.where(iota((PIECE, height), 1) == spot.astype(i32), 1.0, 0.0))
    chosen = jnp.concatenate(parts, axis=0).astype(bf16)
    out[...] = jnp.dot(chosen, table[...], preferred_element_type=f32).astype(bf16)


def start_kernel(
    state, from_left, from_right, bath, blocks,
    q_result, side_result, bath_result, place_result,
    q_out, side_out, held, bath_out, halo, near, bath_in, blocks_in, place, ring, band,
    sems, sems_out, *, count,
):
    tracers, levels, columns, lanes = state.shape
    rows = columns + EDGE
    many = tracers * levels
    chunks = chunks_of(levels)
    copies = []
    for n, (low, size) in enumerate(chunks):
        copies.append(
            pltpu.make_async_copy(
                state.at[:, pl.ds(low, size)], held.at[:, pl.ds(low, size)], sems.at[n]
            )
        )
    bath_copy = pltpu.make_async_copy(bath, bath_in, sems.at[len(chunks)])
    blocks_copy = pltpu.make_async_copy(blocks, blocks_in, sems.at[len(chunks) + 1])
    blocks_copy.start()
    bath_copy.start()
    for copy in reversed(copies):
        copy.start()
    leaving = []

    def send(source, target, number):
        copy = pltpu.make_async_copy(source, target, sems_out.at[number])
        copy.start()
        leaving.append(copy)

    for c in range(2):
        part = pl.ds(c * many, many)
        halo[pl.ds(c, many, stride=8), :] = from_right[part].astype(f32)
        halo[pl.ds(EDGE - 2 + c, many, stride=8), :] = from_left[part].astype(f32)
    right = from_right[pl.ds(2 * many, EXTRA)].astype(f32)
    left = from_left[pl.ds(2 * many, EXTRA)].astype(f32)
    row = iota((EDGE, lanes), 0)
    edge = jnp.where(
        row == 0,
        right[0:1],
        jnp.where(
            row == 1,
            right[1:2],
            jnp.where(row == EDGE - 2, left[0:1], jnp.where(row == EDGE - 1, left[1:2], 0.0)),
        ),
    )
    bath_copy.wait()
    depth = jnp.concatenate([bath_in[...], edge.astype(i32)], axis=0)
    bath_out[...] = depth
    send(bath_out, bath_result, 2 * len(chunks))
    blocks_copy.wait()
    for k, (_, rank) in enumerate(ranks(blocks_in, count)):
        arrives = blocks_in[k : k + 1, :].astype(f32) * PIECE + rank
        spread = jnp.transpose(jnp.broadcast_to(arrives, (128, columns)))
        place[k * columns : (k + 1) * columns, :] = spread.astype(i32)
    send(place, place_result, 2 * len(chunks) + 1)
    lane = iota((rows, lanes), 1)
    a = pltpu.roll(depth, 1, 0)
    b = pltpu.roll(depth, rows - 1, 0)
    c = jnp.where(lane == 0, 0, pltpu.roll(depth, 1, 1))
    d = jnp.where(lane == lanes - 1, 0, pltpu.roll(depth, lanes - 1, 1))
    a, b = jnp.maximum(a, b), jnp.minimum(a, b)
    c, d = jnp.maximum(c, d), jnp.minimum(c, d)
    a, c = jnp.maximum(a, c), jnp.minimum(a, c)
    b, d = jnp.maximum(b, d), jnp.minimum(b, d)
    near[0], near[1], near[2], near[3] = a, jnp.maximum(b, c), jnp.minimum(b, c), d


    band[...] = band_matrix(lanes)

    def side(level, slot):
        wet = level < bath_out[...]
        own = 0.5 * SCALE
        for n in range(4):
            own = jnp.where(level < near[n], 0.5 * SCALE - (n + 1), own)
        side_out[level] = own[:columns].astype(bf16)
        starts, masked = [], []
        for n in range(tracers):
            spot = (n * levels + level) * 8
            if not isinstance(level, int):
                spot = pl.multiple_of(spot, 8)
            full = jnp.concatenate([held[n, level], halo[pl.ds(spot, 8), :]], axis=0)
            starts.append(full)
            masked.append(jnp.where(wet, full, 0.0))
        along = sums_along_lanes(masked, band)
        halves = []
        for n, h in enumerate(masked):
            across = sum_along_rows(h, columns, ring.at[slot, n], True)
            halves.append(own * h + (across + along[n]))
        return wet, starts, halves

    def deep(step, slot, below, top):
        level = top - step
        wet, starts, halves = side(level, slot)
        rho = ratio_at(bath_out[...], level)
        solved = []
        for n in range(tracers):
            q = rho * (halves[n] + below[n])
            q_out[n, level] = jnp.where(wet, q, starts[n])
            solved.append(q)
        return tuple(solved)

    carry = tuple(jnp.zeros((rows, lanes), f32) for _ in range(tracers))
    for n in reversed(range(len(chunks))):
        low, size = chunks[n]
        copies[n].wait()
        first = max(low, 2)
        top = low + size - 1
        carry = sweep(top - first + 1, functools.partial(deep, top=top), carry, UNROLL)
        if n == 0:
            for level in (1, 0):
                wet, starts, halves = side(level, level)
                for m in range(tracers):
                    q_out[m, level] = jnp.where(wet, halves[m], starts[m])
        part = pl.ds(low, size)
        send(q_out.at[:, part], q_result.at[:, part], 2 * n)
        send(side_out.at[part], side_result.at[part], 2 * n + 1)
    for copy in leaving:
        copy.wait()


def ratio_at(depth, level):
    height = depth - level
    power = jnp.exp2((2.0 * math.log2(FIXED)) * height.astype(f32))
    divisor = 1.0 + FIXED * power
    inverse = pl.reciprocal(divisor, approx=True)
    scaled = ((1.0 - FIXED * FIXED) * power) * inverse
    return jnp.where(height > 0, FIXED + scaled * (2.0 - divisor * inverse), 0.0)


def remap_kernel(
    columns_in, place_from, from_left, from_right, weights, own_fields,
    out, picked, solved, held, fields_in, place, sems,
):
    fields, rows, width = out.shape[0] // 2, out.shape[1], out.shape[2]
    columns = rows - EDGE
    slots = weights.shape[0] // (columns * width)
    tall = slots * width
    many = from_left.shape[0] - tall - EXTRA
    group = 8
    place_copy = pltpu.make_async_copy(place_from, place, sems.at[0])
    fields_copy = pltpu.make_async_copy(own_fields, fields_in, sems.at[1])
    copies = []
    for n in range(columns // group):
        part = pl.ds(n * group * tall, group * tall)
        copies.append(pltpu.make_async_copy(weights.at[part], held.at[part], sems.at[2 + n]))
    for copy in [place_copy] + copies + [fields_copy]:
        copy.start()
    right = from_right[pl.ds(many, EXTRA)].astype(f32)
    left = from_left[pl.ds(many, EXTRA)].astype(f32)
    row = iota((EDGE, 1), 0)
    picked[...] = jnp.zeros_like(picked)
    place_copy.wait()
    wanted = []
    for k in range(slots):
        edge = jnp.where(
            row == 0,
            right[8 + k : 9 + k, 0:1] * PIECE + MOST,
            jnp.where(row == EDGE - 1, left[8 + k : 9 + k, 0:1] * PIECE + MOST + 1, -PIECE),
        ).astype(i32)
        wanted += [place[k * columns : (k + 1) * columns, 0:1], edge]
    wanted = jnp.concatenate(wanted, axis=0)
    spots = iota((slots * rows, columns_in.shape[0]), 1)
    for f in range(fields):
        chosen = jnp.where(spots == wanted + f * SLOTS, 1.0, 0.0).astype(bf16)
        found = jnp.dot(chosen, columns_in[...], preferred_element_type=f32)
        for k in range(slots):
            picked[k, pl.ds(f, rows, stride=8), :] = found[k * rows : (k + 1) * rows]

    def one(row, table_of):
        spot = pl.ds(row * 8, 8)
        vector = jnp.concatenate([picked[k, spot, :] for k in range(slots)], axis=1)
        matrix = jnp.concatenate([table_of(k) for k in range(slots)], axis=1)
        solved[spot, :] = lax.dot_general(
            vector.astype(bf16), matrix, (((1,), (1,)), ((), ())), preferred_element_type=f32
        )

    solved[...] = jnp.zeros_like(solved)
    below = many + EXTRA
    one(columns, lambda k: from_right[pl.ds(below + k * width, width)])
    one(rows - 1, lambda k: from_left[pl.ds(below + k * width, width)])
    for n in range(columns // group):
        copies[n].wait()
        for m in range(group):
            spot = n * group + m
            one(spot, lambda k: held[pl.ds((spot * slots + k) * width, width)])
    fields_copy.wait()
    for f in range(fields):
        out[f, pl.ds(0, columns)] = solved[pl.ds(f, columns, stride=8), :]
        out[f, pl.ds(columns, EDGE)] = solved[pl.ds(columns * 8 + f, EDGE, stride=8), :]
        out[fields + f, pl.ds(0, columns)] = fields_in[f].astype(f32)
        out[fields + f, pl.ds(columns, EDGE)] = edge_tile(
            right[2 + f : 3 + f], left[2 + f : 3 + f]
        )


def finish_kernel(
    section, mine, other, bath_from, q_from, side_from, surface, result,
    q, side, bath, padded, rho, solved, done, band, sems, sems_out,
):
    tracers, levels, columns, lanes = result.shape
    rows = columns + EDGE
    chunks = chunks_of(levels)
    bath_copy = pltpu.make_async_copy(bath_from, bath, sems.at[len(chunks), 0])
    bath_copy.start()
    arrivals = []
    for n, (low, size) in enumerate(chunks):
        part = pl.ds(low, size)
        arrivals.append(
            (
                pltpu.make_async_copy(q_from.at[:, part], q.at[:, part], sems.at[n, 0]),
                pltpu.make_async_copy(side_from.at[part], side.at[part], sems.at[n, 1]),
            )
        )
    for group in arrivals:
        for copy in group:
            copy.start()
    bath_copy.wait()
    for copy in arrivals[0]:
        copy.wait()
    on_ocean = section[0] == 1
    band[...] = band_matrix(lanes)
    flux = [jnp.where(on_ocean, other[f], mine[f]) for f in range(3)]
    own = [jnp.where(on_ocean, mine[3 + f], other[3 + f]) for f in range(3)]
    forcing = [flux[0] + own[0], flux[1] + own[1]]
    top_mix = TOP_MIX * (1.0 + flux[2] * flux[2] + own[2] * own[2])
    depth = bath[...]

    def top_levels(count, halves, below, rho_below, scale):
        wet = 1 < depth[:count]
        link = jnp.where(wet, top_mix[:count], 0.0)
        deeper = jnp.where(2 < depth[:count], DEEP_MIX - DEEP_MIX * rho_below, 0.0)
        second = 1.0 / (1.0 + link + deeper)
        rho_second = link * second
        first = 1.0 / (1.0 + link - link * rho_second)
        values = []
        for n in range(tracers):
            partial = 2.0 * (halves[n][1] + below[n]) * second
            source = 2.0 * halves[n][0] + scale * FLUX_GAIN * forcing[n][:count]
            surface_value = (source + link * partial) * first
            next_value = jnp.where(wet, partial, 0.0) + rho_second * surface_value
            values.append((surface_value, next_value))
        return values

    def put(level, values):
        for n, h in enumerate(values):
            padded[n, level, pl.ds(0, EDGE)] = h[columns:]
            padded[n, level, pl.ds(EDGE, columns)] = h[:columns]
            padded[n, level, pl.ds(EDGE + columns, EDGE)] = h[columns:]

    values = top_levels(
        rows,
        [(q[n, 0], q[n, 1]) for n in range(tracers)],
        [jnp.where(2 < depth, q[n, 2], 0.0) for n in range(tracers)],
        ratio_at(depth, 2),
        SCALE,
    )
    put(0, [jnp.where(0 < depth, values[n][0], 0.0) for n in range(tracers)])
    carry = tuple(values[n][1] for n in range(tracers))
    put(1, carry)

    def down(step, slot, carry, low):
        level = low + step
        ratio = ratio_at(bath[...], level)
        rho[level] = ratio[:columns]
        wet = level < bath[...]
        out = [jnp.where(wet, q[n, level], 0.0) + ratio * carry[n] for n in range(tracers)]
        put(level, out)
        return tuple(out)

    for n, (low, size) in enumerate(chunks):
        if n > 0:
            for copy in arrivals[n]:
                copy.wait()
        first = max(low, 2)
        carry = sweep(low + size - first, functools.partial(down, low=first), carry, UNROLL)

    def halves_at(level):
        middle = [padded[n, level, pl.ds(EDGE, columns)] for n in range(tracers)]
        along = sums_along_lanes(middle, band)
        own = side[level].astype(f32)
        out = []
        for n in range(tracers):
            across = padded[n, level, pl.ds(EDGE - 1, columns)]
            across = across + padded[n, level, pl.ds(EDGE + 1, columns)]
            out.append(own * middle[n] + (across + along[n]))
        return out

    def up(step, slot, carry):
        level = levels - 1 - step
        ratio = rho[level]
        halves = halves_at(level)
        out = [ratio * (halves[n] + carry[n]) for n in range(tracers)]
        for n in range(tracers):
            solved[n, level] = out[n]
        return tuple(out)

    zero = jnp.zeros((columns, lanes), f32)
    carry = sweep(levels - 2, up, (zero,) * tracers, 6)
    values = top_levels(columns, list(zip(halves_at(0), halves_at(1))), carry, rho[2], SCALE * SCALE)
    unscale = 1.0 / (SCALE * SCALE)
    for n in range(tracers):
        surface[n] = jnp.where(on_ocean, values[n][0] * unscale, other[n, pl.ds(0, columns)])
    surface[2] = jnp.where(on_ocean, top_mix[:columns], other[2, pl.ds(0, columns)])

    def last(step, slot, carry, low):
        level = low + step
        ratio = rho[level]
        wet = level < bath[pl.ds(0, columns)]
        out = []
        for n in range(tracers):
            h = solved[n, level] + ratio * carry[n]
            done[n, level] = jnp.where(wet, h * unscale, q[n, level, pl.ds(0, columns)])
            out.append(h)
        return tuple(out)

    wet = 1 < depth[:columns]
    for n in range(tracers):
        done[n, 0] = values[n][0] * unscale
        done[n, 1] = jnp.where(wet, values[n][1] * unscale, q[n, 1, pl.ds(0, columns)])
    carry = tuple(values[n][1] for n in range(tracers))
    leaving = []
    for n, (low, size) in enumerate(chunks):
        first = max(low, 2)
        carry = sweep(low + size - first, functools.partial(last, low=first), carry, 10)
        part = pl.ds(low, size)
        leaving.append(
            pltpu.make_async_copy(done.at[:, part], result.at[:, part], sems_out.at[n])
        )
        leaving[-1].start()
    for copy in leaving:
        copy.wait()


def shift(value, axis, by):
    count = lax.axis_size(axis)
    return lax.ppermute(value, axis, [(i, (i + by) % count) for i in range(count)])


def in_hbm(value):
    return pltpu.with_memory_space_constraint(value, pltpu.HBM)


def per_device(
    surface_fields, source_blocks, source_columns, remap_weights, ocean_state, bathymetry
):
    tracers, levels, columns, lanes = ocean_state.shape
    slots = source_blocks.shape[2]
    count = lax.axis_size("blk")
    rows = columns + EDGE
    section = lax.axis_index("sec").astype(i32).reshape(1)
    fields = surface_fields[0]
    blocks = jnp.transpose(source_blocks[0])
    spots = jnp.transpose(source_columns[0])
    weights = remap_weights[0].reshape(columns * slots * lanes, lanes)
    tall = slots * lanes
    many = tracers * levels

    hbm = pl.BlockSpec(memory_space=pltpu.HBM)
    vmem = pl.BlockSpec(memory_space=pltpu.VMEM)
    smem = pl.BlockSpec(memory_space=pltpu.SMEM)
    shaped = jax.ShapeDtypeStruct
    pieces = len(chunks_of(levels))
    cells = rows * lanes

    request = pl.pallas_call(
        ask_kernel,
        out_shape=shaped((count, 128), i32),
        in_specs=[hbm, hbm],
        out_specs=vmem,
        scratch_shapes=[
            pltpu.VMEM(blocks.shape, i32),
            pltpu.VMEM(spots.shape, i32),
            pltpu.SemaphoreType.DMA((2,)),
        ],
        compiler_params=pltpu.CompilerParams(vmem_limit_bytes=4 * MIB),
        cost_estimate=pl.CostEstimate(flops=10**6, bytes_accessed=10**5, transcendentals=0),
    )(in_hbm(blocks), in_hbm(spots))
    asked = lax.all_to_all(request, "blk", split_axis=0, concat_axis=0, tiled=True)

    payload = shaped((2 * many + EXTRA + tall, lanes), bf16)
    to_left, to_right, table = pl.pallas_call(
        pack_kernel,
        out_shape=(
            payload,
            payload,
            shaped((FIELDS * columns, lanes), bf16),
        ),
        in_specs=[smem] + [hbm] * 5,
        out_specs=(vmem, vmem, vmem),
        scratch_shapes=[
            pltpu.VMEM((tracers, levels, 8, lanes), f32),
            pltpu.VMEM((tracers, levels, 8, lanes), f32),
            pltpu.VMEM((tracers, columns, lanes), f32),
            pltpu.VMEM(bathymetry.shape, i32),
            pltpu.VMEM(fields.shape, bf16),
            pltpu.VMEM(blocks.shape, i32),
            pltpu.VMEM((EXTRA, lanes), f32),
            pltpu.SemaphoreType.DMA((8,)),
        ],
        compiler_params=pltpu.CompilerParams(vmem_limit_bytes=8 * MIB),
        cost_estimate=pl.CostEstimate(
            flops=10**6, bytes_accessed=4 * 10**6, transcendentals=0
        ),
    )(
        section,
        in_hbm(ocean_state),
        in_hbm(bathymetry),
        in_hbm(fields),
        in_hbm(blocks),
        in_hbm(weights),
    )
    from_left = shift(to_right, "blk", 1)
    from_right = shift(to_left, "blk", -1)

    served = pl.pallas_call(
        serve_kernel,
        out_shape=shaped((count * PIECE, lanes), bf16),
        in_specs=[vmem] * 4,
        out_specs=vmem,
        compiler_params=pltpu.CompilerParams(vmem_limit_bytes=8 * MIB),
        cost_estimate=pl.CostEstimate(
            flops=10**7, bytes_accessed=10**6, transcendentals=0
        ),
    )(asked, table, from_left, from_right)
    columns_in = lax.all_to_all(served, "blk", split_axis=0, concat_axis=0, tiled=True)

    q, side, bath, place = pl.pallas_call(
        functools.partial(start_kernel, count=count),
        out_shape=(
            pltpu.HBM((tracers, levels, rows, lanes), f32),
            pltpu.HBM((levels, columns, lanes), bf16),
            pltpu.HBM((rows, lanes), i32),
            pltpu.HBM((slots * columns, 128), i32),
        ),
        in_specs=[hbm, vmem, vmem, hbm, hbm],
        out_specs=(hbm,) * 4,
        scratch_shapes=[
            pltpu.VMEM((tracers, levels, rows, lanes), f32),
            pltpu.VMEM((levels, columns, lanes), bf16),
            pltpu.VMEM(ocean_state.shape, f32),
            pltpu.VMEM((rows, lanes), i32),
            pltpu.VMEM((many * 8, lanes), f32),
            pltpu.VMEM((4, rows, lanes), i32),
            pltpu.VMEM(bathymetry.shape, i32),
            pltpu.VMEM(blocks.shape, i32),
            pltpu.VMEM((slots * columns, 128), i32),
            pltpu.VMEM((UNROLL, tracers, columns + 3 * EDGE, lanes), f32),
            pltpu.VMEM((2 * lanes, lanes), bf16),
            pltpu.SemaphoreType.DMA((pieces + 2,)),
            pltpu.SemaphoreType.DMA((2 * pieces + 2,)),
        ],
        compiler_params=pltpu.CompilerParams(vmem_limit_bytes=28 * MIB),
        cost_estimate=pl.CostEstimate(
            flops=60 * levels * cells, bytes_accessed=200 * levels * cells, transcendentals=0
        ),
    )(
        in_hbm(ocean_state),
        from_left,
        from_right,
        in_hbm(bathymetry),
        in_hbm(blocks),
    )

    mine = pl.pallas_call(
        remap_kernel,
        out_shape=shaped((6, rows, lanes), f32),
        in_specs=[vmem, hbm, vmem, vmem, hbm, hbm],
        out_specs=vmem,
        scratch_shapes=[
            pltpu.VMEM((slots, rows * 8, lanes), f32),
            pltpu.VMEM((rows * 8, lanes), f32),
            pltpu.VMEM(weights.shape, bf16),
            pltpu.VMEM(fields.shape, bf16),
            pltpu.VMEM((slots * columns, 128), i32),
            pltpu.SemaphoreType.DMA((2 + columns // 8,)),
        ],
        compiler_params=pltpu.CompilerParams(vmem_limit_bytes=20 * MIB),
        cost_estimate=pl.CostEstimate(
            flops=16 * weights.size, bytes_accessed=2 * weights.size, transcendentals=0
        ),
    )(
        columns_in,
        in_hbm(place),
        from_left,
        from_right,
        in_hbm(weights),
        in_hbm(fields),
    )
    other = lax.ppermute(mine, "sec", [(0, 1), (1, 0)])

    surface, result = pl.pallas_call(
        finish_kernel,
        out_shape=(shaped((3, columns, lanes), f32), shaped(ocean_state.shape, f32)),
        in_specs=[smem] + [vmem] * 2 + [hbm] * 3,
        out_specs=(vmem, hbm),
        scratch_shapes=[
            pltpu.VMEM((tracers, levels, rows, lanes), f32),
            pltpu.VMEM((levels, columns, lanes), bf16),
            pltpu.VMEM((rows, lanes), i32),
            pltpu.VMEM((tracers, levels, columns + 2 * EDGE, lanes), f32),
            pltpu.VMEM((levels, columns, lanes), f32),
            pltpu.VMEM(ocean_state.shape, f32),
            pltpu.VMEM(ocean_state.shape, f32),
            pltpu.VMEM((2 * lanes, lanes), bf16),
            pltpu.SemaphoreType.DMA((pieces + 1, 2)),
            pltpu.SemaphoreType.DMA((pieces,)),
        ],
        compiler_params=pltpu.CompilerParams(vmem_limit_bytes=36 * MIB),
        cost_estimate=pl.CostEstimate(
            flops=60 * levels * cells, bytes_accessed=32 * levels * cells, transcendentals=0
        ),
    )(
        section,
        mine,
        other,
        in_hbm(bath),
        in_hbm(q),
        in_hbm(side),
    )
    return (surface[None], result)


def solution(mesh):
    return jax.shard_map(
        per_device,
        mesh=mesh,
        in_specs=(
            P("sec", None, "blk", None),
            P("sec", "blk", None),
            P("sec", "blk", None),
            P("sec", "blk", None, None, None),
            P(None, None, "blk", None),
            P("blk", None),
        ),
        out_specs=(P("sec", None, "blk", None), P(None, None, "blk", None)),
        check_vma=False,
    )
```

```python
import functools

import jax
import jax.numpy as jnp
import numpy as np
from jax import lax
from jax.experimental import pallas as pl
from jax.experimental.pallas import tpu as pltpu
from jax.sharding import PartitionSpec as P

FLUX_GAIN = 0.5
SIDE_MIX = 0.2
TOP_MIX = 1.0
DEEP_MIX = 2.0
SCALE = 1.0 / (0.5 * SIDE_MIX)

MOST = 16
SLOTS = MOST + 2
FIELDS = 3
PIECE = 56
EDGE = 8
EXTRA = 16
UNROLL = 5
MIB = 2**20
bf16, f32, i32 = jnp.bfloat16, jnp.float32, jnp.int32


def iota(shape, axis):
    return lax.broadcasted_iota(i32, shape, axis)


def adjacency(across, band, used):
    row, other = iota(across.shape, 0), iota(across.shape, 1)
    near = (row - other == 1) | (other - row == 1)
    near = near | ((row == 0) & (other == used - 1)) | ((row == used - 1) & (other == 0))
    across[...] = jnp.where(near & (row < used) & (other < used), 1.0, 0.0).astype(bf16)
    apart = iota(band.shape, 0) - iota(band.shape, 1)
    band[...] = jnp.where(jnp.abs(apart) == 1, 1.0, 0.0).astype(bf16)


def rounded(h):
    rows = -h.shape[0] % 16
    if rows:
        h = jnp.concatenate([h, jnp.zeros((rows, h.shape[1]), h.dtype)], axis=0)
    return h.astype(bf16)


def neighbour_sum(h, across, band, rows):
    tall, lanes = h.shape
    left = jnp.concatenate([across[pl.ds(0, rows), :], h[:rows]], axis=1)
    gap = jnp.zeros((across.shape[1] - tall, lanes), bf16)
    right = jnp.concatenate([h, gap, band[...]], axis=0)
    return jnp.dot(left, right, preferred_element_type=f32)


def edge_tile(right, left):
    row = iota((EDGE, right.shape[1]), 0)
    return jnp.where(row == 0, right, jnp.where(row == EDGE - 1, left, 0.0))


def chunks_of(levels):
    size = 10 if levels % 10 == 0 else levels
    return [(start, size) for start in range(0, levels, size)]


def sweep(count, body, carry, unroll):
    rounds = count // unroll

    def several(number, carry):
        for n in range(unroll):
            carry = body(number * unroll + n, n, carry)
        return carry

    carry = lax.fori_loop(0, rounds, several, carry)
    for step in range(rounds * unroll, count):
        carry = body(step, step - rounds * unroll, carry)
    return carry


def ranks(blocks, count):
    slots, columns = blocks.shape
    before = jnp.where(iota((columns, columns), 0) < iota((columns, columns), 1), 1.0, 0.0)
    before = before.astype(bf16)
    used = jnp.zeros((count, 1), f32)
    result = []
    for k in range(slots):
        owner = iota((count, columns), 0) == blocks[k : k + 1, :]
        one_hot = jnp.where(owner, 1.0, 0.0)
        earlier = used + jnp.dot(one_hot.astype(bf16), before, preferred_element_type=f32)
        rank = jnp.sum(one_hot * earlier, axis=0, keepdims=True)
        used = used + jnp.sum(one_hot, axis=1, keepdims=True)
        result.append((owner, rank))
    return result


def ask_kernel(blocks, spots, request, blocks_in, spots_in, sems):
    copies = [
        pltpu.make_async_copy(blocks, blocks_in, sems.at[0]),
        pltpu.make_async_copy(spots, spots_in, sems.at[1]),
    ]
    for copy in copies:
        copy.start()
    for copy in copies:
        copy.wait()
    count, columns = request.shape[0], blocks.shape[1]
    place = iota((128, columns), 0)
    field = place // SLOTS
    slot = jnp.where(field < FIELDS, place - field * SLOTS, -1)
    here = iota((128, columns), 1)
    marks = ((slot == MOST) & (here == 0)) | ((slot == MOST + 1) & (here == columns - 1))
    asked = jnp.zeros(request.shape, f32)
    for k, (owner, rank) in enumerate(ranks(blocks_in, count)):
        filled = jnp.where((slot == rank.astype(i32)) | marks, 1.0, 0.0).astype(bf16)
        named = jnp.where(owner, spots_in[k : k + 1, :].astype(f32), 0.0).astype(bf16)
        asked = asked + lax.dot_general(
            named, filled, (((1,), (1,)), ((), ())), preferred_element_type=f32
        )
    request[...] = asked.astype(i32) + (iota(request.shape, 1) // SLOTS) * columns


def pack_kernel(
    section, state, bath, fields, blocks, weights,
    to_left, to_right, table,
    low, high, surface, bath_in, fields_in, blocks_in, extra, sems,
):
    tracers, levels, columns, lanes = state.shape
    slots = blocks.shape[0]
    many = tracers * levels
    wide = to_left.shape[0] - 2 * many - EXTRA
    below = pl.ds(2 * many + EXTRA, wide)
    pairs = [
        (state.at[:, :, pl.ds(0, 8)], low),
        (state.at[:, :, pl.ds(columns - 8, 8)], high),
        (blocks, blocks_in),
        (bath, bath_in),
        (fields, fields_in),
        (state.at[:, 0], surface),
        (weights.at[pl.ds(0, wide)], to_left.at[below]),
        (weights.at[pl.ds((columns - 1) * wide, wide)], to_right.at[below]),
    ]
    copies = [pltpu.make_async_copy(src, dst, sems.at[n]) for n, (src, dst) in enumerate(pairs)]
    for copy in copies:
        copy.start()
    for copy in copies[2:6]:
        copy.wait()
    for out, first, at in ((to_left, 0, 0), (to_right, columns - 2, columns - 1)):
        extra[...] = jnp.zeros_like(extra)
        extra[0:2] = bath_in[first : first + 2].astype(f32)
        for f in range(3):
            extra[2 + f : 3 + f] = fields_in[f].astype(f32)[at : at + 1]
        extra[8 : 8 + slots] = jnp.broadcast_to(
            blocks_in[:, at : at + 1].astype(f32), (slots, lanes)
        )
        out[pl.ds(2 * many, EXTRA)] = extra[...].astype(bf16)
    on_ocean = section[0] == 1
    for f in range(3):
        own = fields_in[f]
        if f < 2:
            own = jnp.where(on_ocean, surface[f], own.astype(f32)).astype(bf16)
        table[f * columns : (f + 1) * columns, :] = own
    copies[0].wait()
    copies[1].wait()
    for c in range(2):
        for n in range(tracers):
            part = pl.ds(c * many + n * levels, levels)
            tiles = low.at[n].reshape(levels * 8, lanes)
            to_left[part] = tiles[pl.ds(c, levels, stride=8), :].astype(bf16)
            tiles = high.at[n].reshape(levels * 8, lanes)
            to_right[part] = tiles[pl.ds(6 + c, levels, stride=8), :].astype(bf16)
    copies[6].wait()
    copies[7].wait()


def serve_kernel(asked, table, from_left, from_right, out):
    count = asked.shape[0]
    wanted = jnp.transpose(asked[...].astype(f32))[:PIECE]
    height = table.shape[0]
    slot = lax.rem(iota((PIECE, 1), 0), SLOTS)
    parts = []
    for e in range(count):
        after, before = (e + 1) % count, (e - 1) % count
        spot = jnp.where(
            slot == MOST,
            wanted[:, after : after + 1],
            jnp.where(slot == MOST + 1, wanted[:, before : before + 1], wanted[:, e : e + 1]),
        )
        parts.append(jnp.where(iota((PIECE, height), 1) == spot.astype(i32), 1.0, 0.0))
    chosen = jnp.concatenate(parts, axis=0).astype(bf16)
    out[...] = jnp.dot(chosen, table[...], preferred_element_type=f32).astype(bf16)


def start_kernel(
    state, from_left, from_right, bath, blocks, ratios,
    q_result, side_result, bath_result, place_result,
    q_out, side_out, held, bath_out, halo, bath_in, blocks_in, place, across, band,
    sems, sems_out, *, count,
):
    tracers, levels, columns, lanes = state.shape
    rows = columns + EDGE
    many = tracers * levels
    chunks = chunks_of(levels)
    copies = []
    for n, (low, size) in enumerate(chunks):
        copies.append(
            pltpu.make_async_copy(
                state.at[:, pl.ds(low, size)], held.at[:, pl.ds(low, size)], sems.at[n]
            )
        )
    bath_copy = pltpu.make_async_copy(bath, bath_in, sems.at[len(chunks)])
    blocks_copy = pltpu.make_async_copy(blocks, blocks_in, sems.at[len(chunks) + 1])
    blocks_copy.start()
    bath_copy.start()
    for copy in reversed(copies):
        copy.start()
    leaving = []

    def send(source, target, number):
        copy = pltpu.make_async_copy(source, target, sems_out.at[number])
        copy.start()
        leaving.append(copy)

    halo[...] = jnp.zeros_like(halo)
    for c in range(2):
        part = pl.ds(c * many, many)
        halo[pl.ds(c, many, stride=8), :] = from_right[part].astype(f32)
        halo[pl.ds(EDGE - 2 + c, many, stride=8), :] = from_left[part].astype(f32)
    right = from_right[pl.ds(2 * many, EXTRA)].astype(f32)
    left = from_left[pl.ds(2 * many, EXTRA)].astype(f32)
    row = iota((EDGE, lanes), 0)
    edge = jnp.where(
        row == 0,
        right[0:1],
        jnp.where(
            row == 1,
            right[1:2],
            jnp.where(row == EDGE - 2, left[0:1], jnp.where(row == EDGE - 1, left[1:2], 0.0)),
        ),
    )
    bath_copy.wait()
    depth = jnp.concatenate([bath_in[...], edge.astype(i32)], axis=0)
    bath_out[...] = depth
    send(bath_out, bath_result, 2 * len(chunks))
    blocks_copy.wait()
    for k, (_, rank) in enumerate(ranks(blocks_in, count)):
        arrives = blocks_in[k : k + 1, :].astype(f32) * PIECE + rank
        spread = jnp.transpose(jnp.broadcast_to(arrives, (128, columns)))
        place[k * columns : (k + 1) * columns, :] = spread.astype(i32)
    send(place, place_result, 2 * len(chunks) + 1)
    adjacency(across, band, rows)

    def side(level):
        wet = level < bath_out[...]
        starts, masked = [], []
        for n in range(tracers):
            spot = (n * levels + level) * 8
            if not isinstance(level, int):
                spot = pl.multiple_of(spot, 8)
            full = jnp.concatenate([held[n, level], halo[pl.ds(spot, 8), :]], axis=0)
            starts.append(full)
            masked.append(jnp.where(wet, full, 0.0))
        tall = across.shape[0]
        count = neighbour_sum(rounded(jnp.where(wet, 1.0, 0.0)), across, band, tall)[:rows]
        own = 0.5 * SCALE - count
        side_out[level] = own[:columns].astype(bf16)
        halves = []
        for h in masked:
            halves.append(own * h + neighbour_sum(rounded(h), across, band, tall)[:rows])
        return wet, starts, halves

    def deep(step, slot, below, top):
        level = top - step
        wet, starts, halves = side(level)
        rho = ratio_at(ratios, bath_out[...], level)
        solved = []
        for n in range(tracers):
            q = rho * (halves[n] + below[n])
            q_out[n, level] = jnp.where(wet, q, starts[n])
            solved.append(q)
        return tuple(solved)

    carry = tuple(jnp.zeros((rows, lanes), f32) for _ in range(tracers))
    for n in reversed(range(len(chunks))):
        low, size = chunks[n]
        copies[n].wait()
        first = max(low, 2)
        top = low + size - 1
        carry = sweep(top - first + 1, functools.partial(deep, top=top), carry, UNROLL)
        if n == 0:
            for level in (1, 0):
                wet, starts, halves = side(level)
                for m in range(tracers):
                    q_out[m, level] = jnp.where(wet, halves[m], starts[m])
        part = pl.ds(low, size)
        send(q_out.at[:, part], q_result.at[:, part], 2 * n)
        send(side_out.at[part], side_result.at[part], 2 * n + 1)
    for copy in leaving:
        copy.wait()


def ratio_at(ratios, depth, level):
    lookup = jnp.broadcast_to(ratios[0:1], depth.shape)
    height = jnp.maximum(depth - level, 0)
    return jnp.take_along_axis(lookup, height, axis=1, mode="promise_in_bounds")


def ratios_by_height(levels, lanes):
    values = [0.0]
    ratio = DEEP_MIX / (1.0 + DEEP_MIX)
    for _ in range(levels):
        values.append(ratio)
        ratio = DEEP_MIX / (1.0 + DEEP_MIX + DEEP_MIX - DEEP_MIX * ratio)
    values += [0.0] * (lanes - len(values))
    return jnp.broadcast_to(jnp.asarray(np.array(values, np.float32)), (8, lanes))


def remap_kernel(
    columns_in, place_from, from_left, from_right, weights, own_fields,
    out, picked, solved, held, fields_in, place, sems,
):
    fields, rows, width = out.shape[0] // 2, out.shape[1], out.shape[2]
    columns = rows - EDGE
    slots = weights.shape[0] // (columns * width)
    tall = slots * width
    many = from_left.shape[0] - tall - EXTRA
    group = 8
    place_copy = pltpu.make_async_copy(place_from, place, sems.at[0])
    fields_copy = pltpu.make_async_copy(own_fields, fields_in, sems.at[1])
    copies = []
    for n in range(columns // group):
        part = pl.ds(n * group * tall, group * tall)
        copies.append(pltpu.make_async_copy(weights.at[part], held.at[part], sems.at[2 + n]))
    for copy in [place_copy] + copies + [fields_copy]:
        copy.start()
    right = from_right[pl.ds(many, EXTRA)].astype(f32)
    left = from_left[pl.ds(many, EXTRA)].astype(f32)
    row = iota((EDGE, 1), 0)
    picked[...] = jnp.zeros_like(picked)
    place_copy.wait()
    wanted = []
    for k in range(slots):
        edge = jnp.where(
            row == 0,
            right[8 + k : 9 + k, 0:1] * PIECE + MOST,
            jnp.where(row == EDGE - 1, left[8 + k : 9 + k, 0:1] * PIECE + MOST + 1, -PIECE),
        ).astype(i32)
        wanted += [place[k * columns : (k + 1) * columns, 0:1], edge]
    wanted = jnp.concatenate(wanted, axis=0)
    spots = iota((slots * rows, columns_in.shape[0]), 1)
    for f in range(fields):
        chosen = jnp.where(spots == wanted + f * SLOTS, 1.0, 0.0).astype(bf16)
        found = jnp.dot(chosen, columns_in[...], preferred_element_type=f32)
        for k in range(slots):
            picked[k, pl.ds(f, rows, stride=8), :] = found[k * rows : (k + 1) * rows]

    def one(row, table_of):
        spot = pl.ds(row * 8, 8)
        vector = jnp.concatenate([picked[k, spot, :] for k in range(slots)], axis=1)
        matrix = jnp.concatenate([table_of(k) for k in range(slots)], axis=1)
        solved[spot, :] = lax.dot_general(
            vector.astype(bf16), matrix, (((1,), (1,)), ((), ())), preferred_element_type=f32
        )

    solved[...] = jnp.zeros_like(solved)
    below = many + EXTRA
    one(columns, lambda k: from_right[pl.ds(below + k * width, width)])
    one(rows - 1, lambda k: from_left[pl.ds(below + k * width, width)])
    for n in range(columns // group):
        copies[n].wait()
        for m in range(group):
            spot = n * group + m
            one(spot, lambda k: held[pl.ds((spot * slots + k) * width, width)])
    fields_copy.wait()
    for f in range(fields):
        out[f, pl.ds(0, columns)] = solved[pl.ds(f, columns, stride=8), :]
        out[f, pl.ds(columns, EDGE)] = solved[pl.ds(columns * 8 + f, EDGE, stride=8), :]
        out[fields + f, pl.ds(0, columns)] = fields_in[f].astype(f32)
        out[fields + f, pl.ds(columns, EDGE)] = edge_tile(
            right[2 + f : 3 + f], left[2 + f : 3 + f]
        )


def finish_kernel(
    section, mine, other, bath_from, q_from, side_from, ratios, surface, result,
    q, side, bath, values_at, rounded_at, rho, solved, done, across, band, sems, sems_out,
):
    tracers, levels, columns, lanes = result.shape
    rows = columns + EDGE
    chunks = chunks_of(levels)
    bath_copy = pltpu.make_async_copy(bath_from, bath, sems.at[len(chunks), 0])
    bath_copy.start()
    arrivals = []
    for n, (low, size) in enumerate(chunks):
        part = pl.ds(low, size)
        arrivals.append(
            (
                pltpu.make_async_copy(q_from.at[:, part], q.at[:, part], sems.at[n, 0]),
                pltpu.make_async_copy(side_from.at[part], side.at[part], sems.at[n, 1]),
            )
        )
    for group in arrivals:
        for copy in group:
            copy.start()
    bath_copy.wait()
    for copy in arrivals[0]:
        copy.wait()
    on_ocean = section[0] == 1
    adjacency(across, band, rows)
    flux = [jnp.where(on_ocean, other[f], mine[f]) for f in range(3)]
    own = [jnp.where(on_ocean, mine[3 + f], other[3 + f]) for f in range(3)]
    forcing = [flux[0] + own[0], flux[1] + own[1]]
    top_mix = TOP_MIX * (1.0 + flux[2] * flux[2] + own[2] * own[2])
    depth = bath[...]

    def top_levels(count, halves, below, rho_below, scale):
        wet = 1 < depth[:count]
        link = jnp.where(wet, top_mix[:count], 0.0)
        deeper = jnp.where(2 < depth[:count], DEEP_MIX - DEEP_MIX * rho_below, 0.0)
        second = 1.0 / (1.0 + link + deeper)
        rho_second = link * second
        first = 1.0 / (1.0 + link - link * rho_second)
        values = []
        for n in range(tracers):
            partial = 2.0 * (halves[n][1] + below[n]) * second
            source = 2.0 * halves[n][0] + scale * FLUX_GAIN * forcing[n][:count]
            surface_value = (source + link * partial) * first
            next_value = jnp.where(wet, partial, 0.0) + rho_second * surface_value
            values.append((surface_value, next_value))
        return values

    def put(level, values):
        for n, h in enumerate(values):
            values_at[n, level] = h[:columns]
            rounded_at[n, level] = rounded(h)

    values = top_levels(
        rows,
        [(q[n, 0], q[n, 1]) for n in range(tracers)],
        [jnp.where(2 < depth, q[n, 2], 0.0) for n in range(tracers)],
        ratio_at(ratios, depth, 2),
        SCALE,
    )
    put(0, [jnp.where(0 < depth, values[n][0], 0.0) for n in range(tracers)])
    carry = tuple(values[n][1] for n in range(tracers))
    put(1, carry)

    def down(step, slot, carry, low):
        level = low + step
        ratio = ratio_at(ratios, bath[...], level)
        rho[level] = ratio[:columns]
        wet = level < bath[...]
        out = [jnp.where(wet, q[n, level], 0.0) + ratio * carry[n] for n in range(tracers)]
        put(level, out)
        return tuple(out)

    for n, (low, size) in enumerate(chunks):
        if n > 0:
            for copy in arrivals[n]:
                copy.wait()
        first = max(low, 2)
        carry = sweep(low + size - first, functools.partial(down, low=first), carry, UNROLL)

    def halves_at(level):
        own = side[level].astype(f32)
        out = []
        for n in range(tracers):
            around = neighbour_sum(rounded_at[n, level], across, band, columns)
            out.append(own * values_at[n, level] + around)
        return out

    def up(step, slot, carry):
        level = levels - 1 - step
        ratio = rho[level]
        halves = halves_at(level)
        out = [ratio * (halves[n] + carry[n]) for n in range(tracers)]
        for n in range(tracers):
            solved[n, level] = out[n]
        return tuple(out)

    zero = jnp.zeros((columns, lanes), f32)
    carry = sweep(levels - 2, up, (zero,) * tracers, 6)
    values = top_levels(columns, list(zip(halves_at(0), halves_at(1))), carry, rho[2], SCALE * SCALE)
    unscale = 1.0 / (SCALE * SCALE)
    for n in range(tracers):
        surface[n] = jnp.where(on_ocean, values[n][0] * unscale, other[n, pl.ds(0, columns)])
    surface[2] = jnp.where(on_ocean, top_mix[:columns], other[2, pl.ds(0, columns)])

    def last(step, slot, carry, low):
        level = low + step
        ratio = rho[level]
        wet = level < bath[pl.ds(0, columns)]
        out = []
        for n in range(tracers):
            h = solved[n, level] + ratio * carry[n]
            done[n, level] = jnp.where(wet, h * unscale, q[n, level, pl.ds(0, columns)])
            out.append(h)
        return tuple(out)

    wet = 1 < depth[:columns]
    for n in range(tracers):
        done[n, 0] = values[n][0] * unscale
        done[n, 1] = jnp.where(wet, values[n][1] * unscale, q[n, 1, pl.ds(0, columns)])
    carry = tuple(values[n][1] for n in range(tracers))
    leaving = []
    for n, (low, size) in enumerate(chunks):
        first = max(low, 2)
        carry = sweep(low + size - first, functools.partial(last, low=first), carry, 10)
        part = pl.ds(low, size)
        leaving.append(
            pltpu.make_async_copy(done.at[:, part], result.at[:, part], sems_out.at[n])
        )
        leaving[-1].start()
    for copy in leaving:
        copy.wait()


def shift(value, axis, by):
    count = lax.axis_size(axis)
    return lax.ppermute(value, axis, [(i, (i + by) % count) for i in range(count)])


def in_hbm(value):
    return pltpu.with_memory_space_constraint(value, pltpu.HBM)


def per_device(
    surface_fields, source_blocks, source_columns, remap_weights, ocean_state, bathymetry
):
    tracers, levels, columns, lanes = ocean_state.shape
    slots = source_blocks.shape[2]
    count = lax.axis_size("blk")
    rows = columns + EDGE
    section = lax.axis_index("sec").astype(i32).reshape(1)
    fields = surface_fields[0]
    blocks = jnp.transpose(source_blocks[0])
    spots = jnp.transpose(source_columns[0])
    weights = remap_weights[0].reshape(columns * slots * lanes, lanes)
    tall = slots * lanes
    many = tracers * levels

    hbm = pl.BlockSpec(memory_space=pltpu.HBM)
    vmem = pl.BlockSpec(memory_space=pltpu.VMEM)
    smem = pl.BlockSpec(memory_space=pltpu.SMEM)
    shaped = jax.ShapeDtypeStruct
    pieces = len(chunks_of(levels))
    cells = rows * lanes
    tall_rows = rows + -rows % 16

    request = pl.pallas_call(
        ask_kernel,
        out_shape=shaped((count, 128), i32),
        in_specs=[hbm, hbm],
        out_specs=vmem,
        scratch_shapes=[
            pltpu.VMEM(blocks.shape, i32),
            pltpu.VMEM(spots.shape, i32),
            pltpu.SemaphoreType.DMA((2,)),
        ],
        compiler_params=pltpu.CompilerParams(vmem_limit_bytes=4 * MIB),
        cost_estimate=pl.CostEstimate(flops=10**6, bytes_accessed=10**5, transcendentals=0),
    )(in_hbm(blocks), in_hbm(spots))
    asked = lax.all_to_all(request, "blk", split_axis=0, concat_axis=0, tiled=True)

    payload = shaped((2 * many + EXTRA + tall, lanes), bf16)
    to_left, to_right, table = pl.pallas_call(
        pack_kernel,
        out_shape=(
            payload,
            payload,
            shaped((FIELDS * columns, lanes), bf16),
        ),
        in_specs=[smem] + [hbm] * 5,
        out_specs=(vmem, vmem, vmem),
        scratch_shapes=[
            pltpu.VMEM((tracers, levels, 8, lanes), f32),
            pltpu.VMEM((tracers, levels, 8, lanes), f32),
            pltpu.VMEM((tracers, columns, lanes), f32),
            pltpu.VMEM(bathymetry.shape, i32),
            pltpu.VMEM(fields.shape, bf16),
            pltpu.VMEM(blocks.shape, i32),
            pltpu.VMEM((EXTRA, lanes), f32),
            pltpu.SemaphoreType.DMA((8,)),
        ],
        compiler_params=pltpu.CompilerParams(vmem_limit_bytes=8 * MIB),
        cost_estimate=pl.CostEstimate(
            flops=10**6, bytes_accessed=4 * 10**6, transcendentals=0
        ),
    )(
        section,
        in_hbm(ocean_state),
        in_hbm(bathymetry),
        in_hbm(fields),
        in_hbm(blocks),
        in_hbm(weights),
    )
    from_left = shift(to_right, "blk", 1)
    from_right = shift(to_left, "blk", -1)

    served = pl.pallas_call(
        serve_kernel,
        out_shape=shaped((count * PIECE, lanes), bf16),
        in_specs=[vmem] * 4,
        out_specs=vmem,
        compiler_params=pltpu.CompilerParams(vmem_limit_bytes=8 * MIB),
        cost_estimate=pl.CostEstimate(
            flops=10**7, bytes_accessed=10**6, transcendentals=0
        ),
    )(asked, table, from_left, from_right)
    columns_in = lax.all_to_all(served, "blk", split_axis=0, concat_axis=0, tiled=True)

    ratios = ratios_by_height(levels, lanes)
    q, side, bath, place = pl.pallas_call(
        functools.partial(start_kernel, count=count),
        out_shape=(
            pltpu.HBM((tracers, levels, rows, lanes), f32),
            pltpu.HBM((levels, columns, lanes), bf16),
            pltpu.HBM((rows, lanes), i32),
            pltpu.HBM((slots * columns, 128), i32),
        ),
        in_specs=[hbm, vmem, vmem, hbm, hbm, vmem],
        out_specs=(hbm,) * 4,
        scratch_shapes=[
            pltpu.VMEM((tracers, levels, rows, lanes), f32),
            pltpu.VMEM((levels, columns, lanes), bf16),
            pltpu.VMEM(ocean_state.shape, f32),
            pltpu.VMEM((rows, lanes), i32),
            pltpu.VMEM((many * 8, lanes), f32),
            pltpu.VMEM(bathymetry.shape, i32),
            pltpu.VMEM(blocks.shape, i32),
            pltpu.VMEM((slots * columns, 128), i32),
            pltpu.VMEM((tall_rows, lanes), bf16),
            pltpu.VMEM((lanes, lanes), bf16),
            pltpu.SemaphoreType.DMA((pieces + 2,)),
            pltpu.SemaphoreType.DMA((2 * pieces + 2,)),
        ],
        compiler_params=pltpu.CompilerParams(vmem_limit_bytes=28 * MIB),
        cost_estimate=pl.CostEstimate(
            flops=60 * levels * cells, bytes_accessed=200 * levels * cells, transcendentals=0
        ),
    )(
        in_hbm(ocean_state),
        from_left,
        from_right,
        in_hbm(bathymetry),
        in_hbm(blocks),
        ratios,
    )

    mine = pl.pallas_call(
        remap_kernel,
        out_shape=shaped((6, rows, lanes), f32),
        in_specs=[vmem, hbm, vmem, vmem, hbm, hbm],
        out_specs=vmem,
        scratch_shapes=[
            pltpu.VMEM((slots, rows * 8, lanes), f32),
            pltpu.VMEM((rows * 8, lanes), f32),
            pltpu.VMEM(weights.shape, bf16),
            pltpu.VMEM(fields.shape, bf16),
            pltpu.VMEM((slots * columns, 128), i32),
            pltpu.SemaphoreType.DMA((2 + columns // 8,)),
        ],
        compiler_params=pltpu.CompilerParams(vmem_limit_bytes=20 * MIB),
        cost_estimate=pl.CostEstimate(
            flops=16 * weights.size, bytes_accessed=2 * weights.size, transcendentals=0
        ),
    )(
        columns_in,
        in_hbm(place),
        from_left,
        from_right,
        in_hbm(weights),
        in_hbm(fields),
    )
    other = lax.ppermute(mine, "sec", [(0, 1), (1, 0)])

    surface, result = pl.pallas_call(
        finish_kernel,
        out_shape=(shaped((3, columns, lanes), f32), shaped(ocean_state.shape, f32)),
        in_specs=[smem] + [vmem] * 2 + [hbm] * 3 + [vmem],
        out_specs=(vmem, hbm),
        scratch_shapes=[
            pltpu.VMEM((tracers, levels, rows, lanes), f32),
            pltpu.VMEM((levels, columns, lanes), bf16),
            pltpu.VMEM((rows, lanes), i32),
            pltpu.VMEM(ocean_state.shape, f32),
            pltpu.VMEM((tracers, levels, tall_rows, lanes), bf16),
            pltpu.VMEM((levels, columns, lanes), f32),
            pltpu.VMEM(ocean_state.shape, f32),
            pltpu.VMEM(ocean_state.shape, f32),
            pltpu.VMEM((tall_rows, lanes), bf16),
            pltpu.VMEM((lanes, lanes), bf16),
            pltpu.SemaphoreType.DMA((pieces + 1, 2)),
            pltpu.SemaphoreType.DMA((pieces,)),
        ],
        compiler_params=pltpu.CompilerParams(vmem_limit_bytes=36 * MIB),
        cost_estimate=pl.CostEstimate(
            flops=60 * levels * cells, bytes_accessed=32 * levels * cells, transcendentals=0
        ),
    )(
        section,
        mine,
        other,
        in_hbm(bath),
        in_hbm(q),
        in_hbm(side),
        ratios,
    )
    return (surface[None], result)


def solution(mesh):
    return jax.shard_map(
        per_device,
        mesh=mesh,
        in_specs=(
            P("sec", None, "blk", None),
            P("sec", "blk", None),
            P("sec", "blk", None),
            P("sec", "blk", None, None, None),
            P(None, None, "blk", None),
            P("blk", None),
        ),
        out_specs=(P("sec", None, "blk", None), P(None, None, "blk", None)),
        check_vma=False,
    )
```

```python
import functools

import jax
import jax.numpy as jnp
import numpy as np
from jax import lax
from jax.experimental import pallas as pl
from jax.experimental.pallas import tpu as pltpu
from jax.sharding import PartitionSpec as P

FLUX_GAIN = 0.5
SIDE_MIX = 0.2
TOP_MIX = 1.0
DEEP_MIX = 2.0
SCALE = 1.0 / (0.5 * SIDE_MIX)

MOST = 16
SLOTS = MOST + 2
FIELDS = 3
PIECE = 56
EDGE = 8
EXTRA = 16
MIB = 2**20
bf16, f32, i32 = jnp.bfloat16, jnp.float32, jnp.int32


def iota(shape, axis):
    return lax.broadcasted_iota(i32, shape, axis)


def adjacency(across, band, used):
    row, other = iota(across.shape, 0), iota(across.shape, 1)
    near = (row - other == 1) | (other - row == 1)
    near = near | ((row == 0) & (other == used - 1)) | ((row == used - 1) & (other == 0))
    across[...] = jnp.where(near & (row < used) & (other < used), 1.0, 0.0).astype(bf16)
    apart = iota(band.shape, 0) - iota(band.shape, 1)
    band[...] = jnp.where(jnp.abs(apart) == 1, 1.0, 0.0).astype(bf16)


def rounded(h):
    rows = -h.shape[0] % 16
    if rows:
        h = jnp.concatenate([h, jnp.zeros((rows, h.shape[1]), h.dtype)], axis=0)
    return h.astype(bf16)


def neighbour_sum(h, across, band, rows):
    tall, lanes = h.shape
    left = jnp.concatenate([across[pl.ds(0, rows), :], h[:rows]], axis=1)
    gap = jnp.zeros((across.shape[1] - tall, lanes), bf16)
    right = jnp.concatenate([h, gap, band[...]], axis=0)
    return jnp.dot(left, right, preferred_element_type=f32)


def edge_tile(right, left):
    row = iota((EDGE, right.shape[1]), 0)
    return jnp.where(row == 0, right, jnp.where(row == EDGE - 1, left, 0.0))


def chunks_of(levels):
    size = 10 if levels % 10 == 0 else levels
    return [(start, size) for start in range(0, levels, size)]


def sweep(count, body, carry):
    for step in range(count):
        carry = body(step, carry)
    return carry


def ranks(blocks, count):
    slots, columns = blocks.shape
    before = jnp.where(iota((columns, columns), 0) < iota((columns, columns), 1), 1.0, 0.0)
    before = before.astype(bf16)
    used = jnp.zeros((count, 1), f32)
    result = []
    for k in range(slots):
        owner = iota((count, columns), 0) == blocks[k : k + 1, :]
        one_hot = jnp.where(owner, 1.0, 0.0)
        earlier = used + jnp.dot(one_hot.astype(bf16), before, preferred_element_type=f32)
        rank = jnp.sum(one_hot * earlier, axis=0, keepdims=True)
        used = used + jnp.sum(one_hot, axis=1, keepdims=True)
        result.append((owner, rank))
    return result


def ask_kernel(blocks, spots, request, blocks_in, spots_in, sems):
    copies = [
        pltpu.make_async_copy(blocks, blocks_in, sems.at[0]),
        pltpu.make_async_copy(spots, spots_in, sems.at[1]),
    ]
    for copy in copies:
        copy.start()
    for copy in copies:
        copy.wait()
    count, columns = request.shape[0], blocks.shape[1]
    place = iota((128, columns), 0)
    field = place // SLOTS
    slot = jnp.where(field < FIELDS, place - field * SLOTS, -1)
    here = iota((128, columns), 1)
    marks = ((slot == MOST) & (here == 0)) | ((slot == MOST + 1) & (here == columns - 1))
    asked = jnp.zeros(request.shape, f32)
    for k, (owner, rank) in enumerate(ranks(blocks_in, count)):
        filled = jnp.where((slot == rank.astype(i32)) | marks, 1.0, 0.0).astype(bf16)
        named = jnp.where(owner, spots_in[k : k + 1, :].astype(f32), 0.0).astype(bf16)
        asked = asked + lax.dot_general(
            named, filled, (((1,), (1,)), ((), ())), preferred_element_type=f32
        )
    request[...] = asked.astype(i32) + (iota(request.shape, 1) // SLOTS) * columns


def pack_kernel(
    section, state, bath, fields, blocks, weights,
    to_left, to_right, table,
    low, high, surface, bath_in, fields_in, blocks_in, extra, sems,
):
    tracers, levels, columns, lanes = state.shape
    slots = blocks.shape[0]
    many = tracers * levels
    wide = to_left.shape[0] - 2 * many - EXTRA
    below = pl.ds(2 * many + EXTRA, wide)
    pairs = [
        (state.at[:, :, pl.ds(0, 8)], low),
        (state.at[:, :, pl.ds(columns - 8, 8)], high),
        (blocks, blocks_in),
        (bath, bath_in),
        (fields, fields_in),
        (state.at[:, 0], surface),
        (weights.at[pl.ds(0, wide)], to_left.at[below]),
        (weights.at[pl.ds((columns - 1) * wide, wide)], to_right.at[below]),
    ]
    copies = [pltpu.make_async_copy(src, dst, sems.at[n]) for n, (src, dst) in enumerate(pairs)]
    for copy in copies:
        copy.start()
    for copy in copies[2:6]:
        copy.wait()
    for out, first, at in ((to_left, 0, 0), (to_right, columns - 2, columns - 1)):
        extra[...] = jnp.zeros_like(extra)
        extra[0:2] = bath_in[first : first + 2].astype(f32)
        for f in range(3):
            extra[2 + f : 3 + f] = fields_in[f].astype(f32)[at : at + 1]
        extra[8 : 8 + slots] = jnp.broadcast_to(
            blocks_in[:, at : at + 1].astype(f32), (slots, lanes)
        )
        out[pl.ds(2 * many, EXTRA)] = extra[...].astype(bf16)
    on_ocean = section[0] == 1
    for f in range(3):
        own = fields_in[f]
        if f < 2:
            own = jnp.where(on_ocean, surface[f], own.astype(f32)).astype(bf16)
        table[f * columns : (f + 1) * columns, :] = own
    copies[0].wait()
    copies[1].wait()
    for c in range(2):
        for n in range(tracers):
            part = pl.ds(c * many + n * levels, levels)
            tiles = low.at[n].reshape(levels * 8, lanes)
            to_left[part] = tiles[pl.ds(c, levels, stride=8), :].astype(bf16)
            tiles = high.at[n].reshape(levels * 8, lanes)
            to_right[part] = tiles[pl.ds(6 + c, levels, stride=8), :].astype(bf16)
    copies[6].wait()
    copies[7].wait()


def serve_kernel(asked, table, from_left, from_right, out):
    count = asked.shape[0]
    wanted = jnp.transpose(asked[...].astype(f32))[:PIECE]
    height = table.shape[0]
    slot = lax.rem(iota((PIECE, 1), 0), SLOTS)
    parts = []
    for e in range(count):
        after, before = (e + 1) % count, (e - 1) % count
        spot = jnp.where(
            slot == MOST,
            wanted[:, after : after + 1],
            jnp.where(slot == MOST + 1, wanted[:, before : before + 1], wanted[:, e : e + 1]),
        )
        parts.append(jnp.where(iota((PIECE, height), 1) == spot.astype(i32), 1.0, 0.0))
    chosen = jnp.concatenate(parts, axis=0).astype(bf16)
    out[...] = jnp.dot(chosen, table[...], preferred_element_type=f32).astype(bf16)


def start_kernel(
    state, from_left, from_right, bath, blocks, ratios,
    q_result, side_result, bath_result, place_result,
    q_out, side_out, held, bath_out, halo, bath_in, blocks_in, place, across, band,
    sems, sems_out, *, count,
):
    tracers, levels, columns, lanes = state.shape
    rows = columns + EDGE
    many = tracers * levels
    chunks = chunks_of(levels)
    copies = []
    for n, (low, size) in enumerate(chunks):
        copies.append(
            pltpu.make_async_copy(
                state.at[:, pl.ds(low, size)], held.at[:, pl.ds(low, size)], sems.at[n]
            )
        )
    bath_copy = pltpu.make_async_copy(bath, bath_in, sems.at[len(chunks)])
    blocks_copy = pltpu.make_async_copy(blocks, blocks_in, sems.at[len(chunks) + 1])
    blocks_copy.start()
    bath_copy.start()
    for copy in reversed(copies):
        copy.start()
    leaving = []

    def send(source, target, number):
        copy = pltpu.make_async_copy(source, target, sems_out.at[number])
        copy.start()
        leaving.append(copy)

    halo[...] = jnp.zeros_like(halo)
    for c in range(2):
        part = pl.ds(c * many, many)
        halo[pl.ds(c, many, stride=8), :] = from_right[part].astype(f32)
        halo[pl.ds(EDGE - 2 + c, many, stride=8), :] = from_left[part].astype(f32)
    right = from_right[pl.ds(2 * many, EXTRA)].astype(f32)
    left = from_left[pl.ds(2 * many, EXTRA)].astype(f32)
    row = iota((EDGE, lanes), 0)
    edge = jnp.where(
        row == 0,
        right[0:1],
        jnp.where(
            row == 1,
            right[1:2],
            jnp.where(row == EDGE - 2, left[0:1], jnp.where(row == EDGE - 1, left[1:2], 0.0)),
        ),
    )
    bath_copy.wait()
    depth = jnp.concatenate([bath_in[...], edge.astype(i32)], axis=0)
    bath_out[...] = depth
    send(bath_out, bath_result, 2 * len(chunks))
    blocks_copy.wait()
    for k, (_, rank) in enumerate(ranks(blocks_in, count)):
        arrives = blocks_in[k : k + 1, :].astype(f32) * PIECE + rank
        spread = jnp.transpose(jnp.broadcast_to(arrives, (128, columns)))
        place[k * columns : (k + 1) * columns, :] = spread.astype(i32)
    send(place, place_result, 2 * len(chunks) + 1)
    adjacency(across, band, rows)

    def side(level):
        wet = level < bath_out[...]
        starts, masked = [], []
        for n in range(tracers):
            spot = (n * levels + level) * 8
            full = jnp.concatenate([held[n, level], halo[pl.ds(spot, 8), :]], axis=0)
            starts.append(full)
            masked.append(jnp.where(wet, full, 0.0))
        tall = across.shape[0]
        count = neighbour_sum(rounded(jnp.where(wet, 1.0, 0.0)), across, band, tall)[:rows]
        own = 0.5 * SCALE - count
        side_out[level] = own[:columns].astype(bf16)
        halves = []
        for h in masked:
            halves.append(own * h + neighbour_sum(rounded(h), across, band, tall)[:rows])
        return wet, starts, halves

    def deep(step, below, top):
        level = top - step
        wet, starts, halves = side(level)
        rho = ratio_at(ratios, bath_out[...], level)
        solved = []
        for n in range(tracers):
            q = rho * (halves[n] + below[n])
            q_out[n, level] = jnp.where(wet, q, starts[n])
            solved.append(q)
        return tuple(solved)

    carry = tuple(jnp.zeros((rows, lanes), f32) for _ in range(tracers))
    for n in reversed(range(len(chunks))):
        low, size = chunks[n]
        copies[n].wait()
        first = max(low, 2)
        top = low + size - 1
        carry = sweep(top - first + 1, functools.partial(deep, top=top), carry)
        if n == 0:
            for level in (1, 0):
                wet, starts, halves = side(level)
                for m in range(tracers):
                    q_out[m, level] = jnp.where(wet, halves[m], starts[m])
        part = pl.ds(low, size)
        send(q_out.at[:, part], q_result.at[:, part], 2 * n)
        send(side_out.at[part], side_result.at[part], 2 * n + 1)
    for copy in leaving:
        copy.wait()


def ratio_at(ratios, depth, level):
    lookup = jnp.broadcast_to(ratios[0:1], depth.shape)
    height = jnp.maximum(depth - level, 0)
    return jnp.take_along_axis(lookup, height, axis=1, mode="promise_in_bounds")


def ratios_by_height(levels, lanes):
    values = [0.0]
    ratio = DEEP_MIX / (1.0 + DEEP_MIX)
    for _ in range(levels):
        values.append(ratio)
        ratio = DEEP_MIX / (1.0 + DEEP_MIX + DEEP_MIX - DEEP_MIX * ratio)
    values += [0.0] * (lanes - len(values))
    return jnp.broadcast_to(jnp.asarray(np.array(values, np.float32)), (8, lanes))


def remap_kernel(
    columns_in, place_from, from_left, from_right, weights, own_fields,
    out, picked, solved, held, fields_in, place, sems,
):
    fields, rows, width = out.shape[0] // 2, out.shape[1], out.shape[2]
    columns = rows - EDGE
    slots = weights.shape[0] // (columns * width)
    tall = slots * width
    many = from_left.shape[0] - tall - EXTRA
    group = 8
    place_copy = pltpu.make_async_copy(place_from, place, sems.at[0])
    fields_copy = pltpu.make_async_copy(own_fields, fields_in, sems.at[1])
    copies = []
    for n in range(columns // group):
        part = pl.ds(n * group * tall, group * tall)
        copies.append(pltpu.make_async_copy(weights.at[part], held.at[part], sems.at[2 + n]))
    for copy in [place_copy] + copies + [fields_copy]:
        copy.start()
    right = from_right[pl.ds(many, EXTRA)].astype(f32)
    left = from_left[pl.ds(many, EXTRA)].astype(f32)
    row = iota((EDGE, 1), 0)
    picked[...] = jnp.zeros_like(picked)
    place_copy.wait()
    wanted = []
    for k in range(slots):
        edge = jnp.where(
            row == 0,
            right[8 + k : 9 + k, 0:1] * PIECE + MOST,
            jnp.where(row == EDGE - 1, left[8 + k : 9 + k, 0:1] * PIECE + MOST + 1, -PIECE),
        ).astype(i32)
        wanted += [place[k * columns : (k + 1) * columns, 0:1], edge]
    wanted = jnp.concatenate(wanted, axis=0)
    spots = iota((slots * rows, columns_in.shape[0]), 1)
    for f in range(fields):
        chosen = jnp.where(spots == wanted + f * SLOTS, 1.0, 0.0).astype(bf16)
        found = jnp.dot(chosen, columns_in[...], preferred_element_type=f32)
        for k in range(slots):
            picked[k, pl.ds(f, rows, stride=8), :] = found[k * rows : (k + 1) * rows]

    def one(row, table_of):
        spot = pl.ds(row * 8, 8)
        vector = jnp.concatenate([picked[k, spot, :] for k in range(slots)], axis=1)
        matrix = jnp.concatenate([table_of(k) for k in range(slots)], axis=1)
        solved[spot, :] = lax.dot_general(
            vector.astype(bf16), matrix, (((1,), (1,)), ((), ())), preferred_element_type=f32
        )

    solved[...] = jnp.zeros_like(solved)
    below = many + EXTRA
    one(columns, lambda k: from_right[pl.ds(below + k * width, width)])
    one(rows - 1, lambda k: from_left[pl.ds(below + k * width, width)])
    for n in range(columns // group):
        copies[n].wait()
        for m in range(group):
            spot = n * group + m
            one(spot, lambda k: held[pl.ds((spot * slots + k) * width, width)])
    fields_copy.wait()
    for f in range(fields):
        out[f, pl.ds(0, columns)] = solved[pl.ds(f, columns, stride=8), :]
        out[f, pl.ds(columns, EDGE)] = solved[pl.ds(columns * 8 + f, EDGE, stride=8), :]
        out[fields + f, pl.ds(0, columns)] = fields_in[f].astype(f32)
        out[fields + f, pl.ds(columns, EDGE)] = edge_tile(
            right[2 + f : 3 + f], left[2 + f : 3 + f]
        )


def finish_kernel(
    section, mine, other, bath_from, q_from, side_from, ratios, surface, result,
    q, side, bath, values_at, rounded_at, rho, solved, done, across, band, sems, sems_out,
):
    tracers, levels, columns, lanes = result.shape
    rows = columns + EDGE
    chunks = chunks_of(levels)
    bath_copy = pltpu.make_async_copy(bath_from, bath, sems.at[len(chunks), 0])
    bath_copy.start()
    arrivals = []
    for n, (low, size) in enumerate(chunks):
        part = pl.ds(low, size)
        arrivals.append(
            (
                pltpu.make_async_copy(q_from.at[:, part], q.at[:, part], sems.at[n, 0]),
                pltpu.make_async_copy(side_from.at[part], side.at[part], sems.at[n, 1]),
            )
        )
    for group in arrivals:
        for copy in group:
            copy.start()
    bath_copy.wait()
    for copy in arrivals[0]:
        copy.wait()
    on_ocean = section[0] == 1
    adjacency(across, band, rows)
    flux = [jnp.where(on_ocean, other[f], mine[f]) for f in range(3)]
    own = [jnp.where(on_ocean, mine[3 + f], other[3 + f]) for f in range(3)]
    forcing = [flux[0] + own[0], flux[1] + own[1]]
    top_mix = TOP_MIX * (1.0 + flux[2] * flux[2] + own[2] * own[2])
    depth = bath[...]

    def top_levels(count, halves, below, rho_below, scale):
        wet = 1 < depth[:count]
        link = jnp.where(wet, top_mix[:count], 0.0)
        deeper = jnp.where(2 < depth[:count], DEEP_MIX - DEEP_MIX * rho_below, 0.0)
        second = 1.0 / (1.0 + link + deeper)
        rho_second = link * second
        first = 1.0 / (1.0 + link - link * rho_second)
        values = []
        for n in range(tracers):
            partial = 2.0 * (halves[n][1] + below[n]) * second
            source = 2.0 * halves[n][0] + scale * FLUX_GAIN * forcing[n][:count]
            surface_value = (source + link * partial) * first
            next_value = jnp.where(wet, partial, 0.0) + rho_second * surface_value
            values.append((surface_value, next_value))
        return values

    def put(level, values):
        for n, h in enumerate(values):
            values_at[n, level] = h[:columns]
            rounded_at[n, level] = rounded(h)

    values = top_levels(
        rows,
        [(q[n, 0], q[n, 1]) for n in range(tracers)],
        [jnp.where(2 < depth, q[n, 2], 0.0) for n in range(tracers)],
        ratio_at(ratios, depth, 2),
        SCALE,
    )
    put(0, [jnp.where(0 < depth, values[n][0], 0.0) for n in range(tracers)])
    carry = tuple(values[n][1] for n in range(tracers))
    put(1, carry)

    def down(step, carry, low):
        level = low + step
        ratio = ratio_at(ratios, bath[...], level)
        rho[level] = ratio[:columns]
        wet = level < bath[...]
        out = [jnp.where(wet, q[n, level], 0.0) + ratio * carry[n] for n in range(tracers)]
        put(level, out)
        return tuple(out)

    for n, (low, size) in enumerate(chunks):
        if n > 0:
            for copy in arrivals[n]:
                copy.wait()
        first = max(low, 2)
        carry = sweep(low + size - first, functools.partial(down, low=first), carry)

    def halves_at(level):
        own = side[level].astype(f32)
        out = []
        for n in range(tracers):
            around = neighbour_sum(rounded_at[n, level], across, band, columns)
            out.append(own * values_at[n, level] + around)
        return out

    def up(step, carry):
        level = levels - 1 - step
        ratio = rho[level]
        halves = halves_at(level)
        out = [ratio * (halves[n] + carry[n]) for n in range(tracers)]
        for n in range(tracers):
            solved[n, level] = out[n]
        return tuple(out)

    zero = jnp.zeros((columns, lanes), f32)
    carry = sweep(levels - 2, up, (zero,) * tracers)
    values = top_levels(columns, list(zip(halves_at(0), halves_at(1))), carry, rho[2], SCALE * SCALE)
    unscale = 1.0 / (SCALE * SCALE)
    for n in range(tracers):
        surface[n] = jnp.where(on_ocean, values[n][0] * unscale, other[n, pl.ds(0, columns)])
    surface[2] = jnp.where(on_ocean, top_mix[:columns], other[2, pl.ds(0, columns)])

    def last(step, carry, low):
        level = low + step
        ratio = rho[level]
        wet = level < bath[pl.ds(0, columns)]
        out = []
        for n in range(tracers):
            h = solved[n, level] + ratio * carry[n]
            done[n, level] = jnp.where(wet, h * unscale, q[n, level, pl.ds(0, columns)])
            out.append(h)
        return tuple(out)

    wet = 1 < depth[:columns]
    for n in range(tracers):
        done[n, 0] = values[n][0] * unscale
        done[n, 1] = jnp.where(wet, values[n][1] * unscale, q[n, 1, pl.ds(0, columns)])
    carry = tuple(values[n][1] for n in range(tracers))
    leaving = []
    for n, (low, size) in enumerate(chunks):
        first = max(low, 2)
        carry = sweep(low + size - first, functools.partial(last, low=first), carry)
        part = pl.ds(low, size)
        leaving.append(
            pltpu.make_async_copy(done.at[:, part], result.at[:, part], sems_out.at[n])
        )
        leaving[-1].start()
    for copy in leaving:
        copy.wait()


def shift(value, axis, by):
    count = lax.axis_size(axis)
    return lax.ppermute(value, axis, [(i, (i + by) % count) for i in range(count)])


def in_hbm(value):
    return pltpu.with_memory_space_constraint(value, pltpu.HBM)


def per_device(
    surface_fields, source_blocks, source_columns, remap_weights, ocean_state, bathymetry
):
    tracers, levels, columns, lanes = ocean_state.shape
    slots = source_blocks.shape[2]
    count = lax.axis_size("blk")
    rows = columns + EDGE
    section = lax.axis_index("sec").astype(i32).reshape(1)
    fields = surface_fields[0]
    blocks = jnp.transpose(source_blocks[0])
    spots = jnp.transpose(source_columns[0])
    weights = remap_weights[0].reshape(columns * slots * lanes, lanes)
    tall = slots * lanes
    many = tracers * levels

    hbm = pl.BlockSpec(memory_space=pltpu.HBM)
    vmem = pl.BlockSpec(memory_space=pltpu.VMEM)
    smem = pl.BlockSpec(memory_space=pltpu.SMEM)
    shaped = jax.ShapeDtypeStruct
    pieces = len(chunks_of(levels))
    cells = rows * lanes
    tall_rows = rows + -rows % 16

    request = pl.pallas_call(
        ask_kernel,
        out_shape=shaped((count, 128), i32),
        in_specs=[hbm, hbm],
        out_specs=vmem,
        scratch_shapes=[
            pltpu.VMEM(blocks.shape, i32),
            pltpu.VMEM(spots.shape, i32),
            pltpu.SemaphoreType.DMA((2,)),
        ],
        compiler_params=pltpu.CompilerParams(vmem_limit_bytes=4 * MIB),
        cost_estimate=pl.CostEstimate(flops=10**6, bytes_accessed=10**5, transcendentals=0),
    )(in_hbm(blocks), in_hbm(spots))
    asked = lax.all_to_all(request, "blk", split_axis=0, concat_axis=0, tiled=True)

    payload = shaped((2 * many + EXTRA + tall, lanes), bf16)
    to_left, to_right, table = pl.pallas_call(
        pack_kernel,
        out_shape=(
            payload,
            payload,
            shaped((FIELDS * columns, lanes), bf16),
        ),
        in_specs=[smem] + [hbm] * 5,
        out_specs=(vmem, vmem, vmem),
        scratch_shapes=[
            pltpu.VMEM((tracers, levels, 8, lanes), f32),
            pltpu.VMEM((tracers, levels, 8, lanes), f32),
            pltpu.VMEM((tracers, columns, lanes), f32),
            pltpu.VMEM(bathymetry.shape, i32),
            pltpu.VMEM(fields.shape, bf16),
            pltpu.VMEM(blocks.shape, i32),
            pltpu.VMEM((EXTRA, lanes), f32),
            pltpu.SemaphoreType.DMA((8,)),
        ],
        compiler_params=pltpu.CompilerParams(vmem_limit_bytes=8 * MIB),
        cost_estimate=pl.CostEstimate(
            flops=10**6, bytes_accessed=4 * 10**6, transcendentals=0
        ),
    )(
        section,
        in_hbm(ocean_state),
        in_hbm(bathymetry),
        in_hbm(fields),
        in_hbm(blocks),
        in_hbm(weights),
    )
    from_left = shift(to_right, "blk", 1)
    from_right = shift(to_left, "blk", -1)

    served = pl.pallas_call(
        serve_kernel,
        out_shape=shaped((count * PIECE, lanes), bf16),
        in_specs=[vmem] * 4,
        out_specs=vmem,
        compiler_params=pltpu.CompilerParams(vmem_limit_bytes=8 * MIB),
        cost_estimate=pl.CostEstimate(
            flops=10**7, bytes_accessed=10**6, transcendentals=0
        ),
    )(asked, table, from_left, from_right)
    columns_in = lax.all_to_all(served, "blk", split_axis=0, concat_axis=0, tiled=True)

    ratios = ratios_by_height(levels, lanes)
    q, side, bath, place = pl.pallas_call(
        functools.partial(start_kernel, count=count),
        out_shape=(
            pltpu.HBM((tracers, levels, rows, lanes), f32),
            pltpu.HBM((levels, columns, lanes), bf16),
            pltpu.HBM((rows, lanes), i32),
            pltpu.HBM((slots * columns, 128), i32),
        ),
        in_specs=[hbm, vmem, vmem, hbm, hbm, vmem],
        out_specs=(hbm,) * 4,
        scratch_shapes=[
            pltpu.VMEM((tracers, levels, rows, lanes), f32),
            pltpu.VMEM((levels, columns, lanes), bf16),
            pltpu.VMEM(ocean_state.shape, f32),
            pltpu.VMEM((rows, lanes), i32),
            pltpu.VMEM((many * 8, lanes), f32),
            pltpu.VMEM(bathymetry.shape, i32),
            pltpu.VMEM(blocks.shape, i32),
            pltpu.VMEM((slots * columns, 128), i32),
            pltpu.VMEM((tall_rows, lanes), bf16),
            pltpu.VMEM((lanes, lanes), bf16),
            pltpu.SemaphoreType.DMA((pieces + 2,)),
            pltpu.SemaphoreType.DMA((2 * pieces + 2,)),
        ],
        compiler_params=pltpu.CompilerParams(vmem_limit_bytes=28 * MIB),
        cost_estimate=pl.CostEstimate(
            flops=60 * levels * cells, bytes_accessed=200 * levels * cells, transcendentals=0
        ),
    )(
        in_hbm(ocean_state),
        from_left,
        from_right,
        in_hbm(bathymetry),
        in_hbm(blocks),
        ratios,
    )

    mine = pl.pallas_call(
        remap_kernel,
        out_shape=shaped((6, rows, lanes), f32),
        in_specs=[vmem, hbm, vmem, vmem, hbm, hbm],
        out_specs=vmem,
        scratch_shapes=[
            pltpu.VMEM((slots, rows * 8, lanes), f32),
            pltpu.VMEM((rows * 8, lanes), f32),
            pltpu.VMEM(weights.shape, bf16),
            pltpu.VMEM(fields.shape, bf16),
            pltpu.VMEM((slots * columns, 128), i32),
            pltpu.SemaphoreType.DMA((2 + columns // 8,)),
        ],
        compiler_params=pltpu.CompilerParams(vmem_limit_bytes=20 * MIB),
        cost_estimate=pl.CostEstimate(
            flops=16 * weights.size, bytes_accessed=2 * weights.size, transcendentals=0
        ),
    )(
        columns_in,
        in_hbm(place),
        from_left,
        from_right,
        in_hbm(weights),
        in_hbm(fields),
    )
    other = lax.ppermute(mine, "sec", [(0, 1), (1, 0)])

    surface, result = pl.pallas_call(
        finish_kernel,
        out_shape=(shaped((3, columns, lanes), f32), shaped(ocean_state.shape, f32)),
        in_specs=[smem] + [vmem] * 2 + [hbm] * 3 + [vmem],
        out_specs=(vmem, hbm),
        scratch_shapes=[
            pltpu.VMEM((tracers, levels, rows, lanes), f32),
            pltpu.VMEM((levels, columns, lanes), bf16),
            pltpu.VMEM((rows, lanes), i32),
            pltpu.VMEM(ocean_state.shape, f32),
            pltpu.VMEM((tracers, levels, tall_rows, lanes), bf16),
            pltpu.VMEM((levels, columns, lanes), f32),
            pltpu.VMEM(ocean_state.shape, f32),
            pltpu.VMEM(ocean_state.shape, f32),
            pltpu.VMEM((tall_rows, lanes), bf16),
            pltpu.VMEM((lanes, lanes), bf16),
            pltpu.SemaphoreType.DMA((pieces + 1, 2)),
            pltpu.SemaphoreType.DMA((pieces,)),
        ],
        compiler_params=pltpu.CompilerParams(vmem_limit_bytes=36 * MIB),
        cost_estimate=pl.CostEstimate(
            flops=60 * levels * cells, bytes_accessed=32 * levels * cells, transcendentals=0
        ),
    )(
        section,
        mine,
        other,
        in_hbm(bath),
        in_hbm(q),
        in_hbm(side),
        ratios,
    )
    return (surface[None], result)


def solution(mesh):
    return jax.shard_map(
        per_device,
        mesh=mesh,
        in_specs=(
            P("sec", None, "blk", None),
            P("sec", "blk", None),
            P("sec", "blk", None),
            P("sec", "blk", None, None, None),
            P(None, None, "blk", None),
            P("blk", None),
        ),
        out_specs=(P("sec", None, "blk", None), P(None, None, "blk", None)),
        check_vma=False,
    )
```

```python
import functools

import jax
import jax.numpy as jnp
import numpy as np
from jax import lax
from jax.experimental import pallas as pl
from jax.experimental.pallas import tpu as pltpu
from jax.sharding import PartitionSpec as P

FLUX_GAIN = 0.5
SIDE_MIX = 0.2
TOP_MIX = 1.0
DEEP_MIX = 2.0
SCALE = 1.0 / (0.5 * SIDE_MIX)

MOST = 16
SLOTS = MOST + 2
FIELDS = 3
PIECE = 56
EDGE = 8
EXTRA = 16
IN_FLIGHT = 3
MIB = 2**20
bf16, f32, i32 = jnp.bfloat16, jnp.float32, jnp.int32


def iota(shape, axis):
    return lax.broadcasted_iota(i32, shape, axis)


def adjacency(across, band, used):
    row, other = iota(across.shape, 0), iota(across.shape, 1)
    near = (row - other == 1) | (other - row == 1)
    near = near | ((row == 0) & (other == used - 1)) | ((row == used - 1) & (other == 0))
    across[...] = jnp.where(near & (row < used) & (other < used), 1.0, 0.0).astype(bf16)
    apart = iota(band.shape, 0) - iota(band.shape, 1)
    band[...] = jnp.where(jnp.abs(apart) == 1, 1.0, 0.0).astype(bf16)


def rounded(h):
    rows = -h.shape[0] % 16
    if rows:
        h = jnp.concatenate([h, jnp.zeros((rows, h.shape[1]), h.dtype)], axis=0)
    return h.astype(bf16)


def neighbour_sum(h, across, band, rows):
    tall, lanes = h.shape
    left = jnp.concatenate([across[pl.ds(0, rows), :], h[:rows]], axis=1)
    gap = jnp.zeros((across.shape[1] - tall, lanes), bf16)
    right = jnp.concatenate([h, gap, band[...]], axis=0)
    return jnp.dot(left, right, preferred_element_type=f32)


def edge_tile(right, left):
    row = iota((EDGE, right.shape[1]), 0)
    return jnp.where(row == 0, right, jnp.where(row == EDGE - 1, left, 0.0))


def chunks_of(levels):
    size = 10 if levels % 10 == 0 else levels
    return [(start, size) for start in range(0, levels, size)]


def sweep(count, body, carry):
    for step in range(count):
        carry = body(step, carry)
    return carry


def ranks(blocks, count):
    slots, columns = blocks.shape
    before = jnp.where(iota((columns, columns), 0) < iota((columns, columns), 1), 1.0, 0.0)
    before = before.astype(bf16)
    used = jnp.zeros((count, 1), f32)
    result = []
    for k in range(slots):
        owner = iota((count, columns), 0) == blocks[k : k + 1, :]
        one_hot = jnp.where(owner, 1.0, 0.0)
        earlier = used + jnp.dot(one_hot.astype(bf16), before, preferred_element_type=f32)
        rank = jnp.sum(one_hot * earlier, axis=0, keepdims=True)
        used = used + jnp.sum(one_hot, axis=1, keepdims=True)
        result.append((owner, rank))
    return result


def ask_kernel(blocks, spots, request, blocks_in, spots_in, sems):
    copies = [
        pltpu.make_async_copy(blocks, blocks_in, sems.at[0]),
        pltpu.make_async_copy(spots, spots_in, sems.at[1]),
    ]
    for copy in copies:
        copy.start()
    for copy in copies:
        copy.wait()
    count, columns = request.shape[0], blocks.shape[1]
    place = iota((128, columns), 0)
    field = place // SLOTS
    slot = jnp.where(field < FIELDS, place - field * SLOTS, -1)
    here = iota((128, columns), 1)
    marks = ((slot == MOST) & (here == 0)) | ((slot == MOST + 1) & (here == columns - 1))
    asked = jnp.zeros(request.shape, f32)
    for k, (owner, rank) in enumerate(ranks(blocks_in, count)):
        filled = jnp.where((slot == rank.astype(i32)) | marks, 1.0, 0.0).astype(bf16)
        named = jnp.where(owner, spots_in[k : k + 1, :].astype(f32), 0.0).astype(bf16)
        asked = asked + lax.dot_general(
            named, filled, (((1,), (1,)), ((), ())), preferred_element_type=f32
        )
    request[...] = asked.astype(i32) + (iota(request.shape, 1) // SLOTS) * columns


def pack_kernel(
    section, state, bath, fields, blocks, weights,
    to_left, to_right, table,
    low, high, surface, bath_in, fields_in, blocks_in, extra, sems,
):
    tracers, levels, columns, lanes = state.shape
    slots = blocks.shape[0]
    many = tracers * levels
    wide = to_left.shape[0] - 2 * many - EXTRA
    below = pl.ds(2 * many + EXTRA, wide)
    pairs = [
        (state.at[:, :, pl.ds(0, 8)], low),
        (state.at[:, :, pl.ds(columns - 8, 8)], high),
        (blocks, blocks_in),
        (bath, bath_in),
        (fields, fields_in),
        (state.at[:, 0], surface),
        (weights.at[pl.ds(0, wide)], to_left.at[below]),
        (weights.at[pl.ds((columns - 1) * wide, wide)], to_right.at[below]),
    ]
    copies = [pltpu.make_async_copy(src, dst, sems.at[n]) for n, (src, dst) in enumerate(pairs)]
    for copy in copies:
        copy.start()
    for copy in copies[2:6]:
        copy.wait()
    for out, first, at in ((to_left, 0, 0), (to_right, columns - 2, columns - 1)):
        extra[...] = jnp.zeros_like(extra)
        extra[0:2] = bath_in[first : first + 2].astype(f32)
        for f in range(3):
            extra[2 + f : 3 + f] = fields_in[f].astype(f32)[at : at + 1]
        extra[8 : 8 + slots] = jnp.broadcast_to(
            blocks_in[:, at : at + 1].astype(f32), (slots, lanes)
        )
        out[pl.ds(2 * many, EXTRA)] = extra[...].astype(bf16)
    on_ocean = section[0] == 1
    for f in range(3):
        own = fields_in[f]
        if f < 2:
            own = jnp.where(on_ocean, surface[f], own.astype(f32)).astype(bf16)
        table[f * columns : (f + 1) * columns, :] = own
    copies[0].wait()
    copies[1].wait()
    for c in range(2):
        for n in range(tracers):
            part = pl.ds(c * many + n * levels, levels)
            tiles = low.at[n].reshape(levels * 8, lanes)
            to_left[part] = tiles[pl.ds(c, levels, stride=8), :].astype(bf16)
            tiles = high.at[n].reshape(levels * 8, lanes)
            to_right[part] = tiles[pl.ds(6 + c, levels, stride=8), :].astype(bf16)
    copies[6].wait()
    copies[7].wait()


def serve_kernel(asked, table, out):
    count = asked.shape[0]
    wanted = jnp.transpose(asked[...].astype(f32))[:PIECE]
    height = table.shape[0]
    slot = lax.rem(iota((PIECE, 1), 0), SLOTS)
    parts = []
    for e in range(count):
        after, before = (e + 1) % count, (e - 1) % count
        spot = jnp.where(
            slot == MOST,
            wanted[:, after : after + 1],
            jnp.where(slot == MOST + 1, wanted[:, before : before + 1], wanted[:, e : e + 1]),
        )
        parts.append(jnp.where(iota((PIECE, height), 1) == spot.astype(i32), 1.0, 0.0))
    chosen = jnp.concatenate(parts, axis=0).astype(bf16)
    out[...] = jnp.dot(chosen, table[...], preferred_element_type=f32).astype(bf16)


def start_kernel(
    state, from_left, from_right, bath, blocks, ratios,
    q_result, side_result, bath_result, place_result,
    q_out, side_out, held, bath_out, halo, bath_in, blocks_in, place, across, band,
    sems, sems_out, *, count,
):
    tracers, levels, columns, lanes = state.shape
    rows = columns + EDGE
    many = tracers * levels
    chunks = chunks_of(levels)
    copies = []
    for n, (low, size) in enumerate(chunks):
        copies.append(
            pltpu.make_async_copy(
                state.at[:, pl.ds(low, size)], held.at[:, pl.ds(low, size)], sems.at[n]
            )
        )
    bath_copy = pltpu.make_async_copy(bath, bath_in, sems.at[len(chunks)])
    blocks_copy = pltpu.make_async_copy(blocks, blocks_in, sems.at[len(chunks) + 1])
    blocks_copy.start()
    bath_copy.start()
    for copy in reversed(copies[-IN_FLIGHT:]):
        copy.start()
    leaving = []

    def send(source, target, number):
        copy = pltpu.make_async_copy(source, target, sems_out.at[number])
        copy.start()
        leaving.append(copy)

    halo[...] = jnp.zeros_like(halo)
    for c in range(2):
        part = pl.ds(c * many, many)
        halo[pl.ds(c, many, stride=8), :] = from_right[part].astype(f32)
        halo[pl.ds(EDGE - 2 + c, many, stride=8), :] = from_left[part].astype(f32)
    right = from_right[pl.ds(2 * many, EXTRA)].astype(f32)
    left = from_left[pl.ds(2 * many, EXTRA)].astype(f32)
    row = iota((EDGE, lanes), 0)
    edge = jnp.where(
        row == 0,
        right[0:1],
        jnp.where(
            row == 1,
            right[1:2],
            jnp.where(row == EDGE - 2, left[0:1], jnp.where(row == EDGE - 1, left[1:2], 0.0)),
        ),
    )
    bath_copy.wait()
    depth = jnp.concatenate([bath_in[...], edge.astype(i32)], axis=0)
    bath_out[...] = depth
    send(bath_out, bath_result, 2 * len(chunks))
    blocks_copy.wait()
    for k, (_, rank) in enumerate(ranks(blocks_in, count)):
        arrives = blocks_in[k : k + 1, :].astype(f32) * PIECE + rank
        spread = jnp.transpose(jnp.broadcast_to(arrives, (128, columns)))
        place[k * columns : (k + 1) * columns, :] = spread.astype(i32)
    send(place, place_result, 2 * len(chunks) + 1)
    adjacency(across, band, rows)

    def side(level):
        wet = level < bath_out[...]
        starts, masked = [], []
        for n in range(tracers):
            spot = (n * levels + level) * 8
            full = jnp.concatenate([held[n, level], halo[pl.ds(spot, 8), :]], axis=0)
            starts.append(full)
            masked.append(jnp.where(wet, full, 0.0))
        tall = across.shape[0]
        count = neighbour_sum(rounded(jnp.where(wet, 1.0, 0.0)), across, band, tall)[:rows]
        own = 0.5 * SCALE - count
        side_out[level] = own[:columns].astype(bf16)
        halves = []
        for h in masked:
            halves.append(own * h + neighbour_sum(rounded(h), across, band, tall)[:rows])
        return wet, starts, halves

    def deep(step, below, top):
        level = top - step
        wet, starts, halves = side(level)
        rho = ratio_at(ratios, bath_out[...], level)
        solved = []
        for n in range(tracers):
            q = rho * (halves[n] + below[n])
            q_out[n, level] = jnp.where(wet, q, starts[n])
            solved.append(q)
        return tuple(solved)

    carry = tuple(jnp.zeros((rows, lanes), f32) for _ in range(tracers))
    for n in reversed(range(len(chunks))):
        low, size = chunks[n]
        copies[n].wait()
        if n >= IN_FLIGHT:
            copies[n - IN_FLIGHT].start()
        first = max(low, 2)
        top = low + size - 1
        carry = sweep(top - first + 1, functools.partial(deep, top=top), carry)
        if n == 0:
            for level in (1, 0):
                wet, starts, halves = side(level)
                for m in range(tracers):
                    q_out[m, level] = jnp.where(wet, halves[m], starts[m])
        part = pl.ds(low, size)
        send(q_out.at[:, part], q_result.at[:, part], 2 * n)
        send(side_out.at[part], side_result.at[part], 2 * n + 1)
    for copy in leaving:
        copy.wait()


def ratio_at(ratios, depth, level):
    lookup = jnp.broadcast_to(ratios[0:1], depth.shape)
    height = jnp.maximum(depth - level, 0)
    return jnp.take_along_axis(lookup, height, axis=1, mode="promise_in_bounds")


def ratios_by_height(levels, lanes):
    values = [0.0]
    ratio = DEEP_MIX / (1.0 + DEEP_MIX)
    for _ in range(levels):
        values.append(ratio)
        ratio = DEEP_MIX / (1.0 + DEEP_MIX + DEEP_MIX - DEEP_MIX * ratio)
    values += [0.0] * (lanes - len(values))
    return jnp.broadcast_to(jnp.asarray(np.array(values, np.float32)), (8, lanes))


def remap_kernel(
    columns_in, place_from, from_left, from_right, weights, own_fields,
    out, picked, solved, held, fields_in, place, sems,
):
    fields, rows, width = out.shape[0] // 2, out.shape[1], out.shape[2]
    columns = rows - EDGE
    slots = weights.shape[0] // (columns * width)
    tall = slots * width
    many = from_left.shape[0] - tall - EXTRA
    group = 8
    place_copy = pltpu.make_async_copy(place_from, place, sems.at[0])
    fields_copy = pltpu.make_async_copy(own_fields, fields_in, sems.at[1])
    copies = []
    for n in range(columns // group):
        part = pl.ds(n * group * tall, group * tall)
        copies.append(pltpu.make_async_copy(weights.at[part], held.at[part], sems.at[2 + n]))
    for copy in [place_copy] + copies + [fields_copy]:
        copy.start()
    right = from_right[pl.ds(many, EXTRA)].astype(f32)
    left = from_left[pl.ds(many, EXTRA)].astype(f32)
    row = iota((EDGE, 1), 0)
    picked[...] = jnp.zeros_like(picked)
    place_copy.wait()
    wanted = []
    for k in range(slots):
        edge = jnp.where(
            row == 0,
            right[8 + k : 9 + k, 0:1] * PIECE + MOST,
            jnp.where(row == EDGE - 1, left[8 + k : 9 + k, 0:1] * PIECE + MOST + 1, -PIECE),
        ).astype(i32)
        wanted += [place[k * columns : (k + 1) * columns, 0:1], edge]
    wanted = jnp.concatenate(wanted, axis=0)
    spots = iota((slots * rows, columns_in.shape[0]), 1)
    for f in range(fields):
        chosen = jnp.where(spots == wanted + f * SLOTS, 1.0, 0.0).astype(bf16)
        found = jnp.dot(chosen, columns_in[...], preferred_element_type=f32)
        for k in range(slots):
            picked[k, pl.ds(f, rows, stride=8), :] = found[k * rows : (k + 1) * rows]

    def one(row, table_of):
        spot = pl.ds(row * 8, 8)
        vector = jnp.concatenate([picked[k, spot, :] for k in range(slots)], axis=1)
        matrix = jnp.concatenate([table_of(k) for k in range(slots)], axis=1)
        solved[spot, :] = lax.dot_general(
            vector.astype(bf16), matrix, (((1,), (1,)), ((), ())), preferred_element_type=f32
        )

    solved[...] = jnp.zeros_like(solved)
    below = many + EXTRA
    one(columns, lambda k: from_right[pl.ds(below + k * width, width)])
    one(rows - 1, lambda k: from_left[pl.ds(below + k * width, width)])
    for n in range(columns // group):
        copies[n].wait()
        for m in range(group):
            spot = n * group + m
            one(spot, lambda k: held[pl.ds((spot * slots + k) * width, width)])
    fields_copy.wait()
    for f in range(fields):
        out[f, pl.ds(0, columns)] = solved[pl.ds(f, columns, stride=8), :]
        out[f, pl.ds(columns, EDGE)] = solved[pl.ds(columns * 8 + f, EDGE, stride=8), :]
        out[fields + f, pl.ds(0, columns)] = fields_in[f].astype(f32)
        out[fields + f, pl.ds(columns, EDGE)] = edge_tile(
            right[2 + f : 3 + f], left[2 + f : 3 + f]
        )


def finish_kernel(
    section, mine, other, bath, q, side, ratios, surface, result,
    values_at, rounded_at, rho, solved, done, across, band, sems_out,
):
    tracers, levels, columns, lanes = result.shape
    rows = columns + EDGE
    chunks = chunks_of(levels)
    on_ocean = section[0] == 1
    adjacency(across, band, rows)
    flux = [jnp.where(on_ocean, other[f], mine[f]) for f in range(3)]
    own = [jnp.where(on_ocean, mine[3 + f], other[3 + f]) for f in range(3)]
    forcing = [flux[0] + own[0], flux[1] + own[1]]
    top_mix = TOP_MIX * (1.0 + flux[2] * flux[2] + own[2] * own[2])
    depth = bath[...]

    def top_levels(count, halves, below, rho_below, scale):
        wet = 1 < depth[:count]
        link = jnp.where(wet, top_mix[:count], 0.0)
        deeper = jnp.where(2 < depth[:count], DEEP_MIX - DEEP_MIX * rho_below, 0.0)
        second = 1.0 / (1.0 + link + deeper)
        rho_second = link * second
        first = 1.0 / (1.0 + link - link * rho_second)
        values = []
        for n in range(tracers):
            partial = 2.0 * (halves[n][1] + below[n]) * second
            source = 2.0 * halves[n][0] + scale * FLUX_GAIN * forcing[n][:count]
            surface_value = (source + link * partial) * first
            next_value = jnp.where(wet, partial, 0.0) + rho_second * surface_value
            values.append((surface_value, next_value))
        return values

    def put(level, values):
        for n, h in enumerate(values):
            values_at[n, level] = h[:columns]
            rounded_at[n, level] = rounded(h)

    values = top_levels(
        rows,
        [(q[n, 0], q[n, 1]) for n in range(tracers)],
        [jnp.where(2 < depth, q[n, 2], 0.0) for n in range(tracers)],
        ratio_at(ratios, depth, 2),
        SCALE,
    )
    put(0, [jnp.where(0 < depth, values[n][0], 0.0) for n in range(tracers)])
    carry = tuple(values[n][1] for n in range(tracers))
    put(1, carry)

    def down(step, carry, low):
        level = low + step
        ratio = ratio_at(ratios, bath[...], level)
        rho[level] = ratio[:columns]
        wet = level < bath[...]
        out = [jnp.where(wet, q[n, level], 0.0) + ratio * carry[n] for n in range(tracers)]
        put(level, out)
        return tuple(out)

    sweep(levels - 2, functools.partial(down, low=2), carry)

    def halves_at(level):
        own = side[level].astype(f32)
        out = []
        for n in range(tracers):
            around = neighbour_sum(rounded_at[n, level], across, band, columns)
            out.append(own * values_at[n, level] + around)
        return out

    def up(step, carry):
        level = levels - 1 - step
        ratio = rho[level]
        halves = halves_at(level)
        out = [ratio * (halves[n] + carry[n]) for n in range(tracers)]
        for n in range(tracers):
            solved[n, level] = out[n]
        return tuple(out)

    zero = jnp.zeros((columns, lanes), f32)
    carry = sweep(levels - 2, up, (zero,) * tracers)
    values = top_levels(columns, list(zip(halves_at(0), halves_at(1))), carry, rho[2], SCALE * SCALE)
    unscale = 1.0 / (SCALE * SCALE)
    for n in range(tracers):
        surface[n] = jnp.where(on_ocean, values[n][0] * unscale, other[n, pl.ds(0, columns)])
    surface[2] = jnp.where(on_ocean, top_mix[:columns], other[2, pl.ds(0, columns)])

    def last(step, carry, low):
        level = low + step
        ratio = rho[level]
        wet = level < bath[pl.ds(0, columns)]
        out = []
        for n in range(tracers):
            h = solved[n, level] + ratio * carry[n]
            done[n, level] = jnp.where(wet, h * unscale, q[n, level, pl.ds(0, columns)])
            out.append(h)
        return tuple(out)

    wet = 1 < depth[:columns]
    for n in range(tracers):
        done[n, 0] = values[n][0] * unscale
        done[n, 1] = jnp.where(wet, values[n][1] * unscale, q[n, 1, pl.ds(0, columns)])
    carry = tuple(values[n][1] for n in range(tracers))
    leaving = []
    for n, (low, size) in enumerate(chunks):
        first = max(low, 2)
        carry = sweep(low + size - first, functools.partial(last, low=first), carry)
        part = pl.ds(low, size)
        leaving.append(
            pltpu.make_async_copy(done.at[:, part], result.at[:, part], sems_out.at[n])
        )
        leaving[-1].start()
    for copy in leaving:
        copy.wait()


def shift(value, axis, by):
    count = lax.axis_size(axis)
    return lax.ppermute(value, axis, [(i, (i + by) % count) for i in range(count)])


def in_hbm(value):
    return pltpu.with_memory_space_constraint(value, pltpu.HBM)


def in_vmem(value):
    return pltpu.with_memory_space_constraint(value, pltpu.VMEM)


def per_device(
    surface_fields, source_blocks, source_columns, remap_weights, ocean_state, bathymetry
):
    tracers, levels, columns, lanes = ocean_state.shape
    slots = source_blocks.shape[2]
    count = lax.axis_size("blk")
    rows = columns + EDGE
    section = lax.axis_index("sec").astype(i32).reshape(1)
    fields = surface_fields[0]
    blocks = jnp.transpose(source_blocks[0])
    spots = jnp.transpose(source_columns[0])
    weights = remap_weights[0].reshape(columns * slots * lanes, lanes)
    tall = slots * lanes
    many = tracers * levels

    hbm = pl.BlockSpec(memory_space=pltpu.HBM)
    vmem = pl.BlockSpec(memory_space=pltpu.VMEM)
    smem = pl.BlockSpec(memory_space=pltpu.SMEM)
    shaped = jax.ShapeDtypeStruct
    pieces = len(chunks_of(levels))
    cells = rows * lanes
    tall_rows = rows + -rows % 16

    request = pl.pallas_call(
        ask_kernel,
        out_shape=shaped((count, 128), i32),
        in_specs=[hbm, hbm],
        out_specs=vmem,
        scratch_shapes=[
            pltpu.VMEM(blocks.shape, i32),
            pltpu.VMEM(spots.shape, i32),
            pltpu.SemaphoreType.DMA((2,)),
        ],
        compiler_params=pltpu.CompilerParams(vmem_limit_bytes=4 * MIB),
        cost_estimate=pl.CostEstimate(flops=10**6, bytes_accessed=10**5, transcendentals=0),
    )(in_hbm(blocks), in_hbm(spots))
    asked = lax.all_to_all(request, "blk", split_axis=0, concat_axis=0, tiled=True)

    payload = shaped((2 * many + EXTRA + tall, lanes), bf16)
    to_left, to_right, table = pl.pallas_call(
        pack_kernel,
        out_shape=(
            payload,
            payload,
            shaped((FIELDS * columns, lanes), bf16),
        ),
        in_specs=[smem] + [hbm] * 5,
        out_specs=(vmem, vmem, vmem),
        scratch_shapes=[
            pltpu.VMEM((tracers, levels, 8, lanes), f32),
            pltpu.VMEM((tracers, levels, 8, lanes), f32),
            pltpu.VMEM((tracers, columns, lanes), f32),
            pltpu.VMEM(bathymetry.shape, i32),
            pltpu.VMEM(fields.shape, bf16),
            pltpu.VMEM(blocks.shape, i32),
            pltpu.VMEM((EXTRA, lanes), f32),
            pltpu.SemaphoreType.DMA((8,)),
        ],
        compiler_params=pltpu.CompilerParams(vmem_limit_bytes=8 * MIB),
        cost_estimate=pl.CostEstimate(
            flops=10**6, bytes_accessed=4 * 10**6, transcendentals=0
        ),
    )(
        section,
        in_hbm(ocean_state),
        in_hbm(bathymetry),
        in_hbm(fields),
        in_hbm(blocks),
        in_hbm(weights),
    )
    from_left = shift(to_right, "blk", 1)
    from_right = shift(to_left, "blk", -1)

    served = pl.pallas_call(
        serve_kernel,
        out_shape=shaped((count * PIECE, lanes), bf16),
        in_specs=[vmem] * 2,
        out_specs=vmem,
        compiler_params=pltpu.CompilerParams(vmem_limit_bytes=8 * MIB),
        cost_estimate=pl.CostEstimate(
            flops=10**7, bytes_accessed=10**6, transcendentals=0
        ),
    )(asked, table)
    columns_in = lax.all_to_all(served, "blk", split_axis=0, concat_axis=0, tiled=True)

    ratios = ratios_by_height(levels, lanes)
    q, side, bath, place = pl.pallas_call(
        functools.partial(start_kernel, count=count),
        out_shape=(
            pltpu.HBM((tracers, levels, rows, lanes), f32),
            pltpu.HBM((levels, columns, lanes), bf16),
            pltpu.HBM((rows, lanes), i32),
            pltpu.HBM((slots * columns, 128), i32),
        ),
        in_specs=[hbm, vmem, vmem, hbm, hbm, vmem],
        out_specs=(hbm,) * 4,
        scratch_shapes=[
            pltpu.VMEM((tracers, levels, rows, lanes), f32),
            pltpu.VMEM((levels, columns, lanes), bf16),
            pltpu.VMEM(ocean_state.shape, f32),
            pltpu.VMEM((rows, lanes), i32),
            pltpu.VMEM((many * 8, lanes), f32),
            pltpu.VMEM(bathymetry.shape, i32),
            pltpu.VMEM(blocks.shape, i32),
            pltpu.VMEM((slots * columns, 128), i32),
            pltpu.VMEM((tall_rows, lanes), bf16),
            pltpu.VMEM((lanes, lanes), bf16),
            pltpu.SemaphoreType.DMA((pieces + 2,)),
            pltpu.SemaphoreType.DMA((2 * pieces + 2,)),
        ],
        compiler_params=pltpu.CompilerParams(vmem_limit_bytes=28 * MIB),
        cost_estimate=pl.CostEstimate(
            flops=60 * levels * cells, bytes_accessed=20000 * levels * cells, transcendentals=0
        ),
    )(
        in_hbm(ocean_state),
        from_left,
        from_right,
        in_hbm(bathymetry),
        in_hbm(blocks),
        ratios,
    )

    mine = pl.pallas_call(
        remap_kernel,
        out_shape=shaped((6, rows, lanes), f32),
        in_specs=[vmem, hbm, vmem, vmem, hbm, hbm],
        out_specs=vmem,
        scratch_shapes=[
            pltpu.VMEM((slots, rows * 8, lanes), f32),
            pltpu.VMEM((rows * 8, lanes), f32),
            pltpu.VMEM(weights.shape, bf16),
            pltpu.VMEM(fields.shape, bf16),
            pltpu.VMEM((slots * columns, 128), i32),
            pltpu.SemaphoreType.DMA((2 + columns // 8,)),
        ],
        compiler_params=pltpu.CompilerParams(vmem_limit_bytes=20 * MIB),
        cost_estimate=pl.CostEstimate(
            flops=16 * weights.size, bytes_accessed=2 * weights.size, transcendentals=0
        ),
    )(
        columns_in,
        in_hbm(place),
        from_left,
        from_right,
        in_hbm(weights),
        in_hbm(fields),
    )
    other = lax.ppermute(mine, "sec", [(0, 1), (1, 0)])

    surface, result = pl.pallas_call(
        finish_kernel,
        out_shape=(shaped((3, columns, lanes), f32), shaped(ocean_state.shape, f32)),
        in_specs=[smem] + [vmem] * 6,
        out_specs=(vmem, hbm),
        scratch_shapes=[
            pltpu.VMEM(ocean_state.shape, f32),
            pltpu.VMEM((tracers, levels, tall_rows, lanes), bf16),
            pltpu.VMEM((levels, columns, lanes), f32),
            pltpu.VMEM(ocean_state.shape, f32),
            pltpu.VMEM(ocean_state.shape, f32),
            pltpu.VMEM((tall_rows, lanes), bf16),
            pltpu.VMEM((lanes, lanes), bf16),
            pltpu.SemaphoreType.DMA((pieces,)),
        ],
        compiler_params=pltpu.CompilerParams(vmem_limit_bytes=26 * MIB),
        cost_estimate=pl.CostEstimate(
            flops=60 * levels * cells, bytes_accessed=32 * levels * cells, transcendentals=0
        ),
    )(
        section,
        mine,
        other,
        in_vmem(bath),
        in_vmem(q),
        in_vmem(side),
        ratios,
    )
    return (surface[None], result)


def solution(mesh):
    return jax.shard_map(
        per_device,
        mesh=mesh,
        in_specs=(
            P("sec", None, "blk", None),
            P("sec", "blk", None),
            P("sec", "blk", None),
            P("sec", "blk", None, None, None),
            P(None, None, "blk", None),
            P("blk", None),
        ),
        out_specs=(P("sec", None, "blk", None), P(None, None, "blk", None)),
        check_vma=False,
    )
```

```python
import functools

import jax
import jax.numpy as jnp
import numpy as np
from jax import lax
from jax.experimental import pallas as pl
from jax.experimental.pallas import tpu as pltpu
from jax.sharding import PartitionSpec as P

FLUX_GAIN = 0.5
SIDE_MIX = 0.2
TOP_MIX = 1.0
DEEP_MIX = 2.0
SCALE = 1.0 / (0.5 * SIDE_MIX)

MOST = 16
SLOTS = MOST + 2
FIELDS = 3
PIECE = 56
EDGE = 8
EXTRA = 16
IN_FLIGHT = 3
GROUP = 5
MIB = 2**20
bf16, f32, i32 = jnp.bfloat16, jnp.float32, jnp.int32


def iota(shape, axis):
    return lax.broadcasted_iota(i32, shape, axis)


def adjacency(across, band, used):
    row, other = iota(across.shape, 0), iota(across.shape, 1)
    near = (row - other == 1) | (other - row == 1)
    near = near | ((row == 0) & (other == used - 1)) | ((row == used - 1) & (other == 0))
    across[...] = jnp.where(near & (row < used) & (other < used), 1.0, 0.0).astype(bf16)
    apart = iota(band.shape, 0) - iota(band.shape, 1)
    band[...] = jnp.where(jnp.abs(apart) == 1, 1.0, 0.0).astype(bf16)


def rounded(h):
    rows = -h.shape[0] % 16
    if rows:
        h = jnp.concatenate([h, jnp.zeros((rows, h.shape[1]), h.dtype)], axis=0)
    return h.astype(bf16)


def neighbour_sum(h, across, band, rows):
    tall, lanes = h.shape
    left = jnp.concatenate([across[pl.ds(0, rows), :], h[:rows]], axis=1)
    gap = jnp.zeros((across.shape[1] - tall, lanes), bf16)
    right = jnp.concatenate([h, gap, band[...]], axis=0)
    return jnp.dot(left, right, preferred_element_type=f32)


def edge_tile(right, left):
    row = iota((EDGE, right.shape[1]), 0)
    return jnp.where(row == 0, right, jnp.where(row == EDGE - 1, left, 0.0))


def chunks_of(levels):
    size = 10 if levels % 10 == 0 else levels
    return [(start, size) for start in range(0, levels, size)]


def sweep(count, body, carry):
    for step in range(count):
        carry = body(step, carry)
    return carry


def ranks(blocks, count, block_of=lambda row: row):
    slots, columns = blocks.shape
    before = jnp.where(iota((columns, columns), 0) < iota((columns, columns), 1), 1.0, 0.0)
    before = before.astype(bf16)
    used = jnp.zeros((count, 1), f32)
    result = []
    for k in range(slots):
        owner = block_of(iota((count, columns), 0)) == blocks[k : k + 1, :]
        one_hot = jnp.where(owner, 1.0, 0.0)
        earlier = used + jnp.dot(one_hot.astype(bf16), before, preferred_element_type=f32)
        rank = jnp.sum(one_hot * earlier, axis=0, keepdims=True)
        used = used + jnp.sum(one_hot, axis=1, keepdims=True)
        result.append((owner, rank))
    return result


def ask_kernel(blocks, spots, request, blocks_in, spots_in, sems):
    copies = [
        pltpu.make_async_copy(blocks, blocks_in, sems.at[0]),
        pltpu.make_async_copy(spots, spots_in, sems.at[1]),
    ]
    for copy in copies:
        copy.start()
    for copy in copies:
        copy.wait()
    count, columns = request.shape[0], blocks.shape[1]
    place = iota((128, columns), 0)
    field = place // SLOTS
    slot = jnp.where(field < FIELDS, place - field * SLOTS, -1)
    here = iota((128, columns), 1)
    marks = ((slot == MOST) & (here == 0)) | ((slot == MOST + 1) & (here == columns - 1))
    asked = jnp.zeros(request.shape, f32)
    inner = inner_of(count)
    outer = count // inner
    listed = ranks(blocks_in, count, lambda row: lax.rem(row, outer) * inner + row // outer)
    for k, (owner, rank) in enumerate(listed):
        filled = jnp.where((slot == rank.astype(i32)) | marks, 1.0, 0.0).astype(bf16)
        named = jnp.where(owner, spots_in[k : k + 1, :].astype(f32), 0.0).astype(bf16)
        asked = asked + lax.dot_general(
            named, filled, (((1,), (1,)), ((), ())), preferred_element_type=f32
        )
    request[...] = asked.astype(i32) + (iota(request.shape, 1) // SLOTS) * columns


def pack_kernel(
    section, state, bath, fields, blocks, weights,
    to_left, to_right, table,
    low, high, surface, bath_in, fields_in, blocks_in, extra, sems,
):
    tracers, levels, columns, lanes = state.shape
    slots = blocks.shape[0]
    many = tracers * levels
    wide = to_left.shape[0] - 2 * many - EXTRA
    below = pl.ds(2 * many + EXTRA, wide)
    pairs = [
        (state.at[:, :, pl.ds(0, 8)], low),
        (state.at[:, :, pl.ds(columns - 8, 8)], high),
        (blocks, blocks_in),
        (bath, bath_in),
        (fields, fields_in),
        (state.at[:, 0], surface),
        (weights.at[pl.ds(0, wide)], to_left.at[below]),
        (weights.at[pl.ds((columns - 1) * wide, wide)], to_right.at[below]),
    ]
    copies = [pltpu.make_async_copy(src, dst, sems.at[n]) for n, (src, dst) in enumerate(pairs)]
    for copy in copies:
        copy.start()
    for copy in copies[2:6]:
        copy.wait()
    for out, first, at in ((to_left, 0, 0), (to_right, columns - 2, columns - 1)):
        extra[...] = jnp.zeros_like(extra)
        extra[0:2] = bath_in[first : first + 2].astype(f32)
        for f in range(3):
            extra[2 + f : 3 + f] = fields_in[f].astype(f32)[at : at + 1]
        extra[8 : 8 + slots] = jnp.broadcast_to(
            blocks_in[:, at : at + 1].astype(f32), (slots, lanes)
        )
        out[pl.ds(2 * many, EXTRA)] = extra[...].astype(bf16)
    on_ocean = section[0] == 1
    for f in range(3):
        own = fields_in[f]
        if f < 2:
            own = jnp.where(on_ocean, surface[f], own.astype(f32)).astype(bf16)
        table[f * columns : (f + 1) * columns, :] = own
    copies[0].wait()
    copies[1].wait()
    for c in range(2):
        for n in range(tracers):
            part = pl.ds(c * many + n * levels, levels)
            tiles = low.at[n].reshape(levels * 8, lanes)
            to_left[part] = tiles[pl.ds(c, levels, stride=8), :].astype(bf16)
            tiles = high.at[n].reshape(levels * 8, lanes)
            to_right[part] = tiles[pl.ds(6 + c, levels, stride=8), :].astype(bf16)
    copies[6].wait()
    copies[7].wait()


def serve_kernel(asked, table, from_left, from_right, out):
    count = asked.shape[0]
    wanted = jnp.transpose(asked[...].astype(f32))[:PIECE]
    height = table.shape[0]
    slot = lax.rem(iota((PIECE, 1), 0), SLOTS)
    parts = []
    for e in range(count):
        after, before = (e + 1) % count, (e - 1) % count
        spot = jnp.where(
            slot == MOST,
            wanted[:, after : after + 1],
            jnp.where(slot == MOST + 1, wanted[:, before : before + 1], wanted[:, e : e + 1]),
        )
        parts.append(jnp.where(iota((PIECE, height), 1) == spot.astype(i32), 1.0, 0.0))
    chosen = jnp.concatenate(parts, axis=0).astype(bf16)
    out[...] = jnp.dot(chosen, table[...], preferred_element_type=f32).astype(bf16)


def start_kernel(
    state, from_left, from_right, bath, blocks, ratios,
    q_result, side_result, bath_result, place_result,
    q_out, side_out, held, bath_out, halo, bath_in, blocks_in, place, across, band,
    sems, sems_out, *, count,
):
    tracers, levels, columns, lanes = state.shape
    rows = columns + EDGE
    many = tracers * levels
    chunks = chunks_of(levels)
    copies = []
    for n, (low, size) in enumerate(chunks):
        copies.append(
            pltpu.make_async_copy(
                state.at[:, pl.ds(low, size)], held.at[:, pl.ds(low, size)], sems.at[n]
            )
        )
    bath_copy = pltpu.make_async_copy(bath, bath_in, sems.at[len(chunks)])
    blocks_copy = pltpu.make_async_copy(blocks, blocks_in, sems.at[len(chunks) + 1])
    blocks_copy.start()
    bath_copy.start()
    for copy in reversed(copies[-IN_FLIGHT:]):
        copy.start()
    leaving = []

    def send(source, target, number):
        copy = pltpu.make_async_copy(source, target, sems_out.at[number])
        copy.start()
        leaving.append(copy)

    halo[...] = jnp.zeros_like(halo)
    for c in range(2):
        part = pl.ds(c * many, many)
        halo[pl.ds(c, many, stride=8), :] = from_right[part].astype(f32)
        halo[pl.ds(EDGE - 2 + c, many, stride=8), :] = from_left[part].astype(f32)
    right = from_right[pl.ds(2 * many, EXTRA)].astype(f32)
    left = from_left[pl.ds(2 * many, EXTRA)].astype(f32)
    row = iota((EDGE, lanes), 0)
    edge = jnp.where(
        row == 0,
        right[0:1],
        jnp.where(
            row == 1,
            right[1:2],
            jnp.where(row == EDGE - 2, left[0:1], jnp.where(row == EDGE - 1, left[1:2], 0.0)),
        ),
    )
    bath_copy.wait()
    depth = jnp.concatenate([bath_in[...], edge.astype(i32)], axis=0)
    bath_out[...] = depth
    send(bath_out, bath_result, 2 * len(chunks))
    blocks_copy.wait()
    for k, (_, rank) in enumerate(ranks(blocks_in, count)):
        arrives = blocks_in[k : k + 1, :].astype(f32) * PIECE + rank
        spread = jnp.transpose(jnp.broadcast_to(arrives, (128, columns)))
        place[k * columns : (k + 1) * columns, :] = spread.astype(i32)
    send(place, place_result, 2 * len(chunks) + 1)
    adjacency(across, band, rows)

    def side(level):
        wet = level < bath_out[...]
        starts, masked = [], []
        for n in range(tracers):
            spot = (n * levels + level) * 8
            full = jnp.concatenate([held[n, level], halo[pl.ds(spot, 8), :]], axis=0)
            starts.append(full)
            masked.append(jnp.where(wet, full, 0.0))
        tall = across.shape[0]
        count = neighbour_sum(rounded(jnp.where(wet, 1.0, 0.0)), across, band, tall)[:rows]
        own = 0.5 * SCALE - count
        side_out[level] = own[:columns].astype(bf16)
        halves = []
        for h in masked:
            halves.append(own * h + neighbour_sum(rounded(h), across, band, tall)[:rows])
        return wet, starts, halves

    def deep(step, below, top):
        level = top - step
        wet, starts, halves = side(level)
        rho = ratio_at(ratios, bath_out[...], level)
        solved = []
        for n in range(tracers):
            q = rho * (halves[n] + below[n])
            q_out[n, level] = jnp.where(wet, q, starts[n])
            solved.append(q)
        return tuple(solved)

    carry = tuple(jnp.zeros((rows, lanes), f32) for _ in range(tracers))
    for n in reversed(range(len(chunks))):
        low, size = chunks[n]
        copies[n].wait()
        if n >= IN_FLIGHT:
            copies[n - IN_FLIGHT].start()
        first = max(low, 2)
        top = low + size - 1
        carry = sweep(top - first + 1, functools.partial(deep, top=top), carry)
        if n == 0:
            for level in (1, 0):
                wet, starts, halves = side(level)
                for m in range(tracers):
                    q_out[m, level] = jnp.where(wet, halves[m], starts[m])
        part = pl.ds(low, size)
        send(q_out.at[:, part], q_result.at[:, part], 2 * n)
        send(side_out.at[part], side_result.at[part], 2 * n + 1)
    for copy in leaving:
        copy.wait()


def ratio_at(ratios, depth, level):
    lookup = jnp.broadcast_to(ratios[0:1], depth.shape)
    height = jnp.maximum(depth - level, 0)
    return jnp.take_along_axis(lookup, height, axis=1, mode="promise_in_bounds")


def ratios_by_height(levels, lanes):
    values = [0.0]
    ratio = DEEP_MIX / (1.0 + DEEP_MIX)
    for _ in range(levels):
        values.append(ratio)
        ratio = DEEP_MIX / (1.0 + DEEP_MIX + DEEP_MIX - DEEP_MIX * ratio)
    values += [0.0] * (lanes - len(values))
    return jnp.broadcast_to(jnp.asarray(np.array(values, np.float32)), (8, lanes))


def remap_kernel(
    columns_in, place_from, from_left, from_right, weights, own_fields,
    out, picked, solved, held, fields_in, place, sems,
):
    fields, rows, width = out.shape[0] // 2, out.shape[1], out.shape[2]
    columns = rows - EDGE
    slots = weights.shape[0] // (columns * width)
    tall = slots * width
    many = from_left.shape[0] - tall - EXTRA
    group = 8
    place_copy = pltpu.make_async_copy(place_from, place, sems.at[0])
    fields_copy = pltpu.make_async_copy(own_fields, fields_in, sems.at[1])
    copies = []
    for n in range(columns // group):
        part = pl.ds(n * group * tall, group * tall)
        copies.append(pltpu.make_async_copy(weights.at[part], held.at[part], sems.at[2 + n]))
    for copy in [place_copy] + copies + [fields_copy]:
        copy.start()
    right = from_right[pl.ds(many, EXTRA)].astype(f32)
    left = from_left[pl.ds(many, EXTRA)].astype(f32)
    row = iota((EDGE, 1), 0)
    picked[...] = jnp.zeros_like(picked)
    place_copy.wait()
    wanted = []
    for k in range(slots):
        edge = jnp.where(
            row == 0,
            right[8 + k : 9 + k, 0:1] * PIECE + MOST,
            jnp.where(row == EDGE - 1, left[8 + k : 9 + k, 0:1] * PIECE + MOST + 1, -PIECE),
        ).astype(i32)
        wanted += [place[k * columns : (k + 1) * columns, 0:1], edge]
    wanted = jnp.concatenate(wanted, axis=0)
    spots = iota((slots * rows, columns_in.shape[0]), 1)
    for f in range(fields):
        chosen = jnp.where(spots == wanted + f * SLOTS, 1.0, 0.0).astype(bf16)
        found = jnp.dot(chosen, columns_in[...], preferred_element_type=f32)
        for k in range(slots):
            picked[k, pl.ds(f, rows, stride=8), :] = found[k * rows : (k + 1) * rows]

    def one(row, table_of):
        spot = pl.ds(row * 8, 8)
        vector = jnp.concatenate([picked[k, spot, :] for k in range(slots)], axis=1)
        matrix = jnp.concatenate([table_of(k) for k in range(slots)], axis=1)
        solved[spot, :] = lax.dot_general(
            vector.astype(bf16), matrix, (((1,), (1,)), ((), ())), preferred_element_type=f32
        )

    solved[...] = jnp.zeros_like(solved)
    below = many + EXTRA
    one(columns, lambda k: from_right[pl.ds(below + k * width, width)])
    one(rows - 1, lambda k: from_left[pl.ds(below + k * width, width)])
    for n in range(columns // group):
        copies[n].wait()
        for m in range(group):
            spot = n * group + m
            one(spot, lambda k: held[pl.ds((spot * slots + k) * width, width)])
    fields_copy.wait()
    for f in range(fields):
        out[f, pl.ds(0, columns)] = solved[pl.ds(f, columns, stride=8), :]
        out[f, pl.ds(columns, EDGE)] = solved[pl.ds(columns * 8 + f, EDGE, stride=8), :]
        out[fields + f, pl.ds(0, columns)] = fields_in[f].astype(f32)
        out[fields + f, pl.ds(columns, EDGE)] = edge_tile(
            right[2 + f : 3 + f], left[2 + f : 3 + f]
        )


def finish_kernel(
    section, mine, other, bath, q, side, ratios, surface, result,
    values_at, rounded_at, rho, solved, done, across, band, sems_out,
):
    tracers, levels, columns, lanes = result.shape
    rows = columns + EDGE
    chunks = chunks_of(levels)
    on_ocean = section[0] == 1
    adjacency(across, band, rows)
    flux = [jnp.where(on_ocean, other[f], mine[f]) for f in range(3)]
    own = [jnp.where(on_ocean, mine[3 + f], other[3 + f]) for f in range(3)]
    forcing = [flux[0] + own[0], flux[1] + own[1]]
    top_mix = TOP_MIX * (1.0 + flux[2] * flux[2] + own[2] * own[2])
    depth = bath[...]

    def top_levels(count, halves, below, rho_below, scale):
        wet = 1 < depth[:count]
        link = jnp.where(wet, top_mix[:count], 0.0)
        deeper = jnp.where(2 < depth[:count], DEEP_MIX - DEEP_MIX * rho_below, 0.0)
        second = 1.0 / (1.0 + link + deeper)
        rho_second = link * second
        first = 1.0 / (1.0 + link - link * rho_second)
        values = []
        for n in range(tracers):
            partial = 2.0 * (halves[n][1] + below[n]) * second
            source = 2.0 * halves[n][0] + scale * FLUX_GAIN * forcing[n][:count]
            surface_value = (source + link * partial) * first
            next_value = jnp.where(wet, partial, 0.0) + rho_second * surface_value
            values.append((surface_value, next_value))
        return values

    def put(level, values):
        for n, h in enumerate(values):
            values_at[n, level] = h[:columns]
            rounded_at[n, level] = rounded(h)

    values = top_levels(
        rows,
        [(q[n, 0], q[n, 1]) for n in range(tracers)],
        [jnp.where(2 < depth, q[n, 2], 0.0) for n in range(tracers)],
        ratio_at(ratios, depth, 2),
        SCALE,
    )
    put(0, [jnp.where(0 < depth, values[n][0], 0.0) for n in range(tracers)])
    carry = tuple(values[n][1] for n in range(tracers))
    put(1, carry)

    def down(step, carry, low):
        level = low + step
        ratio = ratio_at(ratios, bath[...], level)
        rho[level] = ratio[:columns]
        wet = level < bath[...]
        out = [jnp.where(wet, q[n, level], 0.0) + ratio * carry[n] for n in range(tracers)]
        put(level, out)
        return tuple(out)

    sweep(levels - 2, functools.partial(down, low=2), carry)

    def halves_at(group):
        stacked = [rounded_at[n, level][:columns] for level in group for n in range(tracers)]
        along = jnp.dot(
            jnp.concatenate(stacked, axis=0), band[...], preferred_element_type=f32
        )
        tall = rounded_at.shape[2]
        result = []
        for place, level in enumerate(group):
            side_by_side = jnp.concatenate(
                [rounded_at[n, level] for n in range(tracers)], axis=1
            )
            sums = jnp.dot(
                across[pl.ds(0, columns), pl.ds(0, tall)],
                side_by_side,
                preferred_element_type=f32,
            )
            own = side[level].astype(f32)
            out = []
            for n in range(tracers):
                first = (place * tracers + n) * columns
                around = sums[:, n * lanes : (n + 1) * lanes] + along[first : first + columns]
                out.append(own * values_at[n, level] + around)
            result.append(out)
        return result

    carry = [jnp.zeros((columns, lanes), f32)] * tracers
    top = levels - 1
    while top >= 2:
        group = list(range(top, max(top - GROUP, 1), -1))
        top -= len(group)
        for level, halves in zip(group, halves_at(group)):
            carry = [rho[level] * (halves[n] + carry[n]) for n in range(tracers)]
            for n in range(tracers):
                solved[n, level] = carry[n]
    values = top_levels(columns, list(zip(*halves_at([0, 1]))), carry, rho[2], SCALE * SCALE)
    unscale = 1.0 / (SCALE * SCALE)
    for n in range(tracers):
        surface[n] = jnp.where(on_ocean, values[n][0] * unscale, other[n, pl.ds(0, columns)])
    surface[2] = jnp.where(on_ocean, top_mix[:columns], other[2, pl.ds(0, columns)])

    def last(step, carry, low):
        level = low + step
        ratio = rho[level]
        wet = level < bath[pl.ds(0, columns)]
        out = []
        for n in range(tracers):
            h = solved[n, level] + ratio * carry[n]
            done[n, level] = jnp.where(wet, h * unscale, q[n, level, pl.ds(0, columns)])
            out.append(h)
        return tuple(out)

    wet = 1 < depth[:columns]
    for n in range(tracers):
        done[n, 0] = values[n][0] * unscale
        done[n, 1] = jnp.where(wet, values[n][1] * unscale, q[n, 1, pl.ds(0, columns)])
    carry = tuple(values[n][1] for n in range(tracers))
    leaving = []
    for n, (low, size) in enumerate(chunks):
        first = max(low, 2)
        carry = sweep(low + size - first, functools.partial(last, low=first), carry)
        part = pl.ds(low, size)
        leaving.append(
            pltpu.make_async_copy(done.at[:, part], result.at[:, part], sems_out.at[n])
        )
        leaving[-1].start()
    for copy in leaving:
        copy.wait()


def inner_of(count):
    inner = 1
    while inner * inner < count:
        inner *= 2
    return inner


def exchange_requests(value, axis):
    count = lax.axis_size(axis)
    inner = inner_of(count)
    outer = count // inner
    close = [[z * inner + w for w in range(inner)] for z in range(outer)]
    far = [[z * inner + w for z in range(outer)] for w in range(inner)]
    value = lax.all_to_all(value, axis, 0, 0, axis_index_groups=close, tiled=True)
    value = jnp.swapaxes(value.reshape(inner, outer, -1), 0, 1).reshape(value.shape)
    return lax.all_to_all(value, axis, 0, 0, axis_index_groups=far, tiled=True)


def shift(value, axis, by):
    count = lax.axis_size(axis)
    return lax.ppermute(value, axis, [(i, (i + by) % count) for i in range(count)])


def in_hbm(value):
    return pltpu.with_memory_space_constraint(value, pltpu.HBM)


def in_vmem(value):
    return pltpu.with_memory_space_constraint(value, pltpu.VMEM)


def per_device(
    surface_fields, source_blocks, source_columns, remap_weights, ocean_state, bathymetry
):
    tracers, levels, columns, lanes = ocean_state.shape
    slots = source_blocks.shape[2]
    count = lax.axis_size("blk")
    rows = columns + EDGE
    section = lax.axis_index("sec").astype(i32).reshape(1)
    fields = surface_fields[0]
    blocks = jnp.transpose(source_blocks[0])
    spots = jnp.transpose(source_columns[0])
    weights = remap_weights[0].reshape(columns * slots * lanes, lanes)
    tall = slots * lanes
    many = tracers * levels

    hbm = pl.BlockSpec(memory_space=pltpu.HBM)
    vmem = pl.BlockSpec(memory_space=pltpu.VMEM)
    smem = pl.BlockSpec(memory_space=pltpu.SMEM)
    shaped = jax.ShapeDtypeStruct
    pieces = len(chunks_of(levels))
    cells = rows * lanes
    tall_rows = rows + -rows % 16

    request = pl.pallas_call(
        ask_kernel,
        out_shape=shaped((count, 128), i32),
        in_specs=[hbm, hbm],
        out_specs=vmem,
        scratch_shapes=[
            pltpu.VMEM(blocks.shape, i32),
            pltpu.VMEM(spots.shape, i32),
            pltpu.SemaphoreType.DMA((2,)),
        ],
        compiler_params=pltpu.CompilerParams(vmem_limit_bytes=4 * MIB),
        cost_estimate=pl.CostEstimate(flops=10**6, bytes_accessed=10**5, transcendentals=0),
    )(in_hbm(blocks), in_hbm(spots))
    asked = exchange_requests(request, "blk")

    payload = shaped((2 * many + EXTRA + tall, lanes), bf16)
    to_left, to_right, table = pl.pallas_call(
        pack_kernel,
        out_shape=(
            payload,
            payload,
            shaped((FIELDS * columns, lanes), bf16),
        ),
        in_specs=[smem] + [hbm] * 5,
        out_specs=(vmem, vmem, vmem),
        scratch_shapes=[
            pltpu.VMEM((tracers, levels, 8, lanes), f32),
            pltpu.VMEM((tracers, levels, 8, lanes), f32),
            pltpu.VMEM((tracers, columns, lanes), f32),
            pltpu.VMEM(bathymetry.shape, i32),
            pltpu.VMEM(fields.shape, bf16),
            pltpu.VMEM(blocks.shape, i32),
            pltpu.VMEM((EXTRA, lanes), f32),
            pltpu.SemaphoreType.DMA((8,)),
        ],
        compiler_params=pltpu.CompilerParams(vmem_limit_bytes=8 * MIB),
        cost_estimate=pl.CostEstimate(
            flops=10**6, bytes_accessed=4 * 10**6, transcendentals=0
        ),
    )(
        section,
        in_hbm(ocean_state),
        in_hbm(bathymetry),
        in_hbm(fields),
        in_hbm(blocks),
        in_hbm(weights),
    )
    from_left = shift(to_right, "blk", 1)
    from_right = shift(to_left, "blk", -1)

    served = pl.pallas_call(
        serve_kernel,
        out_shape=shaped((count * PIECE, lanes), bf16),
        in_specs=[vmem] * 4,
        out_specs=vmem,
        compiler_params=pltpu.CompilerParams(vmem_limit_bytes=8 * MIB),
        cost_estimate=pl.CostEstimate(
            flops=10**7, bytes_accessed=10**6, transcendentals=0
        ),
    )(asked, table, from_left, from_right)
    columns_in = lax.all_to_all(served, "blk", split_axis=0, concat_axis=0, tiled=True)

    ratios = ratios_by_height(levels, lanes)
    q, side, bath, place = pl.pallas_call(
        functools.partial(start_kernel, count=count),
        out_shape=(
            pltpu.HBM((tracers, levels, rows, lanes), f32),
            pltpu.HBM((levels, columns, lanes), bf16),
            pltpu.HBM((rows, lanes), i32),
            pltpu.HBM((slots * columns, 128), i32),
        ),
        in_specs=[hbm, vmem, vmem, hbm, hbm, vmem],
        out_specs=(hbm,) * 4,
        scratch_shapes=[
            pltpu.VMEM((tracers, levels, rows, lanes), f32),
            pltpu.VMEM((levels, columns, lanes), bf16),
            pltpu.VMEM(ocean_state.shape, f32),
            pltpu.VMEM((rows, lanes), i32),
            pltpu.VMEM((many * 8, lanes), f32),
            pltpu.VMEM(bathymetry.shape, i32),
            pltpu.VMEM(blocks.shape, i32),
            pltpu.VMEM((slots * columns, 128), i32),
            pltpu.VMEM((tall_rows, lanes), bf16),
            pltpu.VMEM((lanes, lanes), bf16),
            pltpu.SemaphoreType.DMA((pieces + 2,)),
            pltpu.SemaphoreType.DMA((2 * pieces + 2,)),
        ],
        compiler_params=pltpu.CompilerParams(vmem_limit_bytes=28 * MIB),
        cost_estimate=pl.CostEstimate(
            flops=60 * levels * cells, bytes_accessed=200 * levels * cells, transcendentals=0
        ),
    )(
        in_hbm(ocean_state),
        from_left,
        from_right,
        in_hbm(bathymetry),
        in_hbm(blocks),
        ratios,
    )

    mine = pl.pallas_call(
        remap_kernel,
        out_shape=shaped((6, rows, lanes), f32),
        in_specs=[vmem, hbm, vmem, vmem, hbm, hbm],
        out_specs=vmem,
        scratch_shapes=[
            pltpu.VMEM((slots, rows * 8, lanes), f32),
            pltpu.VMEM((rows * 8, lanes), f32),
            pltpu.VMEM(weights.shape, bf16),
            pltpu.VMEM(fields.shape, bf16),
            pltpu.VMEM((slots * columns, 128), i32),
            pltpu.SemaphoreType.DMA((2 + columns // 8,)),
        ],
        compiler_params=pltpu.CompilerParams(vmem_limit_bytes=20 * MIB),
        cost_estimate=pl.CostEstimate(
            flops=16 * weights.size, bytes_accessed=2 * weights.size, transcendentals=0
        ),
    )(
        columns_in,
        in_hbm(place),
        from_left,
        from_right,
        in_hbm(weights),
        in_hbm(fields),
    )
    other = lax.ppermute(mine, "sec", [(0, 1), (1, 0)])

    surface, result = pl.pallas_call(
        finish_kernel,
        out_shape=(shaped((3, columns, lanes), f32), shaped(ocean_state.shape, f32)),
        in_specs=[smem] + [vmem] * 6,
        out_specs=(vmem, hbm),
        scratch_shapes=[
            pltpu.VMEM(ocean_state.shape, f32),
            pltpu.VMEM((tracers, levels, tall_rows, lanes), bf16),
            pltpu.VMEM((levels, columns, lanes), f32),
            pltpu.VMEM(ocean_state.shape, f32),
            pltpu.VMEM(ocean_state.shape, f32),
            pltpu.VMEM((tall_rows, lanes), bf16),
            pltpu.VMEM((lanes, lanes), bf16),
            pltpu.SemaphoreType.DMA((pieces,)),
        ],
        compiler_params=pltpu.CompilerParams(vmem_limit_bytes=26 * MIB),
        cost_estimate=pl.CostEstimate(
            flops=60 * levels * cells, bytes_accessed=32 * levels * cells, transcendentals=0
        ),
    )(
        section,
        mine,
        other,
        in_vmem(bath),
        in_vmem(q),
        in_vmem(side),
        ratios,
    )
    return (surface[None], result)


def solution(mesh):
    return jax.shard_map(
        per_device,
        mesh=mesh,
        in_specs=(
            P("sec", None, "blk", None),
            P("sec", "blk", None),
            P("sec", "blk", None),
            P("sec", "blk", None, None, None),
            P(None, None, "blk", None),
            P("blk", None),
        ),
        out_specs=(P("sec", None, "blk", None), P(None, None, "blk", None)),
        check_vma=False,
    )
```

```python
import functools

import jax
import jax.numpy as jnp
import numpy as np
from jax import lax
from jax.experimental import pallas as pl
from jax.experimental.pallas import tpu as pltpu
from jax.sharding import PartitionSpec as P

FLUX_GAIN = 0.5
SIDE_MIX = 0.2
TOP_MIX = 1.0
DEEP_MIX = 2.0
SCALE = 1.0 / (0.5 * SIDE_MIX)

MOST = 16
SLOTS = MOST + 2
FIELDS = 3
PIECE = 56
EDGE = 8
EXTRA = 16
IN_FLIGHT = 3
MIB = 2**20
bf16, f32, i32 = jnp.bfloat16, jnp.float32, jnp.int32


def iota(shape, axis):
    return lax.broadcasted_iota(i32, shape, axis)


def adjacency(across, band, used):
    row, other = iota(across.shape, 0), iota(across.shape, 1)
    near = (row - other == 1) | (other - row == 1)
    near = near | ((row == 0) & (other == used - 1)) | ((row == used - 1) & (other == 0))
    across[...] = jnp.where(near & (row < used) & (other < used), 1.0, 0.0).astype(bf16)
    apart = iota(band.shape, 0) - iota(band.shape, 1)
    band[...] = jnp.where(jnp.abs(apart) == 1, 1.0, 0.0).astype(bf16)


def rounded(h):
    rows = -h.shape[0] % 16
    if rows:
        h = jnp.concatenate([h, jnp.zeros((rows, h.shape[1]), h.dtype)], axis=0)
    return h.astype(bf16)


def neighbour_sum(h, across, band, rows):
    tall, lanes = h.shape
    left = jnp.concatenate([across[pl.ds(0, rows), :], h[:rows]], axis=1)
    gap = jnp.zeros((across.shape[1] - tall, lanes), bf16)
    right = jnp.concatenate([h, gap, band[...]], axis=0)
    return jnp.dot(left, right, preferred_element_type=f32)


def edge_tile(right, left):
    row = iota((EDGE, right.shape[1]), 0)
    return jnp.where(row == 0, right, jnp.where(row == EDGE - 1, left, 0.0))


def chunks_of(levels):
    size = 10 if levels % 10 == 0 else levels
    return [(start, size) for start in range(0, levels, size)]


def sweep(count, body, carry):
    for step in range(count):
        carry = body(step, carry)
    return carry


def ranks(blocks, count):
    slots, columns = blocks.shape
    before = jnp.where(iota((columns, columns), 0) < iota((columns, columns), 1), 1.0, 0.0)
    before = before.astype(bf16)
    used = jnp.zeros((count, 1), f32)
    result = []
    for k in range(slots):
        owner = iota((count, columns), 0) == blocks[k : k + 1, :]
        one_hot = jnp.where(owner, 1.0, 0.0)
        earlier = used + jnp.dot(one_hot.astype(bf16), before, preferred_element_type=f32)
        rank = jnp.sum(one_hot * earlier, axis=0, keepdims=True)
        used = used + jnp.sum(one_hot, axis=1, keepdims=True)
        result.append((owner, rank))
    return result


def ask_kernel(blocks, spots, request, blocks_in, spots_in, sems):
    copies = [
        pltpu.make_async_copy(blocks, blocks_in, sems.at[0]),
        pltpu.make_async_copy(spots, spots_in, sems.at[1]),
    ]
    for copy in copies:
        copy.start()
    for copy in copies:
        copy.wait()
    count, columns = request.shape[0], blocks.shape[1]
    place = iota((128, columns), 0)
    field = place // SLOTS
    slot = jnp.where(field < FIELDS, place - field * SLOTS, -1)
    here = iota((128, columns), 1)
    marks = ((slot == MOST) & (here == 0)) | ((slot == MOST + 1) & (here == columns - 1))
    asked = jnp.zeros(request.shape, f32)
    for k, (owner, rank) in enumerate(ranks(blocks_in, count)):
        filled = jnp.where((slot == rank.astype(i32)) | marks, 1.0, 0.0).astype(bf16)
        named = jnp.where(owner, spots_in[k : k + 1, :].astype(f32), 0.0).astype(bf16)
        asked = asked + lax.dot_general(
            named, filled, (((1,), (1,)), ((), ())), preferred_element_type=f32
        )
    request[...] = asked.astype(i32) + (iota(request.shape, 1) // SLOTS) * columns


def pack_kernel(
    section, state, bath, fields, blocks, weights,
    to_left, to_right, table,
    low, high, surface, bath_in, fields_in, blocks_in, extra, sems,
):
    tracers, levels, columns, lanes = state.shape
    slots = blocks.shape[0]
    many = tracers * levels
    wide = to_left.shape[0] - 2 * many - EXTRA
    below = pl.ds(2 * many + EXTRA, wide)
    pairs = [
        (state.at[:, :, pl.ds(0, 8)], low),
        (state.at[:, :, pl.ds(columns - 8, 8)], high),
        (blocks, blocks_in),
        (bath, bath_in),
        (fields, fields_in),
        (state.at[:, 0], surface),
        (weights.at[pl.ds(0, wide)], to_left.at[below]),
        (weights.at[pl.ds((columns - 1) * wide, wide)], to_right.at[below]),
    ]
    copies = [pltpu.make_async_copy(src, dst, sems.at[n]) for n, (src, dst) in enumerate(pairs)]
    for copy in copies:
        copy.start()
    for copy in copies[2:6]:
        copy.wait()
    for out, first, at in ((to_left, 0, 0), (to_right, columns - 2, columns - 1)):
        extra[...] = jnp.zeros_like(extra)
        extra[0:2] = bath_in[first : first + 2].astype(f32)
        for f in range(3):
            extra[2 + f : 3 + f] = fields_in[f].astype(f32)[at : at + 1]
        extra[8 : 8 + slots] = jnp.broadcast_to(
            blocks_in[:, at : at + 1].astype(f32), (slots, lanes)
        )
        out[pl.ds(2 * many, EXTRA)] = extra[...].astype(bf16)
    on_ocean = section[0] == 1
    for f in range(3):
        own = fields_in[f]
        if f < 2:
            own = jnp.where(on_ocean, surface[f], own.astype(f32)).astype(bf16)
        table[f * columns : (f + 1) * columns, :] = own
    copies[0].wait()
    copies[1].wait()
    for c in range(2):
        for n in range(tracers):
            part = pl.ds(c * many + n * levels, levels)
            tiles = low.at[n].reshape(levels * 8, lanes)
            to_left[part] = tiles[pl.ds(c, levels, stride=8), :].astype(bf16)
            tiles = high.at[n].reshape(levels * 8, lanes)
            to_right[part] = tiles[pl.ds(6 + c, levels, stride=8), :].astype(bf16)
    copies[6].wait()
    copies[7].wait()


def serve_kernel(asked, table, from_left, from_right, out):
    count = asked.shape[0]
    wanted = jnp.transpose(asked[...].astype(f32))[:PIECE]
    height = table.shape[0]
    slot = lax.rem(iota((PIECE, 1), 0), SLOTS)
    parts = []
    for e in range(count):
        after, before = (e + 1) % count, (e - 1) % count
        spot = jnp.where(
            slot == MOST,
            wanted[:, after : after + 1],
            jnp.where(slot == MOST + 1, wanted[:, before : before + 1], wanted[:, e : e + 1]),
        )
        parts.append(jnp.where(iota((PIECE, height), 1) == spot.astype(i32), 1.0, 0.0))
    chosen = jnp.concatenate(parts, axis=0).astype(bf16)
    out[...] = jnp.dot(chosen, table[...], preferred_element_type=f32).astype(bf16)


def start_kernel(
    state, from_left, from_right, bath, blocks, ratios,
    q_result, side_result, bath_result, place_result,
    q_out, side_out, held, bath_out, halo, bath_in, blocks_in, place, across, band,
    sems, sems_out, *, count,
):
    tracers, levels, columns, lanes = state.shape
    rows = columns + EDGE
    many = tracers * levels
    chunks = chunks_of(levels)
    copies = []
    for n, (low, size) in enumerate(chunks):
        copies.append(
            pltpu.make_async_copy(
                state.at[:, pl.ds(low, size)], held.at[:, pl.ds(low, size)], sems.at[n]
            )
        )
    bath_copy = pltpu.make_async_copy(bath, bath_in, sems.at[len(chunks)])
    blocks_copy = pltpu.make_async_copy(blocks, blocks_in, sems.at[len(chunks) + 1])
    blocks_copy.start()
    bath_copy.start()
    for copy in reversed(copies[-IN_FLIGHT:]):
        copy.start()
    leaving = []

    def send(source, target, number):
        copy = pltpu.make_async_copy(source, target, sems_out.at[number])
        copy.start()
        leaving.append(copy)

    halo[...] = jnp.zeros_like(halo)
    for c in range(2):
        part = pl.ds(c * many, many)
        halo[pl.ds(c, many, stride=8), :] = from_right[part].astype(f32)
        halo[pl.ds(EDGE - 2 + c, many, stride=8), :] = from_left[part].astype(f32)
    right = from_right[pl.ds(2 * many, EXTRA)].astype(f32)
    left = from_left[pl.ds(2 * many, EXTRA)].astype(f32)
    row = iota((EDGE, lanes), 0)
    edge = jnp.where(
        row == 0,
        right[0:1],
        jnp.where(
            row == 1,
            right[1:2],
            jnp.where(row == EDGE - 2, left[0:1], jnp.where(row == EDGE - 1, left[1:2], 0.0)),
        ),
    )
    bath_copy.wait()
    depth = jnp.concatenate([bath_in[...], edge.astype(i32)], axis=0)
    bath_out[...] = depth
    send(bath_out, bath_result, 2 * len(chunks))
    blocks_copy.wait()
    for k, (_, rank) in enumerate(ranks(blocks_in, count)):
        arrives = blocks_in[k : k + 1, :].astype(f32) * PIECE + rank
        spread = jnp.transpose(jnp.broadcast_to(arrives, (128, columns)))
        place[k * columns : (k + 1) * columns, :] = spread.astype(i32)
    send(place, place_result, 2 * len(chunks) + 1)
    adjacency(across, band, rows)

    def side(level):
        wet = level < bath_out[...]
        starts, masked = [], []
        for n in range(tracers):
            spot = (n * levels + level) * 8
            full = jnp.concatenate([held[n, level], halo[pl.ds(spot, 8), :]], axis=0)
            starts.append(full)
            masked.append(jnp.where(wet, full, 0.0))
        tall = across.shape[0]
        count = neighbour_sum(rounded(jnp.where(wet, 1.0, 0.0)), across, band, tall)[:rows]
        own = 0.5 * SCALE - count
        side_out[level] = own[:columns].astype(bf16)
        halves = []
        for h in masked:
            halves.append(own * h + neighbour_sum(rounded(h), across, band, tall)[:rows])
        return wet, starts, halves

    def deep(step, below, top):
        level = top - step
        wet, starts, halves = side(level)
        rho = ratio_at(ratios, bath_out[...], level)
        solved = []
        for n in range(tracers):
            q = rho * (halves[n] + below[n])
            q_out[n, level] = jnp.where(wet, q, starts[n])
            solved.append(q)
        return tuple(solved)

    carry = tuple(jnp.zeros((rows, lanes), f32) for _ in range(tracers))
    for n in reversed(range(len(chunks))):
        low, size = chunks[n]
        copies[n].wait()
        if n >= IN_FLIGHT:
            copies[n - IN_FLIGHT].start()
        first = max(low, 2)
        top = low + size - 1
        carry = sweep(top - first + 1, functools.partial(deep, top=top), carry)
        if n == 0:
            for level in (1, 0):
                wet, starts, halves = side(level)
                for m in range(tracers):
                    q_out[m, level] = jnp.where(wet, halves[m], starts[m])
        part = pl.ds(low, size)
        send(q_out.at[:, part], q_result.at[:, part], 2 * n)
        send(side_out.at[part], side_result.at[part], 2 * n + 1)
    for copy in leaving:
        copy.wait()


def ratio_at(ratios, depth, level):
    lookup = jnp.broadcast_to(ratios[0:1], depth.shape)
    height = jnp.maximum(depth - level, 0)
    return jnp.take_along_axis(lookup, height, axis=1, mode="promise_in_bounds")


def ratios_by_height(levels, lanes):
    values = [0.0]
    ratio = DEEP_MIX / (1.0 + DEEP_MIX)
    for _ in range(levels):
        values.append(ratio)
        ratio = DEEP_MIX / (1.0 + DEEP_MIX + DEEP_MIX - DEEP_MIX * ratio)
    values += [0.0] * (lanes - len(values))
    return jnp.broadcast_to(jnp.asarray(np.array(values, np.float32)), (8, lanes))


def remap_kernel(
    columns_in, place_from, from_left, from_right, weights, own_fields,
    out, picked, solved, held, fields_in, place, sems,
):
    fields, rows, width = out.shape[0] // 2, out.shape[1], out.shape[2]
    columns = rows - EDGE
    slots = weights.shape[0] // (columns * width)
    tall = slots * width
    many = from_left.shape[0] - tall - EXTRA
    group = 8
    place_copy = pltpu.make_async_copy(place_from, place, sems.at[0])
    fields_copy = pltpu.make_async_copy(own_fields, fields_in, sems.at[1])
    copies = []
    for n in range(columns // group):
        part = pl.ds(n * group * tall, group * tall)
        copies.append(pltpu.make_async_copy(weights.at[part], held.at[part], sems.at[2 + n]))
    for copy in [place_copy] + copies + [fields_copy]:
        copy.start()
    right = from_right[pl.ds(many, EXTRA)].astype(f32)
    left = from_left[pl.ds(many, EXTRA)].astype(f32)
    row = iota((EDGE, 1), 0)
    picked[...] = jnp.zeros_like(picked)
    place_copy.wait()
    wanted = []
    for k in range(slots):
        edge = jnp.where(
            row == 0,
            right[8 + k : 9 + k, 0:1] * PIECE + MOST,
            jnp.where(row == EDGE - 1, left[8 + k : 9 + k, 0:1] * PIECE + MOST + 1, -PIECE),
        ).astype(i32)
        wanted += [place[k * columns : (k + 1) * columns, 0:1], edge]
    wanted = jnp.concatenate(wanted, axis=0)
    spots = iota((slots * rows, columns_in.shape[0]), 1)
    for f in range(fields):
        chosen = jnp.where(spots == wanted + f * SLOTS, 1.0, 0.0).astype(bf16)
        found = jnp.dot(chosen, columns_in[...], preferred_element_type=f32)
        for k in range(slots):
            picked[k, pl.ds(f, rows, stride=8), :] = found[k * rows : (k + 1) * rows]

    def one(row, table_of):
        spot = pl.ds(row * 8, 8)
        vector = jnp.concatenate([picked[k, spot, :] for k in range(slots)], axis=1)
        matrix = jnp.concatenate([table_of(k) for k in range(slots)], axis=1)
        solved[spot, :] = lax.dot_general(
            vector.astype(bf16), matrix, (((1,), (1,)), ((), ())), preferred_element_type=f32
        )

    solved[...] = jnp.zeros_like(solved)
    below = many + EXTRA
    one(columns, lambda k: from_right[pl.ds(below + k * width, width)])
    one(rows - 1, lambda k: from_left[pl.ds(below + k * width, width)])
    for n in range(columns // group):
        copies[n].wait()
        for m in range(group):
            spot = n * group + m
            one(spot, lambda k: held[pl.ds((spot * slots + k) * width, width)])
    fields_copy.wait()
    for f in range(fields):
        out[f, pl.ds(0, columns)] = solved[pl.ds(f, columns, stride=8), :]
        out[f, pl.ds(columns, EDGE)] = solved[pl.ds(columns * 8 + f, EDGE, stride=8), :]
        out[fields + f, pl.ds(0, columns)] = fields_in[f].astype(f32)
        out[fields + f, pl.ds(columns, EDGE)] = edge_tile(
            right[2 + f : 3 + f], left[2 + f : 3 + f]
        )


def finish_kernel(
    section, mine, other, bath, q, side, ratios, surface, result,
    values_at, rounded_at, rho, solved, done, across, band, sems_out,
):
    tracers, levels, columns, lanes = result.shape
    chunks = chunks_of(levels)
    on_ocean = section[0] == 1
    adjacency(across, band, columns + EDGE)
    flux = [jnp.where(on_ocean, other[f], mine[f]) for f in range(3)]
    own = [jnp.where(on_ocean, mine[3 + f], other[3 + f]) for f in range(3)]
    forcing = [flux[0] + own[0], flux[1] + own[1]]
    top_mix = TOP_MIX * (1.0 + flux[2] * flux[2] + own[2] * own[2])
    depth = bath[...]
    unscale = 1.0 / (SCALE * SCALE)

    rho[2] = ratio_at(ratios, depth, 2)
    link = jnp.where(1 < depth, top_mix, 0.0)
    deeper = jnp.where(2 < depth, DEEP_MIX - DEEP_MIX * rho[2], 0.0)
    second = 1.0 / (1.0 + link + deeper)
    rho_second = link * second
    first = 1.0 / (1.0 + link - link * rho_second)

    def top_levels(n, count, halves, below, scale):
        partial = 2.0 * (halves[1] + below) * second[:count]
        source = 2.0 * halves[0] + scale * FLUX_GAIN * forcing[n][:count]
        value = (source + link[:count] * partial) * first[:count]
        below = jnp.where(1 < depth[:count], partial, 0.0) + rho_second[:count] * value
        return value, below

    def put(n, level, h):
        values_at[n, level] = h[:columns]
        rounded_at[n, level] = rounded(h)

    def half_at(n, level):
        around = neighbour_sum(rounded_at[n, level], across, band, columns)
        return side[level].astype(f32) * values_at[n, level] + around

    leaving = []
    for n in range(tracers):
        below = jnp.where(2 < depth, q[n, 2], 0.0)
        value, carry = top_levels(n, columns + EDGE, (q[n, 0], q[n, 1]), below, SCALE)
        put(n, 0, jnp.where(0 < depth, value, 0.0))
        put(n, 1, carry)
        for level in range(2, levels):
            if n == 0 and level > 2:
                rho[level] = ratio_at(ratios, depth, level)
            carry = jnp.where(level < depth, q[n, level], 0.0) + rho[level] * carry
            put(n, level, carry)

        carry = jnp.zeros((columns, lanes), f32)
        for level in range(levels - 1, 1, -1):
            carry = rho[level, pl.ds(0, columns)] * (half_at(n, level) + carry)
            solved[n, level] = carry

        value, carry = top_levels(
            n, columns, (half_at(n, 0), half_at(n, 1)), carry, SCALE * SCALE
        )
        surface[n] = jnp.where(on_ocean, value * unscale, other[n, pl.ds(0, columns)])
        done[n, 0] = value * unscale
        for low, size in chunks:
            for level in range(max(low, 1), low + size):
                if level > 1:
                    carry = solved[n, level] + rho[level, pl.ds(0, columns)] * carry
                start = q[n, level, pl.ds(0, columns)]
                done[n, level] = jnp.where(level < depth[:columns], carry * unscale, start)
            part = pl.ds(low, size)
            leaving.append(
                pltpu.make_async_copy(
                    done.at[n, part], result.at[n, part], sems_out.at[len(leaving)]
                )
            )
            leaving[-1].start()
    surface[2] = jnp.where(on_ocean, top_mix[:columns], other[2, pl.ds(0, columns)])
    for copy in leaving:
        copy.wait()


def shift(value, axis, by):
    count = lax.axis_size(axis)
    return lax.ppermute(value, axis, [(i, (i + by) % count) for i in range(count)])


def in_hbm(value):
    return pltpu.with_memory_space_constraint(value, pltpu.HBM)


def in_vmem(value):
    return pltpu.with_memory_space_constraint(value, pltpu.VMEM)


def per_device(
    surface_fields, source_blocks, source_columns, remap_weights, ocean_state, bathymetry
):
    tracers, levels, columns, lanes = ocean_state.shape
    slots = source_blocks.shape[2]
    count = lax.axis_size("blk")
    rows = columns + EDGE
    section = lax.axis_index("sec").astype(i32).reshape(1)
    fields = surface_fields[0]
    blocks = jnp.transpose(source_blocks[0])
    spots = jnp.transpose(source_columns[0])
    weights = remap_weights[0].reshape(columns * slots * lanes, lanes)
    tall = slots * lanes
    many = tracers * levels

    hbm = pl.BlockSpec(memory_space=pltpu.HBM)
    vmem = pl.BlockSpec(memory_space=pltpu.VMEM)
    smem = pl.BlockSpec(memory_space=pltpu.SMEM)
    shaped = jax.ShapeDtypeStruct
    pieces = len(chunks_of(levels))
    cells = rows * lanes
    tall_rows = rows + -rows % 16

    request = pl.pallas_call(
        ask_kernel,
        out_shape=shaped((count, 128), i32),
        in_specs=[hbm, hbm],
        out_specs=vmem,
        scratch_shapes=[
            pltpu.VMEM(blocks.shape, i32),
            pltpu.VMEM(spots.shape, i32),
            pltpu.SemaphoreType.DMA((2,)),
        ],
        compiler_params=pltpu.CompilerParams(vmem_limit_bytes=4 * MIB),
        cost_estimate=pl.CostEstimate(flops=10**6, bytes_accessed=10**5, transcendentals=0),
    )(in_hbm(blocks), in_hbm(spots))
    asked = lax.all_to_all(request, "blk", split_axis=0, concat_axis=0, tiled=True)

    payload = shaped((2 * many + EXTRA + tall, lanes), bf16)
    to_left, to_right, table = pl.pallas_call(
        pack_kernel,
        out_shape=(
            payload,
            payload,
            shaped((FIELDS * columns, lanes), bf16),
        ),
        in_specs=[smem] + [hbm] * 5,
        out_specs=(vmem, vmem, vmem),
        scratch_shapes=[
            pltpu.VMEM((tracers, levels, 8, lanes), f32),
            pltpu.VMEM((tracers, levels, 8, lanes), f32),
            pltpu.VMEM((tracers, columns, lanes), f32),
            pltpu.VMEM(bathymetry.shape, i32),
            pltpu.VMEM(fields.shape, bf16),
            pltpu.VMEM(blocks.shape, i32),
            pltpu.VMEM((EXTRA, lanes), f32),
            pltpu.SemaphoreType.DMA((8,)),
        ],
        compiler_params=pltpu.CompilerParams(vmem_limit_bytes=8 * MIB),
        cost_estimate=pl.CostEstimate(
            flops=10**6, bytes_accessed=4 * 10**6, transcendentals=0
        ),
    )(
        section,
        in_hbm(ocean_state),
        in_hbm(bathymetry),
        in_hbm(fields),
        in_hbm(blocks),
        in_hbm(weights),
    )
    from_left = shift(to_right, "blk", 1)
    from_right = shift(to_left, "blk", -1)

    served = pl.pallas_call(
        serve_kernel,
        out_shape=shaped((count * PIECE, lanes), bf16),
        in_specs=[vmem] * 4,
        out_specs=vmem,
        compiler_params=pltpu.CompilerParams(vmem_limit_bytes=8 * MIB),
        cost_estimate=pl.CostEstimate(
            flops=10**7, bytes_accessed=10**6, transcendentals=0
        ),
    )(asked, table, from_left, from_right)
    columns_in = lax.all_to_all(served, "blk", split_axis=0, concat_axis=0, tiled=True)

    ratios = ratios_by_height(levels, lanes)
    q, side, bath, place = pl.pallas_call(
        functools.partial(start_kernel, count=count),
        out_shape=(
            pltpu.HBM((tracers, levels, rows, lanes), f32),
            pltpu.HBM((levels, columns, lanes), bf16),
            pltpu.HBM((rows, lanes), i32),
            pltpu.HBM((slots * columns, 128), i32),
        ),
        in_specs=[hbm, vmem, vmem, hbm, hbm, vmem],
        out_specs=(hbm,) * 4,
        scratch_shapes=[
            pltpu.VMEM((tracers, levels, rows, lanes), f32),
            pltpu.VMEM((levels, columns, lanes), bf16),
            pltpu.VMEM(ocean_state.shape, f32),
            pltpu.VMEM((rows, lanes), i32),
            pltpu.VMEM((many * 8, lanes), f32),
            pltpu.VMEM(bathymetry.shape, i32),
            pltpu.VMEM(blocks.shape, i32),
            pltpu.VMEM((slots * columns, 128), i32),
            pltpu.VMEM((tall_rows, lanes), bf16),
            pltpu.VMEM((lanes, lanes), bf16),
            pltpu.SemaphoreType.DMA((pieces + 2,)),
            pltpu.SemaphoreType.DMA((2 * pieces + 2,)),
        ],
        compiler_params=pltpu.CompilerParams(vmem_limit_bytes=28 * MIB),
        cost_estimate=pl.CostEstimate(
            flops=60 * levels * cells, bytes_accessed=200 * levels * cells, transcendentals=0
        ),
    )(
        in_hbm(ocean_state),
        from_left,
        from_right,
        in_hbm(bathymetry),
        in_hbm(blocks),
        ratios,
    )

    mine = pl.pallas_call(
        remap_kernel,
        out_shape=shaped((6, rows, lanes), f32),
        in_specs=[vmem, hbm, vmem, vmem, hbm, hbm],
        out_specs=vmem,
        scratch_shapes=[
            pltpu.VMEM((slots, rows * 8, lanes), f32),
            pltpu.VMEM((rows * 8, lanes), f32),
            pltpu.VMEM(weights.shape, bf16),
            pltpu.VMEM(fields.shape, bf16),
            pltpu.VMEM((slots * columns, 128), i32),
            pltpu.SemaphoreType.DMA((2 + columns // 8,)),
        ],
        compiler_params=pltpu.CompilerParams(vmem_limit_bytes=20 * MIB),
        cost_estimate=pl.CostEstimate(
            flops=16 * weights.size, bytes_accessed=2 * weights.size, transcendentals=0
        ),
    )(
        columns_in,
        in_hbm(place),
        from_left,
        from_right,
        in_hbm(weights),
        in_hbm(fields),
    )
    other = lax.ppermute(mine, "sec", [(0, 1), (1, 0)])

    surface, result = pl.pallas_call(
        finish_kernel,
        out_shape=(shaped((3, columns, lanes), f32), shaped(ocean_state.shape, f32)),
        in_specs=[smem] + [vmem] * 6,
        out_specs=(vmem, hbm),
        scratch_shapes=[
            pltpu.VMEM(ocean_state.shape, f32),
            pltpu.VMEM((tracers, levels, tall_rows, lanes), bf16),
            pltpu.VMEM((levels, rows, lanes), f32),
            pltpu.VMEM(ocean_state.shape, f32),
            pltpu.VMEM(ocean_state.shape, f32),
            pltpu.VMEM((tall_rows, lanes), bf16),
            pltpu.VMEM((lanes, lanes), bf16),
            pltpu.SemaphoreType.DMA((tracers * pieces,)),
        ],
        compiler_params=pltpu.CompilerParams(vmem_limit_bytes=26 * MIB),
        cost_estimate=pl.CostEstimate(
            flops=60 * levels * cells, bytes_accessed=32 * levels * cells, transcendentals=0
        ),
    )(
        section,
        mine,
        other,
        in_vmem(bath),
        in_vmem(q),
        in_vmem(side),
        ratios,
    )
    return (surface[None], result)


def solution(mesh):
    return jax.shard_map(
        per_device,
        mesh=mesh,
        in_specs=(
            P("sec", None, "blk", None),
            P("sec", "blk", None),
            P("sec", "blk", None),
            P("sec", "blk", None, None, None),
            P(None, None, "blk", None),
            P("blk", None),
        ),
        out_specs=(P("sec", None, "blk", None), P(None, None, "blk", None)),
        check_vma=False,
    )
```

```python
import functools
import math

import jax
import jax.numpy as jnp
import numpy as np
from jax import lax
from jax.experimental import pallas as pl
from jax.experimental.pallas import tpu as pltpu
from jax.sharding import PartitionSpec as P

FLUX_GAIN = 0.5
SIDE_MIX = 0.2
TOP_MIX = 1.0
DEEP_MIX = 2.0
FIXED = (1.0 + 2.0 * DEEP_MIX - math.sqrt(1.0 + 4.0 * DEEP_MIX)) / (2.0 * DEEP_MIX)
SCALE = 1.0 / (0.5 * SIDE_MIX)

MOST = 16
SLOTS = MOST + 2
FIELDS = 3
PIECE = 56
EDGE = 8
EXTRA = 16
IN_FLIGHT = 3
MIB = 2**20
bf16, f32, i32 = jnp.bfloat16, jnp.float32, jnp.int32


def iota(shape, axis):
    return lax.broadcasted_iota(i32, shape, axis)


def adjacency(across, band, used):
    row, other = iota(across.shape, 0), iota(across.shape, 1)
    near = (row - other == 1) | (other - row == 1)
    near = near | ((row == 0) & (other == used - 1)) | ((row == used - 1) & (other == 0))
    across[...] = jnp.where(near & (row < used) & (other < used), 1.0, 0.0).astype(bf16)
    apart = iota(band.shape, 0) - iota(band.shape, 1)
    band[...] = jnp.where(jnp.abs(apart) == 1, 1.0, 0.0).astype(bf16)


def rounded(h):
    rows = -h.shape[0] % 16
    if rows:
        h = jnp.concatenate([h, jnp.zeros((rows, h.shape[1]), h.dtype)], axis=0)
    return h.astype(bf16)


def neighbour_sum(h, across, band, rows):
    tall, lanes = h.shape
    left = jnp.concatenate([across[pl.ds(0, rows), :], h[:rows]], axis=1)
    gap = jnp.zeros((across.shape[1] - tall, lanes), bf16)
    right = jnp.concatenate([h, gap, band[...]], axis=0)
    return jnp.dot(left, right, preferred_element_type=f32)


def edge_tile(right, left):
    row = iota((EDGE, right.shape[1]), 0)
    return jnp.where(row == 0, right, jnp.where(row == EDGE - 1, left, 0.0))


def chunks_of(levels):
    size = 10 if levels % 10 == 0 else levels
    return [(start, size) for start in range(0, levels, size)]


def sweep(count, body, carry):
    for step in range(count):
        carry = body(step, carry)
    return carry


def ranks(blocks, count):
    slots, columns = blocks.shape
    before = jnp.where(iota((columns, columns), 0) < iota((columns, columns), 1), 1.0, 0.0)
    before = before.astype(bf16)
    used = jnp.zeros((count, 1), f32)
    result = []
    for k in range(slots):
        owner = iota((count, columns), 0) == blocks[k : k + 1, :]
        one_hot = jnp.where(owner, 1.0, 0.0)
        earlier = used + jnp.dot(one_hot.astype(bf16), before, preferred_element_type=f32)
        rank = jnp.sum(one_hot * earlier, axis=0, keepdims=True)
        used = used + jnp.sum(one_hot, axis=1, keepdims=True)
        result.append((owner, rank))
    return result


def ask_kernel(blocks, spots, request):
    count, columns = request.shape[0], blocks.shape[1]
    place = iota((128, columns), 0)
    field = place // SLOTS
    slot = jnp.where(field < FIELDS, place - field * SLOTS, -1)
    here = iota((128, columns), 1)
    marks = ((slot == MOST) & (here == 0)) | ((slot == MOST + 1) & (here == columns - 1))
    asked = jnp.zeros(request.shape, f32)
    for k, (owner, rank) in enumerate(ranks(blocks, count)):
        filled = jnp.where((slot == rank.astype(i32)) | marks, 1.0, 0.0).astype(bf16)
        named = jnp.where(owner, spots[k : k + 1, :].astype(f32), 0.0).astype(bf16)
        asked = asked + lax.dot_general(
            named, filled, (((1,), (1,)), ((), ())), preferred_element_type=f32
        )
    request[...] = asked.astype(i32) + (iota(request.shape, 1) // SLOTS) * columns


def pack_kernel(
    section, state, bath, fields, blocks, spots, weights,
    to_left, to_right, table, blocks_in, spots_in,
    low, high, surface, bath_in, fields_in, extra, sems,
):
    tracers, levels, columns, lanes = state.shape
    slots = blocks.shape[0]
    many = tracers * levels
    wide = to_left.shape[0] - 2 * many - EXTRA
    below = pl.ds(2 * many + EXTRA, wide)
    pairs = [
        (state.at[:, :, pl.ds(0, 8)], low),
        (state.at[:, :, pl.ds(columns - 8, 8)], high),
        (blocks, blocks_in),
        (bath, bath_in),
        (fields, fields_in),
        (state.at[:, 0], surface),
        (weights.at[pl.ds(0, wide)], to_left.at[below]),
        (weights.at[pl.ds((columns - 1) * wide, wide)], to_right.at[below]),
        (spots, spots_in),
    ]
    copies = [pltpu.make_async_copy(src, dst, sems.at[n]) for n, (src, dst) in enumerate(pairs)]
    for copy in copies:
        copy.start()
    for copy in copies[2:6]:
        copy.wait()
    for out, first, at in ((to_left, 0, 0), (to_right, columns - 2, columns - 1)):
        extra[...] = jnp.zeros_like(extra)
        extra[0:2] = bath_in[first : first + 2].astype(f32)
        for f in range(3):
            extra[2 + f : 3 + f] = fields_in[f].astype(f32)[at : at + 1]
        extra[8 : 8 + slots] = jnp.broadcast_to(
            blocks_in[:, at : at + 1].astype(f32), (slots, lanes)
        )
        out[pl.ds(2 * many, EXTRA)] = extra[...].astype(bf16)
    on_ocean = section[0] == 1
    for f in range(3):
        own = fields_in[f]
        if f < 2:
            own = jnp.where(on_ocean, surface[f], own.astype(f32)).astype(bf16)
        table[f * columns : (f + 1) * columns, :] = own
    copies[0].wait()
    copies[1].wait()
    for c in range(2):
        for n in range(tracers):
            part = pl.ds(c * many + n * levels, levels)
            tiles = low.at[n].reshape(levels * 8, lanes)
            to_left[part] = tiles[pl.ds(c, levels, stride=8), :].astype(bf16)
            tiles = high.at[n].reshape(levels * 8, lanes)
            to_right[part] = tiles[pl.ds(6 + c, levels, stride=8), :].astype(bf16)
    for copy in copies[6:]:
        copy.wait()


def serve_kernel(asked, table, from_left, from_right, out):
    count = asked.shape[0]
    wanted = jnp.transpose(asked[...].astype(f32))[:PIECE]
    height = table.shape[0]
    slot = lax.rem(iota((PIECE, 1), 0), SLOTS)
    parts = []
    for e in range(count):
        after, before = (e + 1) % count, (e - 1) % count
        spot = jnp.where(
            slot == MOST,
            wanted[:, after : after + 1],
            jnp.where(slot == MOST + 1, wanted[:, before : before + 1], wanted[:, e : e + 1]),
        )
        parts.append(jnp.where(iota((PIECE, height), 1) == spot.astype(i32), 1.0, 0.0))
    chosen = jnp.concatenate(parts, axis=0).astype(bf16)
    out[...] = jnp.dot(chosen, table[...], preferred_element_type=f32).astype(bf16)


def start_kernel(
    state, from_left, from_right, bath, blocks, ratios,
    q_result, side_result, bath_result, place_result,
    q_out, side_out, held, bath_out, halo, bath_in, blocks_in, place, across, band,
    sems, sems_out, *, count,
):
    tracers, levels, columns, lanes = state.shape
    rows = columns + EDGE
    many = tracers * levels
    chunks = chunks_of(levels)
    copies = []
    for n, (low, size) in enumerate(chunks):
        copies.append(
            pltpu.make_async_copy(
                state.at[:, pl.ds(low, size)], held.at[:, pl.ds(low, size)], sems.at[n]
            )
        )
    bath_copy = pltpu.make_async_copy(bath, bath_in, sems.at[len(chunks)])
    blocks_copy = pltpu.make_async_copy(blocks, blocks_in, sems.at[len(chunks) + 1])
    blocks_copy.start()
    bath_copy.start()
    for copy in reversed(copies[-IN_FLIGHT:]):
        copy.start()
    leaving = []

    def send(source, target, number):
        copy = pltpu.make_async_copy(source, target, sems_out.at[number])
        copy.start()
        leaving.append(copy)

    halo[...] = jnp.zeros_like(halo)
    for c in range(2):
        part = pl.ds(c * many, many)
        halo[pl.ds(c, many, stride=8), :] = from_right[part].astype(f32)
        halo[pl.ds(EDGE - 2 + c, many, stride=8), :] = from_left[part].astype(f32)
    right = from_right[pl.ds(2 * many, EXTRA)].astype(f32)
    left = from_left[pl.ds(2 * many, EXTRA)].astype(f32)
    row = iota((EDGE, lanes), 0)
    edge = jnp.where(
        row == 0,
        right[0:1],
        jnp.where(
            row == 1,
            right[1:2],
            jnp.where(row == EDGE - 2, left[0:1], jnp.where(row == EDGE - 1, left[1:2], 0.0)),
        ),
    )
    bath_copy.wait()
    depth = jnp.concatenate([bath_in[...], edge.astype(i32)], axis=0)
    bath_out[...] = depth
    send(bath_out, bath_result, 2 * len(chunks))
    blocks_copy.wait()
    for k, (_, rank) in enumerate(ranks(blocks_in, count)):
        arrives = blocks_in[k : k + 1, :].astype(f32) * PIECE + rank
        spread = jnp.transpose(jnp.broadcast_to(arrives, (128, columns)))
        place[k * columns : (k + 1) * columns, :] = spread.astype(i32)
    send(place, place_result, 2 * len(chunks) + 1)
    adjacency(across, band, rows)

    def side(level):
        wet = level < bath_out[...]
        starts, masked = [], []
        for n in range(tracers):
            spot = (n * levels + level) * 8
            full = jnp.concatenate([held[n, level], halo[pl.ds(spot, 8), :]], axis=0)
            starts.append(full)
            masked.append(jnp.where(wet, full, 0.0))
        tall = across.shape[0]
        count = neighbour_sum(rounded(jnp.where(wet, 1.0, 0.0)), across, band, tall)[:rows]
        own = 0.5 * SCALE - count
        side_out[level] = own[:columns].astype(bf16)
        halves = []
        for h in masked:
            halves.append(own * h + neighbour_sum(rounded(h), across, band, tall)[:rows])
        return wet, starts, halves

    def deep(step, below, top):
        level = top - step
        wet, starts, halves = side(level)
        rho = ratio_at(ratios, bath_out[...], level)
        solved = []
        for n in range(tracers):
            q = rho * (halves[n] + below[n])
            q_out[n, level] = jnp.where(wet, q, starts[n])
            solved.append(q)
        return tuple(solved)

    carry = tuple(jnp.zeros((rows, lanes), f32) for _ in range(tracers))
    for n in reversed(range(len(chunks))):
        low, size = chunks[n]
        copies[n].wait()
        if n >= IN_FLIGHT:
            copies[n - IN_FLIGHT].start()
        first = max(low, 2)
        top = low + size - 1
        carry = sweep(top - first + 1, functools.partial(deep, top=top), carry)
        if n == 0:
            for level in (1, 0):
                wet, starts, halves = side(level)
                for m in range(tracers):
                    q_out[m, level] = jnp.where(wet, halves[m], starts[m])
        part = pl.ds(low, size)
        send(q_out.at[:, part], q_result.at[:, part], 2 * n)
        send(side_out.at[part], side_result.at[part], 2 * n + 1)
    for copy in leaving:
        copy.wait()


def ratio_at(ratios, depth, level):
    lookup = jnp.broadcast_to(ratios[0:1], depth.shape)
    height = jnp.maximum(depth - level, 0)
    return jnp.take_along_axis(lookup, height, axis=1, mode="promise_in_bounds")


def ratios_by_height(levels, lanes):
    values = [0.0]
    ratio = DEEP_MIX / (1.0 + DEEP_MIX)
    for _ in range(levels):
        values.append(ratio)
        ratio = DEEP_MIX / (1.0 + DEEP_MIX + DEEP_MIX - DEEP_MIX * ratio)
    values += [0.0] * (lanes - len(values))
    return jnp.broadcast_to(jnp.asarray(np.array(values, np.float32)), (8, lanes))


def remap_kernel(
    columns_in, place_from, from_left, from_right, weights, own_fields,
    out, picked, solved, held, fields_in, place, sems,
):
    fields, rows, width = out.shape[0] // 2, out.shape[1], out.shape[2]
    columns = rows - EDGE
    slots = weights.shape[0] // (columns * width)
    tall = slots * width
    many = from_left.shape[0] - tall - EXTRA
    group = 8
    place_copy = pltpu.make_async_copy(place_from, place, sems.at[0])
    fields_copy = pltpu.make_async_copy(own_fields, fields_in, sems.at[1])
    copies = []
    for n in range(columns // group):
        part = pl.ds(n * group * tall, group * tall)
        copies.append(pltpu.make_async_copy(weights.at[part], held.at[part], sems.at[2 + n]))
    for copy in [place_copy] + copies + [fields_copy]:
        copy.start()
    right = from_right[pl.ds(many, EXTRA)].astype(f32)
    left = from_left[pl.ds(many, EXTRA)].astype(f32)
    row = iota((EDGE, 1), 0)
    picked[...] = jnp.zeros_like(picked)
    place_copy.wait()
    wanted = []
    for k in range(slots):
        edge = jnp.where(
            row == 0,
            right[8 + k : 9 + k, 0:1] * PIECE + MOST,
            jnp.where(row == EDGE - 1, left[8 + k : 9 + k, 0:1] * PIECE + MOST + 1, -PIECE),
        ).astype(i32)
        wanted += [place[k * columns : (k + 1) * columns, 0:1], edge]
    wanted = jnp.concatenate(wanted, axis=0)
    spots = iota((slots * rows, columns_in.shape[0]), 1)
    for f in range(fields):
        chosen = jnp.where(spots == wanted + f * SLOTS, 1.0, 0.0).astype(bf16)
        found = jnp.dot(chosen, columns_in[...], preferred_element_type=f32)
        for k in range(slots):
            picked[k, pl.ds(f, rows, stride=8), :] = found[k * rows : (k + 1) * rows]

    def one(row, table_of):
        spot = pl.ds(row * 8, 8)
        vector = jnp.concatenate([picked[k, spot, :] for k in range(slots)], axis=1)
        matrix = jnp.concatenate([table_of(k) for k in range(slots)], axis=1)
        solved[spot, :] = lax.dot_general(
            vector.astype(bf16), matrix, (((1,), (1,)), ((), ())), preferred_element_type=f32
        )

    solved[...] = jnp.zeros_like(solved)
    below = many + EXTRA
    one(columns, lambda k: from_right[pl.ds(below + k * width, width)])
    one(rows - 1, lambda k: from_left[pl.ds(below + k * width, width)])
    for n in range(columns // group):
        copies[n].wait()
        for m in range(group):
            spot = n * group + m
            one(spot, lambda k: held[pl.ds((spot * slots + k) * width, width)])
    fields_copy.wait()
    for f in range(fields):
        out[f, pl.ds(0, columns)] = solved[pl.ds(f, columns, stride=8), :]
        out[f, pl.ds(columns, EDGE)] = solved[pl.ds(columns * 8 + f, EDGE, stride=8), :]
        out[fields + f, pl.ds(0, columns)] = fields_in[f].astype(f32)
        out[fields + f, pl.ds(columns, EDGE)] = edge_tile(
            right[2 + f : 3 + f], left[2 + f : 3 + f]
        )


def finish_kernel(
    section, mine, other, bath, q, side, ratios, surface, result,
    rho, weight, partial_at, done, across, band, sems_out,
):
    tracers, levels, columns, lanes = result.shape
    chunks = chunks_of(levels)
    on_ocean = section[0] == 1
    adjacency(across, band, columns + EDGE)
    flux = [jnp.where(on_ocean, other[f], mine[f]) for f in range(3)]
    own = [jnp.where(on_ocean, mine[3 + f], other[3 + f]) for f in range(3)]
    forcing = [flux[0] + own[0], flux[1] + own[1]]
    top_mix = TOP_MIX * (1.0 + flux[2] * flux[2] + own[2] * own[2])
    depth = bath[...]
    inner_depth = bath[pl.ds(0, columns)]
    unscale = 1.0 / (SCALE * SCALE)

    rho[2] = ratio_at(ratios, depth, 2)
    link = jnp.where(1 < depth, top_mix, 0.0)
    deeper = jnp.where(2 < depth, DEEP_MIX - DEEP_MIX * rho[2], 0.0)
    second = 1.0 / (1.0 + link + deeper)
    rho_second = link * second
    first = 1.0 / (1.0 + link - link * rho_second)

    inner_link = link[:columns]
    top_weight = 1.0 / (1.0 + inner_link)
    top_ratio = inner_link * top_weight
    below_link = jnp.where(2 < inner_depth, DEEP_MIX, 0.0)
    next_weight = 1.0 / (1.0 + top_ratio + below_link)
    weight[1] = DEEP_MIX * next_weight
    next_ratio = below_link * next_weight
    x = (next_ratio - FIXED) / (next_ratio - 1.0 / FIXED)
    base = 1.0 + DEEP_MIX - DEEP_MIX / FIXED
    rise = DEEP_MIX * (1.0 / FIXED - FIXED)

    def half_at(n, level, h):
        around = neighbour_sum(rounded(h), across, band, columns)
        return side[level].astype(f32) * h[:columns] + around

    leaving = []
    for n in range(tracers):
        below = jnp.where(2 < depth, q[n, 2], 0.0)
        partial = 2.0 * (q[n, 1] + below) * second
        source = 2.0 * q[n, 0] + SCALE * FLUX_GAIN * forcing[n]
        value = (source + link * partial) * first
        carry = jnp.where(1 < depth, partial, 0.0) + rho_second * value
        value = jnp.where(0 < depth, value, 0.0)

        source = 2.0 * half_at(n, 0, value)
        source = source + SCALE * SCALE * FLUX_GAIN * forcing[n][:columns]
        top_partial = source * top_weight
        solved = (2.0 * half_at(n, 1, carry) + inner_link * top_partial) * next_weight
        partial_at[1] = solved
        for level in range(2, levels):
            if n == 0:
                if level > 2:
                    rho[level] = ratio_at(ratios, depth, level)
                linked = level + 1 < inner_depth
                divisor = jnp.where(
                    linked, base + DEEP_MIX + rise - (base + DEEP_MIX) * x, base + rise - base * x
                )
                inverse = pl.reciprocal(divisor, approx=True)
                scaled = (DEEP_MIX - DEEP_MIX * x) * inverse
                weight[level] = scaled * (2.0 - divisor * inverse)
                x = (FIXED * FIXED) * x
            carry = jnp.where(level < depth, q[n, level], 0.0) + rho[level] * carry
            solved = weight[level] * (half_at(n, level, carry) + solved)
            partial_at[level] = solved

        value = jnp.zeros((columns, lanes), f32)
        for low, size in reversed(chunks):
            for level in range(low + size - 1, max(low, 1) - 1, -1):
                wet = level < inner_depth
                value = jnp.where(wet, partial_at[level] + weight[level] * value, 0.0)
                start = q[n, level, pl.ds(0, columns)]
                done[n, level] = jnp.where(wet, value * unscale, start)
            if low == 0:
                value = (top_partial + top_ratio * value) * unscale
                done[n, 0] = value
                surface[n] = jnp.where(on_ocean, value, other[n, pl.ds(0, columns)])
            part = pl.ds(low, size)
            leaving.append(
                pltpu.make_async_copy(
                    done.at[n, part], result.at[n, part], sems_out.at[len(leaving)]
                )
            )
            leaving[-1].start()
    surface[2] = jnp.where(on_ocean, top_mix[:columns], other[2, pl.ds(0, columns)])
    for copy in leaving:
        copy.wait()


def shift(value, axis, by):
    count = lax.axis_size(axis)
    return lax.ppermute(value, axis, [(i, (i + by) % count) for i in range(count)])


def in_hbm(value):
    return pltpu.with_memory_space_constraint(value, pltpu.HBM)


def in_vmem(value):
    return pltpu.with_memory_space_constraint(value, pltpu.VMEM)


def per_device(
    surface_fields, source_blocks, source_columns, remap_weights, ocean_state, bathymetry
):
    tracers, levels, columns, lanes = ocean_state.shape
    slots = source_blocks.shape[2]
    count = lax.axis_size("blk")
    rows = columns + EDGE
    section = lax.axis_index("sec").astype(i32).reshape(1)
    fields = surface_fields[0]
    blocks = jnp.transpose(source_blocks[0])
    spots = jnp.transpose(source_columns[0])
    weights = remap_weights[0].reshape(columns * slots * lanes, lanes)
    tall = slots * lanes
    many = tracers * levels

    hbm = pl.BlockSpec(memory_space=pltpu.HBM)
    vmem = pl.BlockSpec(memory_space=pltpu.VMEM)
    smem = pl.BlockSpec(memory_space=pltpu.SMEM)
    shaped = jax.ShapeDtypeStruct
    pieces = len(chunks_of(levels))
    cells = rows * lanes
    tall_rows = rows + -rows % 16

    payload = shaped((2 * many + EXTRA + tall, lanes), bf16)
    to_left, to_right, table, blocks_in, spots_in = pl.pallas_call(
        pack_kernel,
        out_shape=(
            payload,
            payload,
            shaped((FIELDS * columns, lanes), bf16),
            shaped(blocks.shape, i32),
            shaped(spots.shape, i32),
        ),
        in_specs=[smem] + [hbm] * 6,
        out_specs=(vmem,) * 5,
        scratch_shapes=[
            pltpu.VMEM((tracers, levels, 8, lanes), f32),
            pltpu.VMEM((tracers, levels, 8, lanes), f32),
            pltpu.VMEM((tracers, columns, lanes), f32),
            pltpu.VMEM(bathymetry.shape, i32),
            pltpu.VMEM(fields.shape, bf16),
            pltpu.VMEM((EXTRA, lanes), f32),
            pltpu.SemaphoreType.DMA((9,)),
        ],
        compiler_params=pltpu.CompilerParams(vmem_limit_bytes=8 * MIB),
        cost_estimate=pl.CostEstimate(
            flops=10**6, bytes_accessed=4 * 10**6, transcendentals=0
        ),
    )(
        section,
        in_hbm(ocean_state),
        in_hbm(bathymetry),
        in_hbm(fields),
        in_hbm(blocks),
        in_hbm(spots),
        in_hbm(weights),
    )
    request = pl.pallas_call(
        ask_kernel,
        out_shape=shaped((count, 128), i32),
        in_specs=[vmem, vmem],
        out_specs=vmem,
        compiler_params=pltpu.CompilerParams(vmem_limit_bytes=4 * MIB),
        cost_estimate=pl.CostEstimate(flops=10**6, bytes_accessed=10**5, transcendentals=0),
    )(blocks_in, spots_in)
    asked = lax.all_to_all(request, "blk", split_axis=0, concat_axis=0, tiled=True)
    from_left = shift(to_right, "blk", 1)
    from_right = shift(to_left, "blk", -1)

    served = pl.pallas_call(
        serve_kernel,
        out_shape=shaped((count * PIECE, lanes), bf16),
        in_specs=[vmem] * 4,
        out_specs=vmem,
        compiler_params=pltpu.CompilerParams(vmem_limit_bytes=8 * MIB),
        cost_estimate=pl.CostEstimate(
            flops=10**7, bytes_accessed=10**6, transcendentals=0
        ),
    )(asked, table, from_left, from_right)
    columns_in = lax.all_to_all(served, "blk", split_axis=0, concat_axis=0, tiled=True)

    ratios = ratios_by_height(levels, lanes)
    q, side, bath, place = pl.pallas_call(
        functools.partial(start_kernel, count=count),
        out_shape=(
            pltpu.HBM((tracers, levels, rows, lanes), f32),
            pltpu.HBM((levels, columns, lanes), bf16),
            pltpu.HBM((rows, lanes), i32),
            pltpu.HBM((slots * columns, 128), i32),
        ),
        in_specs=[hbm, vmem, vmem, hbm, hbm, vmem],
        out_specs=(hbm,) * 4,
        scratch_shapes=[
            pltpu.VMEM((tracers, levels, rows, lanes), f32),
            pltpu.VMEM((levels, columns, lanes), bf16),
            pltpu.VMEM(ocean_state.shape, f32),
            pltpu.VMEM((rows, lanes), i32),
            pltpu.VMEM((many * 8, lanes), f32),
            pltpu.VMEM(bathymetry.shape, i32),
            pltpu.VMEM(blocks.shape, i32),
            pltpu.VMEM((slots * columns, 128), i32),
            pltpu.VMEM((tall_rows, lanes), bf16),
            pltpu.VMEM((lanes, lanes), bf16),
            pltpu.SemaphoreType.DMA((pieces + 2,)),
            pltpu.SemaphoreType.DMA((2 * pieces + 2,)),
        ],
        compiler_params=pltpu.CompilerParams(vmem_limit_bytes=28 * MIB),
        cost_estimate=pl.CostEstimate(
            flops=60 * levels * cells, bytes_accessed=200 * levels * cells, transcendentals=0
        ),
    )(
        in_hbm(ocean_state),
        from_left,
        from_right,
        in_hbm(bathymetry),
        in_hbm(blocks),
        ratios,
    )

    mine = pl.pallas_call(
        remap_kernel,
        out_shape=shaped((6, rows, lanes), f32),
        in_specs=[vmem, hbm, vmem, vmem, hbm, hbm],
        out_specs=vmem,
        scratch_shapes=[
            pltpu.VMEM((slots, rows * 8, lanes), f32),
            pltpu.VMEM((rows * 8, lanes), f32),
            pltpu.VMEM(weights.shape, bf16),
            pltpu.VMEM(fields.shape, bf16),
            pltpu.VMEM((slots * columns, 128), i32),
            pltpu.SemaphoreType.DMA((2 + columns // 8,)),
        ],
        compiler_params=pltpu.CompilerParams(vmem_limit_bytes=20 * MIB),
        cost_estimate=pl.CostEstimate(
            flops=16 * weights.size, bytes_accessed=2 * weights.size, transcendentals=0
        ),
    )(
        columns_in,
        in_hbm(place),
        from_left,
        from_right,
        in_hbm(weights),
        in_hbm(fields),
    )
    other = lax.ppermute(mine, "sec", [(0, 1), (1, 0)])

    surface, result = pl.pallas_call(
        finish_kernel,
        out_shape=(shaped((3, columns, lanes), f32), shaped(ocean_state.shape, f32)),
        in_specs=[smem] + [vmem] * 6,
        out_specs=(vmem, hbm),
        scratch_shapes=[
            pltpu.VMEM((levels, rows, lanes), f32),
            pltpu.VMEM((levels, columns, lanes), f32),
            pltpu.VMEM((levels, columns, lanes), f32),
            pltpu.VMEM(ocean_state.shape, f32),
            pltpu.VMEM((tall_rows, lanes), bf16),
            pltpu.VMEM((lanes, lanes), bf16),
            pltpu.SemaphoreType.DMA((tracers * pieces,)),
        ],
        compiler_params=pltpu.CompilerParams(vmem_limit_bytes=26 * MIB),
        cost_estimate=pl.CostEstimate(
            flops=60 * levels * cells, bytes_accessed=32 * levels * cells, transcendentals=0
        ),
    )(
        section,
        mine,
        other,
        in_vmem(bath),
        in_vmem(q),
        in_vmem(side),
        ratios,
    )
    return (surface[None], result)


def solution(mesh):
    return jax.shard_map(
        per_device,
        mesh=mesh,
        in_specs=(
            P("sec", None, "blk", None),
            P("sec", "blk", None),
            P("sec", "blk", None),
            P("sec", "blk", None, None, None),
            P(None, None, "blk", None),
            P("blk", None),
        ),
        out_specs=(P("sec", None, "blk", None), P(None, None, "blk", None)),
        check_vma=False,
    )
```

```python
import functools

import jax
import jax.numpy as jnp
import numpy as np
from jax import lax
from jax.experimental import pallas as pl
from jax.experimental.pallas import tpu as pltpu
from jax.sharding import PartitionSpec as P

FLUX_GAIN = 0.5
SIDE_MIX = 0.2
TOP_MIX = 1.0
DEEP_MIX = 2.0
SCALE = 1.0 / (0.5 * SIDE_MIX)

MOST = 16
SLOTS = MOST + 2
FIELDS = 3
PIECE = 56
EDGE = 8
EXTRA = 16
IN_FLIGHT = 3
MIB = 2**20
bf16, f32, i32 = jnp.bfloat16, jnp.float32, jnp.int32


def iota(shape, axis):
    return lax.broadcasted_iota(i32, shape, axis)


def adjacency(across, band, used):
    row, other = iota(across.shape, 0), iota(across.shape, 1)
    near = (row - other == 1) | (other - row == 1)
    near = near | ((row == 0) & (other == used - 1)) | ((row == used - 1) & (other == 0))
    across[...] = jnp.where(near & (row < used) & (other < used), 1.0, 0.0).astype(bf16)
    apart = iota(band.shape, 0) - iota(band.shape, 1)
    band[...] = jnp.where(jnp.abs(apart) == 1, 1.0, 0.0).astype(bf16)


def rounded(h):
    rows = -h.shape[0] % 16
    if rows:
        h = jnp.concatenate([h, jnp.zeros((rows, h.shape[1]), h.dtype)], axis=0)
    return h.astype(bf16)


def neighbour_sum(h, across, band, rows):
    tall, lanes = h.shape
    left = jnp.concatenate([across[pl.ds(0, rows), :], h[:rows]], axis=1)
    gap = jnp.zeros((across.shape[1] - tall, lanes), bf16)
    right = jnp.concatenate([h, gap, band[...]], axis=0)
    return jnp.dot(left, right, preferred_element_type=f32)


def edge_tile(right, left):
    row = iota((EDGE, right.shape[1]), 0)
    return jnp.where(row == 0, right, jnp.where(row == EDGE - 1, left, 0.0))


def chunks_of(levels):
    size = 10 if levels % 10 == 0 else levels
    return [(start, size) for start in range(0, levels, size)]


def sweep(count, body, carry):
    for step in range(count):
        carry = body(step, carry)
    return carry


def ranks(blocks, count):
    slots, columns = blocks.shape
    before = jnp.where(iota((columns, columns), 0) < iota((columns, columns), 1), 1.0, 0.0)
    before = before.astype(bf16)
    used = jnp.zeros((count, 1), f32)
    result = []
    for k in range(slots):
        owner = iota((count, columns), 0) == blocks[k : k + 1, :]
        one_hot = jnp.where(owner, 1.0, 0.0)
        earlier = used + jnp.dot(one_hot.astype(bf16), before, preferred_element_type=f32)
        rank = jnp.sum(one_hot * earlier, axis=0, keepdims=True)
        used = used + jnp.sum(one_hot, axis=1, keepdims=True)
        result.append((owner, rank))
    return result


def ask_kernel(blocks, spots, request):
    count, columns = request.shape[0], blocks.shape[1]
    place = iota((128, columns), 0)
    field = place // SLOTS
    slot = jnp.where(field < FIELDS, place - field * SLOTS, -1)
    here = iota((128, columns), 1)
    marks = ((slot == MOST) & (here == 0)) | ((slot == MOST + 1) & (here == columns - 1))
    asked = jnp.zeros(request.shape, f32)
    for k, (owner, rank) in enumerate(ranks(blocks, count)):
        filled = jnp.where((slot == rank.astype(i32)) | marks, 1.0, 0.0).astype(bf16)
        named = jnp.where(owner, spots[k : k + 1, :].astype(f32), 0.0).astype(bf16)
        asked = asked + lax.dot_general(
            named, filled, (((1,), (1,)), ((), ())), preferred_element_type=f32
        )
    request[...] = asked.astype(i32) + (iota(request.shape, 1) // SLOTS) * columns


def pack_kernel(
    section, state, bath, fields, blocks, spots, weights,
    to_left, to_right, table, blocks_in, spots_in,
    low, high, surface, bath_in, fields_in, extra, sems,
):
    tracers, levels, columns, lanes = state.shape
    slots = blocks.shape[0]
    many = tracers * levels
    wide = to_left.shape[0] - 2 * many - EXTRA
    below = pl.ds(2 * many + EXTRA, wide)
    pairs = [
        (state.at[:, :, pl.ds(0, 8)], low),
        (state.at[:, :, pl.ds(columns - 8, 8)], high),
        (blocks, blocks_in),
        (bath, bath_in),
        (fields, fields_in),
        (state.at[:, 0], surface),
        (weights.at[pl.ds(0, wide)], to_left.at[below]),
        (weights.at[pl.ds((columns - 1) * wide, wide)], to_right.at[below]),
        (spots, spots_in),
    ]
    copies = [pltpu.make_async_copy(src, dst, sems.at[n]) for n, (src, dst) in enumerate(pairs)]
    for copy in copies:
        copy.start()
    for copy in copies[2:6]:
        copy.wait()
    for out, first, at in ((to_left, 0, 0), (to_right, columns - 2, columns - 1)):
        extra[...] = jnp.zeros_like(extra)
        extra[0:2] = bath_in[first : first + 2].astype(f32)
        for f in range(3):
            extra[2 + f : 3 + f] = fields_in[f].astype(f32)[at : at + 1]
        extra[8 : 8 + slots] = jnp.broadcast_to(
            blocks_in[:, at : at + 1].astype(f32), (slots, lanes)
        )
        out[pl.ds(2 * many, EXTRA)] = extra[...].astype(bf16)
    on_ocean = section[0] == 1
    for f in range(3):
        own = fields_in[f]
        if f < 2:
            own = jnp.where(on_ocean, surface[f], own.astype(f32)).astype(bf16)
        table[f * columns : (f + 1) * columns, :] = own
    copies[0].wait()
    copies[1].wait()
    for c in range(2):
        for n in range(tracers):
            part = pl.ds(c * many + n * levels, levels)
            tiles = low.at[n].reshape(levels * 8, lanes)
            to_left[part] = tiles[pl.ds(c, levels, stride=8), :].astype(bf16)
            tiles = high.at[n].reshape(levels * 8, lanes)
            to_right[part] = tiles[pl.ds(6 + c, levels, stride=8), :].astype(bf16)
    for copy in copies[6:]:
        copy.wait()


def serve_kernel(asked, table, from_left, from_right, out):
    count = asked.shape[0]
    height = table.shape[0]
    request = asked[...].astype(f32)
    slot = lax.rem(iota(request.shape, 1), SLOTS)
    request = jnp.where(
        slot == MOST,
        pltpu.roll(request, count - 1, 0),
        jnp.where(slot == MOST + 1, pltpu.roll(request, 1, 0), request),
    )
    wanted = jnp.transpose(request)[:PIECE].astype(i32)
    parts = []
    for e in range(count):
        here = iota((PIECE, height), 1) == wanted[:, e : e + 1]
        parts.append(jnp.where(here, 1.0, 0.0))
    chosen = jnp.concatenate(parts, axis=0).astype(bf16)
    out[...] = jnp.dot(chosen, table[...], preferred_element_type=f32).astype(bf16)


def start_kernel(
    state, from_left, from_right, bath, blocks, ratios,
    q_result, side_result, bath_result, place_result,
    q_out, side_out, held, bath_out, halo, bath_in, blocks_in, place, across, band,
    sems, sems_out, *, count,
):
    tracers, levels, columns, lanes = state.shape
    rows = columns + EDGE
    many = tracers * levels
    chunks = chunks_of(levels)
    copies = []
    for n, (low, size) in enumerate(chunks):
        copies.append(
            pltpu.make_async_copy(
                state.at[:, pl.ds(low, size)], held.at[:, pl.ds(low, size)], sems.at[n]
            )
        )
    bath_copy = pltpu.make_async_copy(bath, bath_in, sems.at[len(chunks)])
    blocks_copy = pltpu.make_async_copy(blocks, blocks_in, sems.at[len(chunks) + 1])
    blocks_copy.start()
    bath_copy.start()
    for copy in reversed(copies[-IN_FLIGHT:]):
        copy.start()
    leaving = []

    def send(source, target, number):
        copy = pltpu.make_async_copy(source, target, sems_out.at[number])
        copy.start()
        leaving.append(copy)

    halo[...] = jnp.zeros_like(halo)
    for c in range(2):
        part = pl.ds(c * many, many)
        halo[pl.ds(c, many, stride=8), :] = from_right[part].astype(f32)
        halo[pl.ds(EDGE - 2 + c, many, stride=8), :] = from_left[part].astype(f32)
    right = from_right[pl.ds(2 * many, EXTRA)].astype(f32)
    left = from_left[pl.ds(2 * many, EXTRA)].astype(f32)
    row = iota((EDGE, lanes), 0)
    edge = jnp.where(
        row == 0,
        right[0:1],
        jnp.where(
            row == 1,
            right[1:2],
            jnp.where(row == EDGE - 2, left[0:1], jnp.where(row == EDGE - 1, left[1:2], 0.0)),
        ),
    )
    bath_copy.wait()
    depth = jnp.concatenate([bath_in[...], edge.astype(i32)], axis=0)
    bath_out[...] = depth
    send(bath_out, bath_result, 2 * len(chunks))
    blocks_copy.wait()
    for k, (_, rank) in enumerate(ranks(blocks_in, count)):
        arrives = blocks_in[k : k + 1, :].astype(f32) * PIECE + rank
        spread = jnp.transpose(jnp.broadcast_to(arrives, (128, columns)))
        place[k * columns : (k + 1) * columns, :] = spread.astype(i32)
    send(place, place_result, 2 * len(chunks) + 1)
    adjacency(across, band, rows)

    def side(level):
        wet = level < bath_out[...]
        starts, masked = [], []
        for n in range(tracers):
            spot = (n * levels + level) * 8
            full = jnp.concatenate([held[n, level], halo[pl.ds(spot, 8), :]], axis=0)
            starts.append(full)
            masked.append(jnp.where(wet, full, 0.0))
        tall = across.shape[0]
        count = neighbour_sum(rounded(jnp.where(wet, 1.0, 0.0)), across, band, tall)[:rows]
        own = 0.5 * SCALE - count
        side_out[level] = own[:columns].astype(bf16)
        halves = []
        for h in masked:
            halves.append(own * h + neighbour_sum(rounded(h), across, band, tall)[:rows])
        return wet, starts, halves

    def deep(step, below, top):
        level = top - step
        wet, starts, halves = side(level)
        rho = ratio_at(ratios, bath_out[...], level)
        solved = []
        for n in range(tracers):
            q = rho * (halves[n] + below[n])
            q_out[n, level] = jnp.where(wet, q, starts[n])
            solved.append(q)
        return tuple(solved)

    carry = tuple(jnp.zeros((rows, lanes), f32) for _ in range(tracers))
    for n in reversed(range(len(chunks))):
        low, size = chunks[n]
        copies[n].wait()
        if n >= IN_FLIGHT:
            copies[n - IN_FLIGHT].start()
        first = max(low, 2)
        top = low + size - 1
        carry = sweep(top - first + 1, functools.partial(deep, top=top), carry)
        if n == 0:
            for level in (1, 0):
                wet, starts, halves = side(level)
                for m in range(tracers):
                    q_out[m, level] = jnp.where(wet, halves[m], starts[m])
        part = pl.ds(low, size)
        send(q_out.at[:, part], q_result.at[:, part], 2 * n)
        send(side_out.at[part], side_result.at[part], 2 * n + 1)
    for copy in leaving:
        copy.wait()


def ratio_at(ratios, depth, level):
    lookup = jnp.broadcast_to(ratios[0:1], depth.shape)
    height = jnp.maximum(depth - level, 0)
    return jnp.take_along_axis(lookup, height, axis=1, mode="promise_in_bounds")


def ratios_by_height(levels, lanes):
    values = [0.0]
    ratio = DEEP_MIX / (1.0 + DEEP_MIX)
    for _ in range(levels):
        values.append(ratio)
        ratio = DEEP_MIX / (1.0 + DEEP_MIX + DEEP_MIX - DEEP_MIX * ratio)
    values += [0.0] * (lanes - len(values))
    return jnp.broadcast_to(jnp.asarray(np.array(values, np.float32)), (8, lanes))


def remap_kernel(
    columns_in, place_from, from_left, from_right, weights, own_fields,
    out, picked, solved, held, fields_in, place, sems,
):
    fields, rows, width = out.shape[0] // 2, out.shape[1], out.shape[2]
    columns = rows - EDGE
    slots = weights.shape[0] // (columns * width)
    tall = slots * width
    many = from_left.shape[0] - tall - EXTRA
    group = 8
    place_copy = pltpu.make_async_copy(place_from, place, sems.at[0])
    fields_copy = pltpu.make_async_copy(own_fields, fields_in, sems.at[1])
    copies = []
    for n in range(columns // group):
        part = pl.ds(n * group * tall, group * tall)
        copies.append(pltpu.make_async_copy(weights.at[part], held.at[part], sems.at[2 + n]))
    for copy in [place_copy, fields_copy] + copies[:IN_FLIGHT]:
        copy.start()
    right = from_right[pl.ds(many, EXTRA)].astype(f32)
    left = from_left[pl.ds(many, EXTRA)].astype(f32)
    row = iota((EDGE, 1), 0)
    picked[...] = jnp.zeros_like(picked)
    place_copy.wait()
    wanted = []
    for k in range(slots):
        edge = jnp.where(
            row == 0,
            right[8 + k : 9 + k, 0:1] * PIECE + MOST,
            jnp.where(row == EDGE - 1, left[8 + k : 9 + k, 0:1] * PIECE + MOST + 1, -PIECE),
        ).astype(i32)
        wanted += [place[k * columns : (k + 1) * columns, 0:1], edge]
    wanted = jnp.concatenate(wanted, axis=0)
    spots = iota((slots * rows, columns_in.shape[0]), 1)
    for f in range(fields):
        chosen = jnp.where(spots == wanted + f * SLOTS, 1.0, 0.0).astype(bf16)
        found = jnp.dot(chosen, columns_in[...], preferred_element_type=f32)
        for k in range(slots):
            picked[k, pl.ds(f, rows, stride=8), :] = found[k * rows : (k + 1) * rows]

    def one(row, table_of):
        spot = pl.ds(row * 8, 8)
        vector = jnp.concatenate([picked[k, spot, :] for k in range(slots)], axis=1)
        matrix = jnp.concatenate([table_of(k) for k in range(slots)], axis=1)
        solved[spot, :] = lax.dot_general(
            vector.astype(bf16), matrix, (((1,), (1,)), ((), ())), preferred_element_type=f32
        )

    solved[...] = jnp.zeros_like(solved)
    below = many + EXTRA
    one(columns, lambda k: from_right[pl.ds(below + k * width, width)])
    one(rows - 1, lambda k: from_left[pl.ds(below + k * width, width)])
    for n in range(columns // group):
        copies[n].wait()
        if n + IN_FLIGHT < len(copies):
            copies[n + IN_FLIGHT].start()
        for m in range(group):
            spot = n * group + m
            one(spot, lambda k: held[pl.ds((spot * slots + k) * width, width)])
    fields_copy.wait()
    for f in range(fields):
        out[f, pl.ds(0, columns)] = solved[pl.ds(f, columns, stride=8), :]
        out[f, pl.ds(columns, EDGE)] = solved[pl.ds(columns * 8 + f, EDGE, stride=8), :]
        out[fields + f, pl.ds(0, columns)] = fields_in[f].astype(f32)
        out[fields + f, pl.ds(columns, EDGE)] = edge_tile(
            right[2 + f : 3 + f], left[2 + f : 3 + f]
        )


def finish_kernel(
    section, mine, other, bath, q, side, ratios, surface, result,
    values_at, rounded_at, rho, solved, done, across, band, sems_out,
):
    tracers, levels, columns, lanes = result.shape
    chunks = chunks_of(levels)
    on_ocean = section[0] == 1
    adjacency(across, band, columns + EDGE)
    flux = [jnp.where(on_ocean, other[f], mine[f]) for f in range(3)]
    own = [jnp.where(on_ocean, mine[3 + f], other[3 + f]) for f in range(3)]
    forcing = [flux[0] + own[0], flux[1] + own[1]]
    top_mix = TOP_MIX * (1.0 + flux[2] * flux[2] + own[2] * own[2])
    depth = bath[...]
    unscale = 1.0 / (SCALE * SCALE)

    rho[2] = ratio_at(ratios, depth, 2)
    link = jnp.where(1 < depth, top_mix, 0.0)
    deeper = jnp.where(2 < depth, DEEP_MIX - DEEP_MIX * rho[2], 0.0)
    second = 1.0 / (1.0 + link + deeper)
    rho_second = link * second
    first = 1.0 / (1.0 + link - link * rho_second)

    def top_levels(n, count, halves, below, scale):
        partial = 2.0 * (halves[1] + below) * second[:count]
        source = 2.0 * halves[0] + scale * FLUX_GAIN * forcing[n][:count]
        value = (source + link[:count] * partial) * first[:count]
        below = jnp.where(1 < depth[:count], partial, 0.0) + rho_second[:count] * value
        return value, below

    def put(n, level, h):
        values_at[n, level] = h[:columns]
        rounded_at[n, level] = rounded(h)

    def half_at(n, level):
        around = neighbour_sum(rounded_at[n, level], across, band, columns)
        return side[level].astype(f32) * values_at[n, level] + around

    leaving = []
    for n in range(tracers):
        below = jnp.where(2 < depth, q[n, 2], 0.0)
        value, carry = top_levels(n, columns + EDGE, (q[n, 0], q[n, 1]), below, SCALE)
        put(n, 0, jnp.where(0 < depth, value, 0.0))
        put(n, 1, carry)
        for level in range(2, levels):
            if n == 0 and level > 2:
                rho[level] = ratio_at(ratios, depth, level)
            carry = jnp.where(level < depth, q[n, level], 0.0) + rho[level] * carry
            put(n, level, carry)

        carry = jnp.zeros((columns, lanes), f32)
        for level in range(levels - 1, 1, -1):
            carry = rho[level, pl.ds(0, columns)] * (half_at(n, level) + carry)
            solved[n, level] = carry

        value, carry = top_levels(
            n, columns, (half_at(n, 0), half_at(n, 1)), carry, SCALE * SCALE
        )
        surface[n] = jnp.where(on_ocean, value * unscale, other[n, pl.ds(0, columns)])
        done[n, 0] = value * unscale
        for low, size in chunks:
            for level in range(max(low, 1), low + size):
                if level > 1:
                    carry = solved[n, level] + rho[level, pl.ds(0, columns)] * carry
                start = q[n, level, pl.ds(0, columns)]
                done[n, level] = jnp.where(level < depth[:columns], carry * unscale, start)
            part = pl.ds(low, size)
            leaving.append(
                pltpu.make_async_copy(
                    done.at[n, part], result.at[n, part], sems_out.at[len(leaving)]
                )
            )
            leaving[-1].start()
    surface[2] = jnp.where(on_ocean, top_mix[:columns], other[2, pl.ds(0, columns)])
    for copy in leaving:
        copy.wait()


def shift(value, axis, by):
    count = lax.axis_size(axis)
    return lax.ppermute(value, axis, [(i, (i + by) % count) for i in range(count)])


def in_hbm(value):
    return pltpu.with_memory_space_constraint(value, pltpu.HBM)


def in_vmem(value):
    return pltpu.with_memory_space_constraint(value, pltpu.VMEM)


def per_device(
    surface_fields, source_blocks, source_columns, remap_weights, ocean_state, bathymetry
):
    tracers, levels, columns, lanes = ocean_state.shape
    slots = source_blocks.shape[2]
    count = lax.axis_size("blk")
    rows = columns + EDGE
    section = lax.axis_index("sec").astype(i32).reshape(1)
    fields = surface_fields[0]
    blocks = jnp.transpose(source_blocks[0])
    spots = jnp.transpose(source_columns[0])
    weights = remap_weights[0].reshape(columns * slots * lanes, lanes)
    tall = slots * lanes
    many = tracers * levels

    hbm = pl.BlockSpec(memory_space=pltpu.HBM)
    vmem = pl.BlockSpec(memory_space=pltpu.VMEM)
    smem = pl.BlockSpec(memory_space=pltpu.SMEM)
    shaped = jax.ShapeDtypeStruct
    pieces = len(chunks_of(levels))
    cells = rows * lanes
    tall_rows = rows + -rows % 16

    payload = shaped((2 * many + EXTRA + tall, lanes), bf16)
    to_left, to_right, table, blocks_in, spots_in = pl.pallas_call(
        pack_kernel,
        out_shape=(
            payload,
            payload,
            shaped((FIELDS * columns, lanes), bf16),
            shaped(blocks.shape, i32),
            shaped(spots.shape, i32),
        ),
        in_specs=[smem] + [hbm] * 6,
        out_specs=(vmem,) * 5,
        scratch_shapes=[
            pltpu.VMEM((tracers, levels, 8, lanes), f32),
            pltpu.VMEM((tracers, levels, 8, lanes), f32),
            pltpu.VMEM((tracers, columns, lanes), f32),
            pltpu.VMEM(bathymetry.shape, i32),
            pltpu.VMEM(fields.shape, bf16),
            pltpu.VMEM((EXTRA, lanes), f32),
            pltpu.SemaphoreType.DMA((9,)),
        ],
        compiler_params=pltpu.CompilerParams(vmem_limit_bytes=8 * MIB),
        cost_estimate=pl.CostEstimate(
            flops=10**6, bytes_accessed=4 * 10**6, transcendentals=0
        ),
    )(
        section,
        in_hbm(ocean_state),
        in_hbm(bathymetry),
        in_hbm(fields),
        in_hbm(blocks),
        in_hbm(spots),
        in_hbm(weights),
    )
    request = pl.pallas_call(
        ask_kernel,
        out_shape=shaped((count, 128), i32),
        in_specs=[vmem, vmem],
        out_specs=vmem,
        compiler_params=pltpu.CompilerParams(vmem_limit_bytes=4 * MIB),
        cost_estimate=pl.CostEstimate(flops=10**6, bytes_accessed=10**5, transcendentals=0),
    )(blocks_in, spots_in)
    asked = lax.all_to_all(request, "blk", split_axis=0, concat_axis=0, tiled=True)
    from_left = shift(to_right, "blk", 1)
    from_right = shift(to_left, "blk", -1)

    served = pl.pallas_call(
        serve_kernel,
        out_shape=shaped((count * PIECE, lanes), bf16),
        in_specs=[vmem] * 4,
        out_specs=vmem,
        compiler_params=pltpu.CompilerParams(vmem_limit_bytes=8 * MIB),
        cost_estimate=pl.CostEstimate(
            flops=10**7, bytes_accessed=10**6, transcendentals=0
        ),
    )(asked, table, from_left, from_right)
    columns_in = lax.all_to_all(served, "blk", split_axis=0, concat_axis=0, tiled=True)

    ratios = ratios_by_height(levels, lanes)
    q, side, bath, place = pl.pallas_call(
        functools.partial(start_kernel, count=count),
        out_shape=(
            pltpu.HBM((tracers, levels, rows, lanes), f32),
            pltpu.HBM((levels, columns, lanes), bf16),
            pltpu.HBM((rows, lanes), i32),
            pltpu.HBM((slots * columns, 128), i32),
        ),
        in_specs=[hbm, vmem, vmem, hbm, hbm, vmem],
        out_specs=(hbm,) * 4,
        scratch_shapes=[
            pltpu.VMEM((tracers, levels, rows, lanes), f32),
            pltpu.VMEM((levels, columns, lanes), bf16),
            pltpu.VMEM(ocean_state.shape, f32),
            pltpu.VMEM((rows, lanes), i32),
            pltpu.VMEM((many * 8, lanes), f32),
            pltpu.VMEM(bathymetry.shape, i32),
            pltpu.VMEM(blocks.shape, i32),
            pltpu.VMEM((slots * columns, 128), i32),
            pltpu.VMEM((tall_rows, lanes), bf16),
            pltpu.VMEM((lanes, lanes), bf16),
            pltpu.SemaphoreType.DMA((pieces + 2,)),
            pltpu.SemaphoreType.DMA((2 * pieces + 2,)),
        ],
        compiler_params=pltpu.CompilerParams(vmem_limit_bytes=28 * MIB),
        cost_estimate=pl.CostEstimate(
            flops=60 * levels * cells, bytes_accessed=200 * levels * cells, transcendentals=0
        ),
    )(
        in_hbm(ocean_state),
        from_left,
        from_right,
        in_hbm(bathymetry),
        in_hbm(blocks),
        ratios,
    )

    mine = pl.pallas_call(
        remap_kernel,
        out_shape=shaped((6, rows, lanes), f32),
        in_specs=[vmem, hbm, vmem, vmem, hbm, hbm],
        out_specs=vmem,
        scratch_shapes=[
            pltpu.VMEM((slots, rows * 8, lanes), f32),
            pltpu.VMEM((rows * 8, lanes), f32),
            pltpu.VMEM(weights.shape, bf16),
            pltpu.VMEM(fields.shape, bf16),
            pltpu.VMEM((slots * columns, 128), i32),
            pltpu.SemaphoreType.DMA((2 + columns // 8,)),
        ],
        compiler_params=pltpu.CompilerParams(vmem_limit_bytes=20 * MIB),
        cost_estimate=pl.CostEstimate(
            flops=16 * weights.size, bytes_accessed=2 * weights.size, transcendentals=0
        ),
    )(
        columns_in,
        in_hbm(place),
        from_left,
        from_right,
        in_hbm(weights),
        in_hbm(fields),
    )
    other = lax.ppermute(mine, "sec", [(0, 1), (1, 0)])

    surface, result = pl.pallas_call(
        finish_kernel,
        out_shape=(shaped((3, columns, lanes), f32), shaped(ocean_state.shape, f32)),
        in_specs=[smem] + [vmem] * 6,
        out_specs=(vmem, hbm),
        scratch_shapes=[
            pltpu.VMEM(ocean_state.shape, f32),
            pltpu.VMEM((tracers, levels, tall_rows, lanes), bf16),
            pltpu.VMEM((levels, rows, lanes), f32),
            pltpu.VMEM(ocean_state.shape, f32),
            pltpu.VMEM(ocean_state.shape, f32),
            pltpu.VMEM((tall_rows, lanes), bf16),
            pltpu.VMEM((lanes, lanes), bf16),
            pltpu.SemaphoreType.DMA((tracers * pieces,)),
        ],
        compiler_params=pltpu.CompilerParams(vmem_limit_bytes=26 * MIB),
        cost_estimate=pl.CostEstimate(
            flops=60 * levels * cells, bytes_accessed=32 * levels * cells, transcendentals=0
        ),
    )(
        section,
        mine,
        other,
        in_vmem(bath),
        in_vmem(q),
        in_vmem(side),
        ratios,
    )
    return (surface[None], result)


def solution(mesh):
    return jax.shard_map(
        per_device,
        mesh=mesh,
        in_specs=(
            P("sec", None, "blk", None),
            P("sec", "blk", None),
            P("sec", "blk", None),
            P("sec", "blk", None, None, None),
            P(None, None, "blk", None),
            P("blk", None),
        ),
        out_specs=(P("sec", None, "blk", None), P(None, None, "blk", None)),
        check_vma=False,
    )
```

```python
import functools

import jax
import jax.numpy as jnp
import numpy as np
from jax import lax
from jax.experimental import pallas as pl
from jax.experimental.pallas import tpu as pltpu
from jax.sharding import PartitionSpec as P

FLUX_GAIN = 0.5
SIDE_MIX = 0.2
TOP_MIX = 1.0
DEEP_MIX = 2.0
SCALE = 1.0 / (0.5 * SIDE_MIX)

MOST = 16
SLOTS = MOST + 2
FIELDS = 3
PIECE = 56
EDGE = 8
EXTRA = 16
MIB = 2**20
bf16, f32, i32 = jnp.bfloat16, jnp.float32, jnp.int32


def iota(shape, axis):
    return lax.broadcasted_iota(i32, shape, axis)


def adjacency(across, band, used):
    row, other = iota(across.shape, 0), iota(across.shape, 1)
    near = (row - other == 1) | (other - row == 1)
    near = near | ((row == 0) & (other == used - 1)) | ((row == used - 1) & (other == 0))
    across[...] = jnp.where(near & (row < used) & (other < used), 1.0, 0.0).astype(bf16)
    apart = iota(band.shape, 0) - iota(band.shape, 1)
    band[...] = jnp.where(jnp.abs(apart) == 1, 1.0, 0.0).astype(bf16)


def rounded(h):
    rows = -h.shape[0] % 16
    if rows:
        h = jnp.concatenate([h, jnp.zeros((rows, h.shape[1]), h.dtype)], axis=0)
    return h.astype(bf16)


def neighbour_sum(h, across, band, rows):
    tall, lanes = h.shape
    left = jnp.concatenate([across[pl.ds(0, rows), :], h[:rows]], axis=1)
    gap = jnp.zeros((across.shape[1] - tall, lanes), bf16)
    right = jnp.concatenate([h, gap, band[...]], axis=0)
    return jnp.dot(left, right, preferred_element_type=f32)


def edge_tile(right, left):
    row = iota((EDGE, right.shape[1]), 0)
    return jnp.where(row == 0, right, jnp.where(row == EDGE - 1, left, 0.0))


def chunks_of(levels):
    size = 10 if levels % 10 == 0 else levels
    return [(start, size) for start in range(0, levels, size)]


def sweep(count, body, carry):
    for step in range(count):
        carry = body(step, carry)
    return carry


def ranks(blocks, count):
    slots, columns = blocks.shape
    before = jnp.where(iota((columns, columns), 0) < iota((columns, columns), 1), 1.0, 0.0)
    before = before.astype(bf16)
    used = jnp.zeros((count, 1), f32)
    result = []
    for k in range(slots):
        owner = iota((count, columns), 0) == blocks[k : k + 1, :]
        one_hot = jnp.where(owner, 1.0, 0.0)
        earlier = used + jnp.dot(one_hot.astype(bf16), before, preferred_element_type=f32)
        rank = jnp.sum(one_hot * earlier, axis=0, keepdims=True)
        used = used + jnp.sum(one_hot, axis=1, keepdims=True)
        result.append((owner, rank))
    return result


def ask_kernel(blocks, spots, request):
    count, columns = request.shape[0], blocks.shape[1]
    place = iota((128, columns), 0)
    field = place // SLOTS
    slot = jnp.where(field < FIELDS, place - field * SLOTS, -1)
    here = iota((128, columns), 1)
    marks = ((slot == MOST) & (here == 0)) | ((slot == MOST + 1) & (here == columns - 1))
    asked = jnp.zeros(request.shape, f32)
    for k, (owner, rank) in enumerate(ranks(blocks, count)):
        filled = jnp.where((slot == rank.astype(i32)) | marks, 1.0, 0.0).astype(bf16)
        named = jnp.where(owner, spots[k : k + 1, :].astype(f32), 0.0).astype(bf16)
        asked = asked + lax.dot_general(
            named, filled, (((1,), (1,)), ((), ())), preferred_element_type=f32
        )
    request[...] = asked.astype(i32) + (iota(request.shape, 1) // SLOTS) * columns


def pack_kernel(
    section, state, bath, fields, blocks, spots, weights,
    to_left, to_right, table, blocks_in, spots_in,
    low, high, surface, bath_in, fields_in, extra, sems,
):
    tracers, levels, columns, lanes = state.shape
    slots = blocks.shape[0]
    many = tracers * levels
    wide = to_left.shape[0] - 2 * many - EXTRA
    below = pl.ds(2 * many + EXTRA, wide)
    pairs = [
        (state.at[:, :, pl.ds(0, 8)], low),
        (state.at[:, :, pl.ds(columns - 8, 8)], high),
        (blocks, blocks_in),
        (bath, bath_in),
        (fields, fields_in),
        (state.at[:, 0], surface),
        (weights.at[pl.ds(0, wide)], to_left.at[below]),
        (weights.at[pl.ds((columns - 1) * wide, wide)], to_right.at[below]),
        (spots, spots_in),
    ]
    copies = [pltpu.make_async_copy(src, dst, sems.at[n]) for n, (src, dst) in enumerate(pairs)]
    for copy in copies:
        copy.start()
    for copy in copies[2:6]:
        copy.wait()
    for out, first, at in ((to_left, 0, 0), (to_right, columns - 2, columns - 1)):
        extra[...] = jnp.zeros_like(extra)
        extra[0:2] = bath_in[first : first + 2].astype(f32)
        for f in range(3):
            extra[2 + f : 3 + f] = fields_in[f].astype(f32)[at : at + 1]
        extra[8 : 8 + slots] = jnp.broadcast_to(
            blocks_in[:, at : at + 1].astype(f32), (slots, lanes)
        )
        out[pl.ds(2 * many, EXTRA)] = extra[...].astype(bf16)
    on_ocean = section[0] == 1
    for f in range(3):
        own = fields_in[f]
        if f < 2:
            own = jnp.where(on_ocean, surface[f], own.astype(f32)).astype(bf16)
        table[f * columns : (f + 1) * columns, :] = own
    copies[0].wait()
    copies[1].wait()
    for c in range(2):
        for n in range(tracers):
            part = pl.ds(c * many + n * levels, levels)
            tiles = low.at[n].reshape(levels * 8, lanes)
            to_left[part] = tiles[pl.ds(c, levels, stride=8), :].astype(bf16)
            tiles = high.at[n].reshape(levels * 8, lanes)
            to_right[part] = tiles[pl.ds(6 + c, levels, stride=8), :].astype(bf16)
    for copy in copies[6:]:
        copy.wait()


def serve_kernel(asked, table, from_left, from_right, out):
    count = asked.shape[0]
    height = table.shape[0]
    request = asked[...].astype(f32)
    slot = lax.rem(iota(request.shape, 1), SLOTS)
    request = jnp.where(
        slot == MOST,
        pltpu.roll(request, count - 1, 0),
        jnp.where(slot == MOST + 1, pltpu.roll(request, 1, 0), request),
    )
    wanted = jnp.transpose(request)[:PIECE].astype(i32)
    parts = []
    for e in range(count):
        here = iota((PIECE, height), 1) == wanted[:, e : e + 1]
        parts.append(jnp.where(here, 1.0, 0.0))
    chosen = jnp.concatenate(parts, axis=0).astype(bf16)
    out[...] = jnp.dot(chosen, table[...], preferred_element_type=f32).astype(bf16)


def start_kernel(
    state, from_left, from_right, bath, blocks, ratios,
    q_result, rho_result, side_result, bath_result, place_result,
    q_out, rho_out, side_out, held, bath_out, halo, bath_in, blocks_in, place, across, band,
    sems, sems_out, *, count,
):
    tracers, levels, columns, lanes = state.shape
    rows = columns + EDGE
    many = tracers * levels
    chunks = chunks_of(levels)
    copies = []
    for n, (low, size) in enumerate(chunks):
        copies.append(
            pltpu.make_async_copy(
                state.at[:, pl.ds(low, size)], held.at[:, pl.ds(low, size)], sems.at[n]
            )
        )
    bath_copy = pltpu.make_async_copy(bath, bath_in, sems.at[len(chunks)])
    blocks_copy = pltpu.make_async_copy(blocks, blocks_in, sems.at[len(chunks) + 1])
    blocks_copy.start()
    bath_copy.start()
    for copy in reversed(copies):
        copy.start()
    leaving = []

    def send(source, target, number):
        copy = pltpu.make_async_copy(source, target, sems_out.at[number])
        copy.start()
        leaving.append(copy)

    halo[...] = jnp.zeros_like(halo)
    for c in range(2):
        part = pl.ds(c * many, many)
        halo[pl.ds(c, many, stride=8), :] = from_right[part].astype(f32)
        halo[pl.ds(EDGE - 2 + c, many, stride=8), :] = from_left[part].astype(f32)
    right = from_right[pl.ds(2 * many, EXTRA)].astype(f32)
    left = from_left[pl.ds(2 * many, EXTRA)].astype(f32)
    row = iota((EDGE, lanes), 0)
    edge = jnp.where(
        row == 0,
        right[0:1],
        jnp.where(
            row == 1,
            right[1:2],
            jnp.where(row == EDGE - 2, left[0:1], jnp.where(row == EDGE - 1, left[1:2], 0.0)),
        ),
    )
    bath_copy.wait()
    depth = jnp.concatenate([bath_in[...], edge.astype(i32)], axis=0)
    bath_out[...] = depth
    send(bath_out, bath_result, 3 * len(chunks))
    blocks_copy.wait()
    for k, (_, rank) in enumerate(ranks(blocks_in, count)):
        arrives = blocks_in[k : k + 1, :].astype(f32) * PIECE + rank
        spread = jnp.transpose(jnp.broadcast_to(arrives, (128, columns)))
        place[k * columns : (k + 1) * columns, :] = spread.astype(i32)
    send(place, place_result, 3 * len(chunks) + 1)
    adjacency(across, band, rows)

    def side(level):
        wet = level < bath_out[...]
        masked = []
        for n in range(tracers):
            spot = (n * levels + level) * 8
            full = jnp.concatenate([held[n, level], halo[pl.ds(spot, 8), :]], axis=0)
            masked.append(jnp.where(wet, full, 0.0))
        tall = across.shape[0]
        count = neighbour_sum(rounded(jnp.where(wet, 1.0, 0.0)), across, band, tall)[:rows]
        own = 0.5 * SCALE - count
        side_out[level] = own[:columns].astype(bf16)
        halves = []
        for h in masked:
            halves.append(own * h + neighbour_sum(rounded(h), across, band, tall)[:rows])
        return halves

    def deep(step, below, top):
        level = top - step
        halves = side(level)
        rho = ratio_at(ratios, bath_out[...], level)
        rho_out[level] = rho
        solved = []
        for n in range(tracers):
            q = rho * (halves[n] + below[n])
            q_out[n, level] = q
            solved.append(q)
        return tuple(solved)

    carry = tuple(jnp.zeros((rows, lanes), f32) for _ in range(tracers))
    for n in reversed(range(len(chunks))):
        low, size = chunks[n]
        copies[n].wait()
        first = max(low, 2)
        top = low + size - 1
        carry = sweep(top - first + 1, functools.partial(deep, top=top), carry)
        if n == 0:
            for level in (1, 0):
                halves = side(level)
                rho_out[level] = jnp.zeros((rows, lanes), f32)
                for m in range(tracers):
                    q_out[m, level] = halves[m]
        part = pl.ds(low, size)
        send(q_out.at[:, part], q_result.at[:, part], 3 * n)
        send(rho_out.at[part], rho_result.at[part], 3 * n + 1)
        send(side_out.at[part], side_result.at[part], 3 * n + 2)
    for copy in leaving:
        copy.wait()


def ratio_at(ratios, depth, level):
    lookup = jnp.broadcast_to(ratios[0:1], depth.shape)
    height = jnp.maximum(depth - level, 0)
    return jnp.take_along_axis(lookup, height, axis=1, mode="promise_in_bounds")


def ratios_by_height(levels, lanes):
    values = [0.0]
    ratio = DEEP_MIX / (1.0 + DEEP_MIX)
    for _ in range(levels):
        values.append(ratio)
        ratio = DEEP_MIX / (1.0 + DEEP_MIX + DEEP_MIX - DEEP_MIX * ratio)
    values += [0.0] * (lanes - len(values))
    return jnp.broadcast_to(jnp.asarray(np.array(values, np.float32)), (8, lanes))


def remap_kernel(
    columns_in, place_from, from_left, from_right, weights, own_fields,
    out, picked, solved, held, fields_in, place, sems,
):
    fields, rows, width = out.shape[0] // 2, out.shape[1], out.shape[2]
    columns = rows - EDGE
    slots = weights.shape[0] // (columns * width)
    tall = slots * width
    many = from_left.shape[0] - tall - EXTRA
    group = 4
    place_copy = pltpu.make_async_copy(place_from, place, sems.at[0])
    fields_copy = pltpu.make_async_copy(own_fields, fields_in, sems.at[1])
    copies = []
    for n in range(columns // group):
        part = pl.ds(n * group * tall, group * tall)
        copies.append(pltpu.make_async_copy(weights.at[part], held.at[part], sems.at[2 + n]))
    for copy in [place_copy] + copies + [fields_copy]:
        copy.start()
    right = from_right[pl.ds(many, EXTRA)].astype(f32)
    left = from_left[pl.ds(many, EXTRA)].astype(f32)
    row = iota((EDGE, 1), 0)
    picked[...] = jnp.zeros_like(picked)
    place_copy.wait()
    wanted = []
    for k in range(slots):
        edge = jnp.where(
            row == 0,
            right[8 + k : 9 + k, 0:1] * PIECE + MOST,
            jnp.where(row == EDGE - 1, left[8 + k : 9 + k, 0:1] * PIECE + MOST + 1, -PIECE),
        ).astype(i32)
        wanted += [place[k * columns : (k + 1) * columns, 0:1], edge]
    wanted = jnp.concatenate(wanted, axis=0)
    spots = iota((slots * rows, columns_in.shape[0]), 1)
    for f in range(fields):
        chosen = jnp.where(spots == wanted + f * SLOTS, 1.0, 0.0).astype(bf16)
        found = jnp.dot(chosen, columns_in[...], preferred_element_type=f32)
        for k in range(slots):
            picked[k, pl.ds(f, rows, stride=8), :] = found[k * rows : (k + 1) * rows]

    def one(row, table_of):
        spot = pl.ds(row * 8, 8)
        vector = jnp.concatenate([picked[k, spot, :] for k in range(slots)], axis=1)
        matrix = jnp.concatenate([table_of(k) for k in range(slots)], axis=1)
        solved[spot, :] = lax.dot_general(
            vector.astype(bf16), matrix, (((1,), (1,)), ((), ())), preferred_element_type=f32
        )

    solved[...] = jnp.zeros_like(solved)
    below = many + EXTRA
    one(columns, lambda k: from_right[pl.ds(below + k * width, width)])
    one(rows - 1, lambda k: from_left[pl.ds(below + k * width, width)])
    for n in range(columns // group):
        copies[n].wait()
        for m in range(group):
            spot = n * group + m
            one(spot, lambda k: held[pl.ds((spot * slots + k) * width, width)])
    fields_copy.wait()
    for f in range(fields):
        out[f, pl.ds(0, columns)] = solved[pl.ds(f, columns, stride=8), :]
        out[f, pl.ds(columns, EDGE)] = solved[pl.ds(columns * 8 + f, EDGE, stride=8), :]
        out[fields + f, pl.ds(0, columns)] = fields_in[f].astype(f32)
        out[fields + f, pl.ds(columns, EDGE)] = edge_tile(
            right[2 + f : 3 + f], left[2 + f : 3 + f]
        )


def finish_kernel(
    section, mine, other, bath, q, rho, side, state, surface, result,
    values_at, rounded_at, solved, done, across, band, sems, sems_out,
):
    tracers, levels, columns, lanes = result.shape
    chunks = chunks_of(levels)
    starts = []
    for n in range(tracers):
        for low, size in chunks:
            part = pl.ds(low, size)
            starts.append(
                pltpu.make_async_copy(
                    state.at[n, part], done.at[n, part], sems.at[len(starts)]
                )
            )
            starts[-1].start()
    on_ocean = section[0] == 1
    adjacency(across, band, columns + EDGE)
    flux = [jnp.where(on_ocean, other[f], mine[f]) for f in range(3)]
    own = [jnp.where(on_ocean, mine[3 + f], other[3 + f]) for f in range(3)]
    forcing = [flux[0] + own[0], flux[1] + own[1]]
    top_mix = TOP_MIX * (1.0 + flux[2] * flux[2] + own[2] * own[2])
    depth = bath[...]
    unscale = 1.0 / (SCALE * SCALE)

    link = jnp.where(1 < depth, top_mix, 0.0)
    deeper = jnp.where(2 < depth, DEEP_MIX - DEEP_MIX * rho[2], 0.0)
    second = 1.0 / (1.0 + link + deeper)
    rho_second = link * second
    first = 1.0 / (1.0 + link - link * rho_second)

    def top_levels(n, count, halves, below, scale):
        partial = 2.0 * (halves[1] + below) * second[:count]
        source = 2.0 * halves[0] + scale * FLUX_GAIN * forcing[n][:count]
        value = (source + link[:count] * partial) * first[:count]
        below = jnp.where(1 < depth[:count], partial, 0.0) + rho_second[:count] * value
        return value, below

    def put(n, level, h):
        values_at[n, level] = h[:columns]
        rounded_at[n, level] = rounded(h)

    def half_at(n, level):
        around = neighbour_sum(rounded_at[n, level], across, band, columns)
        return side[level].astype(f32) * values_at[n, level] + around

    leaving = []
    for n in range(tracers):
        value, carry = top_levels(n, columns + EDGE, (q[n, 0], q[n, 1]), q[n, 2], SCALE)
        put(n, 0, jnp.where(0 < depth, value, 0.0))
        put(n, 1, carry)
        for level in range(2, levels):
            carry = q[n, level] + rho[level] * carry
            put(n, level, carry)

        carry = jnp.zeros((columns, lanes), f32)
        for level in range(levels - 1, 1, -1):
            carry = rho[level, pl.ds(0, columns)] * (half_at(n, level) + carry)
            solved[n, level] = carry

        value, carry = top_levels(
            n, columns, (half_at(n, 0), half_at(n, 1)), carry, SCALE * SCALE
        )
        surface[n] = jnp.where(on_ocean, value * unscale, other[n, pl.ds(0, columns)])
        for copy in starts[n * len(chunks) : (n + 1) * len(chunks)]:
            copy.wait()
        done[n, 0] = value * unscale
        for low, size in chunks:
            for level in range(max(low, 1), low + size):
                if level > 1:
                    carry = solved[n, level] + rho[level, pl.ds(0, columns)] * carry
                wet = level < depth[:columns]
                done[n, level] = jnp.where(wet, carry * unscale, done[n, level])
            part = pl.ds(low, size)
            leaving.append(
                pltpu.make_async_copy(
                    done.at[n, part], result.at[n, part], sems_out.at[len(leaving)]
                )
            )
            leaving[-1].start()
    surface[2] = jnp.where(on_ocean, top_mix[:columns], other[2, pl.ds(0, columns)])
    for copy in leaving:
        copy.wait()


def shift(value, axis, by):
    count = lax.axis_size(axis)
    return lax.ppermute(value, axis, [(i, (i + by) % count) for i in range(count)])


def in_hbm(value):
    return pltpu.with_memory_space_constraint(value, pltpu.HBM)


def in_vmem(value):
    return pltpu.with_memory_space_constraint(value, pltpu.VMEM)


def per_device(
    surface_fields, source_blocks, source_columns, remap_weights, ocean_state, bathymetry
):
    tracers, levels, columns, lanes = ocean_state.shape
    slots = source_blocks.shape[2]
    count = lax.axis_size("blk")
    rows = columns + EDGE
    section = lax.axis_index("sec").astype(i32).reshape(1)
    fields = surface_fields[0]
    blocks = jnp.transpose(source_blocks[0])
    spots = jnp.transpose(source_columns[0])
    weights = remap_weights[0].reshape(columns * slots * lanes, lanes)
    tall = slots * lanes
    many = tracers * levels

    hbm = pl.BlockSpec(memory_space=pltpu.HBM)
    vmem = pl.BlockSpec(memory_space=pltpu.VMEM)
    smem = pl.BlockSpec(memory_space=pltpu.SMEM)
    shaped = jax.ShapeDtypeStruct
    pieces = len(chunks_of(levels))
    cells = rows * lanes
    tall_rows = rows + -rows % 16

    payload = shaped((2 * many + EXTRA + tall, lanes), bf16)
    to_left, to_right, table, blocks_in, spots_in = pl.pallas_call(
        pack_kernel,
        out_shape=(
            payload,
            payload,
            shaped((FIELDS * columns, lanes), bf16),
            shaped(blocks.shape, i32),
            shaped(spots.shape, i32),
        ),
        in_specs=[smem] + [hbm] * 6,
        out_specs=(vmem,) * 5,
        scratch_shapes=[
            pltpu.VMEM((tracers, levels, 8, lanes), f32),
            pltpu.VMEM((tracers, levels, 8, lanes), f32),
            pltpu.VMEM((tracers, columns, lanes), f32),
            pltpu.VMEM(bathymetry.shape, i32),
            pltpu.VMEM(fields.shape, bf16),
            pltpu.VMEM((EXTRA, lanes), f32),
            pltpu.SemaphoreType.DMA((9,)),
        ],
        compiler_params=pltpu.CompilerParams(vmem_limit_bytes=8 * MIB),
        cost_estimate=pl.CostEstimate(
            flops=10**6, bytes_accessed=4 * 10**6, transcendentals=0
        ),
    )(
        section,
        in_hbm(ocean_state),
        in_hbm(bathymetry),
        in_hbm(fields),
        in_hbm(blocks),
        in_hbm(spots),
        in_hbm(weights),
    )
    request = pl.pallas_call(
        ask_kernel,
        out_shape=shaped((count, 128), i32),
        in_specs=[vmem, vmem],
        out_specs=vmem,
        compiler_params=pltpu.CompilerParams(vmem_limit_bytes=4 * MIB),
        cost_estimate=pl.CostEstimate(flops=10**6, bytes_accessed=10**5, transcendentals=0),
    )(blocks_in, spots_in)
    asked = lax.all_to_all(request, "blk", split_axis=0, concat_axis=0, tiled=True)
    from_left = shift(to_right, "blk", 1)
    from_right = shift(to_left, "blk", -1)

    served = pl.pallas_call(
        serve_kernel,
        out_shape=shaped((count * PIECE, lanes), bf16),
        in_specs=[vmem] * 4,
        out_specs=vmem,
        compiler_params=pltpu.CompilerParams(vmem_limit_bytes=8 * MIB),
        cost_estimate=pl.CostEstimate(
            flops=10**7, bytes_accessed=10**6, transcendentals=0
        ),
    )(asked, table, from_left, from_right)
    columns_in = lax.all_to_all(served, "blk", split_axis=0, concat_axis=0, tiled=True)

    ratios = ratios_by_height(levels, lanes)
    q, rho, side, bath, place = pl.pallas_call(
        functools.partial(start_kernel, count=count),
        out_shape=(
            pltpu.HBM((tracers, levels, rows, lanes), f32),
            pltpu.HBM((levels, rows, lanes), f32),
            pltpu.HBM((levels, columns, lanes), bf16),
            pltpu.HBM((rows, lanes), i32),
            pltpu.HBM((slots * columns, 128), i32),
        ),
        in_specs=[hbm, vmem, vmem, hbm, hbm, vmem],
        out_specs=(hbm,) * 5,
        scratch_shapes=[
            pltpu.VMEM((tracers, levels, rows, lanes), f32),
            pltpu.VMEM((levels, rows, lanes), f32),
            pltpu.VMEM((levels, columns, lanes), bf16),
            pltpu.VMEM(ocean_state.shape, f32),
            pltpu.VMEM((rows, lanes), i32),
            pltpu.VMEM((many * 8, lanes), f32),
            pltpu.VMEM(bathymetry.shape, i32),
            pltpu.VMEM(blocks.shape, i32),
            pltpu.VMEM((slots * columns, 128), i32),
            pltpu.VMEM((tall_rows, lanes), bf16),
            pltpu.VMEM((lanes, lanes), bf16),
            pltpu.SemaphoreType.DMA((pieces + 2,)),
            pltpu.SemaphoreType.DMA((3 * pieces + 2,)),
        ],
        compiler_params=pltpu.CompilerParams(vmem_limit_bytes=28 * MIB),
        cost_estimate=pl.CostEstimate(
            flops=60 * levels * cells, bytes_accessed=200 * levels * cells, transcendentals=0
        ),
    )(
        in_hbm(ocean_state),
        from_left,
        from_right,
        in_hbm(bathymetry),
        in_hbm(blocks),
        ratios,
    )

    mine = pl.pallas_call(
        remap_kernel,
        out_shape=shaped((6, rows, lanes), f32),
        in_specs=[vmem, hbm, vmem, vmem, hbm, hbm],
        out_specs=vmem,
        scratch_shapes=[
            pltpu.VMEM((slots, rows * 8, lanes), f32),
            pltpu.VMEM((rows * 8, lanes), f32),
            pltpu.VMEM(weights.shape, bf16),
            pltpu.VMEM(fields.shape, bf16),
            pltpu.VMEM((slots * columns, 128), i32),
            pltpu.SemaphoreType.DMA((2 + columns // 4,)),
        ],
        compiler_params=pltpu.CompilerParams(vmem_limit_bytes=20 * MIB),
        cost_estimate=pl.CostEstimate(
            flops=16 * weights.size, bytes_accessed=2 * weights.size, transcendentals=0
        ),
    )(
        columns_in,
        in_hbm(place),
        from_left,
        from_right,
        in_hbm(weights),
        in_hbm(fields),
    )
    other = lax.ppermute(mine, "sec", [(0, 1), (1, 0)])

    surface, result = pl.pallas_call(
        finish_kernel,
        out_shape=(shaped((3, columns, lanes), f32), shaped(ocean_state.shape, f32)),
        in_specs=[smem] + [vmem] * 6 + [hbm],
        out_specs=(vmem, hbm),
        scratch_shapes=[
            pltpu.VMEM(ocean_state.shape, f32),
            pltpu.VMEM((tracers, levels, tall_rows, lanes), bf16),
            pltpu.VMEM(ocean_state.shape, f32),
            pltpu.VMEM(ocean_state.shape, f32),
            pltpu.VMEM((tall_rows, lanes), bf16),
            pltpu.VMEM((lanes, lanes), bf16),
            pltpu.SemaphoreType.DMA((tracers * pieces,)),
            pltpu.SemaphoreType.DMA((tracers * pieces,)),
        ],
        compiler_params=pltpu.CompilerParams(vmem_limit_bytes=26 * MIB),
        cost_estimate=pl.CostEstimate(
            flops=60 * levels * cells, bytes_accessed=32 * levels * cells, transcendentals=0
        ),
    )(
        section,
        mine,
        other,
        in_vmem(bath),
        in_vmem(q),
        in_vmem(rho),
        in_vmem(side),
        in_hbm(ocean_state),
    )
    return (surface[None], result)


def solution(mesh):
    return jax.shard_map(
        per_device,
        mesh=mesh,
        in_specs=(
            P("sec", None, "blk", None),
            P("sec", "blk", None),
            P("sec", "blk", None),
            P("sec", "blk", None, None, None),
            P(None, None, "blk", None),
            P("blk", None),
        ),
        out_specs=(P("sec", None, "blk", None), P(None, None, "blk", None)),
        check_vma=False,
    )
```

```python
import functools

import jax
import jax.numpy as jnp
import numpy as np
from jax import lax
from jax.experimental import pallas as pl
from jax.experimental.pallas import tpu as pltpu
from jax.sharding import PartitionSpec as P

FLUX_GAIN = 0.5
SIDE_MIX = 0.2
TOP_MIX = 1.0
DEEP_MIX = 2.0
SCALE = 1.0 / (0.5 * SIDE_MIX)

MOST = 16
SLOTS = MOST + 2
FIELDS = 3
PIECE = 56
EDGE = 8
EXTRA = 16
MIB = 2**20
bf16, f32, i32 = jnp.bfloat16, jnp.float32, jnp.int32


def iota(shape, axis):
    return lax.broadcasted_iota(i32, shape, axis)


def adjacency(across, band, used):
    row, other = iota(across.shape, 0), iota(across.shape, 1)
    near = (row - other == 1) | (other - row == 1)
    near = near | ((row == 0) & (other == used - 1)) | ((row == used - 1) & (other == 0))
    across[...] = jnp.where(near & (row < used) & (other < used), 1.0, 0.0).astype(bf16)
    apart = iota(band.shape, 0) - iota(band.shape, 1)
    band[...] = jnp.where(jnp.abs(apart) == 1, 1.0, 0.0).astype(bf16)


def rounded(h):
    rows = -h.shape[0] % 16
    if rows:
        h = jnp.concatenate([h, jnp.zeros((rows, h.shape[1]), h.dtype)], axis=0)
    return h.astype(bf16)


def neighbour_sum(h, across, band, rows):
    tall, lanes = h.shape
    left = jnp.concatenate([across[pl.ds(0, rows), :], h[:rows]], axis=1)
    gap = jnp.zeros((across.shape[1] - tall, lanes), bf16)
    right = jnp.concatenate([h, gap, band[...]], axis=0)
    return jnp.dot(left, right, preferred_element_type=f32)


def edge_tile(right, left):
    row = iota((EDGE, right.shape[1]), 0)
    return jnp.where(row == 0, right, jnp.where(row == EDGE - 1, left, 0.0))


def chunks_of(levels):
    size = 10 if levels % 10 == 0 else levels
    return [(start, size) for start in range(0, levels, size)]


def sweep(count, body, carry):
    for step in range(count):
        carry = body(step, carry)
    return carry


def ranks(blocks, count):
    slots, columns = blocks.shape
    before = jnp.where(iota((columns, columns), 0) < iota((columns, columns), 1), 1.0, 0.0)
    before = before.astype(bf16)
    used = jnp.zeros((count, 1), f32)
    result = []
    for k in range(slots):
        owner = iota((count, columns), 0) == blocks[k : k + 1, :]
        one_hot = jnp.where(owner, 1.0, 0.0)
        earlier = used + jnp.dot(one_hot.astype(bf16), before, preferred_element_type=f32)
        rank = jnp.sum(one_hot * earlier, axis=0, keepdims=True)
        used = used + jnp.sum(one_hot, axis=1, keepdims=True)
        result.append((owner, rank))
    return result


def ask_kernel(blocks, spots, request):
    count, columns = request.shape[0], blocks.shape[1]
    place = iota((128, columns), 0)
    field = place // SLOTS
    slot = jnp.where(field < FIELDS, place - field * SLOTS, -1)
    here = iota((128, columns), 1)
    marks = ((slot == MOST) & (here == 0)) | ((slot == MOST + 1) & (here == columns - 1))
    asked = jnp.zeros(request.shape, f32)
    for k, (owner, rank) in enumerate(ranks(blocks, count)):
        filled = jnp.where((slot == rank.astype(i32)) | marks, 1.0, 0.0).astype(bf16)
        named = jnp.where(owner, spots[k : k + 1, :].astype(f32), 0.0).astype(bf16)
        asked = asked + lax.dot_general(
            named, filled, (((1,), (1,)), ((), ())), preferred_element_type=f32
        )
    request[...] = asked.astype(i32) + (iota(request.shape, 1) // SLOTS) * columns


def pack_kernel(
    section, state, bath, fields, blocks, spots, weights,
    to_left, to_right, table, blocks_in, spots_in,
    low, high, surface, bath_in, fields_in, extra, sems,
):
    tracers, levels, columns, lanes = state.shape
    slots = blocks.shape[0]
    many = tracers * levels
    wide = to_left.shape[0] - 2 * many - EXTRA
    below = pl.ds(2 * many + EXTRA, wide)
    pairs = [
        (state.at[:, :, pl.ds(0, 8)], low),
        (state.at[:, :, pl.ds(columns - 8, 8)], high),
        (blocks, blocks_in),
        (bath, bath_in),
        (fields, fields_in),
        (state.at[:, 0], surface),
        (weights.at[pl.ds(0, wide)], to_left.at[below]),
        (weights.at[pl.ds((columns - 1) * wide, wide)], to_right.at[below]),
        (spots, spots_in),
    ]
    copies = [pltpu.make_async_copy(src, dst, sems.at[n]) for n, (src, dst) in enumerate(pairs)]
    for copy in copies:
        copy.start()
    for copy in copies[2:6]:
        copy.wait()
    for out, first, at in ((to_left, 0, 0), (to_right, columns - 2, columns - 1)):
        extra[...] = jnp.zeros_like(extra)
        extra[0:2] = bath_in[first : first + 2].astype(f32)
        for f in range(3):
            extra[2 + f : 3 + f] = fields_in[f].astype(f32)[at : at + 1]
        extra[8 : 8 + slots] = jnp.broadcast_to(
            blocks_in[:, at : at + 1].astype(f32), (slots, lanes)
        )
        out[pl.ds(2 * many, EXTRA)] = extra[...].astype(bf16)
    on_ocean = section[0] == 1
    for f in range(3):
        own = fields_in[f]
        if f < 2:
            own = jnp.where(on_ocean, surface[f], own.astype(f32)).astype(bf16)
        table[f * columns : (f + 1) * columns, :] = own
    copies[0].wait()
    copies[1].wait()
    for c in range(2):
        for n in range(tracers):
            part = pl.ds(c * many + n * levels, levels)
            tiles = low.at[n].reshape(levels * 8, lanes)
            to_left[part] = tiles[pl.ds(c, levels, stride=8), :].astype(bf16)
            tiles = high.at[n].reshape(levels * 8, lanes)
            to_right[part] = tiles[pl.ds(6 + c, levels, stride=8), :].astype(bf16)
    for copy in copies[6:]:
        copy.wait()


def serve_kernel(asked, table, from_left, from_right, out):
    count = asked.shape[0]
    height = table.shape[0]
    request = asked[...].astype(f32)
    slot = lax.rem(iota(request.shape, 1), SLOTS)
    request = jnp.where(
        slot == MOST,
        pltpu.roll(request, count - 1, 0),
        jnp.where(slot == MOST + 1, pltpu.roll(request, 1, 0), request),
    )
    wanted = jnp.transpose(request)[:PIECE].astype(i32)
    parts = []
    for e in range(count):
        here = iota((PIECE, height), 1) == wanted[:, e : e + 1]
        parts.append(jnp.where(here, 1.0, 0.0))
    chosen = jnp.concatenate(parts, axis=0).astype(bf16)
    out[...] = jnp.dot(chosen, table[...], preferred_element_type=f32).astype(bf16)


def start_kernel(
    state, from_left, from_right, bath, blocks, ratios,
    q_result, side_result, bath_result, place_result,
    q_out, side_out, held, bath_out, halo, bath_in, blocks_in, place, across, band,
    sems, sems_out, *, count,
):
    tracers, levels, columns, lanes = state.shape
    rows = columns + EDGE
    many = tracers * levels
    chunks = chunks_of(levels)
    copies = []
    for n, (low, size) in enumerate(chunks):
        copies.append(
            pltpu.make_async_copy(
                state.at[:, pl.ds(low, size)], held.at[:, pl.ds(low, size)], sems.at[n]
            )
        )
    bath_copy = pltpu.make_async_copy(bath, bath_in, sems.at[len(chunks)])
    blocks_copy = pltpu.make_async_copy(blocks, blocks_in, sems.at[len(chunks) + 1])
    blocks_copy.start()
    bath_copy.start()
    for copy in reversed(copies):
        copy.start()
    leaving = []

    def send(source, target, number):
        copy = pltpu.make_async_copy(source, target, sems_out.at[number])
        copy.start()
        leaving.append(copy)

    halo[...] = jnp.zeros_like(halo)
    for c in range(2):
        part = pl.ds(c * many, many)
        halo[pl.ds(c, many, stride=8), :] = from_right[part].astype(f32)
        halo[pl.ds(EDGE - 2 + c, many, stride=8), :] = from_left[part].astype(f32)
    right = from_right[pl.ds(2 * many, EXTRA)].astype(f32)
    left = from_left[pl.ds(2 * many, EXTRA)].astype(f32)
    row = iota((EDGE, lanes), 0)
    edge = jnp.where(
        row == 0,
        right[0:1],
        jnp.where(
            row == 1,
            right[1:2],
            jnp.where(row == EDGE - 2, left[0:1], jnp.where(row == EDGE - 1, left[1:2], 0.0)),
        ),
    )
    bath_copy.wait()
    depth = jnp.concatenate([bath_in[...], edge.astype(i32)], axis=0)
    bath_out[...] = depth
    send(bath_out, bath_result, 2 * len(chunks))
    blocks_copy.wait()
    for k, (_, rank) in enumerate(ranks(blocks_in, count)):
        arrives = blocks_in[k : k + 1, :].astype(f32) * PIECE + rank
        spread = jnp.transpose(jnp.broadcast_to(arrives, (128, columns)))
        place[k * columns : (k + 1) * columns, :] = spread.astype(i32)
    send(place, place_result, 2 * len(chunks) + 1)
    adjacency(across, band, rows)

    def side(level):
        wet = level < bath_out[...]
        masked = []
        for n in range(tracers):
            spot = (n * levels + level) * 8
            full = jnp.concatenate([held[n, level], halo[pl.ds(spot, 8), :]], axis=0)
            masked.append(jnp.where(wet, full, 0.0))
        tall = across.shape[0]
        count = neighbour_sum(rounded(jnp.where(wet, 1.0, 0.0)), across, band, tall)[:rows]
        own = 0.5 * SCALE - count
        side_out[level] = own[:columns].astype(bf16)
        halves = []
        for h in masked:
            halves.append(own * h + neighbour_sum(rounded(h), across, band, tall)[:rows])
        return halves

    def deep(step, below, top):
        level = top - step
        halves = side(level)
        rho = ratio_at(ratios, bath_out[...], level)
        solved = []
        for n in range(tracers):
            q = rho * (halves[n] + below[n])
            q_out[n, level] = q
            solved.append(q)
        return tuple(solved)

    carry = tuple(jnp.zeros((rows, lanes), f32) for _ in range(tracers))
    for n in reversed(range(len(chunks))):
        low, size = chunks[n]
        copies[n].wait()
        first = max(low, 2)
        top = low + size - 1
        carry = sweep(top - first + 1, functools.partial(deep, top=top), carry)
        if n == 0:
            for level in (1, 0):
                halves = side(level)
                for m in range(tracers):
                    q_out[m, level] = halves[m]
        part = pl.ds(low, size)
        send(q_out.at[:, part], q_result.at[:, part], 2 * n)
        send(side_out.at[part], side_result.at[part], 2 * n + 1)
    for copy in leaving:
        copy.wait()


def ratio_at(ratios, depth, level):
    lookup = jnp.broadcast_to(ratios[0:1], depth.shape)
    height = jnp.maximum(depth - level, 0)
    return jnp.take_along_axis(lookup, height, axis=1, mode="promise_in_bounds")


def ratios_by_height(levels, lanes):
    values = [0.0]
    ratio = DEEP_MIX / (1.0 + DEEP_MIX)
    for _ in range(levels):
        values.append(ratio)
        ratio = DEEP_MIX / (1.0 + DEEP_MIX + DEEP_MIX - DEEP_MIX * ratio)
    values += [0.0] * (lanes - len(values))
    return jnp.broadcast_to(jnp.asarray(np.array(values, np.float32)), (8, lanes))


def remap_kernel(
    columns_in, place_from, from_left, from_right, weights, own_fields,
    out, picked, solved, held, fields_in, place, sems,
):
    fields, rows, width = out.shape[0] // 2, out.shape[1], out.shape[2]
    columns = rows - EDGE
    slots = weights.shape[0] // (columns * width)
    tall = slots * width
    many = from_left.shape[0] - tall - EXTRA
    group = 8
    place_copy = pltpu.make_async_copy(place_from, place, sems.at[0])
    fields_copy = pltpu.make_async_copy(own_fields, fields_in, sems.at[1])
    copies = []
    for n in range(columns // group):
        part = pl.ds(n * group * tall, group * tall)
        copies.append(pltpu.make_async_copy(weights.at[part], held.at[part], sems.at[2 + n]))
    for copy in [place_copy] + copies + [fields_copy]:
        copy.start()
    right = from_right[pl.ds(many, EXTRA)].astype(f32)
    left = from_left[pl.ds(many, EXTRA)].astype(f32)
    row = iota((EDGE, 1), 0)
    picked[...] = jnp.zeros_like(picked)
    place_copy.wait()
    wanted = []
    for k in range(slots):
        edge = jnp.where(
            row == 0,
            right[8 + k : 9 + k, 0:1] * PIECE + MOST,
            jnp.where(row == EDGE - 1, left[8 + k : 9 + k, 0:1] * PIECE + MOST + 1, -PIECE),
        ).astype(i32)
        wanted += [place[k * columns : (k + 1) * columns, 0:1], edge]
    wanted = jnp.concatenate(wanted, axis=0)
    spots = iota((slots * rows, columns_in.shape[0]), 1)
    for f in range(fields):
        chosen = jnp.where(spots == wanted + f * SLOTS, 1.0, 0.0).astype(bf16)
        found = jnp.dot(chosen, columns_in[...], preferred_element_type=f32)
        for k in range(slots):
            picked[k, pl.ds(f, rows, stride=8), :] = found[k * rows : (k + 1) * rows]

    def one(row, table_of):
        spot = pl.ds(row * 8, 8)
        vector = jnp.concatenate([picked[k, spot, :] for k in range(slots)], axis=1)
        matrix = jnp.concatenate([table_of(k) for k in range(slots)], axis=1)
        solved[spot, :] = lax.dot_general(
            vector.astype(bf16), matrix, (((1,), (1,)), ((), ())), preferred_element_type=f32
        )

    solved[...] = jnp.zeros_like(solved)
    below = many + EXTRA
    one(columns, lambda k: from_right[pl.ds(below + k * width, width)])
    one(rows - 1, lambda k: from_left[pl.ds(below + k * width, width)])
    for n in range(columns // group):
        copies[n].wait()
        for m in range(group):
            spot = n * group + m
            one(spot, lambda k: held[pl.ds((spot * slots + k) * width, width)])
    fields_copy.wait()
    for f in range(fields):
        out[f, pl.ds(0, columns)] = solved[pl.ds(f, columns, stride=8), :]
        out[f, pl.ds(columns, EDGE)] = solved[pl.ds(columns * 8 + f, EDGE, stride=8), :]
        out[fields + f, pl.ds(0, columns)] = fields_in[f].astype(f32)
        out[fields + f, pl.ds(columns, EDGE)] = edge_tile(
            right[2 + f : 3 + f], left[2 + f : 3 + f]
        )


def finish_kernel(
    section, mine, other, bath, q, side, ratios, state, surface, result,
    values_at, rounded_at, rho, solved, done, across, band, sems, sems_out,
):
    tracers, levels, columns, lanes = result.shape
    chunks = chunks_of(levels)
    starts = []
    for n in range(tracers):
        for low, size in chunks:
            part = pl.ds(low, size)
            starts.append(
                pltpu.make_async_copy(
                    state.at[n, part], done.at[n, part], sems.at[len(starts)]
                )
            )
            starts[-1].start()
    on_ocean = section[0] == 1
    adjacency(across, band, columns + EDGE)
    flux = [jnp.where(on_ocean, other[f], mine[f]) for f in range(3)]
    own = [jnp.where(on_ocean, mine[3 + f], other[3 + f]) for f in range(3)]
    forcing = [flux[0] + own[0], flux[1] + own[1]]
    top_mix = TOP_MIX * (1.0 + flux[2] * flux[2] + own[2] * own[2])
    depth = bath[...]
    unscale = 1.0 / (SCALE * SCALE)

    rho[2] = ratio_at(ratios, depth, 2)
    link = jnp.where(1 < depth, top_mix, 0.0)
    deeper = jnp.where(2 < depth, DEEP_MIX - DEEP_MIX * rho[2], 0.0)
    second = 1.0 / (1.0 + link + deeper)
    rho_second = link * second
    first = 1.0 / (1.0 + link - link * rho_second)

    def top_levels(n, count, halves, below, scale):
        partial = 2.0 * (halves[1] + below) * second[:count]
        source = 2.0 * halves[0] + scale * FLUX_GAIN * forcing[n][:count]
        value = (source + link[:count] * partial) * first[:count]
        below = jnp.where(1 < depth[:count], partial, 0.0) + rho_second[:count] * value
        return value, below

    def put(n, level, h):
        values_at[n, level] = h[:columns]
        rounded_at[n, level] = rounded(h)

    def half_at(n, level):
        around = neighbour_sum(rounded_at[n, level], across, band, columns)
        return side[level].astype(f32) * values_at[n, level] + around

    leaving = []
    for n in range(tracers):
        value, carry = top_levels(n, columns + EDGE, (q[n, 0], q[n, 1]), q[n, 2], SCALE)
        put(n, 0, jnp.where(0 < depth, value, 0.0))
        put(n, 1, carry)
        for level in range(2, levels):
            if n == 0 and level > 2:
                rho[level] = ratio_at(ratios, depth, level)
            carry = q[n, level] + rho[level] * carry
            put(n, level, carry)

        carry = jnp.zeros((columns, lanes), f32)
        for level in range(levels - 1, 1, -1):
            carry = rho[level, pl.ds(0, columns)] * (half_at(n, level) + carry)
            solved[n, level] = carry

        value, carry = top_levels(
            n, columns, (half_at(n, 0), half_at(n, 1)), carry, SCALE * SCALE
        )
        surface[n] = jnp.where(on_ocean, value * unscale, other[n, pl.ds(0, columns)])
        for copy in starts[n * len(chunks) : (n + 1) * len(chunks)]:
            copy.wait()
        done[n, 0] = value * unscale
        for low, size in chunks:
            for level in range(max(low, 1), low + size):
                if level > 1:
                    carry = solved[n, level] + rho[level, pl.ds(0, columns)] * carry
                wet = level < depth[:columns]
                done[n, level] = jnp.where(wet, carry * unscale, done[n, level])
            part = pl.ds(low, size)
            leaving.append(
                pltpu.make_async_copy(
                    done.at[n, part], result.at[n, part], sems_out.at[len(leaving)]
                )
            )
            leaving[-1].start()
    surface[2] = jnp.where(on_ocean, top_mix[:columns], other[2, pl.ds(0, columns)])
    for copy in leaving:
        copy.wait()


def shift(value, axis, by):
    count = lax.axis_size(axis)
    return lax.ppermute(value, axis, [(i, (i + by) % count) for i in range(count)])


def in_hbm(value):
    return pltpu.with_memory_space_constraint(value, pltpu.HBM)


def in_vmem(value):
    return pltpu.with_memory_space_constraint(value, pltpu.VMEM)


def per_device(
    surface_fields, source_blocks, source_columns, remap_weights, ocean_state, bathymetry
):
    tracers, levels, columns, lanes = ocean_state.shape
    slots = source_blocks.shape[2]
    count = lax.axis_size("blk")
    rows = columns + EDGE
    section = lax.axis_index("sec").astype(i32).reshape(1)
    fields = surface_fields[0]
    blocks = jnp.transpose(source_blocks[0])
    spots = jnp.transpose(source_columns[0])
    weights = remap_weights[0].reshape(columns * slots * lanes, lanes)
    tall = slots * lanes
    many = tracers * levels

    hbm = pl.BlockSpec(memory_space=pltpu.HBM)
    vmem = pl.BlockSpec(memory_space=pltpu.VMEM)
    smem = pl.BlockSpec(memory_space=pltpu.SMEM)
    shaped = jax.ShapeDtypeStruct
    pieces = len(chunks_of(levels))
    cells = rows * lanes
    tall_rows = rows + -rows % 16

    payload = shaped((2 * many + EXTRA + tall, lanes), bf16)
    to_left, to_right, table, blocks_in, spots_in = pl.pallas_call(
        pack_kernel,
        out_shape=(
            payload,
            payload,
            shaped((FIELDS * columns, lanes), bf16),
            shaped(blocks.shape, i32),
            shaped(spots.shape, i32),
        ),
        in_specs=[smem] + [hbm] * 6,
        out_specs=(vmem,) * 5,
        scratch_shapes=[
            pltpu.VMEM((tracers, levels, 8, lanes), f32),
            pltpu.VMEM((tracers, levels, 8, lanes), f32),
            pltpu.VMEM((tracers, columns, lanes), f32),
            pltpu.VMEM(bathymetry.shape, i32),
            pltpu.VMEM(fields.shape, bf16),
            pltpu.VMEM((EXTRA, lanes), f32),
            pltpu.SemaphoreType.DMA((9,)),
        ],
        compiler_params=pltpu.CompilerParams(vmem_limit_bytes=8 * MIB),
        cost_estimate=pl.CostEstimate(
            flops=10**6, bytes_accessed=4 * 10**6, transcendentals=0
        ),
    )(
        section,
        in_hbm(ocean_state),
        in_hbm(bathymetry),
        in_hbm(fields),
        in_hbm(blocks),
        in_hbm(spots),
        in_hbm(weights),
    )
    request = pl.pallas_call(
        ask_kernel,
        out_shape=shaped((count, 128), i32),
        in_specs=[vmem, vmem],
        out_specs=vmem,
        compiler_params=pltpu.CompilerParams(vmem_limit_bytes=4 * MIB),
        cost_estimate=pl.CostEstimate(flops=10**6, bytes_accessed=10**5, transcendentals=0),
    )(blocks_in, spots_in)
    asked = lax.all_to_all(request, "blk", split_axis=0, concat_axis=0, tiled=True)
    from_left = shift(to_right, "blk", 1)
    from_right = shift(to_left, "blk", -1)

    served = pl.pallas_call(
        serve_kernel,
        out_shape=shaped((count * PIECE, lanes), bf16),
        in_specs=[vmem] * 4,
        out_specs=vmem,
        compiler_params=pltpu.CompilerParams(vmem_limit_bytes=8 * MIB),
        cost_estimate=pl.CostEstimate(
            flops=10**7, bytes_accessed=10**6, transcendentals=0
        ),
    )(asked, table, from_left, from_right)
    columns_in = lax.all_to_all(served, "blk", split_axis=0, concat_axis=0, tiled=True)

    ratios = ratios_by_height(levels, lanes)
    q, side, bath, place = pl.pallas_call(
        functools.partial(start_kernel, count=count),
        out_shape=(
            pltpu.HBM((tracers, levels, rows, lanes), f32),
            pltpu.HBM((levels, columns, lanes), bf16),
            pltpu.HBM((rows, lanes), i32),
            pltpu.HBM((slots * columns, 128), i32),
        ),
        in_specs=[hbm, vmem, vmem, hbm, hbm, vmem],
        out_specs=(hbm,) * 4,
        scratch_shapes=[
            pltpu.VMEM((tracers, levels, rows, lanes), f32),
            pltpu.VMEM((levels, columns, lanes), bf16),
            pltpu.VMEM(ocean_state.shape, f32),
            pltpu.VMEM((rows, lanes), i32),
            pltpu.VMEM((many * 8, lanes), f32),
            pltpu.VMEM(bathymetry.shape, i32),
            pltpu.VMEM(blocks.shape, i32),
            pltpu.VMEM((slots * columns, 128), i32),
            pltpu.VMEM((tall_rows, lanes), bf16),
            pltpu.VMEM((lanes, lanes), bf16),
            pltpu.SemaphoreType.DMA((pieces + 2,)),
            pltpu.SemaphoreType.DMA((2 * pieces + 2,)),
        ],
        compiler_params=pltpu.CompilerParams(vmem_limit_bytes=28 * MIB),
        cost_estimate=pl.CostEstimate(
            flops=60 * levels * cells, bytes_accessed=200 * levels * cells, transcendentals=0
        ),
    )(
        in_hbm(ocean_state),
        from_left,
        from_right,
        in_hbm(bathymetry),
        in_hbm(blocks),
        ratios,
    )

    mine = pl.pallas_call(
        remap_kernel,
        out_shape=shaped((6, rows, lanes), f32),
        in_specs=[vmem, hbm, vmem, vmem, hbm, hbm],
        out_specs=vmem,
        scratch_shapes=[
            pltpu.VMEM((slots, rows * 8, lanes), f32),
            pltpu.VMEM((rows * 8, lanes), f32),
            pltpu.VMEM(weights.shape, bf16),
            pltpu.VMEM(fields.shape, bf16),
            pltpu.VMEM((slots * columns, 128), i32),
            pltpu.SemaphoreType.DMA((2 + columns // 8,)),
        ],
        compiler_params=pltpu.CompilerParams(vmem_limit_bytes=20 * MIB),
        cost_estimate=pl.CostEstimate(
            flops=16 * weights.size, bytes_accessed=2 * weights.size, transcendentals=0
        ),
    )(
        columns_in,
        in_hbm(place),
        from_left,
        from_right,
        in_hbm(weights),
        in_hbm(fields),
    )
    other = lax.ppermute(mine, "sec", [(0, 1), (1, 0)])

    surface, result = pl.pallas_call(
        finish_kernel,
        out_shape=(shaped((3, columns, lanes), f32), shaped(ocean_state.shape, f32)),
        in_specs=[smem] + [vmem] * 6 + [hbm],
        out_specs=(vmem, hbm),
        scratch_shapes=[
            pltpu.VMEM(ocean_state.shape, f32),
            pltpu.VMEM((tracers, levels, tall_rows, lanes), bf16),
            pltpu.VMEM((levels, rows, lanes), f32),
            pltpu.VMEM(ocean_state.shape, f32),
            pltpu.VMEM(ocean_state.shape, f32),
            pltpu.VMEM((tall_rows, lanes), bf16),
            pltpu.VMEM((lanes, lanes), bf16),
            pltpu.SemaphoreType.DMA((tracers * pieces,)),
            pltpu.SemaphoreType.DMA((tracers * pieces,)),
        ],
        compiler_params=pltpu.CompilerParams(vmem_limit_bytes=26 * MIB),
        cost_estimate=pl.CostEstimate(
            flops=60 * levels * cells, bytes_accessed=32 * levels * cells, transcendentals=0
        ),
    )(
        section,
        mine,
        other,
        in_vmem(bath),
        in_vmem(q),
        in_vmem(side),
        ratios,
        in_hbm(ocean_state),
    )
    return (surface[None], result)


def solution(mesh):
    return jax.shard_map(
        per_device,
        mesh=mesh,
        in_specs=(
            P("sec", None, "blk", None),
            P("sec", "blk", None),
            P("sec", "blk", None),
            P("sec", "blk", None, None, None),
            P(None, None, "blk", None),
            P("blk", None),
        ),
        out_specs=(P("sec", None, "blk", None), P(None, None, "blk", None)),
        check_vma=False,
    )
```

```python
import functools
import math

import jax
import jax.numpy as jnp
import numpy as np
from jax import lax
from jax.experimental import pallas as pl
from jax.experimental.pallas import tpu as pltpu
from jax.sharding import PartitionSpec as P

FLUX_GAIN = 0.5
SIDE_MIX = 0.2
TOP_MIX = 1.0
DEEP_MIX = 2.0
FIXED = (1.0 + 2.0 * DEEP_MIX - math.sqrt(1.0 + 4.0 * DEEP_MIX)) / (2.0 * DEEP_MIX)
SCALE = 1.0 / (0.5 * SIDE_MIX)

MOST = 16
SLOTS = MOST + 2
FIELDS = 3
PIECE = 56
EDGE = 8
EXTRA = 16
MIB = 2**20
bf16, f32, i32 = jnp.bfloat16, jnp.float32, jnp.int32


def iota(shape, axis):
    return lax.broadcasted_iota(i32, shape, axis)


def adjacency(across, band, used):
    row, other = iota(across.shape, 0), iota(across.shape, 1)
    near = (row - other == 1) | (other - row == 1)
    near = near | ((row == 0) & (other == used - 1)) | ((row == used - 1) & (other == 0))
    across[...] = jnp.where(near & (row < used) & (other < used), 1.0, 0.0).astype(bf16)
    apart = iota(band.shape, 0) - iota(band.shape, 1)
    band[...] = jnp.where(jnp.abs(apart) == 1, 1.0, 0.0).astype(bf16)


def rounded(h):
    rows = -h.shape[0] % 16
    if rows:
        h = jnp.concatenate([h, jnp.zeros((rows, h.shape[1]), h.dtype)], axis=0)
    return h.astype(bf16)


def neighbour_sum(h, across, band, rows):
    tall, lanes = h.shape
    left = jnp.concatenate([across[pl.ds(0, rows), :], h[:rows]], axis=1)
    gap = jnp.zeros((across.shape[1] - tall, lanes), bf16)
    right = jnp.concatenate([h, gap, band[...]], axis=0)
    return jnp.dot(left, right, preferred_element_type=f32)


def edge_tile(right, left):
    row = iota((EDGE, right.shape[1]), 0)
    return jnp.where(row == 0, right, jnp.where(row == EDGE - 1, left, 0.0))


def chunks_of(levels):
    size = 10 if levels % 10 == 0 else levels
    return [(start, size) for start in range(0, levels, size)]


def sweep(count, body, carry):
    for step in range(count):
        carry = body(step, carry)
    return carry


def ranks(blocks, count):
    slots, columns = blocks.shape
    before = jnp.where(iota((columns, columns), 0) < iota((columns, columns), 1), 1.0, 0.0)
    before = before.astype(bf16)
    used = jnp.zeros((count, 1), f32)
    result = []
    for k in range(slots):
        owner = iota((count, columns), 0) == blocks[k : k + 1, :]
        one_hot = jnp.where(owner, 1.0, 0.0)
        earlier = used + jnp.dot(one_hot.astype(bf16), before, preferred_element_type=f32)
        rank = jnp.sum(one_hot * earlier, axis=0, keepdims=True)
        used = used + jnp.sum(one_hot, axis=1, keepdims=True)
        result.append((owner, rank))
    return result


def ask_kernel(blocks, spots, request):
    count, columns = request.shape[0], blocks.shape[1]
    place = iota((128, columns), 0)
    field = place // SLOTS
    slot = jnp.where(field < FIELDS, place - field * SLOTS, -1)
    here = iota((128, columns), 1)
    marks = ((slot == MOST) & (here == 0)) | ((slot == MOST + 1) & (here == columns - 1))
    asked = jnp.zeros(request.shape, f32)
    for k, (owner, rank) in enumerate(ranks(blocks, count)):
        filled = jnp.where((slot == rank.astype(i32)) | marks, 1.0, 0.0).astype(bf16)
        named = jnp.where(owner, spots[k : k + 1, :].astype(f32), 0.0).astype(bf16)
        asked = asked + lax.dot_general(
            named, filled, (((1,), (1,)), ((), ())), preferred_element_type=f32
        )
    request[...] = asked.astype(i32) + (iota(request.shape, 1) // SLOTS) * columns


def pack_kernel(
    section, state, bath, fields, blocks, spots, weights,
    to_left, to_right, table, blocks_in, spots_in,
    low, high, surface, bath_in, fields_in, extra, sems,
):
    tracers, levels, columns, lanes = state.shape
    slots = blocks.shape[0]
    many = tracers * levels
    wide = to_left.shape[0] - 2 * many - EXTRA
    below = pl.ds(2 * many + EXTRA, wide)
    pairs = [
        (state.at[:, :, pl.ds(0, 8)], low),
        (state.at[:, :, pl.ds(columns - 8, 8)], high),
        (blocks, blocks_in),
        (bath, bath_in),
        (fields, fields_in),
        (state.at[:, 0], surface),
        (weights.at[pl.ds(0, wide)], to_left.at[below]),
        (weights.at[pl.ds((columns - 1) * wide, wide)], to_right.at[below]),
        (spots, spots_in),
    ]
    copies = [pltpu.make_async_copy(src, dst, sems.at[n]) for n, (src, dst) in enumerate(pairs)]
    for copy in copies:
        copy.start()
    for copy in copies[2:6]:
        copy.wait()
    for out, first, at in ((to_left, 0, 0), (to_right, columns - 2, columns - 1)):
        extra[...] = jnp.zeros_like(extra)
        extra[0:2] = bath_in[first : first + 2].astype(f32)
        for f in range(3):
            extra[2 + f : 3 + f] = fields_in[f].astype(f32)[at : at + 1]
        extra[8 : 8 + slots] = jnp.broadcast_to(
            blocks_in[:, at : at + 1].astype(f32), (slots, lanes)
        )
        out[pl.ds(2 * many, EXTRA)] = extra[...].astype(bf16)
    on_ocean = section[0] == 1
    for f in range(3):
        own = fields_in[f]
        if f < 2:
            own = jnp.where(on_ocean, surface[f], own.astype(f32)).astype(bf16)
        table[f * columns : (f + 1) * columns, :] = own
    copies[0].wait()
    copies[1].wait()
    for c in range(2):
        for n in range(tracers):
            part = pl.ds(c * many + n * levels, levels)
            tiles = low.at[n].reshape(levels * 8, lanes)
            to_left[part] = tiles[pl.ds(c, levels, stride=8), :].astype(bf16)
            tiles = high.at[n].reshape(levels * 8, lanes)
            to_right[part] = tiles[pl.ds(6 + c, levels, stride=8), :].astype(bf16)
    for copy in copies[6:]:
        copy.wait()


def serve_kernel(asked, table, from_left, from_right, out):
    count = asked.shape[0]
    height = table.shape[0]
    request = asked[...].astype(f32)
    slot = lax.rem(iota(request.shape, 1), SLOTS)
    request = jnp.where(
        slot == MOST,
        pltpu.roll(request, count - 1, 0),
        jnp.where(slot == MOST + 1, pltpu.roll(request, 1, 0), request),
    )
    wanted = jnp.transpose(request)[:PIECE].astype(i32)
    parts = []
    for e in range(count):
        here = iota((PIECE, height), 1) == wanted[:, e : e + 1]
        parts.append(jnp.where(here, 1.0, 0.0))
    chosen = jnp.concatenate(parts, axis=0).astype(bf16)
    out[...] = jnp.dot(chosen, table[...], preferred_element_type=f32).astype(bf16)


def start_kernel(
    state, from_left, from_right, bath, blocks, ratios,
    q_result, side_result, bath_result, place_result,
    q_out, side_out, held, bath_out, halo, bath_in, blocks_in, place, across, band,
    sems, sems_out, *, count,
):
    tracers, levels, columns, lanes = state.shape
    rows = columns + EDGE
    many = tracers * levels
    chunks = chunks_of(levels)
    copies = []
    for n, (low, size) in enumerate(chunks):
        copies.append(
            pltpu.make_async_copy(
                state.at[:, pl.ds(low, size)], held.at[:, pl.ds(low, size)], sems.at[n]
            )
        )
    bath_copy = pltpu.make_async_copy(bath, bath_in, sems.at[len(chunks)])
    blocks_copy = pltpu.make_async_copy(blocks, blocks_in, sems.at[len(chunks) + 1])
    blocks_copy.start()
    bath_copy.start()
    for copy in reversed(copies):
        copy.start()
    leaving = []

    def send(source, target, number):
        copy = pltpu.make_async_copy(source, target, sems_out.at[number])
        copy.start()
        leaving.append(copy)

    halo[...] = jnp.zeros_like(halo)
    for c in range(2):
        part = pl.ds(c * many, many)
        halo[pl.ds(c, many, stride=8), :] = from_right[part].astype(f32)
        halo[pl.ds(EDGE - 2 + c, many, stride=8), :] = from_left[part].astype(f32)
    right = from_right[pl.ds(2 * many, EXTRA)].astype(f32)
    left = from_left[pl.ds(2 * many, EXTRA)].astype(f32)
    row = iota((EDGE, lanes), 0)
    edge = jnp.where(
        row == 0,
        right[0:1],
        jnp.where(
            row == 1,
            right[1:2],
            jnp.where(row == EDGE - 2, left[0:1], jnp.where(row == EDGE - 1, left[1:2], 0.0)),
        ),
    )
    bath_copy.wait()
    depth = jnp.concatenate([bath_in[...], edge.astype(i32)], axis=0)
    bath_out[...] = depth
    send(bath_out, bath_result, 2 * len(chunks))
    blocks_copy.wait()
    for k, (_, rank) in enumerate(ranks(blocks_in, count)):
        arrives = blocks_in[k : k + 1, :].astype(f32) * PIECE + rank
        spread = jnp.transpose(jnp.broadcast_to(arrives, (128, columns)))
        place[k * columns : (k + 1) * columns, :] = spread.astype(i32)
    send(place, place_result, 2 * len(chunks) + 1)
    adjacency(across, band, rows)

    def side(level):
        wet = level < bath_out[...]
        masked = []
        for n in range(tracers):
            spot = (n * levels + level) * 8
            full = jnp.concatenate([held[n, level], halo[pl.ds(spot, 8), :]], axis=0)
            masked.append(jnp.where(wet, full, 0.0))
        tall = across.shape[0]
        count = neighbour_sum(rounded(jnp.where(wet, 1.0, 0.0)), across, band, tall)[:rows]
        own = 0.5 * SCALE - count
        side_out[level] = own[:columns].astype(bf16)
        halves = []
        for h in masked:
            halves.append(own * h + neighbour_sum(rounded(h), across, band, tall)[:rows])
        return halves

    def deep(step, below, top):
        level = top - step
        halves = side(level)
        rho = ratio_at(ratios, bath_out[...], level)
        solved = []
        for n in range(tracers):
            q = rho * (halves[n] + below[n])
            q_out[n, level] = q
            solved.append(q)
        return tuple(solved)

    carry = tuple(jnp.zeros((rows, lanes), f32) for _ in range(tracers))
    for n in reversed(range(len(chunks))):
        low, size = chunks[n]
        copies[n].wait()
        first = max(low, 2)
        top = low + size - 1
        carry = sweep(top - first + 1, functools.partial(deep, top=top), carry)
        if n == 0:
            for level in (1, 0):
                halves = side(level)
                for m in range(tracers):
                    q_out[m, level] = halves[m]
        part = pl.ds(low, size)
        send(q_out.at[:, part], q_result.at[:, part], 2 * n)
        send(side_out.at[part], side_result.at[part], 2 * n + 1)
    for copy in leaving:
        copy.wait()


def ratio_at(ratios, depth, level):
    lookup = jnp.broadcast_to(ratios[0:1], depth.shape)
    height = jnp.maximum(depth - level, 0)
    return jnp.take_along_axis(lookup, height, axis=1, mode="promise_in_bounds")


def ratios_by_height(levels, lanes):
    values = [0.0]
    ratio = DEEP_MIX / (1.0 + DEEP_MIX)
    for _ in range(levels):
        values.append(ratio)
        ratio = DEEP_MIX / (1.0 + DEEP_MIX + DEEP_MIX - DEEP_MIX * ratio)
    values += [0.0] * (lanes - len(values))
    return jnp.broadcast_to(jnp.asarray(np.array(values, np.float32)), (8, lanes))


def ratio_in_closed_form(depth, level):
    height = depth - level
    power = jnp.exp2((2.0 * math.log2(FIXED)) * height.astype(f32))
    divisor = 1.0 + FIXED * power
    inverse = pl.reciprocal(divisor, approx=True)
    scaled = ((1.0 - FIXED * FIXED) * power) * inverse
    return jnp.where(height > 0, FIXED + scaled * (2.0 - divisor * inverse), 0.0)


def remap_kernel(
    columns_in, place_from, from_left, from_right, weights, own_fields,
    out, picked, solved, held, fields_in, place, sems,
):
    fields, rows, width = out.shape[0] // 2, out.shape[1], out.shape[2]
    columns = rows - EDGE
    slots = weights.shape[0] // (columns * width)
    tall = slots * width
    many = from_left.shape[0] - tall - EXTRA
    group = 8
    place_copy = pltpu.make_async_copy(place_from, place, sems.at[0])
    fields_copy = pltpu.make_async_copy(own_fields, fields_in, sems.at[1])
    copies = []
    for n in range(columns // group):
        part = pl.ds(n * group * tall, group * tall)
        copies.append(pltpu.make_async_copy(weights.at[part], held.at[part], sems.at[2 + n]))
    for copy in [place_copy] + copies + [fields_copy]:
        copy.start()
    right = from_right[pl.ds(many, EXTRA)].astype(f32)
    left = from_left[pl.ds(many, EXTRA)].astype(f32)
    row = iota((EDGE, 1), 0)
    picked[...] = jnp.zeros_like(picked)
    place_copy.wait()
    wanted = []
    for k in range(slots):
        edge = jnp.where(
            row == 0,
            right[8 + k : 9 + k, 0:1] * PIECE + MOST,
            jnp.where(row == EDGE - 1, left[8 + k : 9 + k, 0:1] * PIECE + MOST + 1, -PIECE),
        ).astype(i32)
        wanted += [place[k * columns : (k + 1) * columns, 0:1], edge]
    wanted = jnp.concatenate(wanted, axis=0)
    spots = iota((slots * rows, columns_in.shape[0]), 1)
    for f in range(fields):
        chosen = jnp.where(spots == wanted + f * SLOTS, 1.0, 0.0).astype(bf16)
        found = jnp.dot(chosen, columns_in[...], preferred_element_type=f32)
        for k in range(slots):
            picked[k, pl.ds(f, rows, stride=8), :] = found[k * rows : (k + 1) * rows]

    def one(row, table_of):
        spot = pl.ds(row * 8, 8)
        vector = jnp.concatenate([picked[k, spot, :] for k in range(slots)], axis=1)
        matrix = jnp.concatenate([table_of(k) for k in range(slots)], axis=1)
        solved[spot, :] = lax.dot_general(
            vector.astype(bf16), matrix, (((1,), (1,)), ((), ())), preferred_element_type=f32
        )

    solved[...] = jnp.zeros_like(solved)
    below = many + EXTRA
    one(columns, lambda k: from_right[pl.ds(below + k * width, width)])
    one(rows - 1, lambda k: from_left[pl.ds(below + k * width, width)])
    for n in range(columns // group):
        copies[n].wait()
        for m in range(group):
            spot = n * group + m
            one(spot, lambda k: held[pl.ds((spot * slots + k) * width, width)])
    fields_copy.wait()
    for f in range(fields):
        out[f, pl.ds(0, columns)] = solved[pl.ds(f, columns, stride=8), :]
        out[f, pl.ds(columns, EDGE)] = solved[pl.ds(columns * 8 + f, EDGE, stride=8), :]
        out[fields + f, pl.ds(0, columns)] = fields_in[f].astype(f32)
        out[fields + f, pl.ds(columns, EDGE)] = edge_tile(
            right[2 + f : 3 + f], left[2 + f : 3 + f]
        )


def finish_kernel(
    section, mine, other, bath, q, side, state, surface, result,
    values_at, rounded_at, rho, solved, done, across, band, sems, sems_out,
):
    tracers, levels, columns, lanes = result.shape
    chunks = chunks_of(levels)
    starts = []
    for n in range(tracers):
        for low, size in chunks:
            part = pl.ds(low, size)
            starts.append(
                pltpu.make_async_copy(
                    state.at[n, part], done.at[n, part], sems.at[len(starts)]
                )
            )
            starts[-1].start()
    on_ocean = section[0] == 1
    adjacency(across, band, columns + EDGE)
    flux = [jnp.where(on_ocean, other[f], mine[f]) for f in range(3)]
    own = [jnp.where(on_ocean, mine[3 + f], other[3 + f]) for f in range(3)]
    forcing = [flux[0] + own[0], flux[1] + own[1]]
    top_mix = TOP_MIX * (1.0 + flux[2] * flux[2] + own[2] * own[2])
    depth = bath[...]
    unscale = 1.0 / (SCALE * SCALE)

    rho[2] = ratio_in_closed_form(depth, 2)
    link = jnp.where(1 < depth, top_mix, 0.0)
    deeper = jnp.where(2 < depth, DEEP_MIX - DEEP_MIX * rho[2], 0.0)
    second = 1.0 / (1.0 + link + deeper)
    rho_second = link * second
    first = 1.0 / (1.0 + link - link * rho_second)

    def top_levels(n, count, halves, below, scale):
        partial = 2.0 * (halves[1] + below) * second[:count]
        source = 2.0 * halves[0] + scale * FLUX_GAIN * forcing[n][:count]
        value = (source + link[:count] * partial) * first[:count]
        below = jnp.where(1 < depth[:count], partial, 0.0) + rho_second[:count] * value
        return value, below

    def put(n, level, h):
        values_at[n, level] = h[:columns]
        rounded_at[n, level] = rounded(h)

    def half_at(n, level):
        around = neighbour_sum(rounded_at[n, level], across, band, columns)
        return side[level].astype(f32) * values_at[n, level] + around

    leaving = []
    for n in range(tracers):
        value, carry = top_levels(n, columns + EDGE, (q[n, 0], q[n, 1]), q[n, 2], SCALE)
        put(n, 0, jnp.where(0 < depth, value, 0.0))
        put(n, 1, carry)
        for level in range(2, levels):
            if n == 0 and level > 2:
                rho[level] = ratio_in_closed_form(depth, level)
            carry = q[n, level] + rho[level] * carry
            put(n, level, carry)

        carry = jnp.zeros((columns, lanes), f32)
        for level in range(levels - 1, 1, -1):
            carry = rho[level, pl.ds(0, columns)] * (half_at(n, level) + carry)
            solved[n, level] = carry

        value, carry = top_levels(
            n, columns, (half_at(n, 0), half_at(n, 1)), carry, SCALE * SCALE
        )
        surface[n] = jnp.where(on_ocean, value * unscale, other[n, pl.ds(0, columns)])
        for copy in starts[n * len(chunks) : (n + 1) * len(chunks)]:
            copy.wait()
        done[n, 0] = value * unscale
        for low, size in chunks:
            for level in range(max(low, 1), low + size):
                if level > 1:
                    carry = solved[n, level] + rho[level, pl.ds(0, columns)] * carry
                wet = level < depth[:columns]
                done[n, level] = jnp.where(wet, carry * unscale, done[n, level])
            part = pl.ds(low, size)
            leaving.append(
                pltpu.make_async_copy(
                    done.at[n, part], result.at[n, part], sems_out.at[len(leaving)]
                )
            )
            leaving[-1].start()
    surface[2] = jnp.where(on_ocean, top_mix[:columns], other[2, pl.ds(0, columns)])
    for copy in leaving:
        copy.wait()


def shift(value, axis, by):
    count = lax.axis_size(axis)
    return lax.ppermute(value, axis, [(i, (i + by) % count) for i in range(count)])


def in_hbm(value):
    return pltpu.with_memory_space_constraint(value, pltpu.HBM)


def in_vmem(value):
    return pltpu.with_memory_space_constraint(value, pltpu.VMEM)


def per_device(
    surface_fields, source_blocks, source_columns, remap_weights, ocean_state, bathymetry
):
    tracers, levels, columns, lanes = ocean_state.shape
    slots = source_blocks.shape[2]
    count = lax.axis_size("blk")
    rows = columns + EDGE
    section = lax.axis_index("sec").astype(i32).reshape(1)
    fields = surface_fields[0]
    blocks = jnp.transpose(source_blocks[0])
    spots = jnp.transpose(source_columns[0])
    weights = remap_weights[0].reshape(columns * slots * lanes, lanes)
    tall = slots * lanes
    many = tracers * levels

    hbm = pl.BlockSpec(memory_space=pltpu.HBM)
    vmem = pl.BlockSpec(memory_space=pltpu.VMEM)
    smem = pl.BlockSpec(memory_space=pltpu.SMEM)
    shaped = jax.ShapeDtypeStruct
    pieces = len(chunks_of(levels))
    cells = rows * lanes
    tall_rows = rows + -rows % 16

    payload = shaped((2 * many + EXTRA + tall, lanes), bf16)
    to_left, to_right, table, blocks_in, spots_in = pl.pallas_call(
        pack_kernel,
        out_shape=(
            payload,
            payload,
            shaped((FIELDS * columns, lanes), bf16),
            shaped(blocks.shape, i32),
            shaped(spots.shape, i32),
        ),
        in_specs=[smem] + [hbm] * 6,
        out_specs=(vmem,) * 5,
        scratch_shapes=[
            pltpu.VMEM((tracers, levels, 8, lanes), f32),
            pltpu.VMEM((tracers, levels, 8, lanes), f32),
            pltpu.VMEM((tracers, columns, lanes), f32),
            pltpu.VMEM(bathymetry.shape, i32),
            pltpu.VMEM(fields.shape, bf16),
            pltpu.VMEM((EXTRA, lanes), f32),
            pltpu.SemaphoreType.DMA((9,)),
        ],
        compiler_params=pltpu.CompilerParams(vmem_limit_bytes=8 * MIB),
        cost_estimate=pl.CostEstimate(
            flops=10**6, bytes_accessed=4 * 10**6, transcendentals=0
        ),
    )(
        section,
        in_hbm(ocean_state),
        in_hbm(bathymetry),
        in_hbm(fields),
        in_hbm(blocks),
        in_hbm(spots),
        in_hbm(weights),
    )
    request = pl.pallas_call(
        ask_kernel,
        out_shape=shaped((count, 128), i32),
        in_specs=[vmem, vmem],
        out_specs=vmem,
        compiler_params=pltpu.CompilerParams(vmem_limit_bytes=4 * MIB),
        cost_estimate=pl.CostEstimate(flops=10**6, bytes_accessed=10**5, transcendentals=0),
    )(blocks_in, spots_in)
    asked = lax.all_to_all(request, "blk", split_axis=0, concat_axis=0, tiled=True)
    from_left = shift(to_right, "blk", 1)
    from_right = shift(to_left, "blk", -1)

    served = pl.pallas_call(
        serve_kernel,
        out_shape=shaped((count * PIECE, lanes), bf16),
        in_specs=[vmem] * 4,
        out_specs=vmem,
        compiler_params=pltpu.CompilerParams(vmem_limit_bytes=8 * MIB),
        cost_estimate=pl.CostEstimate(
            flops=10**7, bytes_accessed=10**6, transcendentals=0
        ),
    )(asked, table, from_left, from_right)
    columns_in = lax.all_to_all(served, "blk", split_axis=0, concat_axis=0, tiled=True)

    ratios = ratios_by_height(levels, lanes)
    q, side, bath, place = pl.pallas_call(
        functools.partial(start_kernel, count=count),
        out_shape=(
            pltpu.HBM((tracers, levels, rows, lanes), f32),
            pltpu.HBM((levels, columns, lanes), bf16),
            pltpu.HBM((rows, lanes), i32),
            pltpu.HBM((slots * columns, 128), i32),
        ),
        in_specs=[hbm, vmem, vmem, hbm, hbm, vmem],
        out_specs=(hbm,) * 4,
        scratch_shapes=[
            pltpu.VMEM((tracers, levels, rows, lanes), f32),
            pltpu.VMEM((levels, columns, lanes), bf16),
            pltpu.VMEM(ocean_state.shape, f32),
            pltpu.VMEM((rows, lanes), i32),
            pltpu.VMEM((many * 8, lanes), f32),
            pltpu.VMEM(bathymetry.shape, i32),
            pltpu.VMEM(blocks.shape, i32),
            pltpu.VMEM((slots * columns, 128), i32),
            pltpu.VMEM((tall_rows, lanes), bf16),
            pltpu.VMEM((lanes, lanes), bf16),
            pltpu.SemaphoreType.DMA((pieces + 2,)),
            pltpu.SemaphoreType.DMA((2 * pieces + 2,)),
        ],
        compiler_params=pltpu.CompilerParams(vmem_limit_bytes=28 * MIB),
        cost_estimate=pl.CostEstimate(
            flops=60 * levels * cells, bytes_accessed=200 * levels * cells, transcendentals=0
        ),
    )(
        in_hbm(ocean_state),
        from_left,
        from_right,
        in_hbm(bathymetry),
        in_hbm(blocks),
        ratios,
    )

    mine = pl.pallas_call(
        remap_kernel,
        out_shape=shaped((6, rows, lanes), f32),
        in_specs=[vmem, hbm, vmem, vmem, hbm, hbm],
        out_specs=vmem,
        scratch_shapes=[
            pltpu.VMEM((slots, rows * 8, lanes), f32),
            pltpu.VMEM((rows * 8, lanes), f32),
            pltpu.VMEM(weights.shape, bf16),
            pltpu.VMEM(fields.shape, bf16),
            pltpu.VMEM((slots * columns, 128), i32),
            pltpu.SemaphoreType.DMA((2 + columns // 8,)),
        ],
        compiler_params=pltpu.CompilerParams(vmem_limit_bytes=20 * MIB),
        cost_estimate=pl.CostEstimate(
            flops=16 * weights.size, bytes_accessed=2 * weights.size, transcendentals=0
        ),
    )(
        columns_in,
        in_hbm(place),
        from_left,
        from_right,
        in_hbm(weights),
        in_hbm(fields),
    )
    other = lax.ppermute(mine, "sec", [(0, 1), (1, 0)])

    surface, result = pl.pallas_call(
        finish_kernel,
        out_shape=(shaped((3, columns, lanes), f32), shaped(ocean_state.shape, f32)),
        in_specs=[smem] + [vmem] * 5 + [hbm],
        out_specs=(vmem, hbm),
        scratch_shapes=[
            pltpu.VMEM(ocean_state.shape, f32),
            pltpu.VMEM((tracers, levels, tall_rows, lanes), bf16),
            pltpu.VMEM((levels, rows, lanes), f32),
            pltpu.VMEM(ocean_state.shape, f32),
            pltpu.VMEM(ocean_state.shape, f32),
            pltpu.VMEM((tall_rows, lanes), bf16),
            pltpu.VMEM((lanes, lanes), bf16),
            pltpu.SemaphoreType.DMA((tracers * pieces,)),
            pltpu.SemaphoreType.DMA((tracers * pieces,)),
        ],
        compiler_params=pltpu.CompilerParams(vmem_limit_bytes=26 * MIB),
        cost_estimate=pl.CostEstimate(
            flops=60 * levels * cells, bytes_accessed=32 * levels * cells, transcendentals=0
        ),
    )(
        section,
        mine,
        other,
        in_vmem(bath),
        in_vmem(q),
        in_vmem(side),
        in_hbm(ocean_state),
    )
    return (surface[None], result)


def solution(mesh):
    return jax.shard_map(
        per_device,
        mesh=mesh,
        in_specs=(
            P("sec", None, "blk", None),
            P("sec", "blk", None),
            P("sec", "blk", None),
            P("sec", "blk", None, None, None),
            P(None, None, "blk", None),
            P("blk", None),
        ),
        out_specs=(P("sec", None, "blk", None), P(None, None, "blk", None)),
        check_vma=False,
    )
```
